32 devices in a mesh: section: 2 (over core), batch: 16 (over z, y, x).
Axes of the slice: x: 2, y: 2, z: 4, core: 2. Of those that a mesh axis runs over, the one named last changes fastest.
Arguments:
- features: bfloat16 [2, 16, 36, 48, 2048], P('section', 'batch'), may hold values from -6 to 6
- reduce_weight: bfloat16 [2048, 512], P('batch'), may hold values from -0.125 to 0.125
- spatial_weight: bfloat16 [3, 3, 512, 512], P(None, None, 'batch'), may hold values from -0.09375 to 0.09375
- expand_weight: bfloat16 [512, 2048], P('batch'), may hold values from -0.25 to 0.25
- bottle_gain: bfloat16 [3072], P('batch'), may hold values from 0.5 to 1.5
- bottle_shift: bfloat16 [3072], P('batch'), may hold values from -1.796875 to 1.796875
- point_weight: bfloat16 [2048, 256], P('batch'), may hold values from -0.125 to 0.125
- near_weight: bfloat16 [3, 3, 2048, 256], P(None, None, 'batch'), may hold values from -0.046875 to 0.046875
- middle_weight: bfloat16 [3, 3, 2048, 256], P(None, None, 'batch'), may hold values from -0.046875 to 0.046875
- far_weight: bfloat16 [3, 3, 2048, 256], P(None, None, 'batch'), may hold values from -0.046875 to 0.046875
- image_weight: bfloat16 [2048, 256], P('batch'), may hold values from -0.125 to 0.125
- project_weight: bfloat16 [1280, 256], P('batch'), may hold values from -0.15625 to 0.15625
- class_weight: bfloat16 [256, 32], P('batch'), may hold values from -0.75 to 0.75
- pyramid_gain: bfloat16 [1280], P('batch'), may hold values from 0.5 to 1.5
- pyramid_shift: bfloat16 [1280], P('batch'), may hold values from -1.796875 to 1.796875
- head_gain: bfloat16 [256], P('batch'), may hold values from 0.5 to 1.5
- head_shift: bfloat16 [256], P('batch'), may hold values from -1.796875 to 1.796875
- crop_masks: int32 [2, 16, 36, 48], P(None, 'batch'), may hold values from 0 to 1, as said below
- crop_tasks: int32 [2, 16], P(None, 'batch'), may hold values from 0 to 1, as said below
- pixel_labels: int32 [2, 16, 36, 48], P(None, 'batch'), may hold values from 0 to 246
- task_norms: int32 [2], replicated, may hold values from 1 to 999
Outputs:
- input_grad: float32 [2, 16, 36, 48, 2048], P('section', 'batch')
- reduce_grad: float32 [2048, 512], P('batch')
- spatial_grad: float32 [3, 3, 512, 512], P(None, None, 'batch')
- expand_grad: float32 [512, 2048], P('batch')
- bottle_gain_grad: float32 [3072], P('batch')
- bottle_shift_grad: float32 [3072], P('batch')
- point_grad: float32 [2048, 256], P('batch')
- near_grad: float32 [3, 3, 2048, 256], P(None, None, 'batch')
- middle_grad: float32 [3, 3, 2048, 256], P(None, None, 'batch')
- far_grad: float32 [3, 3, 2048, 256], P(None, None, 'batch')
- image_grad: float32 [2048, 256], P('batch')
- project_grad: float32 [1280, 256], P('batch')
- class_grad: float32 [256, 32], P('batch')
- pyramid_gain_grad: float32 [1280], P('batch')
- pyramid_shift_grad: float32 [1280], P('batch')
- head_norm_grad: float32 [2, 256], P(None, 'batch')
The draws below stay inside these ranges and needn't reach their ends.
Inputs may be any that keep to these rules, and one draw needn't show every extreme that they name: `crop_tasks`: every micro-batch holds crops of both tasks. `crop_masks`: A Cityscapes crop's valid pixels lie in its first 16 rows and 32 columns; pixel (0, 0) of every crop is valid.
All inputs are finite; a program needn't handle non-finite values.
Results may differ from the reference program's by a relative error of at most 0.035.
The reference program's roundings to bfloat16 on the way count: a program that leaves them out, or rounds other values in their place, can miss the bound.
Values may be sent and summed in bfloat16 or wider, within the bound.
No kernel may reach another device: no remote copies, remote signals or barrier semaphores. Data moves between devices by JAX's collectives and lax.ppermute only.
A program may use at most 576 MiB of HBM per device.

```python
import jax
import jax.numpy as jnp
from jax import lax

CHANNELS = 2048
NARROW = 512
BRANCH = 256
CITY_CLASSES = 19
HOME_CLASSES = 13
BOTTLE_RATE = 4
NEAR_RATE = 12
MIDDLE_RATE = 24
FAR_RATE = 36
HEIGHT = 36
BREADTH = 48
CITY_ROWS = 16
CITY_COLS = 32
CROPS_ALL = 16
MICRO = 2
CLASS_COLS = 32


def task_table(key):
    micro_keys = jax.random.split(key, MICRO)

    def one_micro(micro_key):
        count_key, order_key = jax.random.split(micro_key)
        home_count = jax.random.randint(count_key, (), 1, CROPS_ALL)
        ranking = jax.random.permutation(order_key, CROPS_ALL)
        return (ranking < home_count).astype(jnp.int32)
    return jax.vmap(one_micro)(micro_keys)


def draw_crop_tasks(key, part):
    return task_table(key)


def draw_crop_masks(key, part):
    tasks_drawn = task_table(key)
    key = jax.random.fold_in(key, 7)
    row_index = jnp.arange(HEIGHT)[:, None]
    col_index = jnp.arange(BREADTH)[None, :]
    inside_city = (row_index < CITY_ROWS) & (col_index < CITY_COLS)
    region = (tasks_drawn[:, :, None, None] == 1) | inside_city[None, None]
    kept = jax.random.randint(key, (MICRO, CROPS_ALL, HEIGHT, BREADTH), 0, 8) > 0
    corner = (row_index == 0) & (col_index == 0)
    return (region & (kept | corner[None, None])).astype(jnp.int32)


def set_ends(values, own_key, least, high):
    extent = values.shape
    spot = [jax.random.randint(jax.random.fold_in(own_key, axis), (), 0, extent[axis]) for axis in range(len(extent))]
    values = values.at[tuple(spot)].set(least)
    longest = extent.index(max(extent))
    spot[longest] = (spot[longest] + 1) % extent[longest]
    return values.at[tuple(spot)].set(high)


def levels(rng, shape, cuts, least, largest):
    loudness = 1.0
    for dim, parts in cuts:
        draws = jax.random.uniform(jax.random.fold_in(jax.random.fold_in(rng, 6), dim), (parts,), jnp.float32, least / len(cuts), largest / len(cuts))
        loudness = loudness * jnp.repeat(jnp.exp(draws), shape[dim] // parts).reshape((-1,) + (1,) * (len(shape) - 1 - dim))
    return loudness


def scatter_about(key, shape, width, limit, shards=(), dtype=jnp.bfloat16):
    values = width * jax.random.normal(key, shape, jnp.float32)
    if shards:
        values = values * levels(key, shape, shards, -0.22, 0.18)
    return jnp.clip(values, -limit, limit).astype(dtype)


def setup_inputs(seed: int = 0) -> dict:
    seeds = jax.random.split(jax.random.key(seed), 22)
    return {
        "features": scatter_about(seeds[0], (MICRO, CROPS_ALL, HEIGHT, BREADTH, CHANNELS), 1.0, 6.0, ((0, 2), (1, 16))),
        "reduce_weight": scatter_about(seeds[1], (CHANNELS, NARROW), CHANNELS ** -0.5, 0.125, ((0, 16),)),
        "spatial_weight": scatter_about(seeds[2], (3, 3, NARROW, NARROW), (9 * NARROW) ** -0.5, 0.09375, ((2, 16),)),
        "expand_weight": scatter_about(seeds[3], (NARROW, CHANNELS), NARROW ** -0.5, 0.25, ((0, 16),)),
        "bottle_gain": jnp.clip(1.0 + 0.1 * jax.random.normal(seeds[4], (2 * NARROW + CHANNELS,), jnp.float32), 0.5, 1.5).astype(jnp.bfloat16),
        "bottle_shift": scatter_about(seeds[5], (2 * NARROW + CHANNELS,), 0.3, 1.796875, ((0, 16),)),
        "point_weight": scatter_about(seeds[6], (CHANNELS, BRANCH), CHANNELS ** -0.5, 0.125, ((0, 16),)),
        "near_weight": scatter_about(seeds[7], (3, 3, CHANNELS, BRANCH), (9 * CHANNELS) ** -0.5, 0.046875, ((2, 16),)),
        "middle_weight": scatter_about(seeds[8], (3, 3, CHANNELS, BRANCH), (9 * CHANNELS) ** -0.5, 0.046875, ((2, 16),)),
        "far_weight": scatter_about(seeds[9], (3, 3, CHANNELS, BRANCH), (9 * CHANNELS) ** -0.5, 0.046875, ((2, 16),)),
        "image_weight": scatter_about(seeds[10], (CHANNELS, BRANCH), CHANNELS ** -0.5, 0.125, ((0, 16),)),
        "project_weight": scatter_about(seeds[11], (5 * BRANCH, BRANCH), (5 * BRANCH) ** -0.5, 0.15625, ((0, 16),)),
        "class_weight": scatter_about(seeds[12], (BRANCH, CLASS_COLS), (BRANCH // 4) ** -0.5, 0.75, ((0, 16),)),
        "pyramid_gain": jnp.clip(1.0 + 0.1 * jax.random.normal(seeds[13], (5 * BRANCH,), jnp.float32), 0.5, 1.5).astype(jnp.bfloat16),
        "pyramid_shift": scatter_about(seeds[14], (5 * BRANCH,), 0.3, 1.796875, ((0, 16),)),
        "head_gain": jnp.clip(1.0 + 0.1 * jax.random.normal(seeds[15], (BRANCH,), jnp.float32), 0.5, 1.5).astype(jnp.bfloat16),
        "head_shift": scatter_about(seeds[16], (BRANCH,), 0.3, 1.796875, ((0, 16),)),
        "crop_masks": draw_crop_masks(jax.random.fold_in(seeds[21], 71), 0),
        "crop_tasks": draw_crop_tasks(jax.random.fold_in(seeds[21], 71), 0),
        "pixel_labels": set_ends(jax.random.randint(seeds[19], (MICRO, CROPS_ALL, HEIGHT, BREADTH), 0, 247), jax.random.fold_in(seeds[19], 1), 0, 246).astype(jnp.int32),
        "task_norms": jax.random.randint(seeds[20], (2,), 1, 1000).astype(jnp.int32),
    }


EPSILON = 1e-05
HIGHEST = lax.Precision.HIGHEST

@jax.custom_vjp
def low(v):
    return lax.optimization_barrier(v.astype(jnp.bfloat16)).astype(jnp.float32)

@jax.custom_vjp
def low_back(v):
    return v

def low_keep(v):
    return (low(v), None)

def low_pass(kept, grad):
    return (grad,)

def back_keep(v):
    return (v, None)

def back_low(kept, grad):
    return (low(grad),)
low.defvjp(low_keep, low_pass)
low_back.defvjp(back_keep, back_low)

def tap_ranges(shift_by, length):
    return (max(0, -shift_by), length - max(0, shift_by))

def dilated(source, weight, dilation):
    height, breadth = (source.shape[1], source.shape[2])
    result = jnp.zeros(source.shape[:3] + (weight.shape[3],), jnp.float32)
    for row_tap in range(3):
        for col_tap in range(3):
            row_shift = (row_tap - 1) * dilation
            col_shift = (col_tap - 1) * dilation
            if abs(row_shift) >= height or abs(col_shift) >= breadth:
                continue
            row_start, row_stop = tap_ranges(row_shift, height)
            col_start, col_stop = tap_ranges(col_shift, breadth)
            window = source[:, row_start + row_shift:row_stop + row_shift, col_start + col_shift:col_stop + col_shift, :]
            product = jnp.einsum('nhwc,ce->nhwe', window, weight[row_tap, col_tap], precision=HIGHEST)
            result = result.at[:, row_start:row_stop, col_start:col_stop, :].add(product)
    return result

def batch_norm(values, validity, norm_gain, norm_shift):
    summed_axes = tuple(range(values.ndim - 1))
    counted = jnp.sum(validity)
    mean_value = lax.optimization_barrier(jnp.sum(values * validity, axis=summed_axes)) / counted
    square_mean = lax.optimization_barrier(jnp.sum(values * values * validity, axis=summed_axes)) / counted
    scaling = lax.rsqrt(square_mean - mean_value * mean_value + EPSILON)
    return norm_gain * ((values - mean_value) * scaling) + norm_shift

def bottleneck(source, validity, reduce_weight, spatial_weight, expand_weight, bottle_gain, bottle_shift):
    first_out = low_back(jnp.einsum('nhwc,cd->nhwd', source, reduce_weight, precision=HIGHEST))
    hidden_one = jax.nn.silu(batch_norm(first_out, validity, bottle_gain[:NARROW], bottle_shift[:NARROW]))
    second = low_back(dilated(low(validity * hidden_one), spatial_weight, BOTTLE_RATE))
    hidden_two = low(jax.nn.silu(batch_norm(second, validity, bottle_gain[NARROW:2 * NARROW], bottle_shift[NARROW:2 * NARROW])))
    third_out = low_back(jnp.einsum('nhwc,cd->nhwd', hidden_two, expand_weight, precision=HIGHEST))
    summed = batch_norm(third_out, validity, bottle_gain[2 * NARROW:], bottle_shift[2 * NARROW:]) + source
    return low(validity * jax.nn.silu(summed))

def pyramid(pyramid_in, validity, tasks_now, labels_now, weight_now, point_weight, near_weight, middle_weight, far_weight, image_weight, project_weight, class_weight, pyramid_gain, pyramid_shift, head_gain, head_shift):
    point_out = low_back(jnp.einsum('nhwc,cd->nhwd', pyramid_in, point_weight, precision=HIGHEST))
    near_out = low_back(dilated(pyramid_in, near_weight, NEAR_RATE))
    middle_out = low_back(dilated(pyramid_in, middle_weight, MIDDLE_RATE))
    far_out = low_back(dilated(pyramid_in, far_weight, FAR_RATE))
    branches = jnp.concatenate([point_out, near_out, middle_out, far_out], axis=-1)
    branch_act = jax.nn.silu(batch_norm(branches, validity, pyramid_gain[:4 * BRANCH], pyramid_shift[:4 * BRANCH]))
    crop_valid = lax.optimization_barrier(jnp.sum(validity, axis=(1, 2)))
    pooled = low(lax.optimization_barrier(jnp.sum(pyramid_in, axis=(1, 2))) / crop_valid)
    image_out = jnp.dot(pooled, image_weight, precision=HIGHEST)
    image_act = jax.nn.silu(batch_norm(image_out, jnp.ones_like(crop_valid), pyramid_gain[4 * BRANCH:], pyramid_shift[4 * BRANCH:]))
    spread_image = jnp.broadcast_to(image_act[:, None, None, :], branch_act.shape[:3] + (BRANCH,))
    joined = low(jnp.concatenate([branch_act, spread_image], axis=-1))
    projected = low_back(jnp.einsum('nhwc,cd->nhwd', joined, project_weight, precision=HIGHEST))
    output_act = low(jax.nn.silu(batch_norm(projected, validity, head_gain, head_shift)))
    logits = low_back(jnp.einsum('nhwc,cd->nhwd', output_act, class_weight, precision=HIGHEST))
    columns = jnp.arange(CLASS_COLS)
    column_task = (columns >= CITY_CLASSES).astype(jnp.int32)
    allowed = column_task == tasks_now[:, None, None, None]
    masked = jnp.where(allowed, logits, -1e+30)
    row_peak = lax.optimization_barrier(jnp.max(masked, axis=-1, keepdims=True))
    log_total = row_peak[..., 0] + jnp.log(lax.optimization_barrier(jnp.sum(jnp.exp(masked - row_peak), axis=-1)))
    target = jnp.where(tasks_now[:, None, None] == 0, labels_now % CITY_CLASSES, CITY_CLASSES + labels_now % HOME_CLASSES)
    picked = lax.optimization_barrier(jnp.sum(jnp.where(columns == target[..., None], logits, 0.0), axis=-1))
    return jnp.sum(validity[..., 0] * weight_now * (log_total - picked))

def reference(features, reduce_weight, spatial_weight, expand_weight, bottle_gain, bottle_shift, point_weight, near_weight, middle_weight, far_weight, image_weight, project_weight, class_weight, pyramid_gain, pyramid_shift, head_gain, head_shift, crop_masks, crop_tasks, pixel_labels, task_norms):
    validity = crop_masks.astype(jnp.float32)[..., None]
    inverse = 1.0 / task_norms.astype(jnp.float32)
    task_share = inverse / jnp.sum(inverse)
    home_crop = (crop_tasks == 1).astype(jnp.float32)
    crop_valid = lax.optimization_barrier(jnp.sum(validity, axis=(2, 3, 4)))
    city_pixels = jnp.sum(crop_valid * (1.0 - home_crop))
    home_pixels = jnp.sum(crop_valid * home_crop)
    crop_weight = jnp.where(crop_tasks == 0, task_share[0] / city_pixels, task_share[1] / home_pixels)
    params = tuple((tensor.astype(jnp.float32) for tensor in (reduce_weight, spatial_weight, expand_weight, bottle_gain, bottle_shift, point_weight, near_weight, middle_weight, far_weight, image_weight, project_weight, class_weight, pyramid_gain, pyramid_shift, head_gain, head_shift)))

    def micro_loss(source, weights, validity_now, tasks_now, labels_now, weight_now):
        block_out = bottleneck(source, validity_now, weights[0], weights[1], weights[2], weights[3], weights[4])
        return pyramid(block_out, validity_now, tasks_now, labels_now, weight_now, weights[5], weights[6], weights[7], weights[8], weights[9], weights[10], weights[11], weights[12], weights[13], weights[14], weights[15])
    checked = jax.checkpoint(micro_loss)

    def total_loss(source, weights):
        loss_sum = jnp.zeros((), jnp.float32)
        for micro_index in range(MICRO):
            loss_sum = loss_sum + checked(source[micro_index], weights, validity[micro_index], crop_tasks[micro_index], pixel_labels[micro_index], crop_weight[micro_index][:, None, None])
        return loss_sum
    loss_value, pullback = jax.vjp(total_loss, features.astype(jnp.float32), params)
    input_grad, param_grads = pullback(jnp.ones((), jnp.float32))
    head_norm_grad = jnp.stack([param_grads[14], param_grads[15]])
    return (input_grad, param_grads[0], param_grads[1], param_grads[2], param_grads[3], param_grads[4], param_grads[5], param_grads[6], param_grads[7], param_grads[8], param_grads[9], param_grads[10], param_grads[11], param_grads[12], param_grads[13], head_norm_grad)
```

```python
import functools

import jax
import jax.numpy as jnp
from jax import lax
from jax.experimental import pallas as pl
from jax.experimental.pallas import tpu as pltpu
from jax.sharding import PartitionSpec as P

CITY_CLASSES = 19
HOME_CLASSES = 13
BOTTLE_RATE = 4
NEAR_RATE = 12
MIDDLE_RATE = 24
FAR_RATE = 36
TILE = 4

EPSILON = 1e-05
FLOOR_LOGIT = -1e30
HIGHEST = lax.Precision.HIGHEST
F32 = jnp.float32
BF16 = jnp.bfloat16
VMEM_BYTES = 58 * 1024 * 1024


class Place:
    def __init__(self):
        self.size = lax.axis_size("batch")
        self.direct = self.size == 16
        self.slots = self.size if self.direct else 1
        self.outer = self.size // 4
        self.core = lax.axis_index("section")
        self.index = lax.axis_index("batch")
        self.own_outer = self.index >> 2
        self.own_y = (self.index >> 1) & 1
        self.own_x = self.index & 1
        self.order = list(range(0, self.outer, 2)) + list(range(1, self.outer, 2))
        self.evens = (self.outer + 1) // 2

    def cyclic(self, step):
        return step + jnp.where(step < 0, self.outer, 0)

    def slot_owner(self, slot):
        if not self.direct:
            return jnp.zeros((), jnp.int32)
        step = self.order[slot // 4]
        at_outer = self.cyclic(self.own_outer - step)
        at_y = self.own_y ^ ((slot // 2) % 2)
        at_x = self.own_x ^ (slot % 2)
        return (at_outer * 2 + at_y) * 2 + at_x

    def owner_slot(self, owner):
        if not self.direct:
            return jnp.zeros((), jnp.int32)
        step = self.cyclic(self.own_outer - owner // 4)
        position = (step >> 1) + (step & 1) * self.evens
        return (position * 2 + (self.own_y ^ ((owner // 2) % 2))) * 2 + (self.own_x ^ (owner % 2))

    def meta(self):
        owners = [self.slot_owner(slot) for slot in range(self.slots)]
        return jnp.stack([self.core] + owners).astype(jnp.int32)

    def shift(self, block, step):
        route = []
        for source in range(self.size):
            target_outer = (source // 4 + step) % self.outer
            route.append((source, target_outer * 4 + source % 4))
        return lax.ppermute(block, "batch", route)

    def flip(self, block, bits):
        route = [(source, source ^ bits) for source in range(self.size)]
        return lax.ppermute(block, "batch", route)

    def swap(self, block):
        return lax.ppermute(block, "section", [(0, 1), (1, 0)])

    def total(self, vector):
        if not self.direct:
            return lax.psum(vector, "batch")
        plane = (vector + self.flip(vector, 1)) + (self.flip(vector, 2) + self.flip(vector, 3))
        summed = plane
        for step in range(1, self.outer):
            summed = summed + self.shift(plane, step)
        return summed

    def gather(self, parts, after):
        block = jnp.concatenate(parts)
        if not self.direct:
            full = lax.all_gather(block, "batch")
            pieces, start = [], 0
            for part in parts:
                piece = full[:, start : start + part.shape[0]]
                pieces.append(piece.reshape(-1, block.shape[1]))
                start += part.shape[0]
            return jnp.concatenate(pieces)[None], None
        if after is not None:
            block, _ = lax.optimization_barrier((block, after))
        pieces = [block] + [self.shift(block, step) for step in range(1, self.outer)]
        even = jnp.stack(pieces[0::2])
        odd = jnp.stack(pieces[1::2])
        even_x = self.flip(even, 1)
        odd_y = self.flip(odd, 2)
        even_y = self.flip(even, 2)
        odd_x = self.flip(odd, 1)
        even_xy = self.flip(even_x, 2)
        odd_xy = self.flip(odd_y, 1)
        both = jnp.concatenate(
            [
                jnp.stack([even, even_x, even_y, even_xy], axis=1),
                jnp.stack([odd, odd_x, odd_y, odd_xy], axis=1),
            ],
            axis=0,
        )
        return both.reshape((self.size,) + block.shape), pieces[-1]

    def scatter(self, own, other, count):
        arrived = self.swap(other)
        summed = (own.astype(F32) + arrived.astype(F32)).astype(BF16)
        if not self.direct:
            cut = summed.reshape(count, self.size, -1, own.shape[2]).astype(F32)
            result = lax.psum_scatter(cut, "batch", scatter_dimension=1).reshape(-1, own.shape[2])
            return self.join(result)
        parts = summed.reshape((self.outer, 2, 2) + own.shape[1:])
        even, odd = parts[: self.evens], parts[self.evens :]

        def fold(kept, sent, bits):
            return (kept.astype(F32) + self.flip(sent, bits).astype(F32)).astype(BF16)

        even = fold(even[:, :, 0], even[:, :, 1], 1)
        odd = fold(odd[:, 0], odd[:, 1], 2)
        even = fold(even[:, 0], even[:, 1], 2)
        odd = fold(odd[:, 0], odd[:, 1], 1)
        result = even[0].astype(F32)
        for step in range(1, self.outer):
            piece = even[step // 2] if step % 2 == 0 else odd[step // 2]
            result = result + self.shift(piece, -step).astype(F32)
        return self.join(result)

    def join(self, result):
        opposite = self.swap(result)
        first = self.core == 0
        return jnp.stack([jnp.where(first, result, opposite), jnp.where(first, opposite, result)])

    def unslot(self, own):
        other = self.swap(own)
        first = self.core == 0
        both = jnp.stack([jnp.where(first, own, other), jnp.where(first, other, own)], axis=1)
        return jnp.concatenate(
            [
                lax.dynamic_slice_in_dim(both, self.owner_slot(owner), 1, axis=0)
                for owner in range(self.slots)
            ],
            axis=0,
        )

    def slot(self, full):
        size, rows, columns = full.shape
        half = columns // 2
        picked = []
        for side in (self.core, 1 - self.core):
            picked.append(
                jnp.concatenate(
                    [
                        lax.dynamic_slice(
                            full, (self.slot_owner(slot), 0, side * half), (1, rows, half)
                        )
                        for slot in range(size)
                    ],
                    axis=0,
                )
            )
        return picked[0], picked[1]

    def half(self, block):
        width = block.shape[-1] // 2
        return lax.dynamic_slice_in_dim(block, self.core * width, width, axis=block.ndim - 1)


def span(shift_by, length):
    return max(0, -shift_by), length - max(0, shift_by)


def tap_list(height, breadth, dilation):
    listed = []
    for row_tap in range(3):
        for col_tap in range(3):
            row_shift = (row_tap - 1) * dilation
            col_shift = (col_tap - 1) * dilation
            if abs(row_shift) < height and abs(col_shift) < breadth:
                listed.append((row_tap, col_tap, row_shift // TILE, col_shift // TILE))
    return listed


def row_steps(count):
    return max(step for step in (1, 2, 3, 4) if count % step == 0)


def loop_rows(count, step, body):
    if count == step:
        body(0)
    else:
        lax.fori_loop(0, count // step, lambda turn, carry: (body(turn * step), carry)[1], 0)


def assemble(meta_ref, own_ref, other_ref, weight_ref):
    size, rows, half = own_ref.shape

    def fill(left_ref, right_ref):
        for slot in range(size):
            start = pl.multiple_of(meta_ref[1 + slot] * rows, rows)
            weight_ref[pl.ds(start, rows), :half] = left_ref[slot]
            weight_ref[pl.ds(start, rows), half:] = right_ref[slot]

    @pl.when(meta_ref[0] == 0)
    def _():
        fill(own_ref, other_ref)

    @pl.when(meta_ref[0] != 0)
    def _():
        fill(other_ref, own_ref)


def center_first(step, center):
    return jnp.where(step == 0, center, jnp.where(step <= center, step - 1, step))


def ordered(taps, center):
    return [taps[center]] + [tap for place, tap in enumerate(taps) if place != center]


def forward_tap(tap, fresh, source_ref, weight, result_ref):
    tiles_i, tiles_j, pixels, channels = source_ref.shape
    columns = result_ref.shape[-1]
    shift_i, shift_j = tap
    low_i, high_i = span(shift_i, tiles_i)
    low_j, high_j = span(shift_j, tiles_j)
    step = row_steps(high_i - low_i)
    wide = high_j - low_j

    def body(at):
        window = source_ref[pl.ds(low_i + at + shift_i, step), low_j + shift_j : high_j + shift_j]
        product = jnp.dot(
            window.reshape(step * wide * pixels, channels), weight, preferred_element_type=F32
        ).reshape(step, wide, pixels, columns)
        if fresh:
            result_ref[pl.ds(low_i + at, step), low_j:high_j] = product
        else:
            result_ref[pl.ds(low_i + at, step), low_j:high_j] += product

    loop_rows(high_i - low_i, step, body)


def forward_slotted(taps, meta_ref, source_ref, own_ref, other_ref, result_ref, weight_ref):
    assemble(meta_ref, own_ref, other_ref, weight_ref)
    for place, tap in enumerate(taps):

        @pl.when(pl.program_id(0) == place)
        def _(place=place, tap=tap):
            forward_tap(tap, place == 0, source_ref, weight_ref[...], result_ref)


def forward_plain(taps, source_ref, weight_ref, result_ref):
    for place, tap in enumerate(taps):

        @pl.when(pl.program_id(0) == place)
        def _(place=place, tap=tap):
            forward_tap(tap, place == 0, source_ref, weight_ref[0], result_ref)


def params():
    return pltpu.CompilerParams(vmem_limit_bytes=VMEM_BYTES)


def whole(shape):
    return pl.BlockSpec(
        shape, lambda *_: (0,) * len(shape), pipeline_mode=pl.Buffered(buffer_count=1)
    )


def conv_slotted(source, own, other, meta, taps, center, first_tap):
    channels = source.shape[-1]
    size, _, half = own.shape
    rows = channels // size
    shifts = ordered([(tap[2], tap[3]) for tap in taps], center)
    block = pl.BlockSpec(
        (size, rows, half), lambda step, _: (0, first_tap + center_first(step, center), 0)
    )
    result_shape = source.shape[:3] + (2 * half,)
    return pl.pallas_call(
        functools.partial(forward_slotted, shifts),
        grid_spec=pltpu.PrefetchScalarGridSpec(
            num_scalar_prefetch=1,
            grid=(len(taps),),
            in_specs=[whole(source.shape), block, block],
            out_specs=whole(result_shape),
            scratch_shapes=[pltpu.VMEM((channels, 2 * half), BF16)],
        ),
        out_shape=jax.ShapeDtypeStruct(result_shape, F32),
        compiler_params=params(),
    )(meta, source, own, other)


def conv_plain(source, weight, taps, center):
    channels, columns = weight.shape[1:]
    shifts = ordered([(tap[2], tap[3]) for tap in taps], center)
    result_shape = source.shape[:3] + (columns,)
    return pl.pallas_call(
        functools.partial(forward_plain, shifts),
        grid=(len(taps),),
        in_specs=[
            whole(source.shape),
            pl.BlockSpec((1, channels, columns), lambda step: (center_first(step, center), 0, 0)),
        ],
        out_specs=whole(result_shape),
        out_shape=jax.ShapeDtypeStruct(result_shape, F32),
        compiler_params=params(),
    )(source, weight)


def backward_tap(tap, fresh, upstream, weight_chunk, result_ref):
    tiles_i, tiles_j, pixels, channels = result_ref.shape
    shift_i, shift_j = tap
    low_i, high_i = span(shift_i, tiles_i)
    low_j, high_j = span(shift_j, tiles_j)
    step = row_steps(high_i - low_i)
    wide = high_j - low_j
    piece = min(512, channels)

    def body(at):
        window = upstream(pl.ds(low_i + at, step), low_j, high_j)
        window = window.reshape(step * wide * pixels, window.shape[-1])
        for start in range(0, channels, piece):
            product = lax.dot_general(
                window,
                weight_chunk(start, piece),
                (((1,), (1,)), ((), ())),
                preferred_element_type=F32,
            ).reshape(step, wide, pixels, piece)
            place = (
                pl.ds(low_i + at + shift_i, step),
                slice(low_j + shift_j, high_j + shift_j),
                slice(None),
                slice(start, start + piece),
            )
            if fresh:
                result_ref[place] = product
            else:
                result_ref[place] += product

    loop_rows(high_i - low_i, step, body)


def backward_slotted(plan, meta_ref, up_ref, *refs):
    pairs = [(refs[2 * group], refs[2 * group + 1]) for group in range(len(plan))]
    result_ref, weight_ref, total_ref = refs[2 * len(plan) :]
    width = weight_ref.shape[1]
    step_now = pl.program_id(0)
    begun = 0
    for (own_ref, other_ref), listed in zip(pairs, plan):
        first = begun

        @pl.when((step_now >= first) & (step_now < first + len(listed)))
        def _(own_ref=own_ref, other_ref=other_ref):
            assemble(meta_ref, own_ref, other_ref, weight_ref)

        for place, (tap, column) in enumerate(listed):

            @pl.when(step_now == first + place)
            def _(tap=tap, column=column, fresh=first + place == 0):
                backward_tap(
                    tap,
                    fresh,
                    lambda rows, low, high: up_ref[rows, low:high, :, column : column + width],
                    lambda start, piece: weight_ref[start : start + piece, :],
                    total_ref,
                )

        begun += len(listed)

    @pl.when(step_now == begun - 1)
    def _():
        result_ref[...] = total_ref[...].astype(result_ref.dtype)


def conv_back_slotted(upstream, groups, meta, channels):
    size, _, half = groups[0][0].shape
    rows = channels // size
    plan, arrays, specs, begun = [], [], [], 0
    for own, other, taps, center, columns in groups:
        shifts = ordered([((tap[2], tap[3]), column) for tap, column in zip(taps, columns)], center)
        plan.append(shifts)
        count = len(shifts)

        def index(step, _, first=begun, count=count, center=center):
            return (0, center_first(jnp.clip(step - first, 0, count - 1), center), 0)

        block = pl.BlockSpec((size, rows, half), index)
        arrays += [own, other]
        specs += [block, block]
        begun += count
    result_shape = upstream.shape[:3] + (channels,)
    return pl.pallas_call(
        functools.partial(backward_slotted, plan),
        grid_spec=pltpu.PrefetchScalarGridSpec(
            num_scalar_prefetch=1,
            grid=(begun,),
            in_specs=[whole(upstream.shape)] + specs,
            out_specs=whole(result_shape),
            scratch_shapes=[pltpu.VMEM((channels, 2 * half), BF16), pltpu.VMEM(result_shape, F32)],
        ),
        out_shape=jax.ShapeDtypeStruct(result_shape, BF16),
        compiler_params=params(),
    )(meta, upstream, *arrays)


def backward_plain(taps, up_ref, weight_ref, result_ref):
    for place, tap in enumerate(taps):

        @pl.when(pl.program_id(0) == place)
        def _(place=place, tap=tap):
            backward_tap(
                tap,
                place == 0,
                lambda rows, low, high: up_ref[rows, low:high],
                lambda start, piece: weight_ref[0, start : start + piece, :],
                result_ref,
            )


def conv_back_plain(upstream, weight, taps, center):
    channels, columns = weight.shape[1:]
    shifts = ordered([(tap[2], tap[3]) for tap in taps], center)
    result_shape = upstream.shape[:3] + (channels,)
    return pl.pallas_call(
        functools.partial(backward_plain, shifts),
        grid=(len(taps),),
        in_specs=[
            whole(upstream.shape),
            pl.BlockSpec((1, channels, columns), lambda step: (center_first(step, center), 0, 0)),
        ],
        out_specs=whole(result_shape),
        out_shape=jax.ShapeDtypeStruct(result_shape, F32),
        compiler_params=params(),
    )(upstream, weight)


def weight_tap(tap, tiles, flipped_ref, up_ref, padded_ref):
    tiles_i, tiles_j, pixels = tiles
    shift_i, shift_j = tap
    low_i, high_i = span(shift_i, tiles_i)
    low_j, high_j = span(shift_j, tiles_j)
    padded_ref[...] = jnp.zeros_like(padded_ref)
    wide = (high_j - low_j) * pixels
    for row in range(low_i, high_i):
        target = ((row + shift_i) * tiles_j + low_j + shift_j) * pixels
        source = (row * tiles_j + low_j) * pixels
        padded_ref[target : target + wide] = up_ref[source : source + wide]
    first = (low_i + shift_i) * tiles_j * pixels // 128 * 128
    last = -(-(high_i + shift_i) * tiles_j * pixels // 128) * 128
    return jnp.dot(
        flipped_ref[:, first:last], padded_ref[first:last], preferred_element_type=F32
    )


def weight_slotted(plan, tiles, meta_ref, flipped_ref, up_ref, own_ref, other_ref, padded_ref, full_ref):
    size, rows, half = own_ref.shape
    for place, (tap, column) in enumerate(plan):

        @pl.when(pl.program_id(0) == place)
        def _(tap=tap, column=column):
            full_ref[...] = weight_tap(
                tap, tiles, flipped_ref, up_ref.at[:, column : column + 2 * half], padded_ref
            ).astype(BF16)

    def spread(left_ref, right_ref):
        for slot in range(size):
            start = pl.multiple_of(meta_ref[1 + slot] * rows, rows)
            left_ref[slot] = full_ref[pl.ds(start, rows), :half]
            right_ref[slot] = full_ref[pl.ds(start, rows), half:]

    @pl.when(meta_ref[0] == 0)
    def _():
        spread(own_ref, other_ref)

    @pl.when(meta_ref[0] != 0)
    def _():
        spread(other_ref, own_ref)


def weight_grad_slotted(flipped, upstream, meta, taps, columns, size, tiles, width):
    channels, padded = flipped.shape
    rows = channels // size
    half = width // 2
    plan = [((tap[2], tap[3]), column) for tap, column in zip(taps, columns)]
    block = pl.BlockSpec((size, rows, half), lambda step, _: (0, step, 0))
    shape = jax.ShapeDtypeStruct((size, rows * len(taps), half), BF16)
    return pl.pallas_call(
        functools.partial(weight_slotted, plan, tiles),
        grid_spec=pltpu.PrefetchScalarGridSpec(
            num_scalar_prefetch=1,
            grid=(len(taps),),
            in_specs=[whole(flipped.shape), whole(upstream.shape)],
            out_specs=[block, block],
            scratch_shapes=[pltpu.VMEM((padded, width), BF16), pltpu.VMEM((channels, width), BF16)],
        ),
        out_shape=[shape, shape],
        compiler_params=params(),
    )(meta, flipped, upstream)


def weight_plain(plan, tiles, flipped_ref, up_ref, result_ref, padded_ref):
    for place, tap in enumerate(plan):

        @pl.when(pl.program_id(0) == place)
        def _(tap=tap):
            result_ref[0] = weight_tap(tap, tiles, flipped_ref, up_ref, padded_ref).astype(BF16)


def weight_grad_plain(flipped, upstream, taps, tiles):
    channels, padded = flipped.shape
    columns = upstream.shape[1]
    return pl.pallas_call(
        functools.partial(weight_plain, [(tap[2], tap[3]) for tap in taps], tiles),
        grid=(len(taps),),
        in_specs=[whole(flipped.shape), whole(upstream.shape)],
        out_specs=pl.BlockSpec((1, channels, columns), lambda step: (step, 0, 0)),
        scratch_shapes=[pltpu.VMEM((padded, columns), BF16)],
        out_shape=jax.ShapeDtypeStruct((len(taps), channels, columns), BF16),
        compiler_params=params(),
    )(flipped, upstream)


def flipped(values):
    pixels = values.shape[0]
    extra = -pixels % 128
    return jnp.pad(values.T, ((0, 0), (0, extra)))


def silu(values):
    return values * jax.nn.sigmoid(values)


def silu_slope(values):
    sigmoid_val = jax.nn.sigmoid(values)
    return sigmoid_val * (1.0 + values * (1.0 - sigmoid_val))


def sums(values, validity):
    weighted = values * validity
    return jnp.concatenate([jnp.sum(weighted, axis=0), jnp.sum(weighted * values, axis=0)])


def standard(totals, counted):
    first, second = jnp.split(totals, 2)
    mean_value = first / counted
    return mean_value, lax.rsqrt(second / counted - mean_value * mean_value + EPSILON)


def grad_sums(grad_pre, normed):
    return jnp.concatenate([jnp.sum(grad_pre, axis=0), jnp.sum(grad_pre * normed, axis=0)])


def through_norm(grad_pre, normed, scaling, counted, validity, gain, totals):
    total_grad, paired_grad = jnp.split(totals, 2)
    return (
        gain * scaling * (grad_pre - validity * (total_grad + normed * paired_grad) / counted)
    )


def to_tiles(array):
    height, breadth = array.shape[:2]
    rest = array.shape[2:]
    cut = array.reshape((height // TILE, TILE, breadth // TILE, TILE) + rest)
    return jnp.swapaxes(cut, 1, 2).reshape((height * breadth,) + rest)


def from_tiles(array, height, breadth):
    rest = array.shape[1:]
    cut = array.reshape((height // TILE, breadth // TILE, TILE, TILE) + rest)
    return jnp.swapaxes(cut, 1, 2).reshape((height, breadth) + rest)


def per_device(
    features,
    reduce_weight,
    spatial_weight,
    expand_weight,
    bottle_gain,
    bottle_shift,
    point_weight,
    near_weight,
    middle_weight,
    far_weight,
    image_weight,
    project_weight,
    class_weight,
    pyramid_gain,
    pyramid_shift,
    head_gain,
    head_shift,
    crop_masks,
    crop_tasks,
    pixel_labels,
    task_norms,
):
    place = Place()
    size = place.size
    core = place.core
    first_core = core == 0
    height, breadth, channels = features.shape[2:]
    pixels = height * breadth
    tiles = (height // TILE, breadth // TILE, TILE * TILE)
    narrow = reduce_weight.shape[1]
    branch = point_weight.shape[1]
    four_wide = 4 * branch
    rows = channels // size
    slots = place.slots
    slot_rows = channels // slots
    narrow_rows = narrow // size
    narrow_slot = narrow // slots
    meta = place.meta()

    bottle_taps = tap_list(height, breadth, BOTTLE_RATE)
    near_taps = tap_list(height, breadth, NEAR_RATE)
    middle_taps = tap_list(height, breadth, MIDDLE_RATE)
    far_taps = tap_list(height, breadth, FAR_RATE)

    def center_of(taps):
        return [tap[:2] for tap in taps].index((1, 1))

    def pick(weight, taps):
        if len(taps) == weight.shape[0] * weight.shape[1]:
            return weight.reshape((-1,) + weight.shape[2:])
        return jnp.stack([weight[tap[0], tap[1]] for tap in taps])

    expand_half = place.half(expand_weight)
    quarters = 2 * expand_half.shape[1] // narrow
    expand_rows = jnp.swapaxes(expand_half.reshape(narrow_rows, quarters, narrow // 2), 0, 1)

    def tap_halves(weight, taps):
        return list(place.half(pick(weight, taps)))

    reduce_own, after = place.gather([place.half(reduce_weight)], None)
    bottle_own, after = place.gather(tap_halves(spatial_weight, bottle_taps) + list(expand_rows), after)
    near_own, after = place.gather(tap_halves(near_weight, near_taps), after)
    middle_own, after = place.gather(tap_halves(middle_weight, middle_taps), after)
    wide_parts = tap_halves(far_weight, far_taps)
    wide_parts += [place.half(point_weight), place.half(project_weight)]
    far_own, after = place.gather(wide_parts, after)

    crop_valid_both = jnp.sum(crop_masks, axis=(1, 2, 3)).astype(F32)
    home_crop = (crop_tasks[:, 0] == 1).astype(F32)
    counts = jnp.concatenate(
        [
            crop_valid_both,
            jnp.sum(crop_valid_both * (1.0 - home_crop))[None],
            jnp.sum(crop_valid_both * home_crop)[None],
        ]
    )
    small = [bottle_gain, bottle_shift, pyramid_gain, pyramid_shift, head_gain, head_shift]
    small.append(class_weight.reshape(-1))
    small_widths = [part.shape[0] for part in small]
    small_own = jnp.concatenate(small).astype(F32)
    placed = lax.dynamic_update_slice(
        jnp.zeros((size, small_own.shape[0]), F32), small_own[None], (place.index, 0)
    )
    collected = place.total(jnp.concatenate([placed.reshape(-1), counts]))
    counts_all = collected[placed.size :]
    collected = collected[: placed.size].reshape(size, -1)
    small_all, start = [], 0
    for width in small_widths:
        small_all.append(collected[:, start : start + width].reshape(-1))
        start += width
    gain_bottle, shift_bottle, gain_pyramid, shift_pyramid, gain_head, shift_head = small_all[:6]
    class_full = small_all[6].reshape(size * class_weight.shape[0], -1).astype(BF16)
    counted = jnp.where(first_core, counts_all[0], counts_all[1])
    task_pixels = counts_all[2:4]

    mask = lax.dynamic_index_in_dim(crop_masks, core, 0, keepdims=False)[0]
    labels = lax.dynamic_index_in_dim(pixel_labels, core, 0, keepdims=False)[0]
    task = lax.dynamic_index_in_dim(crop_tasks, core, 0, keepdims=False)[0]
    validity = to_tiles(mask).astype(F32)[:, None]
    labels = to_tiles(labels)
    crop_valid = jnp.where(first_core, crop_valid_both[0], crop_valid_both[1])
    source = to_tiles(features[0, 0])

    reduce_full = place.unslot(reduce_own)
    reduce_full = jnp.swapaxes(reduce_full, 1, 2).reshape(channels, narrow)
    first = jnp.dot(source, reduce_full, preferred_element_type=F32)
    mean_one, scale_one = standard(place.total(sums(first, validity)), counted)
    gain_one, shift_one = gain_bottle[:narrow], shift_bottle[:narrow]
    normed_one = (first - mean_one) * scale_one
    conv_in = (silu(gain_one * normed_one + shift_one) * validity).astype(BF16)

    bottle_full = place.unslot(bottle_own)
    spatial_full = bottle_full[:, :, : len(bottle_taps) * narrow_slot].reshape(
        slots, 2, len(bottle_taps), narrow_slot, narrow // 2
    )
    spatial_full = spatial_full.transpose(2, 0, 3, 1, 4).reshape(len(bottle_taps), narrow, narrow)
    expand_full = bottle_full[:, :, len(bottle_taps) * narrow_slot :].reshape(
        slots, 2, quarters, narrow_slot, narrow // 2
    )
    expand_full = expand_full.transpose(0, 3, 1, 2, 4).reshape(narrow, channels)

    second = conv_plain(
        conv_in.reshape(tiles + (narrow,)), spatial_full, bottle_taps, center_of(bottle_taps)
    ).reshape(pixels, narrow)
    mean_two, scale_two = standard(place.total(sums(second, validity)), counted)
    gain_two, shift_two = gain_bottle[narrow : 2 * narrow], shift_bottle[narrow : 2 * narrow]
    normed_two = (second - mean_two) * scale_two
    middle_act = silu(gain_two * normed_two + shift_two).astype(BF16)

    third = jnp.dot(middle_act, expand_full, preferred_element_type=F32)
    mean_three, scale_three = standard(place.total(sums(third, validity)), counted)
    gain_three, shift_three = gain_bottle[2 * narrow :], shift_bottle[2 * narrow :]

    def summed_of(third_now):
        normed = (third_now - mean_three) * scale_three
        return normed, gain_three * normed + shift_three + source.astype(F32)

    block_out = (validity * silu(summed_of(third)[1])).astype(BF16)
    block_tiles = block_out.reshape(tiles + (channels,))
    block_flipped = flipped(block_out)

    pooled = (jnp.sum(block_out, axis=0, dtype=F32) / crop_valid).astype(BF16)
    pooled_all = place.total(
        lax.dynamic_update_slice(jnp.zeros((size, channels), BF16), pooled[None], (place.index, 0))
    )
    pooled_rows = lax.dynamic_slice_in_dim(pooled_all, place.index * rows, rows, axis=1)
    image_all = place.total(jnp.dot(pooled_rows, image_weight, preferred_element_type=F32))
    image_mean = jnp.sum(image_all, axis=0) / size
    image_scale = lax.rsqrt(
        jnp.sum(image_all * image_all, axis=0) / size - image_mean * image_mean + EPSILON
    )
    image_normed = (image_all - image_mean) * image_scale
    gain_image, shift_image = gain_pyramid[four_wide:], shift_pyramid[four_wide:]
    image_pre = gain_image * image_normed + shift_image
    image_act = silu(image_pre).astype(BF16)

    near_other = place.swap(near_own)
    middle_other = place.swap(middle_own)
    far_other = place.swap(far_own)
    wide_count = len(far_taps) + 1
    near_out = conv_slotted(block_tiles, near_own, near_other, meta, near_taps, center_of(near_taps), 0)
    middle_out = conv_slotted(
        block_tiles, middle_own, middle_other, meta, middle_taps, center_of(middle_taps), 0
    )
    far_out = conv_slotted(block_tiles, far_own, far_other, meta, far_taps, center_of(far_taps), 0)
    point_taps = [(1, 1, 0, 0)]
    point_out = conv_slotted(block_tiles, far_own, far_other, meta, point_taps, 0, len(far_taps))
    outs = [part.reshape(pixels, branch) for part in (point_out, near_out, middle_out, far_out)]
    branches = jnp.concatenate(outs, axis=1)
    mean_branch, scale_branch = standard(place.total(sums(branches, validity)), counted)
    gain_branch, shift_branch = gain_pyramid[:four_wide], shift_pyramid[:four_wide]
    normed_branch = (branches - mean_branch) * scale_branch
    pre_branch = gain_branch * normed_branch + shift_branch
    joined = silu(pre_branch).astype(BF16)

    project_rows = wide_count * slot_rows
    project_own = far_own[:, project_rows:]
    project_other = far_other[:, project_rows:]
    left = jnp.where(first_core, project_own, project_other)
    right = jnp.where(first_core, project_other, project_own)
    project_both = jnp.concatenate([left, right], axis=2)
    project_full = jnp.concatenate(
        [
            lax.dynamic_slice_in_dim(project_both, place.owner_slot(owner), 1, axis=0)
            for owner in range(slots)
        ],
        axis=0,
    ).reshape(-1, branch)

    own_act = lax.dynamic_slice_in_dim(image_act, place.index, 1, axis=0)
    crop_part = jnp.dot(own_act, project_full[four_wide:], preferred_element_type=F32)
    projected = jnp.dot(joined, project_full[:four_wide], preferred_element_type=F32) + crop_part
    mean_head, scale_head = standard(place.total(sums(projected, validity)), counted)
    normed_head = (projected - mean_head) * scale_head
    pre_head = gain_head * normed_head + shift_head
    output_act = silu(pre_head).astype(BF16)
    logits = jnp.dot(output_act, class_full, preferred_element_type=F32)

    columns = jnp.arange(class_full.shape[1])
    allowed = (columns >= CITY_CLASSES) == (task == 1)
    masked = jnp.where(allowed, logits, FLOOR_LOGIT)
    raised = jnp.exp(masked - jnp.max(masked, axis=-1, keepdims=True))
    chances = raised / jnp.sum(raised, axis=-1, keepdims=True)
    target = jnp.where(task == 0, labels % CITY_CLASSES, CITY_CLASSES + labels % HOME_CLASSES)
    chosen = (columns == target[:, None]).astype(F32)
    inverse = 1.0 / task_norms.astype(F32)
    task_share = inverse / jnp.sum(inverse)
    crop_weight = jnp.where(
        task == 0, task_share[0] / task_pixels[0], task_share[1] / task_pixels[1]
    )
    logit_grad = (crop_weight * validity * (chances - chosen)).astype(BF16)
    class_grad = lax.dot_general(
        output_act, logit_grad, (((0,), (0,)), ((), ())), preferred_element_type=F32
    )

    output_grad = lax.dot_general(
        logit_grad, class_full, (((1,), (1,)), ((), ())), preferred_element_type=F32
    )
    grad_head = output_grad * silu_slope(pre_head)
    head_totals = place.total(
        jnp.concatenate([grad_sums(grad_head, normed_head), class_grad.reshape(-1)])
    )
    class_total = head_totals[2 * branch :]
    head_totals = head_totals[: 2 * branch]
    proj_grad = through_norm(
        grad_head, normed_head, scale_head, counted, validity, gain_head, head_totals
    ).astype(BF16)
    crop_grad = jnp.sum(proj_grad, axis=0, dtype=F32)
    joined_grad = lax.dot_general(
        proj_grad, project_full[:four_wide], (((1,), (1,)), ((), ())), preferred_element_type=F32
    )
    act_grad = jnp.dot(
        project_full[four_wide:].astype(F32), crop_grad, precision=HIGHEST
    )
    own_pre = lax.dynamic_slice_in_dim(image_pre, place.index, 1, axis=0)[0]
    image_pre_grad = act_grad * silu_slope(own_pre)
    grad_branch = joined_grad * silu_slope(pre_branch)
    placed_pre = lax.dynamic_update_slice(
        jnp.zeros((size, branch), F32), image_pre_grad[None], (place.index, 0)
    )
    branch_totals = place.total(
        jnp.concatenate([grad_sums(grad_branch, normed_branch), placed_pre.reshape(-1)])
    )
    image_pre_all = branch_totals[2 * four_wide :].reshape(size, branch)
    branch_totals = branch_totals[: 2 * four_wide]
    branch_grad = through_norm(
        grad_branch, normed_branch, scale_branch, counted, validity, gain_branch, branch_totals
    ).astype(BF16)
    image_totals = grad_sums(image_pre_all, image_normed)
    image_in_all = through_norm(
        image_pre_all, image_normed, image_scale, float(size), 1.0, gain_image, image_totals
    )

    def columns_of(taps, block):
        return [block * branch] * len(taps)

    near_parts = weight_grad_slotted(
        block_flipped, branch_grad, meta, near_taps, columns_of(near_taps, 1), slots, tiles, branch
    )
    middle_parts = weight_grad_slotted(
        block_flipped, branch_grad, meta, middle_taps, columns_of(middle_taps, 2), slots, tiles, branch
    )
    wide_taps = far_taps + point_taps
    wide_columns = columns_of(far_taps, 3) + columns_of(point_taps, 0)
    far_parts = weight_grad_slotted(
        block_flipped, branch_grad, meta, wide_taps, wide_columns, slots, tiles, branch
    )
    project_grad = jnp.concatenate(
        [
            lax.dot_general(
                joined, proj_grad, (((0,), (0,)), ((), ())), preferred_element_type=F32
            ),
            own_act[0].astype(F32)[:, None] * crop_grad[None, :],
        ]
    ).astype(BF16)
    project_parts = place.slot(project_grad.reshape(slots, -1, branch))

    near_sum = place.scatter(*near_parts, len(near_taps))
    middle_sum = place.scatter(*middle_parts, len(middle_taps))
    far_sum = place.scatter(*far_parts, wide_count)
    project_sum = place.scatter(*project_parts, 1)

    image_partial = jnp.dot(pooled_rows.astype(F32).T, image_in_all, precision=HIGHEST)
    pooled_partial = lax.dot_general(
        image_in_all, image_weight.astype(F32), (((1,), (1,)), ((), ())), precision=HIGHEST
    )
    pooled_grad_all = place.total(
        lax.dynamic_update_slice(
            jnp.zeros((size, channels), F32), pooled_partial, (0, place.index * rows)
        )
    )
    pooled_grad = lax.dynamic_slice_in_dim(pooled_grad_all, place.index, 1, axis=0) / crop_valid

    groups = [
        (near_own, near_other, near_taps, center_of(near_taps), columns_of(near_taps, 1)),
        (middle_own, middle_other, middle_taps, center_of(middle_taps), columns_of(middle_taps, 2)),
        (far_own, far_other, wide_taps, center_of(far_taps), wide_columns),
    ]
    feature_grad = conv_back_slotted(
        branch_grad.reshape(tiles + (four_wide,)), groups, meta, channels
    ).reshape(pixels, channels)

    normed_three, summed = summed_of(third)
    sum_grad = (feature_grad.astype(F32) + pooled_grad) * validity * silu_slope(summed)
    three_totals = place.total(grad_sums(sum_grad, normed_three))
    third_grad = through_norm(
        sum_grad, normed_three, scale_three, counted, validity, gain_three, three_totals
    ).astype(BF16)
    expand_grad = lax.dot_general(
        middle_act, third_grad, (((0,), (0,)), ((), ())), preferred_element_type=F32
    ).astype(BF16)
    expand_parts = place.slot(expand_grad.reshape(slots, narrow_slot, channels))
    expand_sum = place.scatter(*expand_parts, 1)
    middle_grad = lax.dot_general(
        third_grad, expand_full, (((1,), (1,)), ((), ())), preferred_element_type=F32
    )
    grad_two = middle_grad * silu_slope(gain_two * normed_two + shift_two)
    two_totals = place.total(grad_sums(grad_two, normed_two))
    second_grad = through_norm(
        grad_two, normed_two, scale_two, counted, validity, gain_two, two_totals
    ).astype(BF16)
    spatial_grad = weight_grad_plain(flipped(conv_in), second_grad, bottle_taps, tiles)
    spatial_grad = jnp.swapaxes(
        spatial_grad.reshape(len(bottle_taps), slots, narrow_slot, narrow), 0, 1
    ).reshape(slots, -1, narrow)
    spatial_sum = place.scatter(*place.slot(spatial_grad), len(bottle_taps))
    conv_grad = conv_back_plain(
        second_grad.reshape(tiles + (narrow,)), spatial_full, bottle_taps, center_of(bottle_taps)
    ).reshape(pixels, narrow)
    grad_one = conv_grad * validity * silu_slope(gain_one * normed_one + shift_one)
    one_totals = place.total(grad_sums(grad_one, normed_one))
    first_grad = through_norm(
        grad_one, normed_one, scale_one, counted, validity, gain_one, one_totals
    ).astype(BF16)
    reduce_grad = lax.dot_general(
        source, first_grad, (((0,), (0,)), ((), ())), preferred_element_type=F32
    ).astype(BF16)
    reduce_sum = place.scatter(*place.slot(reduce_grad.reshape(slots, slot_rows, narrow)), 1)
    input_grad = (
        lax.dot_general(
            first_grad, reduce_full, (((1,), (1,)), ((), ())), preferred_element_type=F32
        )
        + sum_grad
    )

    vectors = [one_totals, two_totals, three_totals, branch_totals, image_totals, head_totals]
    vectors += [class_total, image_partial.reshape(-1)]
    packed = jnp.concatenate(vectors)
    packed = packed + place.swap(packed)
    split, start = [], 0
    for vector in vectors:
        split.append(packed[start : start + vector.shape[0]])
        start += vector.shape[0]
    halves = [jnp.split(vector, 2) for vector in split[:6]]

    def own_part(vector):
        length = vector.shape[0] // size
        return lax.dynamic_slice_in_dim(vector, place.index * length, length, axis=0)

    bottle_gain_grad = own_part(jnp.concatenate([halves[0][1], halves[1][1], halves[2][1]]))
    bottle_shift_grad = own_part(jnp.concatenate([halves[0][0], halves[1][0], halves[2][0]]))
    pyramid_gain_grad = own_part(jnp.concatenate([halves[3][1], halves[4][1]]))
    pyramid_shift_grad = own_part(jnp.concatenate([halves[3][0], halves[4][0]]))
    head_norm_grad = jnp.stack([own_part(halves[5][1]), own_part(halves[5][0])])
    class_out = own_part(split[6].reshape(size * class_weight.shape[0], -1))
    image_out = split[7].reshape(rows, branch)

    def taps_out(halves_sum, taps, weight):
        count = len(taps)
        inner, width = weight.shape[2], weight.shape[3]
        full = halves_sum.reshape(2, count, inner, width // 2).transpose(1, 2, 0, 3)
        full = full.reshape(count, inner, width)
        if count == weight.shape[0] * weight.shape[1]:
            return full.reshape(weight.shape)
        result = jnp.zeros(weight.shape, F32)
        for at, tap in enumerate(taps):
            result = result.at[tap[0], tap[1]].set(full[at])
        return result

    def rows_out(halves_sum):
        return jnp.concatenate([halves_sum[0], halves_sum[1]], axis=-1)

    near_out_grad = taps_out(near_sum, near_taps, near_weight)
    middle_out_grad = taps_out(middle_sum, middle_taps, middle_weight)
    far_out_grad = taps_out(far_sum[:, : len(far_taps) * rows], far_taps, far_weight)
    point_out_grad = rows_out(far_sum[:, len(far_taps) * rows :])
    return (
        from_tiles(input_grad, height, breadth)[None, None],
        rows_out(reduce_sum),
        taps_out(spatial_sum, bottle_taps, spatial_weight),
        rows_out(expand_sum),
        bottle_gain_grad,
        bottle_shift_grad,
        point_out_grad,
        near_out_grad,
        middle_out_grad,
        far_out_grad,
        image_out,
        rows_out(project_sum),
        class_out,
        pyramid_gain_grad,
        pyramid_shift_grad,
        head_norm_grad,
    )


def solution(mesh):
    in_specs = (
        P("section", "batch", None, None, None),
        P("batch", None),
        P(None, None, "batch", None),
        P("batch", None),
        P("batch"),
        P("batch"),
        P("batch", None),
        P(None, None, "batch", None),
        P(None, None, "batch", None),
        P(None, None, "batch", None),
        P("batch", None),
        P("batch", None),
        P("batch", None),
        P("batch"),
        P("batch"),
        P("batch"),
        P("batch"),
        P(None, "batch", None, None),
        P(None, "batch"),
        P(None, "batch", None, None),
        P(),
    )
    out_specs = (
        P("section", "batch", None, None, None),
        P("batch", None),
        P(None, None, "batch", None),
        P("batch", None),
        P("batch"),
        P("batch"),
        P("batch", None),
        P(None, None, "batch", None),
        P(None, None, "batch", None),
        P(None, None, "batch", None),
        P("batch", None),
        P("batch", None),
        P("batch", None),
        P("batch"),
        P("batch"),
        P(None, "batch"),
    )
    return jax.shard_map(
        per_device, mesh=mesh, in_specs=in_specs, out_specs=out_specs, check_vma=False
    )
```

```python
import functools

import jax
import jax.numpy as jnp
import numpy as np
from jax import lax
from jax.experimental import pallas as pl
from jax.experimental.pallas import tpu as pltpu
from jax.sharding import PartitionSpec as P

CITY_CLASSES = 19
HOME_CLASSES = 13
BOTTLE_RATE = 4
NEAR_RATE = 12
MIDDLE_RATE = 24
FAR_RATE = 36
TILE = 4

EPSILON = 1e-05
FLOOR_LOGIT = -1e30
HIGHEST = lax.Precision.HIGHEST
F32 = jnp.float32
BF16 = jnp.bfloat16
SLOT_BITS = [0, 4, 2, 6, 1, 5, 3, 7, 8, 12, 9, 13, 10, 14, 11, 15]
VMEM_BYTES = 58 * 1024 * 1024


class Place:
    def __init__(self):
        self.size = lax.axis_size("batch")
        self.direct = self.size == len(SLOT_BITS)
        self.slots = self.size if self.direct else 1
        self.core = lax.axis_index("section")
        self.index = lax.axis_index("batch")

    def meta(self):
        if not self.direct:
            return jnp.stack([self.core, jnp.zeros_like(self.core)]).astype(jnp.int32)
        table = [[SLOT_BITS.index(at ^ owner) for owner in range(self.size)] for at in range(self.size)]
        row = lax.dynamic_index_in_dim(jnp.array(table, jnp.int32), self.index, 0, keepdims=False)
        return jnp.concatenate([self.core[None].astype(jnp.int32), row])

    def flip(self, block, bits):
        return lax.ppermute(block, "batch", [(source, source ^ bits) for source in range(self.size)])

    def swap(self, block):
        return lax.ppermute(block, "section", [(0, 1), (1, 0)])

    def plane_total(self, vector):
        if not self.direct:
            return vector
        return (vector + self.flip(vector, 1)) + (self.flip(vector, 2) + self.flip(vector, 3))

    def line_total(self, plane):
        if not self.direct:
            return lax.psum(plane, "batch")
        return (plane + self.flip(plane, 4)) + (self.flip(plane, 8) + self.flip(plane, 12))

    def total(self, vector):
        return self.line_total(self.plane_total(vector))

    def gather(self, parts, after):
        if not self.direct:
            pieces = []
            for part, count in parts:
                width = part.shape[1] // 2
                half = lax.dynamic_slice_in_dim(part, self.core * width, width, axis=1)
                full = lax.all_gather(half.reshape(count, -1, width), "batch", axis=1, tiled=True)
                pieces.append(full.reshape(-1, width))
            return jnp.concatenate(pieces)[None], []
        block = take_half(self.core, [part for part, _ in parts], after)
        near = jnp.stack([block, self.flip(block, 4)])
        away = self.flip(near, 8)
        near_y = self.flip(near, 2)
        away_x = self.flip(away, 1)
        near = jnp.concatenate([near, near_y])
        away = jnp.concatenate([away, away_x])
        near_x = self.flip(near, 1)
        away_y = self.flip(away, 2)
        return jnp.concatenate([near, near_x, away, away_y]), [near_y, away_x]

    def join(self, result):
        opposite = self.swap(result)
        first = self.core == 0
        return jnp.stack([jnp.where(first, result, opposite), jnp.where(first, opposite, result)])


class Scatter:
    def __init__(self, place, own, other, rows):
        self.place, self.own, self.rows = place, own, rows
        self.arrived = place.swap(other)

    def add(self, kept, arrived):
        return (kept.astype(F32) + arrived.astype(F32)).astype(BF16)

    def first(self):
        if not self.place.direct:
            self.own = self.add(self.own, self.arrived)
            return
        self.kept = []
        sent = []
        for start in (0, 8):
            self.kept.append(self.add(self.own[start : start + 4], self.arrived[start : start + 4]))
            sent.append(self.add(self.own[start + 4 : start + 8], self.arrived[start + 4 : start + 8]))
        self.arrived = [self.place.flip(sent[0], 1), self.place.flip(sent[1], 2)]

    def second(self):
        if not self.place.direct:
            return
        kept, sent = [], []
        for held, came in zip(self.kept, self.arrived):
            kept.append(self.add(held[:2], came[:2]))
            sent.append(self.add(held[2:], came[2:]))
        self.kept = kept
        self.arrived = [self.place.flip(sent[0], 2), self.place.flip(sent[1], 1)]

    def third(self):
        if not self.place.direct:
            return
        near = self.kept[0].astype(F32) + self.arrived[0].astype(F32)
        away = self.kept[1].astype(F32) + self.arrived[1].astype(F32)
        self.kept = near[0]
        sent = [near[1].astype(BF16), away[0].astype(BF16), away[1].astype(BF16)]
        self.arrived = [self.place.flip(piece, bits) for piece, bits in zip(sent, (4, 8, 12))]

    def finish(self):
        if not self.place.direct:
            pieces, start = [], 0
            for rows in self.rows:
                cut = self.own[0, start : start + rows].reshape(self.place.size, -1, self.own.shape[2])
                cut = cut.astype(F32)
                pieces.append(lax.psum_scatter(cut, "batch", scatter_dimension=0))
                start += rows
            return self.place.join(jnp.concatenate(pieces))
        parts = [piece.astype(F32) for piece in self.arrived]
        return self.place.join((self.kept + parts[0]) + (parts[1] + parts[2]))


def call(body, args, specs, grid, outs, out_specs, scratch=(), meta=None, after=(), flops=0):
    used = len(args) + (meta is not None)
    waits = len(after)

    def inner(*refs):
        body(*refs[:used], *refs[used + waits :])

    spec = pltpu.PrefetchScalarGridSpec(
        num_scalar_prefetch=int(meta is not None),
        grid=grid,
        in_specs=list(specs) + [pl.BlockSpec(memory_space=pl.ANY)] * waits,
        out_specs=out_specs,
        scratch_shapes=list(scratch),
    )
    arrays = ([] if meta is None else [meta]) + list(args) + list(after)
    moved = sum(array.size * array.dtype.itemsize for array in list(args) + list(outs))
    return pl.pallas_call(
        inner,
        grid_spec=spec,
        out_shape=list(outs),
        compiler_params=pltpu.CompilerParams(vmem_limit_bytes=VMEM_BYTES),
        cost_estimate=pl.CostEstimate(flops=flops, transcendentals=0, bytes_accessed=moved),
    )(*arrays)


def whole(array):
    shape = array.shape
    return pl.BlockSpec(
        shape, lambda *_: (0,) * len(shape), pipeline_mode=pl.Buffered(buffer_count=1)
    )


def held(shape):
    return pl.BlockSpec(shape, lambda *_: (0,) * len(shape))


def rows_of(array, rows):
    return pl.BlockSpec((rows, array.shape[1]), lambda step, *_: (step, 0))


def shaped(shape, dtype=F32):
    return jax.ShapeDtypeStruct(tuple(shape), dtype)


def half_body(*refs):
    parts, result_ref = refs[1:-1], refs[-1]
    start = 0
    for part in parts:
        result_ref[start : start + part.shape[0]] = part[...]
        start += part.shape[0]


def take_half(core, parts, after):
    half = parts[0].shape[1] // 2
    rows = sum(part.shape[0] for part in parts)
    return call(
        half_body,
        parts,
        [pl.BlockSpec((part.shape[0], half), lambda step, meta: (0, meta[0])) for part in parts],
        (1,),
        [shaped((rows, half), BF16)],
        [held((rows, half))],
        meta=core[None].astype(jnp.int32),
        after=after,
    )[0]


def span(shift_by, length):
    return max(0, -shift_by), length - max(0, shift_by)


def tap_list(height, breadth, dilation):
    listed = []
    for row_tap in range(3):
        for col_tap in range(3):
            row_shift = (row_tap - 1) * dilation
            col_shift = (col_tap - 1) * dilation
            if abs(row_shift) < height and abs(col_shift) < breadth:
                listed.append((row_tap, col_tap, row_shift // TILE, col_shift // TILE))
    return listed


def row_steps(count):
    return max(step for step in (1, 2, 3, 4) if count % step == 0)


def loop_rows(count, step, body):
    if count == step:
        body(0)
    else:
        lax.fori_loop(0, count // step, lambda turn, carry: (body(turn * step), carry)[1], 0)


def by_core(meta_ref, own_ref, other_ref, body):
    @pl.when(meta_ref[0] == 0)
    def _():
        body(own_ref, other_ref)

    @pl.when(meta_ref[0] != 0)
    def _():
        body(other_ref, own_ref)


def assemble(meta_ref, own_ref, other_ref, weight_ref, first=0, count=None, column=0, apart=None):
    slots, rows, half = own_ref.shape
    apart = half if apart is None else apart
    count = slots * rows if count is None else count

    def fill(left_ref, right_ref):
        for start in range(0, count, min(rows, count)):
            if slots == 1:
                take = (0, slice(first, first + count))
            else:
                take = (meta_ref[1 + (first + start) // rows],)
            size = min(rows, count)
            weight_ref[start : start + size, column : column + half] = left_ref[take]
            weight_ref[start : start + size, column + apart : column + apart + half] = right_ref[take]

    by_core(meta_ref, own_ref, other_ref, fill)


def spread(meta_ref, full_ref, own_ref, other_ref, column=0, apart=None, at=0, rows=None):
    slots, _, half = own_ref.shape
    rows = own_ref.shape[1] if rows is None else rows
    apart = half if apart is None else apart

    def fill(left_ref, right_ref):
        for owner in range(slots):
            block = slice(owner * rows, (owner + 1) * rows)
            place = (meta_ref[1 + owner], slice(at, at + rows))
            left_ref[place] = full_ref[block, column : column + half].astype(BF16)
            right_ref[place] = full_ref[block, column + apart : column + apart + half].astype(BF16)

    by_core(meta_ref, own_ref, other_ref, fill)


def center_first(step, center):
    return jnp.where(step == 0, center, jnp.where(step <= center, step - 1, step))


def ordered(taps, center):
    return [taps[center]] + [tap for place, tap in enumerate(taps) if place != center]


def shifts_of(taps):
    return [(tap[2], tap[3]) for tap in taps]


def area(tap, tiles):
    return (tiles[0] - abs(tap[0])) * (tiles[1] - abs(tap[1])) * tiles[2]


def forward_tap(tap, fresh, source_ref, weight, result_ref):
    tiles_i, tiles_j, pixels, channels = source_ref.shape
    columns = result_ref.shape[-1]
    shift_i, shift_j = tap
    low_i, high_i = span(shift_i, tiles_i)
    low_j, high_j = span(shift_j, tiles_j)
    step = row_steps(high_i - low_i)
    wide = high_j - low_j

    def body(at):
        window = source_ref[pl.ds(low_i + at + shift_i, step), low_j + shift_j : high_j + shift_j]
        product = jnp.dot(
            window.reshape(step * wide * pixels, channels), weight, preferred_element_type=F32
        ).reshape(step, wide, pixels, columns)
        if fresh:
            result_ref[pl.ds(low_i + at, step), low_j:high_j] = product
        else:
            result_ref[pl.ds(low_i + at, step), low_j:high_j] += product

    loop_rows(high_i - low_i, step, body)


def unit_of(values, coef):
    unit = (values - coef[0:1]) * coef[1:2]
    return unit, coef[2:3] * unit + coef[3:4]


def masked_sums(values, valid):
    weighted = values * valid
    return jnp.concatenate(
        [jnp.sum(weighted, axis=0, keepdims=True), jnp.sum(weighted * values, axis=0, keepdims=True)]
    )


def sum_rows(ref, valid_ref, sums_ref):
    total = jnp.zeros(sums_ref.shape, F32)
    for row in range(ref.shape[0]):
        values = ref[row].reshape(-1, ref.shape[-1])
        total = total + masked_sums(values, valid_ref[row].reshape(-1, 1))
    sums_ref[...] = total


def branch_body(taps, meta_ref, source_ref, valid_ref, own_ref, other_ref, result_ref, sums_ref, weight_ref):
    assemble(meta_ref, own_ref, other_ref, weight_ref)
    for place, tap in enumerate(taps):

        @pl.when(pl.program_id(0) == place)
        def _(place=place, tap=tap):
            forward_tap(tap, place == 0, source_ref, weight_ref[...], result_ref)

    @pl.when(pl.program_id(0) == len(taps) - 1)
    def _():
        sum_rows(result_ref, valid_ref, sums_ref)


def branch_conv(source, valid, own, other, meta, taps, center, first_tap, after):
    channels = source.shape[-1]
    slots, _, half = own.shape
    rows = channels // slots
    shifts = ordered(shifts_of(taps), center)
    block = pl.BlockSpec(
        (slots, rows, half), lambda step, _: (0, first_tap + center_first(step, center), 0)
    )
    result_shape = source.shape[:3] + (2 * half,)
    macs = sum(area(tap, source.shape) for tap in shifts) * channels * 2 * half
    return call(
        functools.partial(branch_body, shifts),
        [source, valid, own, other],
        [whole(source), whole(valid), block, block],
        (len(taps),),
        [shaped(result_shape), shaped((2, 2 * half))],
        [held(result_shape), held((2, 2 * half))],
        [pltpu.VMEM((channels, 2 * half), BF16)],
        meta,
        after,
        2 * macs,
    )


def spatial_body(
    taps, meta_ref, first_ref, coef_ref, valid_ref, own_ref, other_ref, input_ref, result_ref, sums_ref, weight_ref
):
    @pl.when(pl.program_id(0) == 0)
    def _():
        for row in range(first_ref.shape[0]):
            _, pre = unit_of(first_ref[row], coef_ref[...][:, None, :])
            input_ref[row] = (silu(pre) * valid_ref[row]).astype(BF16)

    branch_body(
        taps, meta_ref, input_ref, valid_ref, own_ref, other_ref, result_ref, sums_ref, weight_ref
    )


def spatial_conv(first, coef, valid, own, other, meta, taps, center):
    channels = first.shape[-1]
    slots, _, half = own.shape
    rows = channels // slots
    shifts = ordered(shifts_of(taps), center)
    block = pl.BlockSpec((slots, rows, half), lambda step, _: (0, center_first(step, center), 0))
    macs = sum(area(tap, first.shape) for tap in shifts) * channels * 2 * half
    return call(
        functools.partial(spatial_body, shifts),
        [first, coef, valid, own, other],
        [whole(first), whole(coef), whole(valid), block, block],
        (len(taps),),
        [shaped(first.shape, BF16), shaped(first.shape), shaped((2, 2 * half))],
        [held(first.shape), held(first.shape), held((2, 2 * half))],
        [pltpu.VMEM((channels, 2 * half), BF16)],
        meta,
        (),
        2 * macs,
    )


def backward_tap(tap, fresh, up_ref, column, weight_ref, result_ref):
    tiles_i, tiles_j, pixels, channels = result_ref.shape
    width = weight_ref.shape[1]
    shift_i, shift_j = tap
    low_i, high_i = span(shift_i, tiles_i)
    low_j, high_j = span(shift_j, tiles_j)
    step = row_steps(high_i - low_i)
    wide = high_j - low_j
    piece = min(512, channels)

    def body(at):
        window = up_ref[pl.ds(low_i + at, step), low_j:high_j, :, column : column + width]
        window = window.reshape(step * wide * pixels, width)
        for start in range(0, channels, piece):
            product = lax.dot_general(
                window,
                weight_ref[start : start + piece, :],
                (((1,), (1,)), ((), ())),
                preferred_element_type=F32,
            ).reshape(step, wide, pixels, piece)
            place = (
                pl.ds(low_i + at + shift_i, step),
                slice(low_j + shift_j, high_j + shift_j),
                slice(None),
                slice(start, start + piece),
            )
            if fresh:
                result_ref[place] = product
            else:
                result_ref[place] += product

    loop_rows(high_i - low_i, step, body)


def grad_moments(grad, unit):
    return jnp.concatenate(
        [jnp.sum(grad, axis=0, keepdims=True), jnp.sum(grad * unit, axis=0, keepdims=True)]
    )


def feature_body(plan, first, meta_ref, up_ref, third_ref, source_ref, coef_ref, pooled_ref, valid_ref, *refs):
    pairs = [(refs[2 * group], refs[2 * group + 1]) for group in range(len(plan))]
    result_ref, sums_ref, weight_ref, total_ref = refs[2 * len(plan) :]
    step_now = pl.program_id(0)
    begun = 0
    for (own_ref, other_ref), listed in zip(pairs, plan):
        start = begun

        @pl.when((step_now >= start) & (step_now < start + len(listed)))
        def _(own_ref=own_ref, other_ref=other_ref):
            assemble(meta_ref, own_ref, other_ref, weight_ref, first, weight_ref.shape[0])

        for place, (tap, column) in enumerate(listed):

            @pl.when(step_now == start + place)
            def _(tap=tap, column=column, fresh=start + place == 0):
                backward_tap(tap, fresh, up_ref, column, weight_ref, total_ref)

        begun += len(listed)

    @pl.when(step_now >= begun)
    def _():
        row = step_now - begun
        width = total_ref.shape[-1]
        unit, pre = unit_of(third_ref[...], coef_ref[...])
        pre = pre + source_ref[...].astype(F32)
        grad = total_ref[row].reshape(-1, width) + pooled_ref[...]
        grad = grad * valid_ref[...] * silu_slope(pre)
        result_ref[...] = grad.astype(BF16)
        moments = grad_moments(grad, unit)

        @pl.when(step_now == begun)
        def _():
            sums_ref[...] = moments

        @pl.when(step_now > begun)
        def _():
            sums_ref[...] += moments


def feature_back(upstream, groups, third, source, coef, pooled, valid, meta, side, sides, after):
    channels = third.shape[1]
    part = channels // sides
    slots, _, half = groups[0][0].shape
    rows = channels // slots
    plan, arrays, specs, begun, macs = [], [], [], 0, 0
    for own, other, taps, center, columns in groups:
        shifts = ordered(list(zip(shifts_of(taps), columns)), center)
        plan.append(shifts)
        count = len(shifts)

        def index(step, _, first=begun, count=count, center=center):
            return (0, center_first(jnp.clip(step - first, 0, count - 1), center), 0)

        block = pl.BlockSpec((slots, rows, half), index)
        arrays += [own, other]
        specs += [block, block]
        begun += count
        macs += sum(area(tap, upstream.shape) for tap, _ in shifts) * part * 2 * half
    turns = upstream.shape[0]
    height = third.shape[0] // turns

    def row_index(step, _):
        return (jnp.clip(step - begun, 0, turns - 1), side)

    row_block = pl.BlockSpec((height, part), row_index)
    return call(
        functools.partial(feature_body, plan, side * part),
        [upstream, third, source, coef, pooled, valid] + arrays,
        [
            whole(upstream),
            row_block,
            row_block,
            pl.BlockSpec((coef.shape[0], part), lambda step, _: (0, side)),
            pl.BlockSpec((1, part), lambda step, _: (0, side)),
            pl.BlockSpec((height, 1), lambda step, _: (jnp.clip(step - begun, 0, turns - 1), 0)),
        ]
        + specs,
        (begun + turns,),
        [shaped((third.shape[0], part), BF16), shaped((2, part))],
        [
            pl.BlockSpec((height, part), lambda step, _: (jnp.clip(step - begun, 0, turns - 1), 0)),
            held((2, part)),
        ],
        [pltpu.VMEM((part, 2 * half), BF16), pltpu.VMEM(upstream.shape[:3] + (part,), F32)],
        meta,
        after,
        2 * macs,
    )


def spatial_back_body(
    taps, meta_ref, up_ref, first_ref, coef_ref, valid_ref, own_ref, other_ref, result_ref, sums_ref, weight_ref
):
    assemble(meta_ref, own_ref, other_ref, weight_ref)
    for place, tap in enumerate(taps):

        @pl.when(pl.program_id(0) == place)
        def _(place=place, tap=tap):
            backward_tap(tap, place == 0, up_ref, 0, weight_ref, result_ref)

    @pl.when(pl.program_id(0) == len(taps) - 1)
    def _():
        total = jnp.zeros(sums_ref.shape, F32)
        width = result_ref.shape[-1]
        for row in range(result_ref.shape[0]):
            unit, pre = unit_of(first_ref[row].reshape(-1, width), coef_ref[...])
            valid = valid_ref[row].reshape(-1, 1)
            grad = result_ref[row].reshape(-1, width) * valid * silu_slope(pre)
            result_ref[row] = grad.reshape(result_ref.shape[1:])
            total = total + grad_moments(grad, unit)
        sums_ref[...] = total


def spatial_back(upstream, first, coef, valid, own, other, meta, taps, center, after):
    channels = first.shape[-1]
    slots, _, half = own.shape
    rows = channels // slots
    shifts = ordered(shifts_of(taps), center)
    block = pl.BlockSpec((slots, rows, half), lambda step, _: (0, center_first(step, center), 0))
    macs = sum(area(tap, first.shape) for tap in shifts) * channels * 2 * half
    return call(
        functools.partial(spatial_back_body, shifts),
        [upstream, first, coef, valid, own, other],
        [whole(upstream), whole(first), whole(coef), whole(valid), block, block],
        (len(taps),),
        [shaped(first.shape), shaped((2, channels))],
        [held(first.shape), held((2, channels))],
        [pltpu.VMEM((channels, 2 * half), BF16)],
        meta,
        after,
        2 * macs,
    )


def weight_tap(tap, tiles, flipped_ref, up_ref, padded_ref):
    tiles_i, tiles_j, pixels = tiles
    shift_i, shift_j = tap
    low_i, high_i = span(shift_i, tiles_i)
    low_j, high_j = span(shift_j, tiles_j)
    padded_ref[...] = jnp.zeros_like(padded_ref)
    wide = (high_j - low_j) * pixels
    for row in range(low_i, high_i):
        target = ((row + shift_i) * tiles_j + low_j + shift_j) * pixels
        source = (row * tiles_j + low_j) * pixels
        padded_ref[target : target + wide] = up_ref[source : source + wide]
    first = (low_i + shift_i) * tiles_j * pixels // 128 * 128
    last = -(-(high_i + shift_i) * tiles_j * pixels // 128) * 128
    return jnp.dot(
        flipped_ref[:, first:last], padded_ref[first:last], preferred_element_type=F32
    )


def weight_body(plan, tiles, meta_ref, flipped_ref, up_ref, own_ref, other_ref, padded_ref, full_ref):
    half = own_ref.shape[2]
    for place, (tap, column) in enumerate(plan):

        @pl.when(pl.program_id(0) == place)
        def _(tap=tap, column=column):
            full_ref[...] = weight_tap(
                tap, tiles, flipped_ref, up_ref.at[:, column : column + 2 * half], padded_ref
            ).astype(BF16)

    spread(meta_ref, full_ref, own_ref, other_ref)


def weight_grad(flipped, upstream, meta, taps, columns, slots, tiles, width, after=()):
    channels, padded = flipped.shape
    rows = channels // slots
    half = width // 2
    plan = list(zip(shifts_of(taps), columns))
    block = pl.BlockSpec((slots, rows, half), lambda step, _: (0, step, 0))
    shape = shaped((slots, rows * len(taps), half), BF16)
    macs = sum(area(tap, tiles) for tap, _ in plan) * channels * width
    return call(
        functools.partial(weight_body, plan, tiles),
        [flipped, upstream],
        [whole(flipped), whole(upstream)],
        (len(taps),),
        [shape, shape],
        [block, block],
        [pltpu.VMEM((padded, width), BF16), pltpu.VMEM((channels, width), BF16)],
        meta,
        after,
        2 * macs,
    )


def tile_matrix(breadth):
    count = TILE * breadth
    matrix = np.zeros((count, count), np.float32)
    for row in range(TILE):
        for column in range(breadth):
            at = (column // TILE * TILE + row) * TILE + column % TILE
            matrix[at, row * breadth + column] = 1.0
    return matrix


def tile_body(matrix_ref, natural_ref, result_ref):
    result_ref[...] = jnp.dot(
        matrix_ref[...], natural_ref[...], preferred_element_type=F32
    ).astype(BF16)


def tile_rows(natural, matrix):
    rows = matrix.shape[0]
    return call(
        tile_body,
        [matrix, natural],
        [whole(matrix), rows_of(natural, rows)],
        (natural.shape[0] // rows,),
        [shaped(natural.shape, BF16)],
        [rows_of(natural, rows)],
        flops=2 * rows * natural.size,
    )[0]


def flip_body(source_ref, result_ref):
    pixels = source_ref.shape[0]
    result_ref[:, :pixels] = source_ref[...].T
    if result_ref.shape[1] > pixels:
        extra = result_ref.shape[1] - pixels
        result_ref[:, pixels:] = jnp.zeros((result_ref.shape[0], extra), BF16)


def flipped(values, after=()):
    pixels, channels = values.shape
    padded = pixels + -pixels % 128
    return call(
        flip_body,
        [values],
        [pl.BlockSpec((pixels, 128), lambda step: (0, step))],
        (channels // 128,),
        [shaped((channels, padded), BF16)],
        [pl.BlockSpec((128, padded), lambda step: (step, 0))],
        after=after,
    )[0]


def add_sums(sums_ref, sums):
    @pl.when(pl.program_id(0) == 0)
    def _():
        sums_ref[...] = sums

    @pl.when(pl.program_id(0) > 0)
    def _():
        sums_ref[...] += sums


def first_body(meta_ref, source_ref, valid_ref, own_ref, other_ref, result_ref, sums_ref, weight_ref):
    @pl.when(pl.program_id(0) == 0)
    def _():
        assemble(meta_ref, own_ref, other_ref, weight_ref)

    product = jnp.dot(source_ref[...], weight_ref[...], preferred_element_type=F32)
    result_ref[...] = product
    add_sums(sums_ref, masked_sums(product, valid_ref[...]))


def first_conv(source, valid, own, other, meta, turns, after):
    pixels, channels = source.shape
    rows = pixels // turns
    width = 2 * own.shape[2]
    return call(
        first_body,
        [source, valid, own, other],
        [rows_of(source, rows), rows_of(valid, rows), whole(own), whole(other)],
        (turns,),
        [shaped((pixels, width)), shaped((2, width))],
        [pl.BlockSpec((rows, width), lambda step, _: (step, 0)), held((2, width))],
        [pltpu.VMEM((channels, width), BF16)],
        meta,
        after,
        2 * pixels * channels * width,
    )


def quarter_specs(own, rows, first, count):
    slots, _, half = own.shape
    return [
        pl.BlockSpec((slots, rows, half), lambda step, _, at=first + quarter: (0, at, 0))
        for quarter in range(count)
    ]


def assemble_wide(meta_ref, quarter_refs, weight_ref):
    count = len(quarter_refs) // 2
    half = quarter_refs[0].shape[2]
    for quarter in range(count):
        assemble(
            meta_ref,
            quarter_refs[quarter],
            quarter_refs[count + quarter],
            weight_ref,
            column=quarter * half,
            apart=count * half,
        )


def third_body(count, meta_ref, second_ref, coef_ref, valid_ref, *refs):
    quarter_refs = refs[: 2 * count]
    middle_ref, result_ref, sums_ref, weight_ref = refs[2 * count :]

    @pl.when(pl.program_id(0) == 0)
    def _():
        assemble_wide(meta_ref, quarter_refs, weight_ref)

    _, pre = unit_of(second_ref[...], coef_ref[...])
    middle_ref[...] = silu(pre).astype(BF16)
    product = jnp.dot(middle_ref[...], weight_ref[...], preferred_element_type=F32)
    result_ref[...] = product
    add_sums(sums_ref, masked_sums(product, valid_ref[...]))


def third_conv(second, coef, valid, own, other, meta, rows, first, count, turns):
    pixels, narrow = second.shape
    height = pixels // turns
    channels = 2 * count * own.shape[2]
    quarters = quarter_specs(own, rows, first, count)
    return call(
        functools.partial(third_body, count),
        [second, coef, valid] + [own] * count + [other] * count,
        [rows_of(second, height), whole(coef), rows_of(valid, height)] + quarters + quarters,
        (turns,),
        [shaped((pixels, narrow), BF16), shaped((pixels, channels)), shaped((2, channels))],
        [
            pl.BlockSpec((height, narrow), lambda step, _: (step, 0)),
            pl.BlockSpec((height, channels), lambda step, _: (step, 0)),
            held((2, channels)),
        ],
        [pltpu.VMEM((narrow, channels), BF16)],
        meta,
        (),
        2 * pixels * narrow * channels,
    )


def output_body(third_ref, source_ref, coef_ref, valid_ref, result_ref, sums_ref):
    _, pre = unit_of(third_ref[...], coef_ref[...])
    values = (valid_ref[...] * silu(pre + source_ref[...].astype(F32))).astype(BF16)
    result_ref[...] = values
    add_sums(sums_ref, jnp.sum(values.astype(F32), axis=0, keepdims=True))


def block_output(third, source, coef, valid, turns):
    pixels, channels = third.shape
    rows = pixels // turns
    return call(
        output_body,
        [third, source, coef, valid],
        [rows_of(third, rows), rows_of(source, rows), whole(coef), rows_of(valid, rows)],
        (turns,),
        [shaped(third.shape, BF16), shaped((1, channels))],
        [rows_of(third, rows), held((1, channels))],
    )


def third_back_body(
    count, meta_ref, low_ref, high_ref, third_ref, coef_ref, totals_ref, valid_ref, middle_ref, *refs
):
    quarter_refs = refs[: 2 * count]
    result_ref, own_ref, other_ref, weight_ref, grad_ref, total_ref = refs[2 * count :]
    step_now = pl.program_id(0)

    @pl.when(step_now == 0)
    def _():
        assemble_wide(meta_ref, quarter_refs, weight_ref)
        total_ref[...] = jnp.zeros_like(total_ref)

    part = low_ref.shape[1]
    coef, totals, valid = coef_ref[...], totals_ref[...], valid_ref[...]
    for start, part_ref in ((0, low_ref), (part, high_ref)):
        at = slice(start, start + part)
        unit = (third_ref[:, at] - coef[0:1, at]) * coef[1:2, at]
        centered = part_ref[...].astype(F32) - valid * (totals[0:1, at] + unit * totals[1:2, at])
        grad_ref[:, at] = (coef[2:3, at] * coef[1:2, at] * centered).astype(BF16)
    grad = grad_ref[...]
    result_ref[...] = lax.dot_general(
        grad, weight_ref[...], (((1,), (1,)), ((), ())), preferred_element_type=F32
    )
    total_ref[...] += lax.dot_general(
        middle_ref[...], grad, (((0,), (0,)), ((), ())), preferred_element_type=F32
    )

    @pl.when(step_now == pl.num_programs(0) - 1)
    def _():
        half = own_ref.shape[2]
        rows = own_ref.shape[1] // count
        for quarter in range(count):
            spread(
                meta_ref,
                total_ref,
                own_ref,
                other_ref,
                column=quarter * half,
                apart=count * half,
                at=quarter * rows,
                rows=rows,
            )


def third_back(low, high, third, coef, totals, valid, middle, own, other, meta, rows, first, count, turns, after):
    pixels, channels = third.shape
    narrow = middle.shape[1]
    height = pixels // turns
    slots, _, half = own.shape
    quarters = quarter_specs(own, rows, first, count)
    shape = shaped((slots, count * rows, half), BF16)
    return call(
        functools.partial(third_back_body, count),
        [low, high, third, coef, totals, valid, middle] + [own] * count + [other] * count,
        [
            rows_of(low, height),
            rows_of(high, height),
            rows_of(third, height),
            whole(coef),
            whole(totals),
            rows_of(valid, height),
            rows_of(middle, height),
        ]
        + quarters
        + quarters,
        (turns,),
        [shaped((pixels, narrow)), shape, shape],
        [pl.BlockSpec((height, narrow), lambda step, _: (step, 0)), held(shape.shape), held(shape.shape)],
        [
            pltpu.VMEM((narrow, channels), BF16),
            pltpu.VMEM((height, channels), BF16),
            pltpu.VMEM((narrow, channels), F32),
        ],
        meta,
        after,
        4 * pixels * narrow * channels,
    )


def input_body(meta_ref, matrix_ref, low_ref, high_ref, grad_ref, own_ref, other_ref, result_ref, weight_ref):
    @pl.when(pl.program_id(0) == 0)
    def _():
        assemble(meta_ref, own_ref, other_ref, weight_ref)

    rows = matrix_ref.shape[0]
    part = low_ref.shape[1]
    matrix = matrix_ref[...]
    for start in range(0, result_ref.shape[0], rows):
        at = slice(start, start + rows)
        moved = jnp.dot(matrix, grad_ref[at], preferred_element_type=F32).astype(BF16)
        for column, part_ref in ((0, low_ref), (part, high_ref)):
            columns = slice(column, column + part)
            result_ref[at, columns] = jnp.dot(
                matrix, part_ref[at], preferred_element_type=F32
            ) + lax.dot_general(
                moved, weight_ref[columns], (((1,), (1,)), ((), ())), preferred_element_type=F32
            )


def input_back(matrix, low, high, grad, own, other, meta, turns):
    pixels, part = low.shape
    rows = pixels // turns
    channels = 2 * part
    width = grad.shape[1]
    return call(
        input_body,
        [matrix, low, high, grad, own, other],
        [whole(matrix), rows_of(low, rows), rows_of(high, rows), rows_of(grad, rows), whole(own), whole(other)],
        (turns,),
        [shaped((pixels, channels))],
        [pl.BlockSpec((rows, channels), lambda step, _: (step, 0))],
        [pltpu.VMEM((channels, width), BF16)],
        meta,
        (),
        2 * pixels * channels * (width + matrix.shape[0]),
    )[0]


def join_body(meta_ref, own_ref, other_ref, result_ref):
    assemble(meta_ref, own_ref, other_ref, result_ref)


def join_slots(own, other, meta):
    slots, rows, half = own.shape
    shape = (slots * rows, 2 * half)
    return call(
        join_body, [own, other], [whole(own), whole(other)], (1,), [shaped(shape, BF16)], [held(shape)], meta=meta
    )[0]


def part_body(meta_ref, full_ref, own_ref, other_ref):
    spread(meta_ref, full_ref, own_ref, other_ref)


def part_slots(full, slots, meta):
    shape = (slots, full.shape[0] // slots, full.shape[1] // 2)
    return call(
        part_body, [full], [whole(full)], (1,), [shaped(shape, BF16)] * 2, [held(shape)] * 2, meta=meta
    )


def silu(values):
    return values * jax.nn.sigmoid(values)


def silu_slope(values):
    sigmoid_val = jax.nn.sigmoid(values)
    return sigmoid_val * (1.0 + values * (1.0 - sigmoid_val))


def sums(values, validity):
    weighted = values * validity
    return jnp.stack([jnp.sum(weighted, axis=0), jnp.sum(weighted * values, axis=0)])


def coefs(totals, counted, gain, shift):
    mean_value = totals[0] / counted
    scaling = lax.rsqrt(totals[1] / counted - mean_value * mean_value + EPSILON)
    return jnp.stack([mean_value, scaling, gain, shift])


def through_norm(grad_pre, unit, coef, counted, validity, totals):
    centered = grad_pre - validity * (totals[0] + unit * totals[1]) / counted
    return coef[2] * coef[1] * centered


def to_tiles(array):
    height, breadth = array.shape[:2]
    rest = array.shape[2:]
    cut = array.reshape((height // TILE, TILE, breadth // TILE, TILE) + rest)
    return jnp.swapaxes(cut, 1, 2).reshape((height * breadth,) + rest)


def per_device(
    features,
    reduce_weight,
    spatial_weight,
    expand_weight,
    bottle_gain,
    bottle_shift,
    point_weight,
    near_weight,
    middle_weight,
    far_weight,
    image_weight,
    project_weight,
    class_weight,
    pyramid_gain,
    pyramid_shift,
    head_gain,
    head_shift,
    crop_masks,
    crop_tasks,
    pixel_labels,
    task_norms,
):
    place = Place()
    size, slots, core = place.size, place.slots, place.core
    first_core = core == 0
    height, breadth, channels = features.shape[2:]
    pixels = height * breadth
    tiles = (height // TILE, breadth // TILE, TILE * TILE)
    narrow = reduce_weight.shape[1]
    branch = point_weight.shape[1]
    four_wide = 4 * branch
    rows = channels // size
    slot_rows = channels // slots
    narrow_slot = narrow // slots
    quarters = channels // narrow
    turns = 3
    meta = place.meta()
    matrix = tile_matrix(breadth)

    bottle_taps = tap_list(height, breadth, BOTTLE_RATE)
    near_taps = tap_list(height, breadth, NEAR_RATE)
    middle_taps = tap_list(height, breadth, MIDDLE_RATE)
    far_taps = tap_list(height, breadth, FAR_RATE)
    point_taps = [(1, 1, 0, 0)]

    def center_of(taps):
        return [tap[:2] for tap in taps].index((1, 1))

    def stacked(weight, taps):
        flat = weight.reshape((-1,) + weight.shape[2:])
        picked = [3 * tap[0] + tap[1] for tap in taps]
        if picked == list(range(picked[0], picked[-1] + 1)):
            flat = flat[picked[0] : picked[-1] + 1]
        else:
            flat = jnp.stack([flat[at] for at in picked])
        return flat.reshape(-1, flat.shape[2]), len(taps)

    mask = lax.dynamic_index_in_dim(crop_masks, core, 0, keepdims=False)[0]
    labels = lax.dynamic_index_in_dim(pixel_labels, core, 0, keepdims=False)[0]
    task = lax.dynamic_index_in_dim(crop_tasks, core, 0, keepdims=False)[0]
    validity = to_tiles(mask).astype(F32)[:, None]
    valid_tiles = validity.reshape(tiles + (1,))
    labels = to_tiles(labels)
    source = tile_rows(features.reshape(pixels, channels), jnp.array(matrix, BF16))
    source_flipped = flipped(source)

    wide_expand = expand_weight.reshape(-1, 2, quarters, narrow // 2)
    expand_parts = [(wide_expand[:, :, at].reshape(-1, narrow), 1) for at in range(quarters)]
    reduce_own, after = place.gather([(reduce_weight, 1)], ())
    reduce_other = place.swap(reduce_own)
    bottle_own, after = place.gather([stacked(spatial_weight, bottle_taps)] + expand_parts, after)
    bottle_other = place.swap(bottle_own)
    near_own, after = place.gather([stacked(near_weight, near_taps)], after)
    near_other = place.swap(near_own)

    crop_valid_both = jnp.sum(crop_masks, axis=(1, 2, 3)).astype(F32)
    home_crop = (crop_tasks[:, 0] == 1).astype(F32)
    counts = jnp.concatenate(
        [
            crop_valid_both,
            jnp.sum(crop_valid_both * (1.0 - home_crop))[None],
            jnp.sum(crop_valid_both * home_crop)[None],
        ]
    )
    small = [bottle_gain, bottle_shift, pyramid_gain, pyramid_shift, head_gain, head_shift]
    small.append(class_weight.reshape(-1))
    small_widths = [part.shape[0] for part in small]
    small_own = jnp.concatenate(small).astype(F32)
    placed = lax.dynamic_update_slice(
        jnp.zeros((size, small_own.shape[0]), F32), small_own[None], (place.index, 0)
    )
    collected = place.total(jnp.concatenate([placed.reshape(-1), counts]))
    counts_all = collected[placed.size :]
    collected = collected[: placed.size].reshape(size, -1)
    small_all, start = [], 0
    for width in small_widths:
        small_all.append(collected[:, start : start + width].reshape(-1))
        start += width
    gain_bottle, shift_bottle, gain_pyramid, shift_pyramid, gain_head, shift_head = small_all[:6]
    class_full = small_all[6].reshape(size * class_weight.shape[0], -1).astype(BF16)
    counted = jnp.where(first_core, counts_all[0], counts_all[1])
    task_pixels = counts_all[2:4]
    crop_valid = jnp.where(first_core, crop_valid_both[0], crop_valid_both[1])

    first, first_sums = first_conv(
        source, validity, reduce_own, reduce_other, meta, turns, [source_flipped]
    )
    coef_one = coefs(place.total(first_sums), counted, gain_bottle[:narrow], shift_bottle[:narrow])
    first_tiles = first.reshape(tiles + (narrow,))
    middle_own, after = place.gather([stacked(middle_weight, middle_taps)], after + [first])
    middle_other = place.swap(middle_own)
    conv_in, second, second_sums = spatial_conv(
        first_tiles, coef_one, valid_tiles, bottle_own, bottle_other, meta, bottle_taps, center_of(bottle_taps)
    )
    second = second.reshape(pixels, narrow)
    coef_two = coefs(
        place.total(second_sums), counted, gain_bottle[narrow : 2 * narrow], shift_bottle[narrow : 2 * narrow]
    )
    expand_at = (narrow_slot, len(bottle_taps), quarters, turns)
    middle_act, third, third_sums = third_conv(
        second, coef_two, validity, bottle_own, bottle_other, meta, *expand_at
    )
    wide_parts = [stacked(far_weight, far_taps), (point_weight, 1), (project_weight, 1)]
    far_own, after = place.gather(wide_parts, after + [third])
    far_other = place.swap(far_own)
    coef_three = coefs(
        place.total(third_sums), counted, gain_bottle[2 * narrow :], shift_bottle[2 * narrow :]
    )
    block_out, pooled_sum = block_output(third, source, coef_three, validity, tiles[0])
    block_tiles = block_out.reshape(tiles + (channels,))

    pooled = (pooled_sum / crop_valid).astype(BF16)
    pooled_plane = place.plane_total(
        lax.dynamic_update_slice(jnp.zeros((size, channels), BF16), pooled, (place.index, 0))
    )
    near_out, near_sums = branch_conv(
        block_tiles, valid_tiles, near_own, near_other, meta, near_taps, center_of(near_taps), 0, ()
    )
    pooled_all = place.line_total(pooled_plane)
    middle_out, middle_sums = branch_conv(
        block_tiles,
        valid_tiles,
        middle_own,
        middle_other,
        meta,
        middle_taps,
        center_of(middle_taps),
        0,
        [pooled_plane, near_sums],
    )
    pooled_rows = lax.dynamic_slice_in_dim(pooled_all, place.index * rows, rows, axis=1)
    image_plane = place.plane_total(
        jnp.dot(pooled_rows, image_weight, preferred_element_type=F32)
    )
    far_out, far_sums = branch_conv(
        block_tiles,
        valid_tiles,
        far_own,
        far_other,
        meta,
        far_taps,
        center_of(far_taps),
        0,
        [pooled_all, middle_sums],
    )
    image_all = place.line_total(image_plane)
    point_out, point_sums = branch_conv(
        block_tiles,
        valid_tiles,
        far_own,
        far_other,
        meta,
        point_taps,
        0,
        len(far_taps),
        [image_plane, far_sums],
    )
    block_flipped = flipped(block_out, [point_sums])
    image_mean = jnp.sum(image_all, axis=0) / size
    image_scale = lax.rsqrt(
        jnp.sum(image_all * image_all, axis=0) / size - image_mean * image_mean + EPSILON
    )
    image_unit = (image_all - image_mean) * image_scale
    gain_image, shift_image = gain_pyramid[four_wide:], shift_pyramid[four_wide:]
    coef_image = jnp.stack([image_mean, image_scale, gain_image, shift_image])
    image_pre = gain_image * image_unit + shift_image
    image_act = silu(image_pre).astype(BF16)

    outs = [part.reshape(pixels, branch) for part in (point_out, near_out, middle_out, far_out)]
    branches = jnp.concatenate(outs, axis=1)
    branch_sums = jnp.concatenate([point_sums, near_sums, middle_sums, far_sums], axis=1)
    coef_branch = coefs(
        place.total(branch_sums), counted, gain_pyramid[:four_wide], shift_pyramid[:four_wide]
    )
    unit_branch, pre_branch = unit_of(branches, coef_branch)
    joined = silu(pre_branch).astype(BF16)

    wide_count = len(far_taps) + 1
    project_full = join_slots(
        far_own[:, wide_count * slot_rows :], far_other[:, wide_count * slot_rows :], meta
    )
    own_act = lax.dynamic_slice_in_dim(image_act, place.index, 1, axis=0)
    crop_part = jnp.dot(own_act, project_full[four_wide:], preferred_element_type=F32)
    projected = jnp.dot(joined, project_full[:four_wide], preferred_element_type=F32) + crop_part
    coef_head = coefs(place.total(sums(projected, validity)), counted, gain_head, shift_head)
    unit_head, pre_head = unit_of(projected, coef_head)
    output_act = silu(pre_head).astype(BF16)
    logits = jnp.dot(output_act, class_full, preferred_element_type=F32)

    columns = jnp.arange(class_full.shape[1])
    allowed = (columns >= CITY_CLASSES) == (task == 1)
    masked = jnp.where(allowed, logits, FLOOR_LOGIT)
    raised = jnp.exp(masked - jnp.max(masked, axis=-1, keepdims=True))
    chances = raised / jnp.sum(raised, axis=-1, keepdims=True)
    target = jnp.where(task == 0, labels % CITY_CLASSES, CITY_CLASSES + labels % HOME_CLASSES)
    chosen = (columns == target[:, None]).astype(F32)
    inverse = 1.0 / task_norms.astype(F32)
    task_share = inverse / jnp.sum(inverse)
    crop_weight = jnp.where(
        task == 0, task_share[0] / task_pixels[0], task_share[1] / task_pixels[1]
    )
    logit_grad = (crop_weight * validity * (chances - chosen)).astype(BF16)
    class_grad = lax.dot_general(
        output_act, logit_grad, (((0,), (0,)), ((), ())), preferred_element_type=F32
    )

    output_grad = lax.dot_general(
        logit_grad, class_full, (((1,), (1,)), ((), ())), preferred_element_type=F32
    )
    grad_head = output_grad * silu_slope(pre_head)
    head_totals = place.total(
        jnp.concatenate([grad_moments(grad_head, unit_head).reshape(-1), class_grad.reshape(-1)])
    )
    class_total = head_totals[2 * branch :]
    head_totals = head_totals[: 2 * branch].reshape(2, branch)
    proj_grad = through_norm(
        grad_head, unit_head, coef_head, counted, validity, head_totals
    ).astype(BF16)
    crop_grad = jnp.sum(proj_grad, axis=0, dtype=F32)
    joined_grad = lax.dot_general(
        proj_grad, project_full[:four_wide], (((1,), (1,)), ((), ())), preferred_element_type=F32
    )
    act_grad = jnp.dot(project_full[four_wide:].astype(F32), crop_grad, precision=HIGHEST)
    own_pre = lax.dynamic_slice_in_dim(image_pre, place.index, 1, axis=0)[0]
    image_pre_grad = act_grad * silu_slope(own_pre)
    grad_branch = joined_grad * silu_slope(pre_branch)
    placed_pre = lax.dynamic_update_slice(
        jnp.zeros((size, branch), F32), image_pre_grad[None], (place.index, 0)
    )
    branch_totals = place.total(
        jnp.concatenate([grad_moments(grad_branch, unit_branch).reshape(-1), placed_pre.reshape(-1)])
    )
    image_pre_all = branch_totals[2 * four_wide :].reshape(size, branch)
    branch_totals = branch_totals[: 2 * four_wide].reshape(2, four_wide)
    branch_grad = through_norm(
        grad_branch, unit_branch, coef_branch, counted, validity, branch_totals
    ).astype(BF16)
    image_totals = grad_moments(image_pre_all, image_unit)
    image_in_all = through_norm(
        image_pre_all, image_unit, coef_image, float(size), 1.0, image_totals
    )
    pooled_partial = lax.dot_general(
        image_in_all, image_weight.astype(F32), (((1,), (1,)), ((), ())), precision=HIGHEST
    )
    pooled_grad_plane = place.plane_total(
        lax.dynamic_update_slice(
            jnp.zeros((size, channels), F32), pooled_partial, (0, place.index * rows)
        )
    )
    image_partial = jnp.dot(pooled_rows.astype(F32).T, image_in_all, precision=HIGHEST)

    def columns_of(taps, block):
        return [block * branch] * len(taps)

    wide_taps = far_taps + point_taps
    wide_columns = columns_of(far_taps, 3) + columns_of(point_taps, 0)

    def branch_weight_grad(taps, tap_columns, after):
        return weight_grad(
            block_flipped, branch_grad, meta, taps, tap_columns, slots, tiles, branch, after
        )

    near_own_grad, near_other_grad = branch_weight_grad(near_taps, columns_of(near_taps, 1), ())
    near_scatter = Scatter(place, near_own_grad, near_other_grad, [slot_rows] * len(near_taps))
    pooled_grad_all = place.line_total(pooled_grad_plane)
    middle_own_grad, middle_other_grad = branch_weight_grad(
        middle_taps, columns_of(middle_taps, 2), [near_own_grad, pooled_grad_plane]
    )
    middle_scatter = Scatter(place, middle_own_grad, middle_other_grad, [slot_rows] * len(middle_taps))
    far_own_grad, far_other_grad = branch_weight_grad(
        wide_taps, wide_columns, [middle_own_grad, near_scatter.arrived, pooled_grad_all]
    )
    near_scatter.first()
    project_grad = jnp.concatenate(
        [
            lax.dot_general(
                joined, proj_grad, (((0,), (0,)), ((), ())), preferred_element_type=F32
            ),
            own_act[0].astype(F32)[:, None] * crop_grad[None, :],
        ]
    ).astype(BF16)
    project_own_grad, project_other_grad = part_slots(project_grad, slots, meta)
    far_scatter = Scatter(
        place,
        jnp.concatenate([far_own_grad, project_own_grad], axis=1),
        jnp.concatenate([far_other_grad, project_other_grad], axis=1),
        [slot_rows] * wide_count + [project_grad.shape[0] // slots],
    )

    pooled_grad = lax.dynamic_slice_in_dim(pooled_grad_all, place.index, 1, axis=0) / crop_valid
    groups = [
        (near_own, near_other, near_taps, center_of(near_taps), columns_of(near_taps, 1)),
        (middle_own, middle_other, middle_taps, center_of(middle_taps), columns_of(middle_taps, 2)),
        (far_own, far_other, wide_taps, center_of(far_taps), wide_columns),
    ]

    def half_back(side, after):
        return feature_back(
            branch_grad.reshape(tiles + (four_wide,)),
            groups,
            third,
            source,
            coef_three,
            pooled_grad,
            validity,
            meta,
            side,
            2,
            after,
        )

    def arrivals(scatter):
        return scatter.arrived if isinstance(scatter.arrived, list) else [scatter.arrived]

    low_grad, low_moments = half_back(0, [far_own_grad] + arrivals(middle_scatter))
    high_grad, high_moments = half_back(1, [low_moments] + arrivals(near_scatter) + arrivals(far_scatter))
    near_scatter.second()
    middle_scatter.first()
    three_totals = place.total(jnp.concatenate([low_moments, high_moments], axis=1))
    middle_grad, expand_own_grad, expand_other_grad = third_back(
        low_grad,
        high_grad,
        third,
        coef_three,
        three_totals / counted,
        validity,
        middle_act,
        bottle_own,
        bottle_other,
        meta,
        *expand_at,
        arrivals(near_scatter) + arrivals(middle_scatter),
    )
    near_scatter.third()
    middle_scatter.second()
    far_scatter.first()
    unit_two, pre_two = unit_of(second, coef_two)
    grad_two = middle_grad * silu_slope(pre_two)
    two_totals = place.total(grad_moments(grad_two, unit_two))
    second_grad = through_norm(
        grad_two, unit_two, coef_two, counted, validity, two_totals
    ).astype(BF16)
    spatial_own_grad, spatial_other_grad = weight_grad(
        flipped(conv_in.reshape(pixels, narrow)),
        second_grad,
        meta,
        bottle_taps,
        [0] * len(bottle_taps),
        slots,
        tiles,
        narrow,
        arrivals(middle_scatter) + arrivals(far_scatter),
    )
    bottle_scatter = Scatter(
        place,
        jnp.concatenate([spatial_own_grad, expand_own_grad], axis=1),
        jnp.concatenate([spatial_other_grad, expand_other_grad], axis=1),
        [narrow_slot] * (len(bottle_taps) + quarters),
    )
    middle_scatter.third()
    far_scatter.second()
    grad_one, one_moments = spatial_back(
        second_grad.reshape(tiles + (narrow,)),
        first_tiles,
        coef_one,
        valid_tiles,
        bottle_own,
        bottle_other,
        meta,
        bottle_taps,
        center_of(bottle_taps),
        [spatial_own_grad] + arrivals(near_scatter),
    )
    bottle_scatter.first()
    far_scatter.third()
    one_totals = place.total(one_moments)
    unit_one, _ = unit_of(first, coef_one)
    first_grad = through_norm(
        grad_one.reshape(pixels, narrow), unit_one, coef_one, counted, validity, one_totals
    ).astype(BF16)
    reduce_own_grad, reduce_other_grad = weight_grad(
        source_flipped, first_grad, meta, point_taps, [0], slots, tiles, narrow
    )
    reduce_scatter = Scatter(place, reduce_own_grad, reduce_other_grad, [slot_rows])
    input_grad = input_back(
        jnp.array(matrix.T, BF16), low_grad, high_grad, first_grad, reduce_own, reduce_other, meta, turns
    )
    bottle_scatter.second()
    reduce_scatter.first()
    bottle_scatter.third()
    reduce_scatter.second()
    reduce_scatter.third()

    vectors = [one_totals, two_totals, three_totals, branch_totals, image_totals, head_totals]
    vectors += [class_total, image_partial]
    packed = jnp.concatenate([vector.reshape(-1) for vector in vectors])
    packed = packed + place.swap(packed)
    split, start = [], 0
    for vector in vectors:
        split.append(packed[start : start + vector.size].reshape(vector.shape))
        start += vector.size

    def own_part(vectors):
        vector = jnp.concatenate(vectors)
        length = vector.shape[0] // size
        return lax.dynamic_slice_in_dim(vector, place.index * length, length, axis=0)

    bottle_gain_grad = own_part([split[0][1], split[1][1], split[2][1]])
    bottle_shift_grad = own_part([split[0][0], split[1][0], split[2][0]])
    pyramid_gain_grad = own_part([split[3][1], split[4][1]])
    pyramid_shift_grad = own_part([split[3][0], split[4][0]])
    head_norm_grad = jnp.stack([own_part([split[5][1]]), own_part([split[5][0]])])
    class_out = own_part([split[6].reshape(size * class_weight.shape[0], -1)])
    image_out = split[7]

    def rows_out(halves):
        return jnp.concatenate([halves[0], halves[1]], axis=-1)

    def taps_out(halves, taps, weight):
        full = rows_out(halves).reshape((len(taps),) + weight.shape[2:])
        if len(taps) == weight.shape[0] * weight.shape[1]:
            return full.reshape(weight.shape)
        result = jnp.zeros(weight.shape, F32)
        for at, tap in enumerate(taps):
            result = result.at[tap[0], tap[1]].set(full[at])
        return result

    narrow_rows = narrow // size
    near_sum, middle_sum = near_scatter.finish(), middle_scatter.finish()
    far_sum, bottle_sum, reduce_sum = far_scatter.finish(), bottle_scatter.finish(), reduce_scatter.finish()
    expand_start = len(bottle_taps) * narrow_rows
    expand_out = bottle_sum[:, expand_start:].reshape(2, quarters, narrow_rows, narrow // 2)
    far_end, point_end = len(far_taps) * rows, wide_count * rows
    return (
        input_grad.reshape(features.shape),
        rows_out(reduce_sum),
        taps_out(bottle_sum[:, :expand_start], bottle_taps, spatial_weight),
        expand_out.transpose(2, 0, 1, 3).reshape(expand_weight.shape),
        bottle_gain_grad,
        bottle_shift_grad,
        rows_out(far_sum[:, far_end:point_end]),
        taps_out(near_sum, near_taps, near_weight),
        taps_out(middle_sum, middle_taps, middle_weight),
        taps_out(far_sum[:, :far_end], far_taps, far_weight),
        image_out,
        rows_out(far_sum[:, point_end:]),
        class_out,
        pyramid_gain_grad,
        pyramid_shift_grad,
        head_norm_grad,
    )


def solution(mesh):
    in_specs = (
        P("section", "batch", None, None, None),
        P("batch", None),
        P(None, None, "batch", None),
        P("batch", None),
        P("batch"),
        P("batch"),
        P("batch", None),
        P(None, None, "batch", None),
        P(None, None, "batch", None),
        P(None, None, "batch", None),
        P("batch", None),
        P("batch", None),
        P("batch", None),
        P("batch"),
        P("batch"),
        P("batch"),
        P("batch"),
        P(None, "batch", None, None),
        P(None, "batch"),
        P(None, "batch", None, None),
        P(),
    )
    out_specs = (
        P("section", "batch", None, None, None),
        P("batch", None),
        P(None, None, "batch", None),
        P("batch", None),
        P("batch"),
        P("batch"),
        P("batch", None),
        P(None, None, "batch", None),
        P(None, None, "batch", None),
        P(None, None, "batch", None),
        P("batch", None),
        P("batch", None),
        P("batch", None),
        P("batch"),
        P("batch"),
        P(None, "batch"),
    )
    return jax.shard_map(
        per_device, mesh=mesh, in_specs=in_specs, out_specs=out_specs, check_vma=False
    )
```

```python
import functools

import jax
import jax.numpy as jnp
import numpy as np
from jax import lax
from jax.experimental import pallas as pl
from jax.experimental.pallas import tpu as pltpu
from jax.sharding import PartitionSpec as P

CITY_CLASSES = 19
HOME_CLASSES = 13
BOTTLE_RATE = 4
NEAR_RATE = 12
MIDDLE_RATE = 24
FAR_RATE = 36
TILE = 4

EPSILON = 1e-05
FLOOR_LOGIT = -1e30
HIGHEST = lax.Precision.HIGHEST
F32 = jnp.float32
BF16 = jnp.bfloat16
SLOT_BITS = [0, 4, 2, 6, 1, 5, 3, 7, 8, 12, 9, 13, 10, 14, 11, 15]
VMEM_BYTES = 58 * 1024 * 1024


class Place:
    def __init__(self):
        self.size = lax.axis_size("batch")
        self.direct = self.size == len(SLOT_BITS)
        self.pieces = 2 * self.size if self.direct else 1
        self.core = lax.axis_index("section")
        self.index = lax.axis_index("batch")

    def meta(self):
        core = self.core[None].astype(jnp.int32)
        if not self.direct:
            return core
        table = [[SLOT_BITS.index(at ^ owner) for owner in range(self.size)] for at in range(self.size)]
        row = lax.dynamic_index_in_dim(jnp.array(table, jnp.int32), self.index, 0, keepdims=False)
        return jnp.concatenate([core, row])

    def flip(self, block, bits):
        return lax.ppermute(block, "batch", [(source, source ^ bits) for source in range(self.size)])

    def swap(self, block):
        return lax.ppermute(block, "section", [(0, 1), (1, 0)])

    def plane_total(self, vector):
        if not self.direct:
            return vector
        return (vector + self.flip(vector, 1)) + (self.flip(vector, 2) + self.flip(vector, 3))

    def line_total(self, plane):
        if not self.direct:
            return lax.psum(plane, "batch")
        return (plane + self.flip(plane, 4)) + (self.flip(plane, 8) + self.flip(plane, 12))

    def total(self, vector):
        return self.line_total(self.plane_total(vector))

    def gather(self, parts):
        blocks = []
        for part, count in parts:
            cut = part.reshape(count, -1, part.shape[1])
            if self.direct:
                half = cut.shape[1] // 2
                cut = lax.dynamic_slice_in_dim(cut, self.core * half, half, axis=1)
            else:
                cut = lax.all_gather(cut, "batch", axis=1, tiled=True)
            blocks.append(cut.reshape(-1, part.shape[1]))
        block = jnp.concatenate(blocks)
        if self.direct:
            return lax.all_gather(block, ("batch", "section"))
        return block[None]


class Scatter:
    def __init__(self, place, grads, rows):
        self.place, self.rows = place, rows
        self.own = grads[0]
        self.kept = []
        self.arrived = [place.swap(grads[1])] if place.direct else []

    def add(self, kept, arrived):
        return (kept.astype(F32) + arrived.astype(F32)).astype(BF16)

    def first(self):
        if not self.place.direct:
            return
        self.kept = []
        sent = []
        arrived = self.arrived[0]
        for start in (0, 8):
            self.kept.append(self.add(self.own[start : start + 4], arrived[start : start + 4]))
            sent.append(self.add(self.own[start + 4 : start + 8], arrived[start + 4 : start + 8]))
        self.arrived = [self.place.flip(sent[0], 1), self.place.flip(sent[1], 2)]

    def second(self):
        if not self.place.direct:
            return
        kept, sent = [], []
        for held, came in zip(self.kept, self.arrived):
            kept.append(self.add(held[:2], came[:2]))
            sent.append(self.add(held[2:], came[2:]))
        self.kept = kept
        self.arrived = [self.place.flip(sent[0], 2), self.place.flip(sent[1], 1)]

    def third(self):
        if not self.place.direct:
            return
        near = self.kept[0].astype(F32) + self.arrived[0].astype(F32)
        away = self.kept[1].astype(F32) + self.arrived[1].astype(F32)
        self.kept = near[0]
        sent = [near[1].astype(BF16), away[0].astype(BF16), away[1].astype(BF16)]
        self.arrived = [self.place.flip(piece, bits) for piece, bits in zip(sent, (4, 8, 12))]

    def finish(self):
        if self.place.direct:
            parts = [piece.astype(F32) for piece in self.arrived]
            result = (self.kept + parts[0]) + (parts[1] + parts[2])
            opposite = self.place.swap(result)
            first = self.place.core == 0
            self.result = [jnp.where(first, result, opposite), jnp.where(first, opposite, result)]
            return self
        pieces, start = [], 0
        for rows in self.rows:
            cut = self.own[0, start : start + rows * self.place.size].astype(F32)
            cut = lax.psum_scatter(cut, "batch", scatter_dimension=0, tiled=True)
            pieces.append(lax.psum(cut, "section"))
            start += rows * self.place.size
        self.result = [jnp.concatenate(pieces)]
        return self

    def piece(self, first, count):
        parts = len(self.result)
        start = sum(self.rows[:first]) // parts
        rows = self.rows[first] // parts
        cut = [part[start : start + count * rows].reshape(count, rows, -1) for part in self.result]
        return jnp.concatenate(cut, axis=1).reshape(count * rows * parts, -1)


def call(body, args, specs, grid, outs, out_specs, scratch=(), meta=None, after=(), flops=0, passed=()):
    used = len(args) + (meta is not None)
    waits = len(after) + len(passed)
    results = len(outs)

    def inner(*refs):
        rest = refs[used + waits :]
        body(*refs[:used], *rest[:results], *rest[results + len(passed) :])

    spec = pltpu.PrefetchScalarGridSpec(
        num_scalar_prefetch=int(meta is not None),
        grid=grid,
        in_specs=list(specs) + [pl.BlockSpec(memory_space=pl.ANY)] * waits,
        out_specs=list(out_specs) + [pl.BlockSpec(memory_space=pl.ANY)] * len(passed),
        scratch_shapes=list(scratch),
    )
    arrays = ([] if meta is None else [meta]) + list(args) + list(after) + list(passed)
    first = len(arrays) - len(passed)
    moved = sum(array.size * array.dtype.itemsize for array in list(args) + list(outs))
    return pl.pallas_call(
        inner,
        grid_spec=spec,
        out_shape=list(outs) + [shaped(array.shape, array.dtype) for array in passed],
        input_output_aliases={first + at: results + at for at in range(len(passed))},
        compiler_params=pltpu.CompilerParams(vmem_limit_bytes=VMEM_BYTES),
        cost_estimate=pl.CostEstimate(flops=flops, transcendentals=0, bytes_accessed=moved),
    )(*arrays)


def whole(array):
    shape = array.shape
    return pl.BlockSpec(
        shape, lambda *_: (0,) * len(shape), pipeline_mode=pl.Buffered(buffer_count=1)
    )


def held(shape):
    return pl.BlockSpec(shape, lambda *_: (0,) * len(shape))


def rows_of(array, rows):
    return pl.BlockSpec((rows, array.shape[1]), lambda step, *_: (step, 0))


def shaped(shape, dtype=F32):
    return jax.ShapeDtypeStruct(tuple(shape), dtype)


def span(shift_by, length):
    return max(0, -shift_by), length - max(0, shift_by)


def tap_list(height, breadth, dilation):
    listed = []
    for row_tap in range(3):
        for col_tap in range(3):
            row_shift = (row_tap - 1) * dilation
            col_shift = (col_tap - 1) * dilation
            if abs(row_shift) < height and abs(col_shift) < breadth:
                listed.append((row_tap, col_tap, row_shift // TILE, col_shift // TILE))
    return listed


def weight_of(ref):
    return ref[...].reshape(-1, ref.shape[-1])


def spread(meta_ref, full_ref, result_refs, column=0, at=0, rows=None):
    width = result_refs[0].shape[2]
    rows = result_refs[0].shape[1] if rows is None else rows
    if len(result_refs) == 1:
        result_refs[0][0, at : at + rows] = full_ref[:, column : column + width].astype(BF16)
        return
    core = meta_ref[0]
    for owner in range(result_refs[0].shape[0]):
        for ref, side in zip(result_refs, (core, 1 - core)):
            start = pl.multiple_of(owner * 2 * rows + side * rows, rows)
            block = full_ref[pl.ds(start, rows), column : column + width]
            ref[meta_ref[1 + owner], at : at + rows] = block.astype(BF16)


def slotted(place, rows, width):
    if place.direct:
        return [shaped((place.size, rows // 2, width), BF16)] * 2
    return [shaped((1, rows * place.size, width), BF16)]


def center_first(step, center):
    return jnp.where(step == 0, center, jnp.where(step <= center, step - 1, step))


def ordered(taps, center):
    return [taps[center]] + [tap for place, tap in enumerate(taps) if place != center]


def shifts_of(taps):
    return [(tap[2], tap[3]) for tap in taps]


def area(tap, tiles):
    return (tiles[0] - abs(tap[0])) * (tiles[1] - abs(tap[1])) * tiles[2]


def forward_tap(tap, fresh, source_ref, weight, result_ref):
    tiles_i, tiles_j, pixels, channels = source_ref.shape
    columns = result_ref.shape[-1]
    shift_i, shift_j = tap
    low_i, high_i = span(shift_i, tiles_i)
    low_j, high_j = span(shift_j, tiles_j)
    window = source_ref[
        low_i + shift_i : high_i + shift_i, low_j + shift_j : high_j + shift_j
    ].reshape(-1, channels)
    product = jnp.dot(window, weight, preferred_element_type=F32)
    product = product.reshape(high_i - low_i, high_j - low_j, pixels, columns)
    if fresh:
        result_ref[low_i:high_i, low_j:high_j] = product
    else:
        result_ref[low_i:high_i, low_j:high_j] += product


def unit_of(values, coef):
    unit = (values - coef[0:1]) * coef[1:2]
    return unit, coef[2:3] * unit + coef[3:4]


def masked_sums(values, valid):
    weighted = values * valid
    return jnp.concatenate(
        [jnp.sum(weighted, axis=0, keepdims=True), jnp.sum(weighted * values, axis=0, keepdims=True)]
    )


def sum_rows(ref, valid_ref, sums_ref):
    total = jnp.zeros(sums_ref.shape, F32)
    for row in range(ref.shape[0]):
        values = ref[row].reshape(-1, ref.shape[-1])
        total = total + masked_sums(values, valid_ref[row].reshape(-1, 1))
    sums_ref[...] = total


def branch_body(taps, source_ref, valid_ref, weight_ref, result_ref, sums_ref):
    for place, tap in enumerate(taps):

        @pl.when(pl.program_id(0) == place)
        def _(place=place, tap=tap):
            forward_tap(tap, place == 0, source_ref, weight_of(weight_ref), result_ref)

    @pl.when(pl.program_id(0) == len(taps) - 1)
    def _():
        sum_rows(result_ref, valid_ref, sums_ref)


def tap_block(weights, channels, first_tap, center, first_step=0, count=None):
    pieces, _, columns = weights.shape

    def index(step):
        if count is not None:
            step = jnp.clip(step - first_step, 0, count - 1)
        return (0, first_tap + center_first(step, center), 0)

    return pl.BlockSpec((pieces, channels // pieces, columns), index)


def branch_conv(source, valid, weights, taps, center, first_tap, after):
    channels, columns = source.shape[-1], weights.shape[2]
    shifts = ordered(shifts_of(taps), center)
    result_shape = source.shape[:3] + (columns,)
    macs = sum(area(tap, source.shape) for tap in shifts) * channels * columns
    return call(
        functools.partial(branch_body, shifts),
        [source, valid, weights],
        [whole(source), whole(valid), tap_block(weights, channels, first_tap, center)],
        (len(taps),),
        [shaped(result_shape), shaped((2, columns))],
        [held(result_shape), held((2, columns))],
        after=after,
        flops=2 * macs,
    )


def spatial_body(taps, first_ref, coef_ref, valid_ref, weight_ref, input_ref, result_ref, sums_ref):
    @pl.when(pl.program_id(0) == 0)
    def _():
        for row in range(first_ref.shape[0]):
            _, pre = unit_of(first_ref[row], coef_ref[...][:, None, :])
            input_ref[row] = (silu(pre) * valid_ref[row]).astype(BF16)

    branch_body(taps, input_ref, valid_ref, weight_ref, result_ref, sums_ref)


def spatial_conv(first, coef, valid, weights, taps, center, first_tap):
    channels, columns = first.shape[-1], weights.shape[2]
    shifts = ordered(shifts_of(taps), center)
    macs = sum(area(tap, first.shape) for tap in shifts) * channels * columns
    return call(
        functools.partial(spatial_body, shifts),
        [first, coef, valid, weights],
        [whole(first), whole(coef), whole(valid), tap_block(weights, channels, first_tap, center)],
        (len(taps),),
        [shaped(first.shape, BF16), shaped(first.shape), shaped((2, columns))],
        [held(first.shape), held(first.shape), held((2, columns))],
        flops=2 * macs,
    )


def backward_tap(tap, fresh, up_ref, column, weight_ref, result_ref):
    tiles_i, tiles_j, pixels, channels = result_ref.shape
    pieces, rows, width = weight_ref.shape
    shift_i, shift_j = tap
    low_i, high_i = span(shift_i, tiles_i)
    low_j, high_j = span(shift_j, tiles_j)
    window = up_ref[low_i:high_i, low_j:high_j, :, column : column + width].reshape(-1, width)
    wide = min(512, channels)
    for start in range(0, channels, wide):
        if pieces == 1:
            weight = weight_ref[0, start : start + wide]
        else:
            weight = weight_ref[start // rows : (start + wide) // rows].reshape(wide, width)
        product = lax.dot_general(
            window, weight, (((1,), (1,)), ((), ())), preferred_element_type=F32
        ).reshape(high_i - low_i, high_j - low_j, pixels, wide)
        place = (
            slice(low_i + shift_i, high_i + shift_i),
            slice(low_j + shift_j, high_j + shift_j),
            slice(None),
            slice(start, start + wide),
        )
        if fresh:
            result_ref[place] = product
        else:
            result_ref[place] += product


def grad_moments(grad, unit):
    return jnp.concatenate(
        [jnp.sum(grad, axis=0, keepdims=True), jnp.sum(grad * unit, axis=0, keepdims=True)]
    )


def feature_body(plan, up_ref, third_ref, source_ref, coef_ref, pooled_ref, valid_ref, *refs):
    weight_refs = refs[: len(plan)]
    result_ref, sums_ref, total_ref = refs[len(plan) :]
    step_now = pl.program_id(0)
    begun = 0
    for weight_ref, listed in zip(weight_refs, plan):
        for tap, column in listed:

            @pl.when(step_now == begun)
            def _(weight_ref=weight_ref, tap=tap, column=column, fresh=begun == 0):
                backward_tap(tap, fresh, up_ref, column, weight_ref, total_ref)

            begun += 1

    @pl.when(step_now >= begun)
    def _():
        row = step_now - begun
        width = total_ref.shape[-1]
        unit, pre = unit_of(third_ref[...], coef_ref[...])
        pre = pre + source_ref[...].astype(F32)
        grad = total_ref[row].reshape(-1, width) + pooled_ref[...]
        grad = grad * valid_ref[...] * silu_slope(pre)
        result_ref[...] = grad.astype(BF16)
        moments = grad_moments(grad, unit)

        @pl.when(step_now == begun)
        def _():
            sums_ref[...] = moments

        @pl.when(step_now > begun)
        def _():
            sums_ref[...] += moments


def feature_back(upstream, groups, third, source, coef, pooled, valid, side, sides, after):
    channels = third.shape[1]
    part = channels // sides
    plan, arrays, specs, begun, macs = [], [], [], 0, 0
    for weights, taps, center, columns, first_tap in groups:
        shifts = ordered(list(zip(shifts_of(taps), columns)), center)
        plan.append(shifts)
        count = len(shifts)
        pieces, _, width = weights.shape
        rows = channels // pieces

        def index(step, first=begun, count=count, center=center, first_tap=first_tap, pieces=pieces):
            tap = first_tap + center_first(jnp.clip(step - first, 0, count - 1), center)
            return (0, tap * sides + side, 0) if pieces == 1 else (side, tap, 0)

        block = (1, rows // sides, width) if pieces == 1 else (pieces // sides, rows, width)
        arrays.append(weights)
        specs.append(pl.BlockSpec(block, index))
        begun += count
        macs += sum(area(tap, upstream.shape) for tap, _ in shifts) * part * width
    turns = upstream.shape[0]
    height = third.shape[0] // turns

    def row_of(step):
        return jnp.clip(step - begun, 0, turns - 1)

    row_block = pl.BlockSpec((height, part), lambda step: (row_of(step), side))
    return call(
        functools.partial(feature_body, plan),
        [upstream, third, source, coef, pooled, valid] + arrays,
        [
            whole(upstream),
            row_block,
            row_block,
            pl.BlockSpec((coef.shape[0], part), lambda step: (0, side)),
            pl.BlockSpec((1, part), lambda step: (0, side)),
            pl.BlockSpec((height, 1), lambda step: (row_of(step), 0)),
        ]
        + specs,
        (begun + turns,),
        [shaped((third.shape[0], part), BF16), shaped((2, part))],
        [pl.BlockSpec((height, part), lambda step: (row_of(step), 0)), held((2, part))],
        [pltpu.VMEM(upstream.shape[:3] + (part,), F32)],
        after=after,
        flops=2 * macs,
    )


def spatial_back_body(taps, up_ref, first_ref, coef_ref, valid_ref, weight_ref, result_ref, sums_ref):
    for place, tap in enumerate(taps):

        @pl.when(pl.program_id(0) == place)
        def _(place=place, tap=tap):
            backward_tap(tap, place == 0, up_ref, 0, weight_ref, result_ref)

    @pl.when(pl.program_id(0) == len(taps) - 1)
    def _():
        total = jnp.zeros(sums_ref.shape, F32)
        width = result_ref.shape[-1]
        for row in range(result_ref.shape[0]):
            unit, pre = unit_of(first_ref[row].reshape(-1, width), coef_ref[...])
            valid = valid_ref[row].reshape(-1, 1)
            grad = result_ref[row].reshape(-1, width) * valid * silu_slope(pre)
            result_ref[row] = grad.reshape(result_ref.shape[1:])
            total = total + grad_moments(grad, unit)
        sums_ref[...] = total


def spatial_back(upstream, first, coef, valid, weights, taps, center, first_tap, after):
    channels, columns = first.shape[-1], weights.shape[2]
    shifts = ordered(shifts_of(taps), center)
    macs = sum(area(tap, first.shape) for tap in shifts) * channels * columns
    return call(
        functools.partial(spatial_back_body, shifts),
        [upstream, first, coef, valid, weights],
        [
            whole(upstream),
            whole(first),
            whole(coef),
            whole(valid),
            tap_block(weights, channels, first_tap, center),
        ],
        (len(taps),),
        [shaped(first.shape), shaped((2, channels))],
        [held(first.shape), held((2, channels))],
        after=after,
        flops=2 * macs,
    )


def weight_tap(tap, tiles, flipped_ref, up_ref, padded_ref):
    tiles_i, tiles_j, pixels = tiles
    shift_i, shift_j = tap
    low_i, high_i = span(shift_i, tiles_i)
    low_j, high_j = span(shift_j, tiles_j)
    padded_ref[...] = jnp.zeros_like(padded_ref)
    wide = (high_j - low_j) * pixels
    for row in range(low_i, high_i):
        target = ((row + shift_i) * tiles_j + low_j + shift_j) * pixels
        source = (row * tiles_j + low_j) * pixels
        padded_ref[target : target + wide] = up_ref[source : source + wide]
    first = (low_i + shift_i) * tiles_j * pixels // 128 * 128
    last = -(-(high_i + shift_i) * tiles_j * pixels // 128) * 128
    return jnp.dot(
        flipped_ref[:, first:last], padded_ref[first:last], preferred_element_type=F32
    )


def weight_body(plan, tiles, extra, count, meta_ref, flipped_ref, up_ref, *refs):
    extra_ref = refs[0] if extra else None
    result_refs = refs[extra : extra + count]
    padded_ref, full_ref = refs[extra + count :]
    width = padded_ref.shape[1]
    for place, (tap, column) in enumerate(plan):

        @pl.when(pl.program_id(0) == place)
        def _(tap=tap, column=column):
            full_ref[...] = weight_tap(
                tap, tiles, flipped_ref, up_ref.at[:, column : column + width], padded_ref
            ).astype(BF16)
            spread(meta_ref, full_ref, result_refs)

    if extra:

        @pl.when(pl.program_id(0) == len(plan))
        def _():
            core = meta_ref[0]
            slots, held_rows, _ = result_refs[0].shape
            rows = extra_ref.shape[0] // slots // 2
            spare = jnp.zeros((held_rows - rows, width), F32)
            for owner in range(slots):
                for ref, side in zip(result_refs, (core, 1 - core)):
                    start = pl.multiple_of(owner * 2 * rows + side * rows, 8)
                    block = jnp.concatenate([extra_ref[pl.ds(start, rows)], spare])
                    ref[meta_ref[1 + owner]] = block.astype(BF16)


def weight_grad(place, flipped, upstream, meta, taps, columns, tiles, width, after=(), extra=None):
    channels, padded = flipped.shape
    plan = list(zip(shifts_of(taps), columns))
    steps = len(taps) + (extra is not None)
    shapes = slotted(place, channels // place.size * steps, width)
    blocks = [
        pl.BlockSpec((shape.shape[0], shape.shape[1] // steps, width), lambda step, _: (0, step, 0))
        for shape in shapes
    ]
    macs = sum(area(tap, tiles) for tap, _ in plan) * channels * width
    more = [] if extra is None else [extra]
    return call(
        functools.partial(weight_body, plan, tiles, len(more), len(shapes)),
        [flipped, upstream] + more,
        [whole(array) for array in [flipped, upstream] + more],
        (steps,),
        shapes,
        blocks,
        [pltpu.VMEM((padded, width), BF16), pltpu.VMEM((channels, width), BF16)],
        meta,
        after,
        2 * macs,
    )


def tile_matrix(breadth):
    count = TILE * breadth
    matrix = np.zeros((count, count), np.float32)
    for row in range(TILE):
        for column in range(breadth):
            at = (column // TILE * TILE + row) * TILE + column % TILE
            matrix[at, row * breadth + column] = 1.0
    return matrix


def tile_body(matrix_ref, natural_ref, result_ref):
    result_ref[...] = jnp.dot(
        matrix_ref[...], natural_ref[...], preferred_element_type=F32
    ).astype(BF16)


def tile_rows(natural, matrix):
    rows = matrix.shape[0]
    return call(
        tile_body,
        [matrix, natural],
        [whole(matrix), rows_of(natural, rows)],
        (natural.shape[0] // rows,),
        [shaped(natural.shape, BF16)],
        [rows_of(natural, rows)],
        flops=2 * rows * natural.size,
    )[0]


def flip_body(source_ref, result_ref):
    pixels = source_ref.shape[0]
    result_ref[:, :pixels] = source_ref[...].T
    if result_ref.shape[1] > pixels:
        extra = result_ref.shape[1] - pixels
        result_ref[:, pixels:] = jnp.zeros((result_ref.shape[0], extra), BF16)


def flipped(values, after=()):
    pixels, channels = values.shape
    padded = pixels + -pixels % 128
    return call(
        flip_body,
        [values],
        [pl.BlockSpec((pixels, 128), lambda step: (0, step))],
        (channels // 128,),
        [shaped((channels, padded), BF16)],
        [pl.BlockSpec((128, padded), lambda step: (step, 0))],
        after=after,
    )[0]


def add_sums(sums_ref, sums):
    @pl.when(pl.program_id(0) == 0)
    def _():
        sums_ref[...] = sums

    @pl.when(pl.program_id(0) > 0)
    def _():
        sums_ref[...] += sums


def first_body(source_ref, valid_ref, weight_ref, result_ref, sums_ref):
    product = jnp.dot(source_ref[...], weight_of(weight_ref), preferred_element_type=F32)
    result_ref[...] = product
    add_sums(sums_ref, masked_sums(product, valid_ref[...]))


def fixed_block(weights, channels, at):
    pieces, _, columns = weights.shape
    return pl.BlockSpec((pieces, channels // pieces, columns), lambda step, *_: (0, at, 0))


def first_conv(source, valid, weights, turns, after):
    pixels, channels = source.shape
    rows = pixels // turns
    width = weights.shape[2]
    return call(
        first_body,
        [source, valid, weights],
        [rows_of(source, rows), rows_of(valid, rows), fixed_block(weights, channels, 0)],
        (turns,),
        [shaped((pixels, width)), shaped((2, width))],
        [pl.BlockSpec((rows, width), lambda step: (step, 0)), held((2, width))],
        after=after,
        flops=2 * pixels * channels * width,
    )


def third_body(count, second_ref, coef_ref, valid_ref, *refs):
    weight_refs = refs[:count]
    middle_ref, result_ref, sums_ref = refs[count:]
    _, pre = unit_of(second_ref[...], coef_ref[...])
    middle = silu(pre).astype(BF16)
    middle_ref[...] = middle
    valid = valid_ref[...]
    sums = []
    for quarter, ref in enumerate(weight_refs):
        product = jnp.dot(middle, weight_of(ref), preferred_element_type=F32)
        width = product.shape[1]
        result_ref[:, quarter * width : (quarter + 1) * width] = product
        sums.append(masked_sums(product, valid))
    add_sums(sums_ref, jnp.concatenate(sums, axis=1))


def third_conv(second, coef, valid, weights, first, count, turns):
    pixels, narrow = second.shape
    height = pixels // turns
    channels = count * weights.shape[2]
    return call(
        functools.partial(third_body, count),
        [second, coef, valid] + [weights] * count,
        [rows_of(second, height), whole(coef), rows_of(valid, height)]
        + [fixed_block(weights, narrow, first + quarter) for quarter in range(count)],
        (turns,),
        [shaped((pixels, narrow), BF16), shaped((pixels, channels)), shaped((2, channels))],
        [
            pl.BlockSpec((height, narrow), lambda step: (step, 0)),
            pl.BlockSpec((height, channels), lambda step: (step, 0)),
            held((2, channels)),
        ],
        flops=2 * pixels * narrow * channels,
    )


def output_body(third_ref, source_ref, coef_ref, valid_ref, result_ref, sums_ref):
    _, pre = unit_of(third_ref[...], coef_ref[...])
    values = (valid_ref[...] * silu(pre + source_ref[...].astype(F32))).astype(BF16)
    result_ref[...] = values
    add_sums(sums_ref, jnp.sum(values.astype(F32), axis=0, keepdims=True))


def block_output(third, source, coef, valid, turns):
    pixels, channels = third.shape
    rows = pixels // turns
    return call(
        output_body,
        [third, source, coef, valid],
        [rows_of(third, rows), rows_of(source, rows), whole(coef), rows_of(valid, rows)],
        (turns,),
        [shaped(third.shape, BF16), shaped((1, channels))],
        [rows_of(third, rows), held((1, channels))],
    )


def third_back_body(
    count, outs, meta_ref, low_ref, high_ref, third_ref, coef_ref, totals_ref, valid_ref, middle_ref, *refs
):
    weight_refs = refs[:count]
    result_ref = refs[count]
    slot_refs = refs[count + 1 : count + 1 + outs]
    grad_ref, total_ref = refs[count + 1 + outs :]
    step_now = pl.program_id(0)

    @pl.when(step_now == 0)
    def _():
        total_ref[...] = jnp.zeros_like(total_ref)

    part = low_ref.shape[1]
    coef, totals, valid = coef_ref[...], totals_ref[...], valid_ref[...]
    for start, part_ref in ((0, low_ref), (part, high_ref)):
        at = slice(start, start + part)
        unit = (third_ref[:, at] - coef[0:1, at]) * coef[1:2, at]
        centered = part_ref[...].astype(F32) - valid * (totals[0:1, at] + unit * totals[1:2, at])
        grad_ref[:, at] = (coef[2:3, at] * coef[1:2, at] * centered).astype(BF16)
    width = weight_refs[0].shape[2]
    result = None
    for quarter, ref in enumerate(weight_refs):
        grad = grad_ref[:, quarter * width : (quarter + 1) * width]
        product = lax.dot_general(
            grad, weight_of(ref), (((1,), (1,)), ((), ())), preferred_element_type=F32
        )
        result = product if result is None else result + product
    result_ref[...] = result
    total_ref[...] += lax.dot_general(
        middle_ref[...], grad_ref[...], (((0,), (0,)), ((), ())), preferred_element_type=F32
    )

    @pl.when(step_now == pl.num_programs(0) - 1)
    def _():
        rows = slot_refs[0].shape[1] // count
        for quarter in range(count):
            spread(meta_ref, total_ref, slot_refs, quarter * width, quarter * rows, rows)


def third_back(place, low, high, third, coef, totals, valid, middle, weights, meta, first, count, turns, after):
    pixels, channels = third.shape
    narrow = middle.shape[1]
    height = pixels // turns
    shapes = slotted(place, narrow // place.size * count, weights.shape[2])
    return call(
        functools.partial(third_back_body, count, len(shapes)),
        [low, high, third, coef, totals, valid, middle] + [weights] * count,
        [
            rows_of(low, height),
            rows_of(high, height),
            rows_of(third, height),
            whole(coef),
            whole(totals),
            rows_of(valid, height),
            rows_of(middle, height),
        ]
        + [fixed_block(weights, narrow, first + quarter) for quarter in range(count)],
        (turns,),
        [shaped((pixels, narrow))] + shapes,
        [pl.BlockSpec((height, narrow), lambda step, _: (step, 0))] + [held(shape.shape) for shape in shapes],
        [pltpu.VMEM((height, channels), BF16), pltpu.VMEM((narrow, channels), F32)],
        meta,
        after,
        4 * pixels * narrow * channels,
    )


def input_body(matrix_ref, low_ref, high_ref, grad_ref, weight_ref, result_ref):
    rows = matrix_ref.shape[0]
    part = low_ref.shape[1]
    matrix = matrix_ref[...]
    moved = []
    for start in range(0, result_ref.shape[0], rows):
        at = slice(start, start + rows)
        moved.append(jnp.dot(matrix, grad_ref[at], preferred_element_type=F32).astype(BF16))
        for column, part_ref in ((0, low_ref), (part, high_ref)):
            result_ref[at, column : column + part] = jnp.dot(
                matrix, part_ref[at], preferred_element_type=F32
            )
    result_ref[...] += lax.dot_general(
        jnp.concatenate(moved), weight_of(weight_ref), (((1,), (1,)), ((), ())), preferred_element_type=F32
    )


def input_back(matrix, low, high, grad, weights, turns, after, passed):
    pixels, part = low.shape
    rows = pixels // turns
    channels = 2 * part
    width = grad.shape[1]
    return call(
        input_body,
        [matrix, low, high, grad, weights],
        [
            whole(matrix),
            rows_of(low, rows),
            rows_of(high, rows),
            rows_of(grad, rows),
            fixed_block(weights, channels, 0),
        ],
        (turns,),
        [shaped((pixels, channels))],
        [pl.BlockSpec((rows, channels), lambda step: (step, 0))],
        after=after,
        passed=passed,
        flops=2 * pixels * channels * (width + matrix.shape[0]),
    )


def sigmoid(values):
    return 0.5 + 0.5 * jnp.tanh(0.5 * values)


def silu(values):
    return values * sigmoid(values)


def silu_slope(values):
    sigmoid_val = sigmoid(values)
    return sigmoid_val * (1.0 + values * (1.0 - sigmoid_val))


def sums(values, validity):
    weighted = values * validity
    return jnp.stack([jnp.sum(weighted, axis=0), jnp.sum(weighted * values, axis=0)])


def coefs(totals, counted, gain, shift):
    mean_value = totals[0] / counted
    scaling = lax.rsqrt(totals[1] / counted - mean_value * mean_value + EPSILON)
    return jnp.stack([mean_value, scaling, gain, shift])


def through_norm(grad_pre, unit, coef, counted, validity, totals):
    centered = grad_pre - validity * (totals[0] + unit * totals[1]) / counted
    return coef[2] * coef[1] * centered


def to_tiles(array):
    height, breadth = array.shape[:2]
    rest = array.shape[2:]
    cut = array.reshape((height // TILE, TILE, breadth // TILE, TILE) + rest)
    return jnp.swapaxes(cut, 1, 2).reshape((height * breadth,) + rest)


def per_device(
    features,
    reduce_weight,
    spatial_weight,
    expand_weight,
    bottle_gain,
    bottle_shift,
    point_weight,
    near_weight,
    middle_weight,
    far_weight,
    image_weight,
    project_weight,
    class_weight,
    pyramid_gain,
    pyramid_shift,
    head_gain,
    head_shift,
    crop_masks,
    crop_tasks,
    pixel_labels,
    task_norms,
):
    place = Place()
    size, core = place.size, place.core
    first_core = core == 0
    height, breadth, channels = features.shape[2:]
    pixels = height * breadth
    tiles = (height // TILE, breadth // TILE, TILE * TILE)
    narrow = reduce_weight.shape[1]
    branch = point_weight.shape[1]
    four_wide = 4 * branch
    rows = channels // size
    narrow_rows = narrow // size
    quarters = channels // narrow
    turns = 3
    meta = place.meta()
    matrix = tile_matrix(breadth)

    bottle_taps = tap_list(height, breadth, BOTTLE_RATE)
    near_taps = tap_list(height, breadth, NEAR_RATE)
    middle_taps = tap_list(height, breadth, MIDDLE_RATE)
    far_taps = tap_list(height, breadth, FAR_RATE)
    point_taps = [(1, 1, 0, 0)]

    def center_of(taps):
        return [tap[:2] for tap in taps].index((1, 1))

    def stacked(weight, taps):
        flat = weight.reshape((-1,) + weight.shape[2:])
        picked = [3 * tap[0] + tap[1] for tap in taps]
        if picked == list(range(picked[0], picked[-1] + 1)):
            flat = flat[picked[0] : picked[-1] + 1]
        else:
            flat = jnp.stack([flat[at] for at in picked])
        return flat.reshape(-1, flat.shape[2]), len(taps)

    mask = lax.dynamic_index_in_dim(crop_masks, core, 0, keepdims=False)[0]
    labels = lax.dynamic_index_in_dim(pixel_labels, core, 0, keepdims=False)[0]
    task = lax.dynamic_index_in_dim(crop_tasks, core, 0, keepdims=False)[0]
    validity = to_tiles(mask).astype(F32)[:, None]
    valid_tiles = validity.reshape(tiles + (1,))
    labels = to_tiles(labels)
    source = tile_rows(features.reshape(pixels, channels), jnp.array(matrix, BF16))
    source_flipped = flipped(source)

    wide_expand = expand_weight.reshape(-1, quarters, narrow)
    expand_parts = [(wide_expand[:, at], 1) for at in range(quarters)]
    bottle_all = place.gather([(reduce_weight, 1), stacked(spatial_weight, bottle_taps)] + expand_parts)
    spatial_at = channels // narrow
    expand_at = spatial_at + len(bottle_taps)
    pyramid_parts = [stacked(near_weight, near_taps), stacked(middle_weight, middle_taps)]
    pyramid_parts += [stacked(far_weight, far_taps), (point_weight, 1), (project_weight, 1)]
    pyramid_all = place.gather(pyramid_parts)
    middle_at = len(near_taps)
    far_at = middle_at + len(middle_taps)
    point_at = far_at + len(far_taps)
    project_at = (point_at + 1) * (channels // place.pieces)
    project_full = pyramid_all[:, project_at:].reshape(-1, branch)

    crop_valid_both = jnp.sum(crop_masks, axis=(1, 2, 3)).astype(F32)
    home_crop = (crop_tasks[:, 0] == 1).astype(F32)
    counts = jnp.concatenate(
        [
            crop_valid_both,
            jnp.sum(crop_valid_both * (1.0 - home_crop))[None],
            jnp.sum(crop_valid_both * home_crop)[None],
        ]
    )
    small = [bottle_gain, bottle_shift, pyramid_gain, pyramid_shift, head_gain, head_shift]
    small.append(class_weight.reshape(-1))
    small_widths = [part.shape[0] for part in small]
    small_own = jnp.concatenate(small).astype(F32)
    placed = lax.dynamic_update_slice(
        jnp.zeros((size, small_own.shape[0]), F32), small_own[None], (place.index, 0)
    )
    collected = place.total(jnp.concatenate([placed.reshape(-1), counts]))
    counts_all = collected[placed.size :]
    collected = collected[: placed.size].reshape(size, -1)
    small_all, start = [], 0
    for width in small_widths:
        small_all.append(collected[:, start : start + width].reshape(-1))
        start += width
    gain_bottle, shift_bottle, gain_pyramid, shift_pyramid, gain_head, shift_head = small_all[:6]
    class_full = small_all[6].reshape(size * class_weight.shape[0], -1).astype(BF16)
    counted = jnp.where(first_core, counts_all[0], counts_all[1])
    task_pixels = counts_all[2:4]
    crop_valid = jnp.where(first_core, crop_valid_both[0], crop_valid_both[1])

    first, first_sums = first_conv(source, validity, bottle_all, turns, [source_flipped])
    coef_one = coefs(place.total(first_sums), counted, gain_bottle[:narrow], shift_bottle[:narrow])
    first_tiles = first.reshape(tiles + (narrow,))
    conv_in, second, second_sums = spatial_conv(
        first_tiles, coef_one, valid_tiles, bottle_all, bottle_taps, center_of(bottle_taps), spatial_at
    )
    second = second.reshape(pixels, narrow)
    coef_two = coefs(
        place.total(second_sums), counted, gain_bottle[narrow : 2 * narrow], shift_bottle[narrow : 2 * narrow]
    )
    middle_act, third, third_sums = third_conv(
        second, coef_two, validity, bottle_all, expand_at, quarters, turns
    )
    coef_three = coefs(
        place.total(third_sums), counted, gain_bottle[2 * narrow :], shift_bottle[2 * narrow :]
    )
    block_out, pooled_sum = block_output(third, source, coef_three, validity, tiles[0])
    block_tiles = block_out.reshape(tiles + (channels,))
    block_flipped = flipped(block_out)
    conv_flipped = flipped(conv_in.reshape(pixels, narrow))

    pooled = (pooled_sum / crop_valid).astype(BF16)
    pooled_plane = place.plane_total(
        lax.dynamic_update_slice(jnp.zeros((size, channels), BF16), pooled, (place.index, 0))
    )
    near_out, near_sums = branch_conv(
        block_tiles,
        valid_tiles,
        pyramid_all,
        near_taps,
        center_of(near_taps),
        0,
        [block_flipped, conv_flipped],
    )
    pooled_all = place.line_total(pooled_plane)
    middle_out, middle_sums = branch_conv(
        block_tiles,
        valid_tiles,
        pyramid_all,
        middle_taps,
        center_of(middle_taps),
        middle_at,
        [pooled_plane, near_sums],
    )
    pooled_rows = lax.dynamic_slice_in_dim(pooled_all, place.index * rows, rows, axis=1)
    image_plane = place.plane_total(
        jnp.dot(pooled_rows, image_weight, preferred_element_type=F32)
    )
    far_out, far_sums = branch_conv(
        block_tiles,
        valid_tiles,
        pyramid_all,
        far_taps,
        center_of(far_taps),
        far_at,
        [pooled_all, middle_sums],
    )
    image_all = place.line_total(image_plane)
    point_out, point_sums = branch_conv(
        block_tiles, valid_tiles, pyramid_all, point_taps, 0, point_at, [image_plane, far_sums]
    )
    image_mean = jnp.sum(image_all, axis=0) / size
    image_scale = lax.rsqrt(
        jnp.sum(image_all * image_all, axis=0) / size - image_mean * image_mean + EPSILON
    )
    image_unit = (image_all - image_mean) * image_scale
    gain_image, shift_image = gain_pyramid[four_wide:], shift_pyramid[four_wide:]
    coef_image = jnp.stack([image_mean, image_scale, gain_image, shift_image])
    image_pre = gain_image * image_unit + shift_image
    image_act = silu(image_pre).astype(BF16)

    outs = [part.reshape(pixels, branch) for part in (point_out, near_out, middle_out, far_out)]
    branches = jnp.concatenate(outs, axis=1)
    branch_sums = jnp.concatenate([point_sums, near_sums, middle_sums, far_sums], axis=1)
    coef_branch = coefs(
        place.total(branch_sums), counted, gain_pyramid[:four_wide], shift_pyramid[:four_wide]
    )
    unit_branch, pre_branch = unit_of(branches, coef_branch)
    joined = silu(pre_branch).astype(BF16)

    own_act = lax.dynamic_slice_in_dim(image_act, place.index, 1, axis=0)
    crop_part = jnp.dot(own_act, project_full[four_wide:], preferred_element_type=F32)
    projected = jnp.dot(joined, project_full[:four_wide], preferred_element_type=F32) + crop_part
    coef_head = coefs(place.total(sums(projected, validity)), counted, gain_head, shift_head)
    unit_head, pre_head = unit_of(projected, coef_head)
    output_act = silu(pre_head).astype(BF16)
    logits = jnp.dot(output_act, class_full, preferred_element_type=F32)

    columns = jnp.arange(class_full.shape[1])
    allowed = (columns >= CITY_CLASSES) == (task == 1)
    masked = jnp.where(allowed, logits, FLOOR_LOGIT)
    raised = jnp.exp(masked - jnp.max(masked, axis=-1, keepdims=True))
    chances = raised / jnp.sum(raised, axis=-1, keepdims=True)
    target = jnp.where(task == 0, labels % CITY_CLASSES, CITY_CLASSES + labels % HOME_CLASSES)
    chosen = (columns == target[:, None]).astype(F32)
    inverse = 1.0 / task_norms.astype(F32)
    task_share = inverse / jnp.sum(inverse)
    crop_weight = jnp.where(
        task == 0, task_share[0] / task_pixels[0], task_share[1] / task_pixels[1]
    )
    logit_grad = (crop_weight * validity * (chances - chosen)).astype(BF16)
    class_grad = lax.dot_general(
        output_act, logit_grad, (((0,), (0,)), ((), ())), preferred_element_type=F32
    )

    output_grad = lax.dot_general(
        logit_grad, class_full, (((1,), (1,)), ((), ())), preferred_element_type=F32
    )
    grad_head = output_grad * silu_slope(pre_head)
    head_totals = place.total(
        jnp.concatenate([grad_moments(grad_head, unit_head).reshape(-1), class_grad.reshape(-1)])
    )
    class_total = head_totals[2 * branch :]
    head_totals = head_totals[: 2 * branch].reshape(2, branch)
    proj_grad = through_norm(
        grad_head, unit_head, coef_head, counted, validity, head_totals
    ).astype(BF16)
    crop_grad = jnp.sum(proj_grad, axis=0, dtype=F32)
    joined_grad = lax.dot_general(
        proj_grad, project_full[:four_wide], (((1,), (1,)), ((), ())), preferred_element_type=F32
    )
    act_grad = jnp.dot(project_full[four_wide:].astype(F32), crop_grad, precision=HIGHEST)
    own_pre = lax.dynamic_slice_in_dim(image_pre, place.index, 1, axis=0)[0]
    image_pre_grad = act_grad * silu_slope(own_pre)
    grad_branch = joined_grad * silu_slope(pre_branch)
    placed_pre = lax.dynamic_update_slice(
        jnp.zeros((size, branch), F32), image_pre_grad[None], (place.index, 0)
    )
    branch_totals = place.total(
        jnp.concatenate([grad_moments(grad_branch, unit_branch).reshape(-1), placed_pre.reshape(-1)])
    )
    image_pre_all = branch_totals[2 * four_wide :].reshape(size, branch)
    branch_totals = branch_totals[: 2 * four_wide].reshape(2, four_wide)
    branch_grad = through_norm(
        grad_branch, unit_branch, coef_branch, counted, validity, branch_totals
    ).astype(BF16)
    image_totals = grad_moments(image_pre_all, image_unit)
    image_in_all = through_norm(
        image_pre_all, image_unit, coef_image, float(size), 1.0, image_totals
    )
    pooled_partial = lax.dot_general(
        image_in_all, image_weight.astype(F32), (((1,), (1,)), ((), ())), precision=HIGHEST
    )
    pooled_grad_plane = place.plane_total(
        lax.dynamic_update_slice(
            jnp.zeros((size, channels), F32), pooled_partial, (0, place.index * rows)
        )
    )
    image_partial = jnp.dot(pooled_rows.astype(F32).T, image_in_all, precision=HIGHEST)

    def columns_of(taps, block):
        return [block * branch] * len(taps)

    wide_taps = far_taps + point_taps
    wide_columns = columns_of(far_taps, 3) + columns_of(point_taps, 0)
    project_grad = jnp.concatenate(
        [
            lax.dot_general(
                joined, proj_grad, (((0,), (0,)), ((), ())), preferred_element_type=F32
            ),
            own_act[0].astype(F32)[:, None] * crop_grad[None, :],
        ]
    )

    def branch_weight_grad(taps, tap_columns, after, extra=None):
        return weight_grad(
            place, block_flipped, branch_grad, meta, taps, tap_columns, tiles, branch, after, extra
        )

    near_grads = branch_weight_grad(near_taps, columns_of(near_taps, 1), ())
    near_scatter = Scatter(place, near_grads, [rows] * len(near_taps))
    pooled_grad_all = place.line_total(pooled_grad_plane)
    middle_grads = branch_weight_grad(
        middle_taps, columns_of(middle_taps, 2), [near_grads[0], pooled_grad_plane]
    )
    middle_scatter = Scatter(place, middle_grads, [rows] * len(middle_taps))
    far_grads = branch_weight_grad(
        wide_taps,
        wide_columns,
        [middle_grads[0], pooled_grad_all] + near_scatter.arrived,
        project_grad if place.direct else None,
    )
    near_scatter.first()
    if not place.direct:
        far_grads = [jnp.concatenate([far_grads[0], project_grad.astype(BF16)[None]], axis=1)]
    far_rows = [rows] * len(wide_taps) + [project_weight.shape[0]]
    far_scatter = Scatter(place, far_grads, far_rows)

    pooled_grad = lax.dynamic_slice_in_dim(pooled_grad_all, place.index, 1, axis=0) / crop_valid
    groups = [
        (pyramid_all, near_taps, center_of(near_taps), columns_of(near_taps, 1), 0),
        (pyramid_all, middle_taps, center_of(middle_taps), columns_of(middle_taps, 2), middle_at),
        (pyramid_all, wide_taps, center_of(far_taps), wide_columns, far_at),
    ]

    def half_back(side, after):
        return feature_back(
            branch_grad.reshape(tiles + (four_wide,)),
            groups,
            third,
            source,
            coef_three,
            pooled_grad,
            validity,
            side,
            2,
            after,
        )

    low_grad, low_moments = half_back(0, [far_grads[0]] + middle_scatter.arrived)
    high_grad, high_moments = half_back(1, [low_moments] + near_scatter.arrived + far_scatter.arrived)
    near_scatter.second()
    middle_scatter.first()
    three_totals = place.total(jnp.concatenate([low_moments, high_moments], axis=1))
    middle_grad, *expand_grads = third_back(
        place,
        low_grad,
        high_grad,
        third,
        coef_three,
        three_totals / counted,
        validity,
        middle_act,
        bottle_all,
        meta,
        expand_at,
        quarters,
        turns,
        near_scatter.arrived + middle_scatter.arrived,
    )
    near_scatter.third()
    middle_scatter.second()
    far_scatter.first()
    unit_two, pre_two = unit_of(second, coef_two)
    grad_two = middle_grad * silu_slope(pre_two)
    two_totals = place.total(grad_moments(grad_two, unit_two))
    second_grad = through_norm(
        grad_two, unit_two, coef_two, counted, validity, two_totals
    ).astype(BF16)
    spatial_grads = weight_grad(
        place,
        conv_flipped,
        second_grad,
        meta,
        bottle_taps,
        [0] * len(bottle_taps),
        tiles,
        narrow,
        middle_scatter.arrived + far_scatter.arrived,
    )
    bottle_grads = [
        jnp.concatenate(pair, axis=1) for pair in zip(spatial_grads, expand_grads)
    ]
    bottle_rows = [narrow_rows] * (len(bottle_taps) + quarters)
    bottle_scatter = Scatter(place, bottle_grads, bottle_rows)
    middle_scatter.third()
    far_scatter.second()
    grad_one, one_moments = spatial_back(
        second_grad.reshape(tiles + (narrow,)),
        first_tiles,
        coef_one,
        valid_tiles,
        bottle_all,
        bottle_taps,
        center_of(bottle_taps),
        spatial_at,
        [spatial_grads[0]] + near_scatter.arrived,
    )
    far_scatter.third()
    one_totals = place.total(one_moments)
    unit_one, _ = unit_of(first, coef_one)
    first_grad = through_norm(
        grad_one.reshape(pixels, narrow), unit_one, coef_one, counted, validity, one_totals
    ).astype(BF16)
    reduce_grads = weight_grad(
        place, source_flipped, first_grad, meta, point_taps, [0], tiles, narrow, bottle_scatter.arrived
    )
    bottle_scatter.first()
    reduce_scatter = Scatter(place, reduce_grads, [rows])
    reduce_scatter.first()
    input_grad, *passed = input_back(
        jnp.array(matrix.T, BF16),
        low_grad,
        high_grad,
        first_grad,
        bottle_all,
        turns,
        bottle_scatter.arrived + far_scatter.arrived,
        reduce_scatter.kept,
    )
    reduce_scatter.kept = passed
    bottle_scatter.second()
    bottle_scatter.third()
    reduce_scatter.second()
    reduce_scatter.third()

    vectors = [one_totals, two_totals, three_totals, branch_totals, image_totals, head_totals]
    vectors += [class_total, image_partial]
    packed = jnp.concatenate([vector.reshape(-1) for vector in vectors])
    packed = packed + place.swap(packed)
    split, start = [], 0
    for vector in vectors:
        split.append(packed[start : start + vector.size].reshape(vector.shape))
        start += vector.size

    def own_part(vectors):
        vector = jnp.concatenate(vectors)
        length = vector.shape[0] // size
        return lax.dynamic_slice_in_dim(vector, place.index * length, length, axis=0)

    bottle_gain_grad = own_part([split[0][1], split[1][1], split[2][1]])
    bottle_shift_grad = own_part([split[0][0], split[1][0], split[2][0]])
    pyramid_gain_grad = own_part([split[3][1], split[4][1]])
    pyramid_shift_grad = own_part([split[3][0], split[4][0]])
    head_norm_grad = jnp.stack([own_part([split[5][1]]), own_part([split[5][0]])])
    class_out = own_part([split[6].reshape(size * class_weight.shape[0], -1)])
    image_out = split[7]

    def taps_out(full, taps, weight):
        full = full.reshape((len(taps),) + weight.shape[2:])
        if len(taps) == weight.shape[0] * weight.shape[1]:
            return full.reshape(weight.shape)
        result = jnp.zeros(weight.shape, F32)
        for at, tap in enumerate(taps):
            result = result.at[tap[0], tap[1]].set(full[at])
        return result

    for scatter in (near_scatter, middle_scatter, far_scatter, bottle_scatter, reduce_scatter):
        scatter.finish()
    near_count, middle_count, far_count = len(near_taps), len(middle_taps), len(far_taps)
    bottle_count = len(bottle_taps)
    expand_out = bottle_scatter.piece(bottle_count, quarters).reshape(quarters, narrow_rows, narrow)
    return (
        input_grad.reshape(features.shape),
        reduce_scatter.piece(0, 1),
        taps_out(bottle_scatter.piece(0, bottle_count), bottle_taps, spatial_weight),
        jnp.swapaxes(expand_out, 0, 1).reshape(expand_weight.shape),
        bottle_gain_grad,
        bottle_shift_grad,
        far_scatter.piece(far_count, 1),
        taps_out(near_scatter.piece(0, near_count), near_taps, near_weight),
        taps_out(middle_scatter.piece(0, middle_count), middle_taps, middle_weight),
        taps_out(far_scatter.piece(0, far_count), far_taps, far_weight),
        image_out,
        far_scatter.piece(far_count + 1, 1),
        class_out,
        pyramid_gain_grad,
        pyramid_shift_grad,
        head_norm_grad,
    )


def solution(mesh):
    in_specs = (
        P("section", "batch", None, None, None),
        P("batch", None),
        P(None, None, "batch", None),
        P("batch", None),
        P("batch"),
        P("batch"),
        P("batch", None),
        P(None, None, "batch", None),
        P(None, None, "batch", None),
        P(None, None, "batch", None),
        P("batch", None),
        P("batch", None),
        P("batch", None),
        P("batch"),
        P("batch"),
        P("batch"),
        P("batch"),
        P(None, "batch", None, None),
        P(None, "batch"),
        P(None, "batch", None, None),
        P(),
    )
    out_specs = (
        P("section", "batch", None, None, None),
        P("batch", None),
        P(None, None, "batch", None),
        P("batch", None),
        P("batch"),
        P("batch"),
        P("batch", None),
        P(None, None, "batch", None),
        P(None, None, "batch", None),
        P(None, None, "batch", None),
        P("batch", None),
        P("batch", None),
        P("batch", None),
        P("batch"),
        P("batch"),
        P(None, "batch"),
    )
    return jax.shard_map(
        per_device, mesh=mesh, in_specs=in_specs, out_specs=out_specs, check_vma=False
    )
```

```python
import functools

import jax
import jax.numpy as jnp
import numpy as np
from jax import lax
from jax.experimental import pallas as pl
from jax.experimental.pallas import tpu as pltpu
from jax.sharding import PartitionSpec as P

CITY_CLASSES = 19
HOME_CLASSES = 13
BOTTLE_RATE = 4
NEAR_RATE = 12
MIDDLE_RATE = 24
FAR_RATE = 36
TILE = 4

EPSILON = 1e-05
FLOOR_LOGIT = -1e30
HIGHEST = lax.Precision.HIGHEST
F32 = jnp.float32
BF16 = jnp.bfloat16
SLOT_BITS = [0, 4, 2, 6, 1, 5, 3, 7, 8, 12, 9, 13, 10, 14, 11, 15]
VMEM_BYTES = 58 * 1024 * 1024


class Place:
    def __init__(self):
        self.size = lax.axis_size("batch")
        self.direct = self.size == len(SLOT_BITS)
        self.pieces = 2 * self.size if self.direct else 1
        self.core = lax.axis_index("section")
        self.index = lax.axis_index("batch")

    def meta(self):
        core = self.core[None].astype(jnp.int32)
        if not self.direct:
            return core
        table = [[SLOT_BITS.index(at ^ owner) for owner in range(self.size)] for at in range(self.size)]
        row = lax.dynamic_index_in_dim(jnp.array(table, jnp.int32), self.index, 0, keepdims=False)
        return jnp.concatenate([core, row])

    def flip(self, block, bits):
        return lax.ppermute(block, "batch", [(source, source ^ bits) for source in range(self.size)])

    def swap(self, block):
        return lax.ppermute(block, "section", [(0, 1), (1, 0)])

    def plane_total(self, vector):
        if not self.direct:
            return vector
        return (vector + self.flip(vector, 1)) + (self.flip(vector, 2) + self.flip(vector, 3))

    def line_total(self, plane):
        if not self.direct:
            return lax.psum(plane, "batch")
        return (plane + self.flip(plane, 4)) + (self.flip(plane, 8) + self.flip(plane, 12))

    def total(self, vector):
        return self.line_total(self.plane_total(vector))

    def everyone(self, vector):
        if not self.direct:
            return lax.all_gather(vector, "batch")
        sent = jnp.broadcast_to(vector, (self.size,) + vector.shape)
        return lax.all_to_all(sent, "batch", 0, 0)

    def gather(self, parts):
        blocks = []
        for part, count in parts:
            cut = part.reshape(count, -1, part.shape[1])
            if self.direct:
                half = cut.shape[1] // 2
                cut = lax.dynamic_slice_in_dim(cut, self.core * half, half, axis=1)
            else:
                cut = lax.all_gather(cut, "batch", axis=1, tiled=True)
            blocks.append(cut.reshape(-1, part.shape[1]))
        block = jnp.concatenate(blocks)
        if self.direct:
            return lax.all_gather(block, ("batch", "section"))
        return block[None]


class Scatter:
    def __init__(self, place, grads, rows):
        self.place, self.rows = place, rows
        self.kept = [grads[0]]
        self.arrived = place.swap(grads[1]) if place.direct else None

    def add(self, kept, arrived):
        return (kept.astype(F32) + arrived.astype(F32)).astype(BF16)

    def first(self):
        if not self.place.direct:
            return
        own, arrived = self.kept[0], self.arrived
        self.kept = []
        sent = []
        for start in (0, 8):
            self.kept.append(self.add(own[start : start + 4], arrived[start : start + 4]))
            sent.append(self.add(own[start + 4 : start + 8], arrived[start + 4 : start + 8]))
        self.arrived = [self.place.flip(sent[0], 1), self.place.flip(sent[1], 2)]

    def second(self):
        if not self.place.direct:
            return
        kept, sent = [], []
        for held, came in zip(self.kept, self.arrived):
            kept.append(self.add(held[:2], came[:2]))
            sent.append(self.add(held[2:], came[2:]))
        self.kept = kept
        self.arrived = [self.place.flip(sent[0], 2), self.place.flip(sent[1], 1)]

    def third(self):
        if not self.place.direct:
            return
        near = self.kept[0].astype(F32) + self.arrived[0].astype(F32)
        away = self.kept[1].astype(F32) + self.arrived[1].astype(F32)
        self.kept = [near[0]]
        sent = [near[1].astype(BF16), away[0].astype(BF16), away[1].astype(BF16)]
        self.arrived = [self.place.flip(piece, bits) for piece, bits in zip(sent, (4, 8, 12))]

    def finish(self):
        if self.place.direct:
            parts = [piece.astype(F32) for piece in self.arrived]
            result = (self.kept[0] + parts[0]) + (parts[1] + parts[2])
            opposite = self.place.swap(result)
            first = self.place.core == 0
            self.result = [jnp.where(first, result, opposite), jnp.where(first, opposite, result)]
            return self
        pieces, start = [], 0
        for rows in self.rows:
            cut = self.kept[0][0, start : start + rows * self.place.size].astype(F32)
            cut = lax.psum_scatter(cut, "batch", scatter_dimension=0, tiled=True)
            pieces.append(lax.psum(cut, "section"))
            start += rows * self.place.size
        self.result = [jnp.concatenate(pieces)]
        return self

    def piece(self, first, count):
        parts = len(self.result)
        start = sum(self.rows[:first]) // parts
        rows = self.rows[first] // parts
        cut = [part[start : start + count * rows].reshape(count, rows, -1) for part in self.result]
        return jnp.concatenate(cut, axis=1).reshape(count * rows * parts, -1)


def call(body, args, specs, grid, outs, out_specs, scratch=(), meta=None, after=(), flops=0, passed=(), into=None):
    used = len(args) + (meta is not None)
    passed = list(passed) if into is None else [into] + list(passed)
    waits = len(after) + len(passed)
    results = len(outs)
    filled = int(into is not None)
    kept = results - filled

    def inner(*refs):
        rest = refs[used + waits :]
        body(*refs[:used], *rest[:results], *rest[results + len(passed) - filled :])

    spec = pltpu.PrefetchScalarGridSpec(
        num_scalar_prefetch=int(meta is not None),
        grid=grid,
        in_specs=list(specs) + [pl.BlockSpec(memory_space=pl.ANY)] * waits,
        out_specs=list(out_specs) + [pl.BlockSpec(memory_space=pl.ANY)] * (len(passed) - filled),
        scratch_shapes=list(scratch),
    )
    arrays = ([] if meta is None else [meta]) + list(args) + list(after) + list(passed)
    first = len(arrays) - len(passed)
    moved = sum(array.size * array.dtype.itemsize for array in list(args) + list(outs))
    return pl.pallas_call(
        inner,
        grid_spec=spec,
        out_shape=list(outs) + [shaped(array.shape, array.dtype) for array in passed[filled:]],
        input_output_aliases={first + at: kept + at for at in range(len(passed))},
        compiler_params=pltpu.CompilerParams(vmem_limit_bytes=VMEM_BYTES),
        cost_estimate=pl.CostEstimate(flops=flops, transcendentals=0, bytes_accessed=moved),
    )(*arrays)


def whole(array):
    shape = array.shape
    return pl.BlockSpec(
        shape, lambda *_: (0,) * len(shape), pipeline_mode=pl.Buffered(buffer_count=1)
    )


def held(shape):
    return pl.BlockSpec(shape, lambda *_: (0,) * len(shape))


def rows_of(array, rows):
    return pl.BlockSpec((rows, array.shape[1]), lambda step, *_: (step, 0))


def shaped(shape, dtype=F32):
    return jax.ShapeDtypeStruct(tuple(shape), dtype)


def span(shift_by, length):
    return max(0, -shift_by), length - max(0, shift_by)


def tap_list(height, breadth, dilation):
    listed = []
    for row_tap in range(3):
        for col_tap in range(3):
            row_shift = (row_tap - 1) * dilation
            col_shift = (col_tap - 1) * dilation
            if abs(row_shift) < height and abs(col_shift) < breadth:
                listed.append((row_tap, col_tap, row_shift // TILE, col_shift // TILE))
    return listed


def weight_of(ref):
    return ref[...].reshape(-1, ref.shape[-1])


def spread(meta_ref, full_ref, result_refs, column=0, at=0, rows=None):
    width = result_refs[0].shape[2]
    rows = result_refs[0].shape[1] if rows is None else rows
    if len(result_refs) == 1:
        result_refs[0][0, at : at + rows] = full_ref[:, column : column + width].astype(BF16)
        return
    core = meta_ref[0]
    for owner in range(result_refs[0].shape[0]):
        for ref, side in zip(result_refs, (core, 1 - core)):
            start = pl.multiple_of(owner * 2 * rows + side * rows, rows)
            block = full_ref[pl.ds(start, rows), column : column + width]
            ref[meta_ref[1 + owner], at : at + rows] = block.astype(BF16)


def slotted(place, rows, width):
    if place.direct:
        return [shaped((place.size, rows // 2, width), BF16)] * 2
    return [shaped((1, rows * place.size, width), BF16)]


def center_first(step, center):
    return jnp.where(step == 0, center, jnp.where(step <= center, step - 1, step))


def ordered(taps, center):
    return [taps[center]] + [tap for place, tap in enumerate(taps) if place != center]


def shifts_of(taps):
    return [(tap[2], tap[3]) for tap in taps]


def area(tap, tiles):
    return (tiles[0] - abs(tap[0])) * (tiles[1] - abs(tap[1])) * tiles[2]


def forward_tap(tap, fresh, source_ref, weight, result_ref):
    tiles_i, tiles_j, pixels, channels = source_ref.shape
    columns = result_ref.shape[-1]
    shift_i, shift_j = tap
    low_i, high_i = span(shift_i, tiles_i)
    low_j, high_j = span(shift_j, tiles_j)
    window = source_ref[
        low_i + shift_i : high_i + shift_i, low_j + shift_j : high_j + shift_j
    ].reshape(-1, channels)
    product = jnp.dot(window, weight, preferred_element_type=F32)
    product = product.reshape(high_i - low_i, high_j - low_j, pixels, columns)
    if fresh:
        result_ref[low_i:high_i, low_j:high_j] = product
    else:
        result_ref[low_i:high_i, low_j:high_j] += product


def unit_of(values, coef):
    unit = (values - coef[0:1]) * coef[1:2]
    return unit, coef[2:3] * unit + coef[3:4]


def masked_sums(values, valid):
    weighted = values * valid
    return jnp.concatenate(
        [jnp.sum(weighted, axis=0, keepdims=True), jnp.sum(weighted * values, axis=0, keepdims=True)]
    )


def sum_rows(ref, valid_ref, sums_ref):
    total = jnp.zeros(sums_ref.shape, F32)
    for row in range(ref.shape[0]):
        values = ref[row].reshape(-1, ref.shape[-1])
        total = total + masked_sums(values, valid_ref[row].reshape(-1, 1))
    sums_ref[...] = total


def branch_body(taps, source_ref, valid_ref, weight_ref, result_ref, sums_ref):
    for place, tap in enumerate(taps):

        @pl.when(pl.program_id(0) == place)
        def _(place=place, tap=tap):
            forward_tap(tap, place == 0, source_ref, weight_of(weight_ref), result_ref)

    @pl.when(pl.program_id(0) == len(taps) - 1)
    def _():
        sum_rows(result_ref, valid_ref, sums_ref)


def tap_block(weights, channels, first_tap, center, first_step=0, count=None):
    pieces, _, columns = weights.shape

    def index(step):
        if count is not None:
            step = jnp.clip(step - first_step, 0, count - 1)
        return (0, first_tap + center_first(step, center), 0)

    return pl.BlockSpec((pieces, channels // pieces, columns), index)


def branch_conv(source, valid, weights, taps, center, first_tap, after):
    channels, columns = source.shape[-1], weights.shape[2]
    shifts = ordered(shifts_of(taps), center)
    result_shape = source.shape[:3] + (columns,)
    macs = sum(area(tap, source.shape) for tap in shifts) * channels * columns
    return call(
        functools.partial(branch_body, shifts),
        [source, valid, weights],
        [whole(source), whole(valid), tap_block(weights, channels, first_tap, center)],
        (len(taps),),
        [shaped(result_shape), shaped((2, columns))],
        [held(result_shape), held((2, columns))],
        after=after,
        flops=2 * macs,
    )


def spatial_body(taps, first_ref, coef_ref, valid_ref, weight_ref, input_ref, result_ref, sums_ref):
    @pl.when(pl.program_id(0) == 0)
    def _():
        for row in range(first_ref.shape[0]):
            _, pre = unit_of(first_ref[row], coef_ref[...][:, None, :])
            input_ref[row] = (silu(pre) * valid_ref[row]).astype(BF16)

    branch_body(taps, input_ref, valid_ref, weight_ref, result_ref, sums_ref)


def spatial_conv(first, coef, valid, weights, taps, center, first_tap):
    channels, columns = first.shape[-1], weights.shape[2]
    shifts = ordered(shifts_of(taps), center)
    macs = sum(area(tap, first.shape) for tap in shifts) * channels * columns
    return call(
        functools.partial(spatial_body, shifts),
        [first, coef, valid, weights],
        [whole(first), whole(coef), whole(valid), tap_block(weights, channels, first_tap, center)],
        (len(taps),),
        [shaped(first.shape, BF16), shaped(first.shape), shaped((2, columns))],
        [held(first.shape), held(first.shape), held((2, columns))],
        flops=2 * macs,
    )


def backward_tap(tap, fresh, up_ref, column, weight_ref, result_ref):
    tiles_i, tiles_j, pixels, channels = result_ref.shape
    pieces, rows, width = weight_ref.shape
    shift_i, shift_j = tap
    low_i, high_i = span(shift_i, tiles_i)
    low_j, high_j = span(shift_j, tiles_j)
    window = up_ref[low_i:high_i, low_j:high_j, :, column : column + width].reshape(-1, width)
    wide = min(512, channels)
    for start in range(0, channels, wide):
        if pieces == 1:
            weight = weight_ref[0, start : start + wide]
        else:
            weight = weight_ref[start // rows : (start + wide) // rows].reshape(wide, width)
        product = lax.dot_general(
            window, weight, (((1,), (1,)), ((), ())), preferred_element_type=F32
        ).reshape(high_i - low_i, high_j - low_j, pixels, wide)
        place = (
            slice(low_i + shift_i, high_i + shift_i),
            slice(low_j + shift_j, high_j + shift_j),
            slice(None),
            slice(start, start + wide),
        )
        if fresh:
            result_ref[place] = product
        else:
            result_ref[place] += product


def grad_moments(grad, unit):
    return jnp.concatenate(
        [jnp.sum(grad, axis=0, keepdims=True), jnp.sum(grad * unit, axis=0, keepdims=True)]
    )


def feature_body(plan, up_ref, third_ref, source_ref, coef_ref, pooled_ref, valid_ref, *refs):
    weight_refs = refs[: len(plan)]
    result_ref, sums_ref, total_ref = refs[len(plan) :]
    step_now = pl.program_id(0)
    begun = 0
    for weight_ref, listed in zip(weight_refs, plan):
        for tap, column in listed:

            @pl.when(step_now == begun)
            def _(weight_ref=weight_ref, tap=tap, column=column, fresh=begun == 0):
                backward_tap(tap, fresh, up_ref, column, weight_ref, total_ref)

            begun += 1

    @pl.when(step_now >= begun)
    def _():
        row = step_now - begun
        width = total_ref.shape[-1]
        unit, pre = unit_of(third_ref[...], coef_ref[...])
        pre = pre + source_ref[...].astype(F32)
        grad = total_ref[row].reshape(-1, width) + pooled_ref[...]
        grad = grad * valid_ref[...] * silu_slope(pre)
        result_ref[...] = grad.astype(BF16)
        moments = grad_moments(grad, unit)

        @pl.when(step_now == begun)
        def _():
            sums_ref[...] = moments

        @pl.when(step_now > begun)
        def _():
            sums_ref[...] += moments


def feature_back(upstream, groups, third, source, coef, pooled, valid, side, sides, after, passed):
    channels = third.shape[1]
    part = channels // sides
    plan, arrays, specs, begun, macs = [], [], [], 0, 0
    for weights, taps, center, columns, first_tap in groups:
        shifts = ordered(list(zip(shifts_of(taps), columns)), center)
        plan.append(shifts)
        count = len(shifts)
        pieces, _, width = weights.shape
        rows = channels // pieces

        def index(step, first=begun, count=count, center=center, first_tap=first_tap, pieces=pieces):
            tap = first_tap + center_first(jnp.clip(step - first, 0, count - 1), center)
            return (0, tap * sides + side, 0) if pieces == 1 else (side, tap, 0)

        block = (1, rows // sides, width) if pieces == 1 else (pieces // sides, rows, width)
        arrays.append(weights)
        specs.append(pl.BlockSpec(block, index))
        begun += count
        macs += sum(area(tap, upstream.shape) for tap, _ in shifts) * part * width
    turns = upstream.shape[0]
    height = third.shape[0] // turns

    def row_of(step):
        return jnp.clip(step - begun, 0, turns - 1)

    row_block = pl.BlockSpec((height, part), lambda step: (row_of(step), side))
    return call(
        functools.partial(feature_body, plan),
        [upstream, third, source, coef, pooled, valid] + arrays,
        [
            whole(upstream),
            row_block,
            row_block,
            pl.BlockSpec((coef.shape[0], part), lambda step: (0, side)),
            pl.BlockSpec((1, part), lambda step: (0, side)),
            pl.BlockSpec((height, 1), lambda step: (row_of(step), 0)),
        ]
        + specs,
        (begun + turns,),
        [shaped((third.shape[0], part), BF16), shaped((2, part))],
        [pl.BlockSpec((height, part), lambda step: (row_of(step), 0)), held((2, part))],
        [pltpu.VMEM(upstream.shape[:3] + (part,), F32)],
        after=after,
        flops=2 * macs,
        passed=passed,
    )


def spatial_back_body(taps, up_ref, first_ref, coef_ref, valid_ref, weight_ref, result_ref, sums_ref):
    for place, tap in enumerate(taps):

        @pl.when(pl.program_id(0) == place)
        def _(place=place, tap=tap):
            backward_tap(tap, place == 0, up_ref, 0, weight_ref, result_ref)

    @pl.when(pl.program_id(0) == len(taps) - 1)
    def _():
        total = jnp.zeros(sums_ref.shape, F32)
        width = result_ref.shape[-1]
        for row in range(result_ref.shape[0]):
            unit, pre = unit_of(first_ref[row].reshape(-1, width), coef_ref[...])
            valid = valid_ref[row].reshape(-1, 1)
            grad = result_ref[row].reshape(-1, width) * valid * silu_slope(pre)
            result_ref[row] = grad.reshape(result_ref.shape[1:])
            total = total + grad_moments(grad, unit)
        sums_ref[...] = total


def spatial_back(upstream, first, coef, valid, weights, taps, center, first_tap, after, passed):
    channels, columns = first.shape[-1], weights.shape[2]
    shifts = ordered(shifts_of(taps), center)
    macs = sum(area(tap, first.shape) for tap in shifts) * channels * columns
    return call(
        functools.partial(spatial_back_body, shifts),
        [upstream, first, coef, valid, weights],
        [
            whole(upstream),
            whole(first),
            whole(coef),
            whole(valid),
            tap_block(weights, channels, first_tap, center),
        ],
        (len(taps),),
        [shaped(first.shape), shaped((2, channels))],
        [held(first.shape), held((2, channels))],
        after=after,
        flops=2 * macs,
        passed=passed,
    )


def weight_tap(tap, tiles, flipped_ref, up_ref, padded_ref):
    tiles_i, tiles_j, pixels = tiles
    shift_i, shift_j = tap
    low_i, high_i = span(shift_i, tiles_i)
    low_j, high_j = span(shift_j, tiles_j)
    padded_ref[...] = jnp.zeros_like(padded_ref)
    wide = (high_j - low_j) * pixels
    for row in range(low_i, high_i):
        target = ((row + shift_i) * tiles_j + low_j + shift_j) * pixels
        source = (row * tiles_j + low_j) * pixels
        padded_ref[target : target + wide] = up_ref[source : source + wide]
    first = (low_i + shift_i) * tiles_j * pixels // 128 * 128
    last = -(-(high_i + shift_i) * tiles_j * pixels // 128) * 128
    return jnp.dot(
        flipped_ref[:, first:last], padded_ref[first:last], preferred_element_type=F32
    )


def weight_body(plan, tiles, extra, count, meta_ref, flipped_ref, up_ref, *refs):
    extra_ref = refs[0] if extra else None
    result_refs = refs[extra : extra + count]
    padded_ref, full_ref = refs[extra + count :]
    width = padded_ref.shape[1]
    for place, (tap, column) in enumerate(plan):

        @pl.when(pl.program_id(0) == place)
        def _(tap=tap, column=column):
            full_ref[...] = weight_tap(
                tap, tiles, flipped_ref, up_ref.at[:, column : column + width], padded_ref
            ).astype(BF16)
            spread(meta_ref, full_ref, result_refs)

    if extra:

        @pl.when(pl.program_id(0) == len(plan))
        def _():
            core = meta_ref[0]
            slots, held_rows, _ = result_refs[0].shape
            rows = extra_ref.shape[0] // slots // 2
            spare = jnp.zeros((held_rows - rows, width), F32)
            for owner in range(slots):
                for ref, side in zip(result_refs, (core, 1 - core)):
                    start = pl.multiple_of(owner * 2 * rows + side * rows, 8)
                    block = jnp.concatenate([extra_ref[pl.ds(start, rows)], spare])
                    ref[meta_ref[1 + owner]] = block.astype(BF16)


def weight_grad(place, flipped, upstream, meta, taps, columns, tiles, width, after=(), extra=None, passed=()):
    channels, padded = flipped.shape
    plan = list(zip(shifts_of(taps), columns))
    steps = len(taps) + (extra is not None)
    shapes = slotted(place, channels // place.size * steps, width)
    blocks = [
        pl.BlockSpec((shape.shape[0], shape.shape[1] // steps, width), lambda step, _: (0, step, 0))
        for shape in shapes
    ]
    macs = sum(area(tap, tiles) for tap, _ in plan) * channels * width
    more = [] if extra is None else [extra]
    return call(
        functools.partial(weight_body, plan, tiles, len(more), len(shapes)),
        [flipped, upstream] + more,
        [whole(array) for array in [flipped, upstream] + more],
        (steps,),
        shapes,
        blocks,
        [pltpu.VMEM((padded, width), BF16), pltpu.VMEM((channels, width), BF16)],
        meta,
        after,
        2 * macs,
        passed,
    )


def tile_matrix(breadth):
    count = TILE * breadth
    matrix = np.zeros((count, count), np.float32)
    for row in range(TILE):
        for column in range(breadth):
            at = (column // TILE * TILE + row) * TILE + column % TILE
            matrix[at, row * breadth + column] = 1.0
    return matrix


def tile_body(matrix_ref, natural_ref, result_ref):
    result_ref[...] = jnp.dot(
        matrix_ref[...], natural_ref[...], preferred_element_type=F32
    ).astype(BF16)


def tile_rows(natural, matrix):
    rows = matrix.shape[0]
    return call(
        tile_body,
        [matrix, natural],
        [whole(matrix), rows_of(natural, rows)],
        (natural.shape[0] // rows,),
        [shaped(natural.shape, BF16)],
        [rows_of(natural, rows)],
        flops=2 * rows * natural.size,
    )[0]


def flip_body(source_ref, result_ref):
    pixels = source_ref.shape[0]
    result_ref[:, :pixels] = source_ref[...].T
    if result_ref.shape[1] > pixels:
        extra = result_ref.shape[1] - pixels
        result_ref[:, pixels:] = jnp.zeros((result_ref.shape[0], extra), BF16)


def flipped(values, after=()):
    pixels, channels = values.shape
    padded = pixels + -pixels % 128
    return call(
        flip_body,
        [values],
        [pl.BlockSpec((pixels, 128), lambda step: (0, step))],
        (channels // 128,),
        [shaped((channels, padded), BF16)],
        [pl.BlockSpec((128, padded), lambda step: (step, 0))],
        after=after,
    )[0]


def add_sums(sums_ref, sums):
    @pl.when(pl.program_id(0) == 0)
    def _():
        sums_ref[...] = sums

    @pl.when(pl.program_id(0) > 0)
    def _():
        sums_ref[...] += sums


def first_body(source_ref, valid_ref, weight_ref, result_ref, sums_ref):
    product = jnp.dot(source_ref[...], weight_of(weight_ref), preferred_element_type=F32)
    result_ref[...] = product
    add_sums(sums_ref, masked_sums(product, valid_ref[...]))


def fixed_block(weights, channels, at):
    pieces, _, columns = weights.shape
    return pl.BlockSpec((pieces, channels // pieces, columns), lambda step, *_: (0, at, 0))


def first_conv(source, valid, weights, turns, after):
    pixels, channels = source.shape
    rows = pixels // turns
    width = weights.shape[2]
    return call(
        first_body,
        [source, valid, weights],
        [rows_of(source, rows), rows_of(valid, rows), fixed_block(weights, channels, 0)],
        (turns,),
        [shaped((pixels, width)), shaped((2, width))],
        [pl.BlockSpec((rows, width), lambda step: (step, 0)), held((2, width))],
        after=after,
        flops=2 * pixels * channels * width,
    )


def third_body(count, second_ref, coef_ref, valid_ref, *refs):
    weight_refs = refs[:count]
    middle_ref, result_ref, sums_ref = refs[count:]
    _, pre = unit_of(second_ref[...], coef_ref[...])
    middle = silu(pre).astype(BF16)
    middle_ref[...] = middle
    valid = valid_ref[...]
    sums = []
    for quarter, ref in enumerate(weight_refs):
        product = jnp.dot(middle, weight_of(ref), preferred_element_type=F32)
        width = product.shape[1]
        result_ref[:, quarter * width : (quarter + 1) * width] = product
        sums.append(masked_sums(product, valid))
    add_sums(sums_ref, jnp.concatenate(sums, axis=1))


def third_conv(second, coef, valid, weights, first, count, turns):
    pixels, narrow = second.shape
    height = pixels // turns
    channels = count * weights.shape[2]
    return call(
        functools.partial(third_body, count),
        [second, coef, valid] + [weights] * count,
        [rows_of(second, height), whole(coef), rows_of(valid, height)]
        + [fixed_block(weights, narrow, first + quarter) for quarter in range(count)],
        (turns,),
        [shaped((pixels, narrow), BF16), shaped((pixels, channels)), shaped((2, channels))],
        [
            pl.BlockSpec((height, narrow), lambda step: (step, 0)),
            pl.BlockSpec((height, channels), lambda step: (step, 0)),
            held((2, channels)),
        ],
        flops=2 * pixels * narrow * channels,
    )


def output_body(third_ref, source_ref, coef_ref, valid_ref, result_ref, sums_ref):
    _, pre = unit_of(third_ref[...], coef_ref[...])
    values = (valid_ref[...] * silu(pre + source_ref[...].astype(F32))).astype(BF16)
    result_ref[...] = values
    add_sums(sums_ref, jnp.sum(values.astype(F32), axis=0, keepdims=True))


def block_output(third, source, coef, valid, turns):
    pixels, channels = third.shape
    rows = pixels // turns
    return call(
        output_body,
        [third, source, coef, valid],
        [rows_of(third, rows), rows_of(source, rows), whole(coef), rows_of(valid, rows)],
        (turns,),
        [shaped(third.shape, BF16), shaped((1, channels))],
        [rows_of(third, rows), held((1, channels))],
    )


def third_back_body(
    count, outs, meta_ref, low_ref, high_ref, third_ref, coef_ref, totals_ref, valid_ref, middle_ref, *refs
):
    weight_refs = refs[:count]
    result_ref = refs[count]
    slot_refs = refs[count + 1 : count + 1 + outs]
    grad_ref, total_ref = refs[count + 1 + outs :]
    step_now = pl.program_id(0)

    @pl.when(step_now == 0)
    def _():
        total_ref[...] = jnp.zeros_like(total_ref)

    part = low_ref.shape[1]
    coef, totals, valid = coef_ref[...], totals_ref[...], valid_ref[...]
    for start, part_ref in ((0, low_ref), (part, high_ref)):
        at = slice(start, start + part)
        unit = (third_ref[:, at] - coef[0:1, at]) * coef[1:2, at]
        centered = part_ref[...].astype(F32) - valid * (totals[0:1, at] + unit * totals[1:2, at])
        grad_ref[:, at] = (coef[2:3, at] * coef[1:2, at] * centered).astype(BF16)
    width = weight_refs[0].shape[2]
    result = None
    for quarter, ref in enumerate(weight_refs):
        grad = grad_ref[:, quarter * width : (quarter + 1) * width]
        product = lax.dot_general(
            grad, weight_of(ref), (((1,), (1,)), ((), ())), preferred_element_type=F32
        )
        result = product if result is None else result + product
    result_ref[...] = result
    total_ref[...] += lax.dot_general(
        middle_ref[...], grad_ref[...], (((0,), (0,)), ((), ())), preferred_element_type=F32
    )

    @pl.when(step_now == pl.num_programs(0) - 1)
    def _():
        rows = slot_refs[0].shape[1] // count
        for quarter in range(count):
            spread(meta_ref, total_ref, slot_refs, quarter * width, quarter * rows, rows)


def third_back(place, low, high, third, coef, totals, valid, middle, weights, meta, first, count, turns, after, passed):
    pixels, channels = third.shape
    narrow = middle.shape[1]
    height = pixels // turns
    shapes = slotted(place, narrow // place.size * count, weights.shape[2])
    return call(
        functools.partial(third_back_body, count, len(shapes)),
        [low, high, third, coef, totals, valid, middle] + [weights] * count,
        [
            rows_of(low, height),
            rows_of(high, height),
            rows_of(third, height),
            whole(coef),
            whole(totals),
            rows_of(valid, height),
            rows_of(middle, height),
        ]
        + [fixed_block(weights, narrow, first + quarter) for quarter in range(count)],
        (turns,),
        [shaped((pixels, narrow))] + shapes,
        [pl.BlockSpec((height, narrow), lambda step, _: (step, 0))] + [held(shape.shape) for shape in shapes],
        [pltpu.VMEM((height, channels), BF16), pltpu.VMEM((narrow, channels), F32)],
        meta,
        after,
        4 * pixels * narrow * channels,
        passed,
    )


def input_body(matrix_ref, low_ref, high_ref, grad_ref, weight_ref, result_ref):
    rows = matrix_ref.shape[0]
    part = low_ref.shape[1]
    matrix = matrix_ref[...]
    moved = []
    for start in range(0, result_ref.shape[0], rows):
        at = slice(start, start + rows)
        moved.append(jnp.dot(matrix, grad_ref[at], preferred_element_type=F32).astype(BF16))
        for column, part_ref in ((0, low_ref), (part, high_ref)):
            result_ref[at, column : column + part] = jnp.dot(
                matrix, part_ref[at], preferred_element_type=F32
            )
    result_ref[...] += lax.dot_general(
        jnp.concatenate(moved), weight_of(weight_ref), (((1,), (1,)), ((), ())), preferred_element_type=F32
    )


def input_back(matrix, low, high, grad, weights, turns, first, count, after, passed, into):
    pixels, part = low.shape
    rows = pixels // turns
    channels = 2 * part
    width = grad.shape[1]

    def block(columns):
        return pl.BlockSpec((rows, columns), lambda step: (first + step, 0))

    return call(
        input_body,
        [matrix, low, high, grad, weights],
        [whole(matrix), block(part), block(part), block(width), fixed_block(weights, channels, 0)],
        (count,),
        [shaped((pixels, channels))],
        [block(channels)],
        after=after,
        flops=2 * count * rows * channels * (width + matrix.shape[0]),
        passed=passed,
        into=into,
    )


def sigmoid(values):
    return 0.5 + 0.5 * jnp.tanh(0.5 * values)


def silu(values):
    return values * sigmoid(values)


def silu_slope(values):
    sigmoid_val = sigmoid(values)
    return sigmoid_val * (1.0 + values * (1.0 - sigmoid_val))


def sums(values, validity):
    weighted = values * validity
    return jnp.stack([jnp.sum(weighted, axis=0), jnp.sum(weighted * values, axis=0)])


def coefs(totals, counted, gain, shift):
    mean_value = totals[0] / counted
    scaling = lax.rsqrt(totals[1] / counted - mean_value * mean_value + EPSILON)
    return jnp.stack([mean_value, scaling, gain, shift])


def through_norm(grad_pre, unit, coef, counted, validity, totals):
    centered = grad_pre - validity * (totals[0] + unit * totals[1]) / counted
    return coef[2] * coef[1] * centered


def to_tiles(array):
    height, breadth = array.shape[:2]
    rest = array.shape[2:]
    cut = array.reshape((height // TILE, TILE, breadth // TILE, TILE) + rest)
    return jnp.swapaxes(cut, 1, 2).reshape((height * breadth,) + rest)


def per_device(
    features,
    reduce_weight,
    spatial_weight,
    expand_weight,
    bottle_gain,
    bottle_shift,
    point_weight,
    near_weight,
    middle_weight,
    far_weight,
    image_weight,
    project_weight,
    class_weight,
    pyramid_gain,
    pyramid_shift,
    head_gain,
    head_shift,
    crop_masks,
    crop_tasks,
    pixel_labels,
    task_norms,
):
    place = Place()
    size, core = place.size, place.core
    first_core = core == 0
    height, breadth, channels = features.shape[2:]
    pixels = height * breadth
    tiles = (height // TILE, breadth // TILE, TILE * TILE)
    narrow = reduce_weight.shape[1]
    branch = point_weight.shape[1]
    four_wide = 4 * branch
    rows = channels // size
    narrow_rows = narrow // size
    quarters = channels // narrow
    turns = 3
    meta = place.meta()
    matrix = tile_matrix(breadth)

    bottle_taps = tap_list(height, breadth, BOTTLE_RATE)
    near_taps = tap_list(height, breadth, NEAR_RATE)
    middle_taps = tap_list(height, breadth, MIDDLE_RATE)
    far_taps = tap_list(height, breadth, FAR_RATE)
    point_taps = [(1, 1, 0, 0)]

    def center_of(taps):
        return [tap[:2] for tap in taps].index((1, 1))

    def stacked(weight, taps):
        flat = weight.reshape((-1,) + weight.shape[2:])
        picked = [3 * tap[0] + tap[1] for tap in taps]
        if picked == list(range(picked[0], picked[-1] + 1)):
            flat = flat[picked[0] : picked[-1] + 1]
        else:
            flat = jnp.stack([flat[at] for at in picked])
        return flat.reshape(-1, flat.shape[2]), len(taps)

    mask = lax.dynamic_index_in_dim(crop_masks, core, 0, keepdims=False)[0]
    labels = lax.dynamic_index_in_dim(pixel_labels, core, 0, keepdims=False)[0]
    task = lax.dynamic_index_in_dim(crop_tasks, core, 0, keepdims=False)[0]
    validity = to_tiles(mask).astype(F32)[:, None]
    valid_tiles = validity.reshape(tiles + (1,))
    labels = to_tiles(labels)
    source = tile_rows(features.reshape(pixels, channels), jnp.array(matrix, BF16))
    source_flipped = flipped(source)

    wide_expand = expand_weight.reshape(-1, quarters, narrow)
    expand_parts = [(wide_expand[:, at], 1) for at in range(quarters)]
    bottle_all = place.gather([(reduce_weight, 1), stacked(spatial_weight, bottle_taps)] + expand_parts)
    spatial_at = channels // narrow
    expand_at = spatial_at + len(bottle_taps)
    pyramid_parts = [stacked(near_weight, near_taps), stacked(middle_weight, middle_taps)]
    pyramid_parts += [stacked(far_weight, far_taps), (point_weight, 1), (project_weight, 1)]
    pyramid_all = place.gather(pyramid_parts)
    middle_at = len(near_taps)
    far_at = middle_at + len(middle_taps)
    point_at = far_at + len(far_taps)
    project_at = (point_at + 1) * (channels // place.pieces)
    project_full = pyramid_all[:, project_at:].reshape(-1, branch)

    crop_valid_both = jnp.sum(crop_masks, axis=(1, 2, 3)).astype(F32)
    home_crop = (crop_tasks[:, 0] == 1).astype(F32)
    counts = jnp.concatenate(
        [
            crop_valid_both,
            jnp.sum(crop_valid_both * (1.0 - home_crop))[None],
            jnp.sum(crop_valid_both * home_crop)[None],
        ]
    )
    small = [bottle_gain, bottle_shift, pyramid_gain, pyramid_shift, head_gain, head_shift]
    small.append(class_weight.reshape(-1))
    small_widths = [part.shape[0] for part in small]
    small_own = jnp.concatenate(small).astype(F32)
    placed = lax.dynamic_update_slice(
        jnp.zeros((size, small_own.shape[0]), F32), small_own[None], (place.index, 0)
    )
    collected = place.total(jnp.concatenate([placed.reshape(-1), counts]))
    counts_all = collected[placed.size :]
    collected = collected[: placed.size].reshape(size, -1)
    small_all, start = [], 0
    for width in small_widths:
        small_all.append(collected[:, start : start + width].reshape(-1))
        start += width
    gain_bottle, shift_bottle, gain_pyramid, shift_pyramid, gain_head, shift_head = small_all[:6]
    class_full = small_all[6].reshape(size * class_weight.shape[0], -1).astype(BF16)
    counted = jnp.where(first_core, counts_all[0], counts_all[1])
    task_pixels = counts_all[2:4]
    crop_valid = jnp.where(first_core, crop_valid_both[0], crop_valid_both[1])

    first, first_sums = first_conv(source, validity, bottle_all, turns, [source_flipped])
    coef_one = coefs(place.total(first_sums), counted, gain_bottle[:narrow], shift_bottle[:narrow])
    first_tiles = first.reshape(tiles + (narrow,))
    conv_in, second, second_sums = spatial_conv(
        first_tiles, coef_one, valid_tiles, bottle_all, bottle_taps, center_of(bottle_taps), spatial_at
    )
    second = second.reshape(pixels, narrow)
    coef_two = coefs(
        place.total(second_sums), counted, gain_bottle[narrow : 2 * narrow], shift_bottle[narrow : 2 * narrow]
    )
    middle_act, third, third_sums = third_conv(
        second, coef_two, validity, bottle_all, expand_at, quarters, turns
    )
    coef_three = coefs(
        place.total(third_sums), counted, gain_bottle[2 * narrow :], shift_bottle[2 * narrow :]
    )
    block_out, pooled_sum = block_output(third, source, coef_three, validity, tiles[0])
    block_tiles = block_out.reshape(tiles + (channels,))

    pooled = (pooled_sum / crop_valid).astype(BF16)
    pooled_plane = place.plane_total(
        lax.dynamic_update_slice(jnp.zeros((size, channels), BF16), pooled, (place.index, 0))
    )
    near_out, near_sums = branch_conv(
        block_tiles,
        valid_tiles,
        pyramid_all,
        near_taps,
        center_of(near_taps),
        0,
        (),
    )
    pooled_all = place.line_total(pooled_plane)
    middle_out, middle_sums = branch_conv(
        block_tiles,
        valid_tiles,
        pyramid_all,
        middle_taps,
        center_of(middle_taps),
        middle_at,
        [pooled_plane, near_sums],
    )
    pooled_rows = lax.dynamic_slice_in_dim(pooled_all, place.index * rows, rows, axis=1)
    image_plane = place.plane_total(
        jnp.dot(pooled_rows, image_weight, preferred_element_type=F32)
    )
    far_out, far_sums = branch_conv(
        block_tiles,
        valid_tiles,
        pyramid_all,
        far_taps,
        center_of(far_taps),
        far_at,
        [pooled_all, middle_sums],
    )
    image_all = place.line_total(image_plane)
    point_out, point_sums = branch_conv(
        block_tiles, valid_tiles, pyramid_all, point_taps, 0, point_at, [image_plane, far_sums]
    )
    image_mean = jnp.sum(image_all, axis=0) / size
    image_scale = lax.rsqrt(
        jnp.sum(image_all * image_all, axis=0) / size - image_mean * image_mean + EPSILON
    )
    image_unit = (image_all - image_mean) * image_scale
    gain_image, shift_image = gain_pyramid[four_wide:], shift_pyramid[four_wide:]
    coef_image = jnp.stack([image_mean, image_scale, gain_image, shift_image])
    image_pre = gain_image * image_unit + shift_image
    image_act = silu(image_pre).astype(BF16)

    outs = [part.reshape(pixels, branch) for part in (point_out, near_out, middle_out, far_out)]
    branches = jnp.concatenate(outs, axis=1)
    branch_sums = jnp.concatenate([point_sums, near_sums, middle_sums, far_sums], axis=1)
    branch_plane = place.plane_total(branch_sums)
    block_flipped = flipped(block_out, [point_sums])
    conv_flipped = flipped(conv_in.reshape(pixels, narrow), [block_flipped, branch_plane])
    coef_branch = coefs(
        place.line_total(branch_plane), counted, gain_pyramid[:four_wide], shift_pyramid[:four_wide]
    )
    unit_branch, pre_branch = unit_of(branches, coef_branch)
    joined = silu(pre_branch).astype(BF16)

    own_act = lax.dynamic_slice_in_dim(image_act, place.index, 1, axis=0)
    crop_part = jnp.dot(own_act, project_full[four_wide:], preferred_element_type=F32)
    projected = jnp.dot(joined, project_full[:four_wide], preferred_element_type=F32) + crop_part
    head_sums = jnp.sum(place.everyone(sums(projected, validity)), axis=0)
    coef_head = coefs(head_sums, counted, gain_head, shift_head)
    unit_head, pre_head = unit_of(projected, coef_head)
    output_act = silu(pre_head).astype(BF16)
    logits = jnp.dot(output_act, class_full, preferred_element_type=F32)

    columns = jnp.arange(class_full.shape[1])
    allowed = (columns >= CITY_CLASSES) == (task == 1)
    masked = jnp.where(allowed, logits, FLOOR_LOGIT)
    raised = jnp.exp(masked - jnp.max(masked, axis=-1, keepdims=True))
    chances = raised / jnp.sum(raised, axis=-1, keepdims=True)
    target = jnp.where(task == 0, labels % CITY_CLASSES, CITY_CLASSES + labels % HOME_CLASSES)
    chosen = (columns == target[:, None]).astype(F32)
    inverse = 1.0 / task_norms.astype(F32)
    task_share = inverse / jnp.sum(inverse)
    crop_weight = jnp.where(
        task == 0, task_share[0] / task_pixels[0], task_share[1] / task_pixels[1]
    )
    logit_grad = (crop_weight * validity * (chances - chosen)).astype(BF16)
    class_grad = lax.dot_general(
        output_act, logit_grad, (((0,), (0,)), ((), ())), preferred_element_type=F32
    )

    output_grad = lax.dot_general(
        logit_grad, class_full, (((1,), (1,)), ((), ())), preferred_element_type=F32
    )
    grad_head = output_grad * silu_slope(pre_head)
    head_totals = jnp.sum(place.everyone(grad_moments(grad_head, unit_head)), axis=0)
    proj_grad = through_norm(
        grad_head, unit_head, coef_head, counted, validity, head_totals
    ).astype(BF16)
    crop_grad = jnp.sum(proj_grad, axis=0, dtype=F32)
    joined_grad = lax.dot_general(
        proj_grad, project_full[:four_wide], (((1,), (1,)), ((), ())), preferred_element_type=F32
    )
    act_grad = jnp.dot(project_full[four_wide:].astype(F32), crop_grad, precision=HIGHEST)
    own_pre = lax.dynamic_slice_in_dim(image_pre, place.index, 1, axis=0)[0]
    image_pre_grad = act_grad * silu_slope(own_pre)
    grad_branch = joined_grad * silu_slope(pre_branch)
    branch_parts = place.everyone(
        jnp.concatenate([grad_moments(grad_branch, unit_branch).reshape(-1), image_pre_grad])
    )
    image_pre_all = branch_parts[:, 2 * four_wide :]
    branch_totals = jnp.sum(branch_parts[:, : 2 * four_wide], axis=0).reshape(2, four_wide)
    branch_grad = through_norm(
        grad_branch, unit_branch, coef_branch, counted, validity, branch_totals
    ).astype(BF16)
    image_totals = grad_moments(image_pre_all, image_unit)
    image_in_all = through_norm(
        image_pre_all, image_unit, coef_image, float(size), 1.0, image_totals
    )
    pooled_partial = lax.dot_general(
        image_in_all, image_weight.astype(F32), (((1,), (1,)), ((), ())), precision=HIGHEST
    )
    pooled_grad_plane = place.plane_total(
        lax.dynamic_update_slice(
            jnp.zeros((size, channels), F32), pooled_partial, (0, place.index * rows)
        )
    )
    image_partial = jnp.dot(pooled_rows.astype(F32).T, image_in_all, precision=HIGHEST)

    def columns_of(taps, block):
        return [block * branch] * len(taps)

    wide_taps = far_taps + point_taps
    wide_columns = columns_of(far_taps, 3) + columns_of(point_taps, 0)
    project_grad = jnp.concatenate(
        [
            lax.dot_general(
                joined, proj_grad, (((0,), (0,)), ((), ())), preferred_element_type=F32
            ),
            own_act[0].astype(F32)[:, None] * crop_grad[None, :],
        ]
    )

    def branch_weight_grad(taps, tap_columns, after, extra=None, passed=()):
        return weight_grad(
            place, block_flipped, branch_grad, meta, taps, tap_columns, tiles, branch, after, extra, passed
        )

    parts = 2 if place.direct else 1
    near_grads = branch_weight_grad(near_taps, columns_of(near_taps, 1), [conv_flipped])
    near_scatter = Scatter(place, near_grads, [rows] * len(near_taps))
    pooled_grad_all = place.line_total(pooled_grad_plane)
    middle_grads = branch_weight_grad(
        middle_taps, columns_of(middle_taps, 2), [near_grads[0], pooled_grad_plane]
    )
    middle_scatter = Scatter(place, middle_grads, [rows] * len(middle_taps))
    near_scatter.first()

    pooled_grad = lax.dynamic_slice_in_dim(pooled_grad_all, place.index, 1, axis=0) / crop_valid
    groups = [
        (pyramid_all, near_taps, center_of(near_taps), columns_of(near_taps, 1), 0),
        (pyramid_all, middle_taps, center_of(middle_taps), columns_of(middle_taps, 2), middle_at),
        (pyramid_all, wide_taps, center_of(far_taps), wide_columns, far_at),
    ]

    def half_back(side, after, scatters):
        low, moments, *passed = feature_back(
            branch_grad.reshape(tiles + (four_wide,)),
            groups,
            third,
            source,
            coef_three,
            pooled_grad,
            validity,
            side,
            2,
            after,
            passing(scatters),
        )
        take_back(scatters, passed)
        return low, moments

    def passing(scatters):
        return [array for scatter in scatters for array in scatter.kept]

    def take_back(scatters, passed):
        for scatter in scatters:
            count = len(scatter.kept)
            scatter.kept, passed = passed[:count], passed[count:]

    low_grad, low_moments = half_back(0, [middle_grads[0]], [near_scatter, middle_scatter])
    near_scatter.second()
    middle_scatter.first()
    high_grad, high_moments = half_back(1, [low_moments], [near_scatter, middle_scatter])
    three_plane = place.plane_total(
        jnp.concatenate([low_moments.reshape(-1), high_moments.reshape(-1), class_grad.reshape(-1)])
    )
    near_scatter.third()
    middle_scatter.second()
    far_grads = branch_weight_grad(
        wide_taps,
        wide_columns,
        [high_moments],
        project_grad if place.direct else None,
        passing([near_scatter, middle_scatter]),
    )
    take_back([near_scatter, middle_scatter], far_grads[parts:])
    far_grads = far_grads[:parts]
    if not place.direct:
        far_grads = [jnp.concatenate([far_grads[0], project_grad.astype(BF16)[None]], axis=1)]
    far_rows = [rows] * len(wide_taps) + [project_weight.shape[0]]
    far_scatter = Scatter(place, far_grads, far_rows)
    middle_scatter.third()
    three_totals = place.line_total(three_plane)
    class_total = three_totals[2 * channels :]
    three_totals = jnp.concatenate(
        [part.reshape(2, -1) for part in jnp.split(three_totals[: 2 * channels], 2)], axis=1
    )

    middle_grad, *expand_grads = third_back(
        place,
        low_grad,
        high_grad,
        third,
        coef_three,
        three_totals / counted,
        validity,
        middle_act,
        bottle_all,
        meta,
        expand_at,
        quarters,
        turns,
        [far_grads[0]],
        passing([middle_scatter, far_scatter]),
    )
    take_back([middle_scatter, far_scatter], expand_grads[parts:])
    expand_grads = expand_grads[:parts]
    far_scatter.first()
    unit_two, pre_two = unit_of(second, coef_two)
    grad_two = middle_grad * silu_slope(pre_two)
    two_totals = place.total(grad_moments(grad_two, unit_two))
    second_grad = through_norm(
        grad_two, unit_two, coef_two, counted, validity, two_totals
    ).astype(BF16)
    spatial_grads = weight_grad(
        place,
        conv_flipped,
        second_grad,
        meta,
        bottle_taps,
        [0] * len(bottle_taps),
        tiles,
        narrow,
        (),
        None,
        passing([far_scatter]),
    )
    take_back([far_scatter], spatial_grads[parts:])
    bottle_grads = [
        jnp.concatenate(pair, axis=1) for pair in zip(spatial_grads[:parts], expand_grads)
    ]
    bottle_rows = [narrow_rows] * (len(bottle_taps) + quarters)
    bottle_scatter = Scatter(place, bottle_grads, bottle_rows)
    far_scatter.second()
    grad_one, one_moments, *passed = spatial_back(
        second_grad.reshape(tiles + (narrow,)),
        first_tiles,
        coef_one,
        valid_tiles,
        bottle_all,
        bottle_taps,
        center_of(bottle_taps),
        spatial_at,
        [spatial_grads[0]],
        passing([far_scatter, bottle_scatter]),
    )
    take_back([far_scatter, bottle_scatter], passed)
    far_scatter.third()
    bottle_scatter.first()
    one_totals = place.total(one_moments)
    unit_one, _ = unit_of(first, coef_one)
    first_grad = through_norm(
        grad_one.reshape(pixels, narrow), unit_one, coef_one, counted, validity, one_totals
    ).astype(BF16)
    reduce_grads = weight_grad(
        place,
        source_flipped,
        first_grad,
        meta,
        point_taps,
        [0],
        tiles,
        narrow,
        (),
        None,
        passing([far_scatter, bottle_scatter]),
    )
    take_back([far_scatter, bottle_scatter], reduce_grads[parts:])
    reduce_scatter = Scatter(place, reduce_grads[:parts], [rows])
    bottle_scatter.second()

    def rows_back(first_turn, count, into, after, scatters):
        result, *passed = input_back(
            jnp.array(matrix.T, BF16),
            low_grad,
            high_grad,
            first_grad,
            bottle_all,
            turns,
            first_turn,
            count,
            after,
            passing(scatters),
            into,
        )
        take_back(scatters, passed)
        return result

    input_grad = rows_back(0, 2, None, [reduce_grads[0]], [bottle_scatter, reduce_scatter])
    reduce_scatter.first()
    bottle_scatter.third()
    input_grad = rows_back(2, turns - 2, input_grad, (), [bottle_scatter, reduce_scatter])
    reduce_scatter.second()
    reduce_scatter.third()

    vectors = [one_totals, two_totals, three_totals, branch_totals, image_totals, head_totals]
    vectors += [class_total, image_partial]
    packed = jnp.concatenate([vector.reshape(-1) for vector in vectors])
    packed = packed + place.swap(packed)
    split, start = [], 0
    for vector in vectors:
        split.append(packed[start : start + vector.size].reshape(vector.shape))
        start += vector.size

    def own_part(vectors):
        vector = jnp.concatenate(vectors)
        length = vector.shape[0] // size
        return lax.dynamic_slice_in_dim(vector, place.index * length, length, axis=0)

    bottle_gain_grad = own_part([split[0][1], split[1][1], split[2][1]])
    bottle_shift_grad = own_part([split[0][0], split[1][0], split[2][0]])
    pyramid_gain_grad = own_part([split[3][1], split[4][1]])
    pyramid_shift_grad = own_part([split[3][0], split[4][0]])
    head_norm_grad = jnp.stack([own_part([split[5][1]]), own_part([split[5][0]])])
    class_out = own_part([split[6].reshape(size * class_weight.shape[0], -1)])
    image_out = split[7]

    def taps_out(full, taps, weight):
        full = full.reshape((len(taps),) + weight.shape[2:])
        if len(taps) == weight.shape[0] * weight.shape[1]:
            return full.reshape(weight.shape)
        result = jnp.zeros(weight.shape, F32)
        for at, tap in enumerate(taps):
            result = result.at[tap[0], tap[1]].set(full[at])
        return result

    for scatter in (near_scatter, middle_scatter, far_scatter, bottle_scatter, reduce_scatter):
        scatter.finish()
    near_count, middle_count, far_count = len(near_taps), len(middle_taps), len(far_taps)
    bottle_count = len(bottle_taps)
    expand_out = bottle_scatter.piece(bottle_count, quarters).reshape(quarters, narrow_rows, narrow)
    return (
        input_grad.reshape(features.shape),
        reduce_scatter.piece(0, 1),
        taps_out(bottle_scatter.piece(0, bottle_count), bottle_taps, spatial_weight),
        jnp.swapaxes(expand_out, 0, 1).reshape(expand_weight.shape),
        bottle_gain_grad,
        bottle_shift_grad,
        far_scatter.piece(far_count, 1),
        taps_out(near_scatter.piece(0, near_count), near_taps, near_weight),
        taps_out(middle_scatter.piece(0, middle_count), middle_taps, middle_weight),
        taps_out(far_scatter.piece(0, far_count), far_taps, far_weight),
        image_out,
        far_scatter.piece(far_count + 1, 1),
        class_out,
        pyramid_gain_grad,
        pyramid_shift_grad,
        head_norm_grad,
    )


def solution(mesh):
    in_specs = (
        P("section", "batch", None, None, None),
        P("batch", None),
        P(None, None, "batch", None),
        P("batch", None),
        P("batch"),
        P("batch"),
        P("batch", None),
        P(None, None, "batch", None),
        P(None, None, "batch", None),
        P(None, None, "batch", None),
        P("batch", None),
        P("batch", None),
        P("batch", None),
        P("batch"),
        P("batch"),
        P("batch"),
        P("batch"),
        P(None, "batch", None, None),
        P(None, "batch"),
        P(None, "batch", None, None),
        P(),
    )
    out_specs = (
        P("section", "batch", None, None, None),
        P("batch", None),
        P(None, None, "batch", None),
        P("batch", None),
        P("batch"),
        P("batch"),
        P("batch", None),
        P(None, None, "batch", None),
        P(None, None, "batch", None),
        P(None, None, "batch", None),
        P("batch", None),
        P("batch", None),
        P("batch", None),
        P("batch"),
        P("batch"),
        P(None, "batch"),
    )
    return jax.shard_map(
        per_device, mesh=mesh, in_specs=in_specs, out_specs=out_specs, check_vma=False
    )
```

```python
import functools

import jax
import jax.numpy as jnp
import numpy as np
from jax import lax
from jax.experimental import pallas as pl
from jax.experimental.pallas import tpu as pltpu
from jax.sharding import PartitionSpec as P

CITY_CLASSES = 19
HOME_CLASSES = 13
BOTTLE_RATE = 4
NEAR_RATE = 12
MIDDLE_RATE = 24
FAR_RATE = 36
TILE = 4

EPSILON = 1e-05
FLOOR_LOGIT = -1e30
HIGHEST = lax.Precision.HIGHEST
F32 = jnp.float32
BF16 = jnp.bfloat16
SLOT_BITS = [0, 4, 2, 6, 1, 5, 3, 7, 8, 12, 9, 13, 10, 14, 11, 15]
VMEM_BYTES = 58 * 1024 * 1024


class Place:
    def __init__(self):
        self.size = lax.axis_size("batch")
        self.direct = self.size == len(SLOT_BITS)
        self.pieces = 2 * self.size if self.direct else 1
        self.core = lax.axis_index("section")
        self.index = lax.axis_index("batch")

    def meta(self):
        core = self.core[None].astype(jnp.int32)
        if not self.direct:
            return core
        table = [[SLOT_BITS.index(at ^ owner) for owner in range(self.size)] for at in range(self.size)]
        row = lax.dynamic_index_in_dim(jnp.array(table, jnp.int32), self.index, 0, keepdims=False)
        return jnp.concatenate([core, row])

    def flip(self, block, bits):
        return lax.ppermute(block, "batch", [(source, source ^ bits) for source in range(self.size)])

    def swap(self, block):
        return lax.ppermute(block, "section", [(0, 1), (1, 0)])

    def total(self, *arrays):
        if not self.direct:
            return lax.psum(arrays, "batch") if len(arrays) > 1 else lax.psum(arrays[0], "batch")
        summed = jnp.sum(self.everyone(jnp.concatenate([array.reshape(-1) for array in arrays])), axis=0)
        results, start = [], 0
        for array in arrays:
            results.append(summed[start : start + array.size].reshape(array.shape))
            start += array.size
        return results if len(arrays) > 1 else results[0]

    def everyone(self, vector):
        if not self.direct:
            return lax.all_gather(vector, "batch")
        sent = jnp.broadcast_to(vector, (self.size,) + vector.shape)
        return lax.all_to_all(sent, "batch", 0, 0)

    def gather(self, parts):
        blocks = []
        for part, count in parts:
            cut = part.reshape(count, -1, part.shape[1])
            if self.direct:
                half = cut.shape[1] // 2
                cut = lax.dynamic_slice_in_dim(cut, self.core * half, half, axis=1)
            else:
                cut = lax.all_gather(cut, "batch", axis=1, tiled=True)
            blocks.append(cut.reshape(-1, part.shape[1]))
        block = jnp.concatenate(blocks)
        if self.direct:
            return lax.all_gather(block, ("batch", "section"))
        return block[None]


class Scatter:
    def __init__(self, place, grads, rows):
        self.place, self.rows = place, rows
        self.kept = [grads[0]]
        self.arrived = place.swap(grads[1]) if place.direct else None

    def add(self, kept, arrived):
        return (kept.astype(F32) + arrived.astype(F32)).astype(BF16)

    def first(self):
        if not self.place.direct:
            return
        own, arrived = self.kept[0], self.arrived
        self.kept = []
        sent = []
        for start in (0, 8):
            self.kept.append(self.add(own[start : start + 4], arrived[start : start + 4]))
            sent.append(self.add(own[start + 4 : start + 8], arrived[start + 4 : start + 8]))
        self.arrived = [self.place.flip(sent[0], 1), self.place.flip(sent[1], 2)]

    def second(self):
        if not self.place.direct:
            return
        kept, sent = [], []
        for held, came in zip(self.kept, self.arrived):
            kept.append(self.add(held[:2], came[:2]))
            sent.append(self.add(held[2:], came[2:]))
        self.kept = kept
        self.arrived = [self.place.flip(sent[0], 2), self.place.flip(sent[1], 1)]

    def third(self):
        if not self.place.direct:
            return
        near = self.kept[0].astype(F32) + self.arrived[0].astype(F32)
        away = self.kept[1].astype(F32) + self.arrived[1].astype(F32)
        self.kept = [near[0]]
        sent = [near[1].astype(BF16), away[0].astype(BF16), away[1].astype(BF16)]
        self.arrived = [self.place.flip(piece, bits) for piece, bits in zip(sent, (4, 8, 12))]

    def finish(self):
        if self.place.direct:
            parts = [piece.astype(F32) for piece in self.arrived]
            result = (self.kept[0] + parts[0]) + (parts[1] + parts[2])
            opposite = self.place.swap(result)
            first = self.place.core == 0
            self.result = [jnp.where(first, result, opposite), jnp.where(first, opposite, result)]
            return self
        pieces, start = [], 0
        for rows in self.rows:
            cut = self.kept[0][0, start : start + rows * self.place.size].astype(F32)
            cut = lax.psum_scatter(cut, "batch", scatter_dimension=0, tiled=True)
            pieces.append(lax.psum(cut, "section"))
            start += rows * self.place.size
        self.result = [jnp.concatenate(pieces)]
        return self

    def extra(self, sizes):
        start = sum(self.rows[:-1]) // 2
        found = []
        for rows in sizes:
            found.append(jnp.concatenate([part[start : start + rows // 2] for part in self.result]))
            start += rows // 2
        return found

    def piece(self, first, count):
        parts = len(self.result)
        start = sum(self.rows[:first]) // parts
        rows = self.rows[first] // parts
        cut = [part[start : start + count * rows].reshape(count, rows, -1) for part in self.result]
        return jnp.concatenate(cut, axis=1).reshape(count * rows * parts, -1)


def call(body, args, specs, grid, outs, out_specs, scratch=(), meta=None, after=(), passed=(), into=None):
    used = len(args) + (meta is not None)
    passed = list(passed) if into is None else [into] + list(passed)
    waits = len(after) + len(passed)
    results = len(outs)
    filled = int(into is not None)
    kept = results - filled

    def inner(*refs):
        rest = refs[used + waits :]
        body(*refs[:used], *rest[:results], *rest[results + len(passed) - filled :])

    spec = pltpu.PrefetchScalarGridSpec(
        num_scalar_prefetch=int(meta is not None),
        grid=grid,
        in_specs=list(specs) + [pl.BlockSpec(memory_space=pl.ANY)] * waits,
        out_specs=list(out_specs) + [pl.BlockSpec(memory_space=pl.ANY)] * (len(passed) - filled),
        scratch_shapes=list(scratch),
    )
    arrays = ([] if meta is None else [meta]) + list(args) + list(after) + list(passed)
    first = len(arrays) - len(passed)
    return pl.pallas_call(
        inner,
        grid_spec=spec,
        out_shape=list(outs) + [shaped(array.shape, array.dtype) for array in passed[filled:]],
        input_output_aliases={first + at: kept + at for at in range(len(passed))},
        compiler_params=pltpu.CompilerParams(vmem_limit_bytes=VMEM_BYTES),
        cost_estimate=pl.CostEstimate(flops=1, transcendentals=0, bytes_accessed=1),
    )(*arrays)


def whole(array):
    shape = array.shape
    return pl.BlockSpec(
        shape, lambda *_: (0,) * len(shape), pipeline_mode=pl.Buffered(buffer_count=1)
    )


def held(shape):
    return pl.BlockSpec(shape, lambda *_: (0,) * len(shape))


def rows_of(array, rows):
    return pl.BlockSpec((rows, array.shape[1]), lambda step, *_: (step, 0))


def shaped(shape, dtype=F32):
    return jax.ShapeDtypeStruct(tuple(shape), dtype)


def span(shift_by, length):
    return max(0, -shift_by), length - max(0, shift_by)


def tap_list(height, breadth, dilation):
    listed = []
    for row_tap in range(3):
        for col_tap in range(3):
            row_shift = (row_tap - 1) * dilation
            col_shift = (col_tap - 1) * dilation
            if abs(row_shift) < height and abs(col_shift) < breadth:
                listed.append((row_tap, col_tap, row_shift // TILE, col_shift // TILE))
    return listed


def weight_of(ref):
    return ref[...].reshape(-1, ref.shape[-1])


def spread(meta_ref, full_ref, result_refs, column=0, at=0, rows=None):
    width = result_refs[0].shape[2]
    rows = result_refs[0].shape[1] if rows is None else rows
    if len(result_refs) == 1:
        result_refs[0][0, at : at + rows] = full_ref[:, column : column + width].astype(BF16)
        return
    core = meta_ref[0]
    for owner in range(result_refs[0].shape[0]):
        for ref, side in zip(result_refs, (core, 1 - core)):
            start = pl.multiple_of(owner * 2 * rows + side * rows, rows)
            block = full_ref[pl.ds(start, rows), column : column + width]
            ref[meta_ref[1 + owner], at : at + rows] = block.astype(BF16)


def slotted(place, rows, width):
    if place.direct:
        return [shaped((place.size, rows // 2, width), BF16)] * 2
    return [shaped((1, rows * place.size, width), BF16)]


def center_first(step, center):
    return jnp.where(step == 0, center, jnp.where(step <= center, step - 1, step))


def ordered(taps, center):
    return [taps[center]] + [tap for place, tap in enumerate(taps) if place != center]


def shifts_of(taps):
    return [(tap[2], tap[3]) for tap in taps]


def area(tap, tiles):
    return (tiles[0] - abs(tap[0])) * (tiles[1] - abs(tap[1])) * tiles[2]


def forward_tap(tap, fresh, source_ref, weight, result_ref):
    tiles_i, tiles_j, pixels, channels = source_ref.shape
    columns = result_ref.shape[-1]
    shift_i, shift_j = tap
    low_i, high_i = span(shift_i, tiles_i)
    low_j, high_j = span(shift_j, tiles_j)
    window = source_ref[
        low_i + shift_i : high_i + shift_i, low_j + shift_j : high_j + shift_j
    ].reshape(-1, channels)
    product = jnp.dot(window, weight, preferred_element_type=F32)
    product = product.reshape(high_i - low_i, high_j - low_j, pixels, columns)
    if fresh:
        result_ref[low_i:high_i, low_j:high_j] = product
    else:
        result_ref[low_i:high_i, low_j:high_j] += product


def unit_of(values, coef):
    unit = (values - coef[0:1]) * coef[1:2]
    return unit, coef[2:3] * unit + coef[3:4]


def masked_sums(values, valid):
    weighted = values * valid
    return jnp.concatenate(
        [jnp.sum(weighted, axis=0, keepdims=True), jnp.sum(weighted * values, axis=0, keepdims=True)]
    )


def sum_rows(ref, valid_ref, sums_ref):
    total = jnp.zeros(sums_ref.shape, F32)
    for row in range(ref.shape[0]):
        values = ref[row].reshape(-1, ref.shape[-1])
        total = total + masked_sums(values, valid_ref[row].reshape(-1, 1))
    sums_ref[...] = total


def branch_body(taps, source_ref, valid_ref, weight_ref, result_ref, sums_ref):
    for place, tap in enumerate(taps):

        @pl.when(pl.program_id(0) == place)
        def _(place=place, tap=tap):
            forward_tap(tap, place == 0, source_ref, weight_of(weight_ref), result_ref)

    @pl.when(pl.program_id(0) == len(taps) - 1)
    def _():
        sum_rows(result_ref, valid_ref, sums_ref)


def tap_block(weights, channels, first_tap, center, first_step=0, count=None):
    pieces, _, columns = weights.shape

    def index(step):
        if count is not None:
            step = jnp.clip(step - first_step, 0, count - 1)
        return (0, first_tap + center_first(step, center), 0)

    return pl.BlockSpec((pieces, channels // pieces, columns), index)


def branch_conv(source, valid, weights, taps, center, first_tap, after):
    channels, columns = source.shape[-1], weights.shape[2]
    shifts = ordered(shifts_of(taps), center)
    result_shape = source.shape[:3] + (columns,)
    return call(
        functools.partial(branch_body, shifts),
        [source, valid, weights],
        [whole(source), whole(valid), tap_block(weights, channels, first_tap, center)],
        (len(taps),),
        [shaped(result_shape), shaped((2, columns))],
        [held(result_shape), held((2, columns))],
        after=after,
    )


def spatial_body(taps, first_ref, coef_ref, valid_ref, weight_ref, input_ref, result_ref, sums_ref):
    @pl.when(pl.program_id(0) == 0)
    def _():
        for row in range(first_ref.shape[0]):
            _, pre = unit_of(first_ref[row], coef_ref[...][:, None, :])
            input_ref[row] = (silu(pre) * valid_ref[row]).astype(BF16)

    branch_body(taps, input_ref, valid_ref, weight_ref, result_ref, sums_ref)


def spatial_conv(first, coef, valid, weights, taps, center, first_tap):
    channels, columns = first.shape[-1], weights.shape[2]
    shifts = ordered(shifts_of(taps), center)
    return call(
        functools.partial(spatial_body, shifts),
        [first, coef, valid, weights],
        [whole(first), whole(coef), whole(valid), tap_block(weights, channels, first_tap, center)],
        (len(taps),),
        [shaped(first.shape, BF16), shaped(first.shape), shaped((2, columns))],
        [held(first.shape), held(first.shape), held((2, columns))],
    )


def backward_tap(tap, fresh, up_ref, column, weight_ref, result_ref):
    tiles_i, tiles_j, pixels, channels = result_ref.shape
    pieces, rows, width = weight_ref.shape
    shift_i, shift_j = tap
    low_i, high_i = span(shift_i, tiles_i)
    low_j, high_j = span(shift_j, tiles_j)
    window = up_ref[low_i:high_i, low_j:high_j, :, column : column + width].reshape(-1, width)
    wide = min(512, channels)
    for start in range(0, channels, wide):
        if pieces == 1:
            weight = weight_ref[0, start : start + wide]
        else:
            weight = weight_ref[start // rows : (start + wide) // rows].reshape(wide, width)
        product = lax.dot_general(
            window, weight, (((1,), (1,)), ((), ())), preferred_element_type=F32
        ).reshape(high_i - low_i, high_j - low_j, pixels, wide)
        place = (
            slice(low_i + shift_i, high_i + shift_i),
            slice(low_j + shift_j, high_j + shift_j),
            slice(None),
            slice(start, start + wide),
        )
        if fresh:
            result_ref[place] = product
        else:
            result_ref[place] += product


def grad_moments(grad, unit):
    return jnp.concatenate(
        [jnp.sum(grad, axis=0, keepdims=True), jnp.sum(grad * unit, axis=0, keepdims=True)]
    )


def feature_body(plan, up_ref, third_ref, source_ref, coef_ref, pooled_ref, valid_ref, *refs):
    weight_refs = refs[: len(plan)]
    result_ref, sums_ref, total_ref = refs[len(plan) :]
    step_now = pl.program_id(0)
    begun = 0
    for weight_ref, listed in zip(weight_refs, plan):
        for tap, column in listed:

            @pl.when(step_now == begun)
            def _(weight_ref=weight_ref, tap=tap, column=column, fresh=begun == 0):
                backward_tap(tap, fresh, up_ref, column, weight_ref, total_ref)

            begun += 1

    @pl.when(step_now >= begun)
    def _():
        row = step_now - begun
        width = total_ref.shape[-1]
        unit, pre = unit_of(third_ref[...], coef_ref[...])
        pre = pre + source_ref[...].astype(F32)
        grad = total_ref[row].reshape(-1, width) + pooled_ref[...]
        grad = grad * valid_ref[...] * silu_slope(pre)
        result_ref[...] = grad.astype(BF16)
        moments = grad_moments(grad, unit)

        @pl.when(step_now == begun)
        def _():
            sums_ref[...] = moments

        @pl.when(step_now > begun)
        def _():
            sums_ref[...] += moments


def feature_back(upstream, groups, third, source, coef, pooled, valid, side, sides, after, passed):
    channels = third.shape[1]
    part = channels // sides
    plan, arrays, specs, begun = [], [], [], 0
    for weights, taps, center, columns, first_tap in groups:
        shifts = ordered(list(zip(shifts_of(taps), columns)), center)
        plan.append(shifts)
        count = len(shifts)
        pieces, _, width = weights.shape
        rows = channels // pieces

        def index(step, first=begun, count=count, center=center, first_tap=first_tap, pieces=pieces):
            tap = first_tap + center_first(jnp.clip(step - first, 0, count - 1), center)
            return (0, tap * sides + side, 0) if pieces == 1 else (side, tap, 0)

        block = (1, rows // sides, width) if pieces == 1 else (pieces // sides, rows, width)
        arrays.append(weights)
        specs.append(pl.BlockSpec(block, index))
        begun += count
    turns = upstream.shape[0]
    height = third.shape[0] // turns

    def row_of(step):
        return jnp.clip(step - begun, 0, turns - 1)

    row_block = pl.BlockSpec((height, part), lambda step: (row_of(step), side))
    return call(
        functools.partial(feature_body, plan),
        [upstream, third, source, coef, pooled, valid] + arrays,
        [
            whole(upstream),
            row_block,
            row_block,
            pl.BlockSpec((coef.shape[0], part), lambda step: (0, side)),
            pl.BlockSpec((1, part), lambda step: (0, side)),
            pl.BlockSpec((height, 1), lambda step: (row_of(step), 0)),
        ]
        + specs,
        (begun + turns,),
        [shaped((third.shape[0], part), BF16), shaped((2, part))],
        [pl.BlockSpec((height, part), lambda step: (row_of(step), 0)), held((2, part))],
        [pltpu.VMEM(upstream.shape[:3] + (part,), F32)],
        after=after,
        passed=passed,
    )


def spatial_back_body(taps, up_ref, first_ref, coef_ref, valid_ref, weight_ref, result_ref, sums_ref):
    for place, tap in enumerate(taps):

        @pl.when(pl.program_id(0) == place)
        def _(place=place, tap=tap):
            backward_tap(tap, place == 0, up_ref, 0, weight_ref, result_ref)

    @pl.when(pl.program_id(0) == len(taps) - 1)
    def _():
        total = jnp.zeros(sums_ref.shape, F32)
        width = result_ref.shape[-1]
        for row in range(result_ref.shape[0]):
            unit, pre = unit_of(first_ref[row].reshape(-1, width), coef_ref[...])
            valid = valid_ref[row].reshape(-1, 1)
            grad = result_ref[row].reshape(-1, width) * valid * silu_slope(pre)
            result_ref[row] = grad.reshape(result_ref.shape[1:])
            total = total + grad_moments(grad, unit)
        sums_ref[...] = total


def spatial_back(upstream, first, coef, valid, weights, taps, center, first_tap, after, passed):
    channels, columns = first.shape[-1], weights.shape[2]
    shifts = ordered(shifts_of(taps), center)
    return call(
        functools.partial(spatial_back_body, shifts),
        [upstream, first, coef, valid, weights],
        [
            whole(upstream),
            whole(first),
            whole(coef),
            whole(valid),
            tap_block(weights, channels, first_tap, center),
        ],
        (len(taps),),
        [shaped(first.shape), shaped((2, channels))],
        [held(first.shape), held((2, channels))],
        after=after,
        passed=passed,
    )


def weight_tap(tap, tiles, flipped_ref, up_ref, padded_ref):
    tiles_i, tiles_j, pixels = tiles
    shift_i, shift_j = tap
    low_i, high_i = span(shift_i, tiles_i)
    low_j, high_j = span(shift_j, tiles_j)
    padded_ref[...] = jnp.zeros_like(padded_ref)
    wide = (high_j - low_j) * pixels
    for row in range(low_i, high_i):
        target = ((row + shift_i) * tiles_j + low_j + shift_j) * pixels
        source = (row * tiles_j + low_j) * pixels
        padded_ref[target : target + wide] = up_ref[source : source + wide]
    first = (low_i + shift_i) * tiles_j * pixels // 128 * 128
    last = -(-(high_i + shift_i) * tiles_j * pixels // 128) * 128
    return jnp.dot(
        flipped_ref[:, first:last], padded_ref[first:last], preferred_element_type=F32
    )


def weight_body(plan, tiles, extra, count, meta_ref, flipped_ref, up_ref, *refs):
    extra_ref = refs[0] if extra else None
    result_refs = refs[extra : extra + count]
    padded_ref, full_ref = refs[extra + count :]
    width = padded_ref.shape[1]
    for place, (tap, column) in enumerate(plan):

        @pl.when(pl.program_id(0) == place)
        def _(tap=tap, column=column):
            full_ref[...] = weight_tap(
                tap, tiles, flipped_ref, up_ref.at[:, column : column + width], padded_ref
            ).astype(BF16)
            spread(meta_ref, full_ref, result_refs)

    if extra:

        @pl.when(pl.program_id(0) == len(plan))
        def _():
            core = meta_ref[0]
            slots, held_rows, _ = result_refs[0].shape
            for owner in range(slots):
                for ref, side in zip(result_refs, (core, 1 - core)):
                    start = pl.multiple_of((owner * 2 + side) * held_rows, held_rows)
                    ref[meta_ref[1 + owner]] = extra_ref[pl.ds(start, held_rows)]


def weight_grad(place, flipped, upstream, meta, taps, columns, tiles, width, after=(), extra=None, passed=()):
    channels, padded = flipped.shape
    plan = list(zip(shifts_of(taps), columns))
    steps = len(taps) + (extra is not None)
    shapes = slotted(place, channels // place.size * steps, width)
    blocks = [
        pl.BlockSpec((shape.shape[0], shape.shape[1] // steps, width), lambda step, _: (0, step, 0))
        for shape in shapes
    ]
    more = [] if extra is None else [extra]
    return call(
        functools.partial(weight_body, plan, tiles, len(more), len(shapes)),
        [flipped, upstream] + more,
        [whole(array) for array in [flipped, upstream] + more],
        (steps,),
        shapes,
        blocks,
        [pltpu.VMEM((padded, width), BF16), pltpu.VMEM((channels, width), BF16)],
        meta,
        after,
        passed,
    )


def tile_matrix(breadth):
    count = TILE * breadth
    matrix = np.zeros((count, count), np.float32)
    for row in range(TILE):
        for column in range(breadth):
            at = (column // TILE * TILE + row) * TILE + column % TILE
            matrix[at, row * breadth + column] = 1.0
    return matrix


def tile_body(matrix_ref, natural_ref, result_ref):
    result_ref[...] = jnp.dot(
        matrix_ref[...], natural_ref[...], preferred_element_type=F32
    ).astype(BF16)


def tile_rows(natural, matrix):
    rows = matrix.shape[0]
    return call(
        tile_body,
        [matrix, natural],
        [whole(matrix), rows_of(natural, rows)],
        (natural.shape[0] // rows,),
        [shaped(natural.shape, BF16)],
        [rows_of(natural, rows)],
    )[0]


def flip_body(source_ref, result_ref):
    pixels = source_ref.shape[0]
    result_ref[:, :pixels] = source_ref[...].T
    if result_ref.shape[1] > pixels:
        extra = result_ref.shape[1] - pixels
        result_ref[:, pixels:] = jnp.zeros((result_ref.shape[0], extra), BF16)


def flipped(values, after=()):
    pixels, channels = values.shape
    padded = pixels + -pixels % 128
    return call(
        flip_body,
        [values],
        [pl.BlockSpec((pixels, 128), lambda step: (0, step))],
        (channels // 128,),
        [shaped((channels, padded), BF16)],
        [pl.BlockSpec((128, padded), lambda step: (step, 0))],
        after=after,
    )[0]


def add_sums(sums_ref, sums):
    @pl.when(pl.program_id(0) == 0)
    def _():
        sums_ref[...] = sums

    @pl.when(pl.program_id(0) > 0)
    def _():
        sums_ref[...] += sums


def first_body(source_ref, valid_ref, weight_ref, result_ref, sums_ref):
    product = jnp.dot(source_ref[...], weight_of(weight_ref), preferred_element_type=F32)
    result_ref[...] = product
    add_sums(sums_ref, masked_sums(product, valid_ref[...]))


def fixed_block(weights, channels, at):
    pieces, _, columns = weights.shape
    return pl.BlockSpec((pieces, channels // pieces, columns), lambda step, *_: (0, at, 0))


def first_conv(source, valid, weights, turns, after):
    pixels, channels = source.shape
    rows = pixels // turns
    width = weights.shape[2]
    return call(
        first_body,
        [source, valid, weights],
        [rows_of(source, rows), rows_of(valid, rows), fixed_block(weights, channels, 0)],
        (turns,),
        [shaped((pixels, width)), shaped((2, width))],
        [pl.BlockSpec((rows, width), lambda step: (step, 0)), held((2, width))],
        after=after,
    )


def third_body(count, second_ref, coef_ref, valid_ref, *refs):
    weight_refs = refs[:count]
    middle_ref, result_ref, sums_ref = refs[count:]
    _, pre = unit_of(second_ref[...], coef_ref[...])
    middle = silu(pre).astype(BF16)
    middle_ref[...] = middle
    valid = valid_ref[...]
    sums = []
    for quarter, ref in enumerate(weight_refs):
        product = jnp.dot(middle, weight_of(ref), preferred_element_type=F32)
        width = product.shape[1]
        result_ref[:, quarter * width : (quarter + 1) * width] = product
        sums.append(masked_sums(product, valid))
    add_sums(sums_ref, jnp.concatenate(sums, axis=1))


def third_conv(second, coef, valid, weights, first, count, turns):
    pixels, narrow = second.shape
    height = pixels // turns
    channels = count * weights.shape[2]
    return call(
        functools.partial(third_body, count),
        [second, coef, valid] + [weights] * count,
        [rows_of(second, height), whole(coef), rows_of(valid, height)]
        + [fixed_block(weights, narrow, first + quarter) for quarter in range(count)],
        (turns,),
        [shaped((pixels, narrow), BF16), shaped((pixels, channels)), shaped((2, channels))],
        [
            pl.BlockSpec((height, narrow), lambda step: (step, 0)),
            pl.BlockSpec((height, channels), lambda step: (step, 0)),
            held((2, channels)),
        ],
    )


def output_body(third_ref, source_ref, coef_ref, valid_ref, result_ref, sums_ref):
    _, pre = unit_of(third_ref[...], coef_ref[...])
    values = (valid_ref[...] * silu(pre + source_ref[...].astype(F32))).astype(BF16)
    result_ref[...] = values
    add_sums(sums_ref, jnp.sum(values.astype(F32), axis=0, keepdims=True))


def block_output(third, source, coef, valid, turns):
    pixels, channels = third.shape
    rows = pixels // turns
    return call(
        output_body,
        [third, source, coef, valid],
        [rows_of(third, rows), rows_of(source, rows), whole(coef), rows_of(valid, rows)],
        (turns,),
        [shaped(third.shape, BF16), shaped((1, channels))],
        [rows_of(third, rows), held((1, channels))],
    )


def third_back_body(
    count, outs, meta_ref, low_ref, high_ref, third_ref, coef_ref, totals_ref, valid_ref, middle_ref, *refs
):
    weight_refs = refs[:count]
    result_ref = refs[count]
    slot_refs = refs[count + 1 : count + 1 + outs]
    grad_ref, total_ref = refs[count + 1 + outs :]
    step_now = pl.program_id(0)

    @pl.when(step_now == 0)
    def _():
        total_ref[...] = jnp.zeros_like(total_ref)

    part = low_ref.shape[1]
    coef, totals, valid = coef_ref[...], totals_ref[...], valid_ref[...]
    for start, part_ref in ((0, low_ref), (part, high_ref)):
        at = slice(start, start + part)
        unit = (third_ref[:, at] - coef[0:1, at]) * coef[1:2, at]
        centered = part_ref[...].astype(F32) - valid * (totals[0:1, at] + unit * totals[1:2, at])
        grad_ref[:, at] = (coef[2:3, at] * coef[1:2, at] * centered).astype(BF16)
    width = weight_refs[0].shape[2]
    result = None
    for quarter, ref in enumerate(weight_refs):
        grad = grad_ref[:, quarter * width : (quarter + 1) * width]
        product = lax.dot_general(
            grad, weight_of(ref), (((1,), (1,)), ((), ())), preferred_element_type=F32
        )
        result = product if result is None else result + product
    result_ref[...] = result
    total_ref[...] += lax.dot_general(
        middle_ref[...], grad_ref[...], (((0,), (0,)), ((), ())), preferred_element_type=F32
    )

    @pl.when(step_now == pl.num_programs(0) - 1)
    def _():
        rows = slot_refs[0].shape[1] // count
        for quarter in range(count):
            spread(meta_ref, total_ref, slot_refs, quarter * width, quarter * rows, rows)


def third_back(place, low, high, third, coef, totals, valid, middle, weights, meta, first, count, turns, after, passed):
    pixels, channels = third.shape
    narrow = middle.shape[1]
    height = pixels // turns
    shapes = slotted(place, narrow // place.size * count, weights.shape[2])
    return call(
        functools.partial(third_back_body, count, len(shapes)),
        [low, high, third, coef, totals, valid, middle] + [weights] * count,
        [
            rows_of(low, height),
            rows_of(high, height),
            rows_of(third, height),
            whole(coef),
            whole(totals),
            rows_of(valid, height),
            rows_of(middle, height),
        ]
        + [fixed_block(weights, narrow, first + quarter) for quarter in range(count)],
        (turns,),
        [shaped((pixels, narrow))] + shapes,
        [pl.BlockSpec((height, narrow), lambda step, _: (step, 0))] + [held(shape.shape) for shape in shapes],
        [pltpu.VMEM((height, channels), BF16), pltpu.VMEM((narrow, channels), F32)],
        meta,
        after,
        passed,
    )


def input_body(matrix_ref, low_ref, high_ref, grad_ref, weight_ref, result_ref):
    rows = matrix_ref.shape[0]
    part = low_ref.shape[1]
    matrix = matrix_ref[...]
    moved = []
    for start in range(0, result_ref.shape[0], rows):
        at = slice(start, start + rows)
        moved.append(jnp.dot(matrix, grad_ref[at], preferred_element_type=F32).astype(BF16))
        for column, part_ref in ((0, low_ref), (part, high_ref)):
            result_ref[at, column : column + part] = jnp.dot(
                matrix, part_ref[at], preferred_element_type=F32
            )
    result_ref[...] += lax.dot_general(
        jnp.concatenate(moved), weight_of(weight_ref), (((1,), (1,)), ((), ())), preferred_element_type=F32
    )


def input_back(matrix, low, high, grad, weights, turns, first, count, after, passed, into):
    pixels, part = low.shape
    rows = pixels // turns
    channels = 2 * part
    width = grad.shape[1]

    def block(columns):
        return pl.BlockSpec((rows, columns), lambda step: (first + step, 0))

    return call(
        input_body,
        [matrix, low, high, grad, weights],
        [whole(matrix), block(part), block(part), block(width), fixed_block(weights, channels, 0)],
        (count,),
        [shaped((pixels, channels))],
        [block(channels)],
        after=after,
        passed=passed,
        into=into,
    )


def sigmoid(values):
    return 0.5 + 0.5 * jnp.tanh(0.5 * values)


def silu(values):
    return values * sigmoid(values)


def silu_slope(values):
    sigmoid_val = sigmoid(values)
    return sigmoid_val * (1.0 + values * (1.0 - sigmoid_val))


def sums(values, validity):
    weighted = values * validity
    return jnp.stack([jnp.sum(weighted, axis=0), jnp.sum(weighted * values, axis=0)])


def coefs(totals, counted, gain, shift):
    mean_value = totals[0] / counted
    scaling = lax.rsqrt(totals[1] / counted - mean_value * mean_value + EPSILON)
    return jnp.stack([mean_value, scaling, gain, shift])


def through_norm(grad_pre, unit, coef, counted, validity, totals):
    centered = grad_pre - validity * (totals[0] + unit * totals[1]) / counted
    return coef[2] * coef[1] * centered


def to_tiles(array):
    height, breadth = array.shape[:2]
    rest = array.shape[2:]
    cut = array.reshape((height // TILE, TILE, breadth // TILE, TILE) + rest)
    return jnp.swapaxes(cut, 1, 2).reshape((height * breadth,) + rest)


def per_device(
    features,
    reduce_weight,
    spatial_weight,
    expand_weight,
    bottle_gain,
    bottle_shift,
    point_weight,
    near_weight,
    middle_weight,
    far_weight,
    image_weight,
    project_weight,
    class_weight,
    pyramid_gain,
    pyramid_shift,
    head_gain,
    head_shift,
    crop_masks,
    crop_tasks,
    pixel_labels,
    task_norms,
):
    place = Place()
    size, core = place.size, place.core
    first_core = core == 0
    height, breadth, channels = features.shape[2:]
    pixels = height * breadth
    tiles = (height // TILE, breadth // TILE, TILE * TILE)
    narrow = reduce_weight.shape[1]
    branch = point_weight.shape[1]
    four_wide = 4 * branch
    rows = channels // size
    narrow_rows = narrow // size
    quarters = channels // narrow
    turns = 3
    meta = place.meta()
    matrix = tile_matrix(breadth)

    bottle_taps = tap_list(height, breadth, BOTTLE_RATE)
    near_taps = tap_list(height, breadth, NEAR_RATE)
    middle_taps = tap_list(height, breadth, MIDDLE_RATE)
    far_taps = tap_list(height, breadth, FAR_RATE)
    point_taps = [(1, 1, 0, 0)]

    def center_of(taps):
        return [tap[:2] for tap in taps].index((1, 1))

    def stacked(weight, taps):
        flat = weight.reshape((-1,) + weight.shape[2:])
        picked = [3 * tap[0] + tap[1] for tap in taps]
        if picked == list(range(picked[0], picked[-1] + 1)):
            flat = flat[picked[0] : picked[-1] + 1]
        else:
            flat = jnp.stack([flat[at] for at in picked])
        return flat.reshape(-1, flat.shape[2]), len(taps)

    mask = lax.dynamic_index_in_dim(crop_masks, core, 0, keepdims=False)[0]
    labels = lax.dynamic_index_in_dim(pixel_labels, core, 0, keepdims=False)[0]
    task = lax.dynamic_index_in_dim(crop_tasks, core, 0, keepdims=False)[0]
    validity = to_tiles(mask).astype(F32)[:, None]
    valid_tiles = validity.reshape(tiles + (1,))
    labels = to_tiles(labels)
    source = tile_rows(features.reshape(pixels, channels), jnp.array(matrix, BF16))
    source_flipped = flipped(source)

    wide_expand = expand_weight.reshape(-1, quarters, narrow)
    expand_parts = [(wide_expand[:, at], 1) for at in range(quarters)]
    bottle_all = place.gather([(reduce_weight, 1), stacked(spatial_weight, bottle_taps)] + expand_parts)
    spatial_at = channels // narrow
    expand_at = spatial_at + len(bottle_taps)
    pyramid_parts = [stacked(near_weight, near_taps), stacked(middle_weight, middle_taps)]
    pyramid_parts += [stacked(far_weight, far_taps), (point_weight, 1), (project_weight, 1)]
    pyramid_all = place.gather(pyramid_parts)
    middle_at = len(near_taps)
    far_at = middle_at + len(middle_taps)
    point_at = far_at + len(far_taps)
    project_at = (point_at + 1) * (channels // place.pieces)
    project_full = pyramid_all[:, project_at:].reshape(-1, branch)

    crop_valid_both = jnp.sum(crop_masks, axis=(1, 2, 3)).astype(F32)
    home_crop = (crop_tasks[:, 0] == 1).astype(F32)
    counts = jnp.concatenate(
        [
            crop_valid_both,
            jnp.sum(crop_valid_both * (1.0 - home_crop))[None],
            jnp.sum(crop_valid_both * home_crop)[None],
        ]
    )
    small = [bottle_gain, bottle_shift, pyramid_gain, pyramid_shift, head_gain, head_shift]
    small.append(class_weight.reshape(-1))
    small_widths = [part.shape[0] for part in small]
    small_own = jnp.concatenate(small).astype(F32)
    collected = place.everyone(jnp.concatenate([small_own, counts]))
    counts_all = jnp.sum(collected[:, small_own.size :], axis=0)
    small_all, start = [], 0
    for width in small_widths:
        small_all.append(collected[:, start : start + width].reshape(-1))
        start += width
    gain_bottle, shift_bottle, gain_pyramid, shift_pyramid, gain_head, shift_head = small_all[:6]
    class_full = small_all[6].reshape(size * class_weight.shape[0], -1).astype(BF16)
    counted = jnp.where(first_core, counts_all[0], counts_all[1])
    task_pixels = counts_all[2:4]
    crop_valid = jnp.where(first_core, crop_valid_both[0], crop_valid_both[1])

    first, first_sums = first_conv(source, validity, bottle_all, turns, [source_flipped])
    coef_one = coefs(place.total(first_sums), counted, gain_bottle[:narrow], shift_bottle[:narrow])
    first_tiles = first.reshape(tiles + (narrow,))
    conv_in, second, second_sums = spatial_conv(
        first_tiles, coef_one, valid_tiles, bottle_all, bottle_taps, center_of(bottle_taps), spatial_at
    )
    second = second.reshape(pixels, narrow)
    coef_two = coefs(
        place.total(second_sums), counted, gain_bottle[narrow : 2 * narrow], shift_bottle[narrow : 2 * narrow]
    )
    middle_act, third, third_sums = third_conv(
        second, coef_two, validity, bottle_all, expand_at, quarters, turns
    )
    coef_three = coefs(
        place.total(third_sums), counted, gain_bottle[2 * narrow :], shift_bottle[2 * narrow :]
    )
    block_out, pooled_sum = block_output(third, source, coef_three, validity, tiles[0])
    block_tiles = block_out.reshape(tiles + (channels,))

    pooled = (pooled_sum / crop_valid).astype(BF16)
    pooled_all = place.everyone(pooled[0])
    near_out, near_sums = branch_conv(
        block_tiles,
        valid_tiles,
        pyramid_all,
        near_taps,
        center_of(near_taps),
        0,
        (),
    )
    middle_out, middle_sums = branch_conv(
        block_tiles,
        valid_tiles,
        pyramid_all,
        middle_taps,
        center_of(middle_taps),
        middle_at,
        [pooled_all, near_sums],
    )
    pooled_rows = lax.dynamic_slice_in_dim(pooled_all, place.index * rows, rows, axis=1)
    image_all = place.total(jnp.dot(pooled_rows, image_weight, preferred_element_type=F32))
    far_out, far_sums = branch_conv(
        block_tiles,
        valid_tiles,
        pyramid_all,
        far_taps,
        center_of(far_taps),
        far_at,
        [middle_sums],
    )
    point_out, point_sums = branch_conv(
        block_tiles, valid_tiles, pyramid_all, point_taps, 0, point_at, [image_all, far_sums]
    )
    image_mean = jnp.sum(image_all, axis=0) / size
    image_scale = lax.rsqrt(
        jnp.sum(image_all * image_all, axis=0) / size - image_mean * image_mean + EPSILON
    )
    image_unit = (image_all - image_mean) * image_scale
    gain_image, shift_image = gain_pyramid[four_wide:], shift_pyramid[four_wide:]
    coef_image = jnp.stack([image_mean, image_scale, gain_image, shift_image])
    image_pre = gain_image * image_unit + shift_image
    image_act = silu(image_pre).astype(BF16)

    outs = [part.reshape(pixels, branch) for part in (point_out, near_out, middle_out, far_out)]
    branches = jnp.concatenate(outs, axis=1)
    branch_sums = jnp.concatenate([point_sums, near_sums, middle_sums, far_sums], axis=1)
    block_flipped = flipped(block_out, [point_sums])
    conv_flipped = flipped(conv_in.reshape(pixels, narrow), [block_flipped])
    coef_branch = coefs(
        place.total(branch_sums), counted, gain_pyramid[:four_wide], shift_pyramid[:four_wide]
    )
    unit_branch, pre_branch = unit_of(branches, coef_branch)
    joined = silu(pre_branch).astype(BF16)

    own_act = lax.dynamic_slice_in_dim(image_act, place.index, 1, axis=0)
    crop_part = jnp.dot(own_act, project_full[four_wide:], preferred_element_type=F32)
    projected = jnp.dot(joined, project_full[:four_wide], preferred_element_type=F32) + crop_part
    coef_head = coefs(place.total(sums(projected, validity)), counted, gain_head, shift_head)
    unit_head, pre_head = unit_of(projected, coef_head)
    output_act = silu(pre_head).astype(BF16)
    logits = jnp.dot(output_act, class_full, preferred_element_type=F32)

    columns = jnp.arange(class_full.shape[1])
    allowed = (columns >= CITY_CLASSES) == (task == 1)
    masked = jnp.where(allowed, logits, FLOOR_LOGIT)
    raised = jnp.exp(masked - jnp.max(masked, axis=-1, keepdims=True))
    chances = raised / jnp.sum(raised, axis=-1, keepdims=True)
    target = jnp.where(task == 0, labels % CITY_CLASSES, CITY_CLASSES + labels % HOME_CLASSES)
    chosen = (columns == target[:, None]).astype(F32)
    inverse = 1.0 / task_norms.astype(F32)
    task_share = inverse / jnp.sum(inverse)
    crop_weight = jnp.where(
        task == 0, task_share[0] / task_pixels[0], task_share[1] / task_pixels[1]
    )
    logit_grad = (crop_weight * validity * (chances - chosen)).astype(BF16)
    class_grad = lax.dot_general(
        output_act, logit_grad, (((0,), (0,)), ((), ())), preferred_element_type=F32
    )

    output_grad = lax.dot_general(
        logit_grad, class_full, (((1,), (1,)), ((), ())), preferred_element_type=F32
    )
    grad_head = output_grad * silu_slope(pre_head)
    head_totals = place.total(grad_moments(grad_head, unit_head))
    proj_grad = through_norm(
        grad_head, unit_head, coef_head, counted, validity, head_totals
    ).astype(BF16)
    crop_grad = jnp.sum(proj_grad, axis=0, dtype=F32)
    joined_grad = lax.dot_general(
        proj_grad, project_full[:four_wide], (((1,), (1,)), ((), ())), preferred_element_type=F32
    )
    act_grad = jnp.dot(project_full[four_wide:].astype(F32), crop_grad, precision=HIGHEST)
    own_pre = lax.dynamic_slice_in_dim(image_pre, place.index, 1, axis=0)[0]
    image_pre_grad = act_grad * silu_slope(own_pre)
    grad_branch = joined_grad * silu_slope(pre_branch)
    branch_parts = place.everyone(
        jnp.concatenate([grad_moments(grad_branch, unit_branch).reshape(-1), image_pre_grad])
    )
    image_pre_all = branch_parts[:, 2 * four_wide :]
    branch_totals = jnp.sum(branch_parts[:, : 2 * four_wide], axis=0).reshape(2, four_wide)
    branch_grad = through_norm(
        grad_branch, unit_branch, coef_branch, counted, validity, branch_totals
    ).astype(BF16)
    image_totals = grad_moments(image_pre_all, image_unit)
    image_in_all = through_norm(
        image_pre_all, image_unit, coef_image, float(size), 1.0, image_totals
    )
    pooled_partial = lax.dot_general(
        image_in_all, image_weight.astype(F32), (((1,), (1,)), ((), ())), precision=HIGHEST
    )
    if place.direct:
        pooled_grad_all = lax.all_to_all(pooled_partial, "batch", 0, 0).reshape(1, channels)
    else:
        pooled_grad_all = lax.dynamic_slice_in_dim(
            lax.all_gather(pooled_partial, "batch", axis=1, tiled=True), place.index, 1, axis=0
        )
    image_partial = jnp.dot(pooled_rows.astype(F32).T, image_in_all, precision=HIGHEST)

    def columns_of(taps, block):
        return [block * branch] * len(taps)

    wide_taps = far_taps + point_taps
    wide_columns = columns_of(far_taps, 3) + columns_of(point_taps, 0)
    project_grad = jnp.concatenate(
        [
            lax.dot_general(
                joined, proj_grad, (((0,), (0,)), ((), ())), preferred_element_type=F32
            ),
            own_act[0].astype(F32)[:, None] * crop_grad[None, :],
        ]
    )

    class_rows = class_grad.size // size // branch if place.direct else 0
    extra_rows = project_grad.shape[0] // size + class_rows

    def extra_halves():
        parts = [project_grad.reshape(size, 2, -1, branch), class_grad.reshape(size, 2, -1, branch)]
        spare = rows // 2 - extra_rows // 2
        parts.append(jnp.zeros((size, 2, spare, branch), F32))
        return jnp.concatenate(parts, axis=2).reshape(-1, branch).astype(BF16)

    def branch_weight_grad(taps, tap_columns, after, extra=None, passed=()):
        return weight_grad(
            place, block_flipped, branch_grad, meta, taps, tap_columns, tiles, branch, after, extra, passed
        )

    parts = 2 if place.direct else 1
    near_grads = branch_weight_grad(near_taps, columns_of(near_taps, 1), [conv_flipped])
    near_scatter = Scatter(place, near_grads, [rows] * len(near_taps))
    middle_grads = branch_weight_grad(
        middle_taps, columns_of(middle_taps, 2), [near_grads[0], pooled_grad_all]
    )
    middle_scatter = Scatter(place, middle_grads, [rows] * len(middle_taps))
    near_scatter.first()

    pooled_grad = pooled_grad_all / crop_valid
    groups = [
        (pyramid_all, near_taps, center_of(near_taps), columns_of(near_taps, 1), 0),
        (pyramid_all, middle_taps, center_of(middle_taps), columns_of(middle_taps, 2), middle_at),
        (pyramid_all, wide_taps, center_of(far_taps), wide_columns, far_at),
    ]

    def half_back(side, after, scatters):
        low, moments, *passed = feature_back(
            branch_grad.reshape(tiles + (four_wide,)),
            groups,
            third,
            source,
            coef_three,
            pooled_grad,
            validity,
            side,
            2,
            after,
            passing(scatters),
        )
        take_back(scatters, passed)
        return low, moments

    def passing(scatters):
        return [array for scatter in scatters for array in scatter.kept]

    def take_back(scatters, passed):
        for scatter in scatters:
            count = len(scatter.kept)
            scatter.kept, passed = passed[:count], passed[count:]

    low_grad, low_moments = half_back(0, [middle_grads[0]], [near_scatter, middle_scatter])
    near_scatter.second()
    middle_scatter.first()
    high_grad, high_moments = half_back(1, [low_moments], [near_scatter, middle_scatter])
    three_parts = place.total(low_moments, high_moments)
    near_scatter.third()
    middle_scatter.second()
    far_grads = branch_weight_grad(
        wide_taps,
        wide_columns,
        [high_moments],
        extra_halves() if place.direct else None,
        passing([near_scatter, middle_scatter]),
    )
    take_back([near_scatter, middle_scatter], far_grads[parts:])
    far_grads = far_grads[:parts]
    far_rows = [rows] * len(wide_taps) + [extra_rows]
    if not place.direct:
        far_grads = [jnp.concatenate([far_grads[0], project_grad.astype(BF16)[None]], axis=1)]
    far_scatter = Scatter(place, far_grads, far_rows)
    middle_scatter.third()
    three_totals = jnp.concatenate(three_parts, axis=1)

    middle_grad, *expand_grads = third_back(
        place,
        low_grad,
        high_grad,
        third,
        coef_three,
        three_totals / counted,
        validity,
        middle_act,
        bottle_all,
        meta,
        expand_at,
        quarters,
        turns,
        [far_grads[0]],
        passing([middle_scatter, far_scatter]),
    )
    take_back([middle_scatter, far_scatter], expand_grads[parts:])
    expand_grads = expand_grads[:parts]
    far_scatter.first()
    unit_two, pre_two = unit_of(second, coef_two)
    grad_two = middle_grad * silu_slope(pre_two)
    two_totals = place.total(grad_moments(grad_two, unit_two))
    second_grad = through_norm(
        grad_two, unit_two, coef_two, counted, validity, two_totals
    ).astype(BF16)
    spatial_grads = weight_grad(
        place,
        conv_flipped,
        second_grad,
        meta,
        bottle_taps,
        [0] * len(bottle_taps),
        tiles,
        narrow,
        (),
        None,
        passing([far_scatter]),
    )
    take_back([far_scatter], spatial_grads[parts:])
    bottle_grads = [
        jnp.concatenate(pair, axis=1) for pair in zip(spatial_grads[:parts], expand_grads)
    ]
    bottle_rows = [narrow_rows] * (len(bottle_taps) + quarters)
    bottle_scatter = Scatter(place, bottle_grads, bottle_rows)
    far_scatter.second()
    grad_one, one_moments, *passed = spatial_back(
        second_grad.reshape(tiles + (narrow,)),
        first_tiles,
        coef_one,
        valid_tiles,
        bottle_all,
        bottle_taps,
        center_of(bottle_taps),
        spatial_at,
        [spatial_grads[0]],
        passing([far_scatter, bottle_scatter]),
    )
    take_back([far_scatter, bottle_scatter], passed)
    far_scatter.third()
    bottle_scatter.first()
    one_totals = place.total(one_moments)
    unit_one, _ = unit_of(first, coef_one)
    first_grad = through_norm(
        grad_one.reshape(pixels, narrow), unit_one, coef_one, counted, validity, one_totals
    ).astype(BF16)
    bottle_scatter.second()
    reduce_grads = weight_grad(
        place,
        source_flipped,
        first_grad,
        meta,
        point_taps,
        [0],
        tiles,
        narrow,
        (),
        None,
        passing([far_scatter, bottle_scatter]),
    )
    take_back([far_scatter, bottle_scatter], reduce_grads[parts:])
    reduce_scatter = Scatter(place, reduce_grads[:parts], [rows])
    bottle_scatter.third()

    def rows_back(first_turn, count, into, after, scatters):
        result, *passed = input_back(
            jnp.array(matrix.T, BF16),
            low_grad,
            high_grad,
            first_grad,
            bottle_all,
            turns,
            first_turn,
            count,
            after,
            passing(scatters),
            into,
        )
        take_back(scatters, passed)
        return result

    input_grad = rows_back(0, 2, None, [reduce_grads[0]], [bottle_scatter, reduce_scatter])
    reduce_scatter.first()
    input_grad = rows_back(2, turns - 2, input_grad, (), [bottle_scatter, reduce_scatter])
    reduce_scatter.second()
    reduce_scatter.third()

    vectors = [one_totals, two_totals, three_totals, branch_totals, image_totals, head_totals]
    vectors += [image_partial]
    packed = jnp.concatenate([vector.reshape(-1) for vector in vectors])
    packed = packed + place.swap(packed)
    split, start = [], 0
    for vector in vectors:
        split.append(packed[start : start + vector.size].reshape(vector.shape))
        start += vector.size

    def own_part(vectors):
        vector = jnp.concatenate(vectors)
        length = vector.shape[0] // size
        return lax.dynamic_slice_in_dim(vector, place.index * length, length, axis=0)

    bottle_gain_grad = own_part([split[0][1], split[1][1], split[2][1]])
    bottle_shift_grad = own_part([split[0][0], split[1][0], split[2][0]])
    pyramid_gain_grad = own_part([split[3][1], split[4][1]])
    pyramid_shift_grad = own_part([split[3][0], split[4][0]])
    head_norm_grad = jnp.stack([own_part([split[5][1]]), own_part([split[5][0]])])
    image_out = split[6]

    def taps_out(full, taps, weight):
        full = full.reshape((len(taps),) + weight.shape[2:])
        if len(taps) == weight.shape[0] * weight.shape[1]:
            return full.reshape(weight.shape)
        result = jnp.zeros(weight.shape, F32)
        for at, tap in enumerate(taps):
            result = result.at[tap[0], tap[1]].set(full[at])
        return result

    for scatter in (near_scatter, middle_scatter, far_scatter, bottle_scatter, reduce_scatter):
        scatter.finish()
    near_count, middle_count, far_count = len(near_taps), len(middle_taps), len(far_taps)
    bottle_count = len(bottle_taps)
    expand_out = bottle_scatter.piece(bottle_count, quarters).reshape(quarters, narrow_rows, narrow)
    if place.direct:
        project_out, class_out = far_scatter.extra([extra_rows - class_rows, class_rows])
    else:
        project_out = far_scatter.piece(far_count + 1, 1)
        class_out = own_part([lax.psum(class_grad, ("batch", "section"))])
    return (
        input_grad.reshape(features.shape),
        reduce_scatter.piece(0, 1),
        taps_out(bottle_scatter.piece(0, bottle_count), bottle_taps, spatial_weight),
        jnp.swapaxes(expand_out, 0, 1).reshape(expand_weight.shape),
        bottle_gain_grad,
        bottle_shift_grad,
        far_scatter.piece(far_count, 1),
        taps_out(near_scatter.piece(0, near_count), near_taps, near_weight),
        taps_out(middle_scatter.piece(0, middle_count), middle_taps, middle_weight),
        taps_out(far_scatter.piece(0, far_count), far_taps, far_weight),
        image_out,
        project_out,
        class_out.reshape(class_weight.shape),
        pyramid_gain_grad,
        pyramid_shift_grad,
        head_norm_grad,
    )


def solution(mesh):
    in_specs = (
        P("section", "batch", None, None, None),
        P("batch", None),
        P(None, None, "batch", None),
        P("batch", None),
        P("batch"),
        P("batch"),
        P("batch", None),
        P(None, None, "batch", None),
        P(None, None, "batch", None),
        P(None, None, "batch", None),
        P("batch", None),
        P("batch", None),
        P("batch", None),
        P("batch"),
        P("batch"),
        P("batch"),
        P("batch"),
        P(None, "batch", None, None),
        P(None, "batch"),
        P(None, "batch", None, None),
        P(),
    )
    out_specs = (
        P("section", "batch", None, None, None),
        P("batch", None),
        P(None, None, "batch", None),
        P("batch", None),
        P("batch"),
        P("batch"),
        P("batch", None),
        P(None, None, "batch", None),
        P(None, None, "batch", None),
        P(None, None, "batch", None),
        P("batch", None),
        P("batch", None),
        P("batch", None),
        P("batch"),
        P("batch"),
        P(None, "batch"),
    )
    return jax.shard_map(
        per_device, mesh=mesh, in_specs=in_specs, out_specs=out_specs, check_vma=False
    )
```

```python
import functools

import jax
import jax.numpy as jnp
import numpy as np
from jax import lax
from jax.experimental import pallas as pl
from jax.experimental.pallas import tpu as pltpu
from jax.sharding import PartitionSpec as P

CITY_CLASSES = 19
HOME_CLASSES = 13
BOTTLE_RATE = 4
NEAR_RATE = 12
MIDDLE_RATE = 24
FAR_RATE = 36
TILE = 4

EPSILON = 1e-05
FLOOR_LOGIT = -1e30
HIGHEST = lax.Precision.HIGHEST
F32 = jnp.float32
BF16 = jnp.bfloat16
SLOT_BITS = [0, 4, 2, 6, 1, 5, 3, 7, 8, 12, 9, 13, 10, 14, 11, 15]
VMEM_BYTES = 58 * 1024 * 1024


class Place:
    def __init__(self):
        self.size = lax.axis_size("batch")
        self.direct = self.size == len(SLOT_BITS)
        self.pieces = 2 * self.size if self.direct else 1
        self.core = lax.axis_index("section")
        self.index = lax.axis_index("batch")

    def meta(self):
        core = self.core[None].astype(jnp.int32)
        if not self.direct:
            return core
        table = [[SLOT_BITS.index(at ^ owner) for owner in range(self.size)] for at in range(self.size)]
        row = lax.dynamic_index_in_dim(jnp.array(table, jnp.int32), self.index, 0, keepdims=False)
        return jnp.concatenate([core, row])

    def flip(self, block, bits):
        return lax.ppermute(block, "batch", [(source, source ^ bits) for source in range(self.size)])

    def swap(self, block):
        return lax.ppermute(block, "section", [(0, 1), (1, 0)])

    def total(self, *arrays):
        if not self.direct:
            return lax.psum(arrays, "batch") if len(arrays) > 1 else lax.psum(arrays[0], "batch")
        summed = jnp.sum(self.everyone(jnp.concatenate([array.reshape(-1) for array in arrays])), axis=0)
        results, start = [], 0
        for array in arrays:
            results.append(summed[start : start + array.size].reshape(array.shape))
            start += array.size
        return results if len(arrays) > 1 else results[0]

    def everyone(self, vector):
        if not self.direct:
            return lax.all_gather(vector, "batch")
        sent = jnp.broadcast_to(vector, (self.size,) + vector.shape)
        return lax.all_to_all(sent, "batch", 0, 0)

    def gather(self, parts):
        blocks = []
        for part, count in parts:
            cut = part.reshape(count, -1, part.shape[1])
            if self.direct:
                half = cut.shape[1] // 2
                cut = lax.dynamic_slice_in_dim(cut, self.core * half, half, axis=1)
            else:
                cut = lax.all_gather(cut, "batch", axis=1, tiled=True)
            blocks.append(cut.reshape(-1, part.shape[1]))
        block = jnp.concatenate(blocks)
        if self.direct:
            return lax.all_gather(block, ("batch", "section"))
        return block[None]


class Scatter:
    def __init__(self, place, grads, rows):
        self.place, self.rows = place, rows
        self.kept, self.sent = [grads[0]], []
        self.arrived = place.swap(grads[1]) if place.direct else None

    def add(self, kept, arrived):
        return (kept.astype(F32) + arrived.astype(F32)).astype(BF16)

    def first(self):
        if not self.place.direct:
            return
        own, arrived = self.kept[0], self.arrived
        self.kept = []
        sent = []
        for start in (0, 8):
            self.kept.append(self.add(own[start : start + 4], arrived[start : start + 4]))
            sent.append(self.add(own[start + 4 : start + 8], arrived[start + 4 : start + 8]))
        self.sent = sent
        self.arrived = [self.place.flip(sent[0], 1), self.place.flip(sent[1], 2)]

    def second(self):
        if not self.place.direct:
            return
        kept, sent = [], []
        for held, came in zip(self.kept, self.arrived):
            kept.append(self.add(held[:2], came[:2]))
            sent.append(self.add(held[2:], came[2:]))
        self.kept, self.sent = kept, sent
        self.arrived = [self.place.flip(sent[0], 2), self.place.flip(sent[1], 1)]

    def third(self):
        if not self.place.direct:
            return
        near = self.kept[0].astype(F32) + self.arrived[0].astype(F32)
        away = self.kept[1].astype(F32) + self.arrived[1].astype(F32)
        self.kept = [near[0]]
        sent = [near[1].astype(BF16), away[0].astype(BF16), away[1].astype(BF16)]
        self.sent = sent

    def launch(self):
        if self.place.direct:
            self.arrived = [
                self.place.flip(piece, bits) for piece, bits in zip(self.sent, (4, 8, 12))
            ]

    def finish(self):
        if self.place.direct:
            parts = [piece.astype(F32) for piece in self.arrived]
            result = (self.kept[0] + parts[0]) + (parts[1] + parts[2])
            opposite = self.place.swap(result)
            first = self.place.core == 0
            self.result = [jnp.where(first, result, opposite), jnp.where(first, opposite, result)]
            return self
        pieces, start = [], 0
        for rows in self.rows:
            cut = self.kept[0][0, start : start + rows * self.place.size].astype(F32)
            cut = lax.psum_scatter(cut, "batch", scatter_dimension=0, tiled=True)
            pieces.append(lax.psum(cut, "section"))
            start += rows * self.place.size
        self.result = [jnp.concatenate(pieces)]
        return self

    def extra(self, sizes):
        start = sum(self.rows[:-1]) // 2
        found = []
        for rows in sizes:
            found.append(jnp.concatenate([part[start : start + rows // 2] for part in self.result]))
            start += rows // 2
        return found

    def piece(self, first, count):
        parts = len(self.result)
        start = sum(self.rows[:first]) // parts
        rows = self.rows[first] // parts
        cut = [part[start : start + count * rows].reshape(count, rows, -1) for part in self.result]
        return jnp.concatenate(cut, axis=1).reshape(count * rows * parts, -1)


def call(body, args, specs, grid, outs, out_specs, scratch=(), meta=None, after=(), passed=(), into=None, flops=1):
    used = len(args) + (meta is not None)
    passed = list(passed) if into is None else [into] + list(passed)
    waits = len(after) + len(passed)
    results = len(outs)
    filled = int(into is not None)
    kept = results - filled

    def inner(*refs):
        rest = refs[used + waits :]
        body(*refs[:used], *rest[:results], *rest[results + len(passed) - filled :])

    spec = pltpu.PrefetchScalarGridSpec(
        num_scalar_prefetch=int(meta is not None),
        grid=grid,
        in_specs=list(specs) + [pl.BlockSpec(memory_space=pl.ANY)] * waits,
        out_specs=list(out_specs) + [pl.BlockSpec(memory_space=pl.ANY)] * (len(passed) - filled),
        scratch_shapes=list(scratch),
    )
    arrays = ([] if meta is None else [meta]) + list(args) + list(after) + list(passed)
    first = len(arrays) - len(passed)
    return pl.pallas_call(
        inner,
        grid_spec=spec,
        out_shape=list(outs) + [shaped(array.shape, array.dtype) for array in passed[filled:]],
        input_output_aliases={first + at: kept + at for at in range(len(passed))},
        compiler_params=pltpu.CompilerParams(vmem_limit_bytes=VMEM_BYTES),
        cost_estimate=pl.CostEstimate(flops=flops, transcendentals=0, bytes_accessed=1),
    )(*arrays)


def copy_body(source_ref, result_ref):
    result_ref[...] = source_ref[...]


def tied(array, after):
    return call(
        copy_body, [array], [whole(array)], (1,), [shaped(array.shape)], [held(array.shape)], after=after
    )[0]


def whole(array):
    shape = array.shape
    return pl.BlockSpec(
        shape, lambda *_: (0,) * len(shape), pipeline_mode=pl.Buffered(buffer_count=1)
    )


def held(shape):
    return pl.BlockSpec(shape, lambda *_: (0,) * len(shape))


def rows_of(array, rows):
    return pl.BlockSpec((rows, array.shape[1]), lambda step, *_: (step, 0))


def shaped(shape, dtype=F32):
    return jax.ShapeDtypeStruct(tuple(shape), dtype)


def span(shift_by, length):
    return max(0, -shift_by), length - max(0, shift_by)


def tap_list(height, breadth, dilation):
    listed = []
    for row_tap in range(3):
        for col_tap in range(3):
            row_shift = (row_tap - 1) * dilation
            col_shift = (col_tap - 1) * dilation
            if abs(row_shift) < height and abs(col_shift) < breadth:
                listed.append((row_tap, col_tap, row_shift // TILE, col_shift // TILE))
    return listed


def weight_of(ref):
    return ref[...].reshape(-1, ref.shape[-1])


def spread(meta_ref, full_ref, result_refs, column=0, at=0, rows=None):
    width = result_refs[0].shape[2]
    rows = result_refs[0].shape[1] if rows is None else rows
    if len(result_refs) == 1:
        result_refs[0][0, at : at + rows] = full_ref[:, column : column + width].astype(BF16)
        return
    core = meta_ref[0]
    for owner in range(result_refs[0].shape[0]):
        for ref, side in zip(result_refs, (core, 1 - core)):
            start = pl.multiple_of(owner * 2 * rows + side * rows, rows)
            block = full_ref[pl.ds(start, rows), column : column + width]
            ref[meta_ref[1 + owner], at : at + rows] = block.astype(BF16)


def slotted(place, rows, width):
    if place.direct:
        return [shaped((place.size, rows // 2, width), BF16)] * 2
    return [shaped((1, rows * place.size, width), BF16)]


def center_first(step, center):
    return jnp.where(step == 0, center, jnp.where(step <= center, step - 1, step))


def ordered(taps, center):
    return [taps[center]] + [tap for place, tap in enumerate(taps) if place != center]


def shifts_of(taps):
    return [(tap[2], tap[3]) for tap in taps]


def area(tap, tiles):
    return (tiles[0] - abs(tap[0])) * (tiles[1] - abs(tap[1])) * tiles[2]


def forward_tap(tap, fresh, source_ref, weight, result_ref, column):
    tiles_i, tiles_j, pixels, channels = source_ref.shape
    columns = weight.shape[1]
    shift_i, shift_j = tap
    low_i, high_i = span(shift_i, tiles_i)
    low_j, high_j = span(shift_j, tiles_j)
    window = source_ref[
        low_i + shift_i : high_i + shift_i, low_j + shift_j : high_j + shift_j
    ].reshape(-1, channels)
    product = jnp.dot(window, weight, preferred_element_type=F32)
    product = product.reshape(high_i - low_i, high_j - low_j, pixels, columns)
    place = (slice(low_i, high_i), slice(low_j, high_j), slice(None), slice(column, column + columns))
    if fresh:
        result_ref[place] = product
    else:
        result_ref[place] += product


def unit_of(values, coef):
    unit = (values - coef[0:1]) * coef[1:2]
    return unit, coef[2:3] * unit + coef[3:4]


def masked_sums(values, valid):
    weighted = values * valid
    return jnp.concatenate(
        [jnp.sum(weighted, axis=0, keepdims=True), jnp.sum(weighted * values, axis=0, keepdims=True)]
    )


def sum_rows(ref, valid_ref, sums_ref):
    total = jnp.zeros(sums_ref.shape, F32)
    for row in range(ref.shape[0]):
        values = ref[row].reshape(-1, ref.shape[-1])
        total = total + masked_sums(values, valid_ref[row].reshape(-1, 1))
    sums_ref[...] = total


def branch_body(plan, source_ref, valid_ref, weight_ref, result_ref, sums_ref):
    for place, (tap, fresh, column) in enumerate(plan):

        @pl.when(pl.program_id(0) == place)
        def _(tap=tap, fresh=fresh, column=column):
            forward_tap(tap, fresh, source_ref, weight_of(weight_ref), result_ref, column)

    @pl.when(pl.program_id(0) == len(plan) - 1)
    def _():
        sum_rows(result_ref, valid_ref, sums_ref)


def tap_plan(groups, first_tap):
    plan, starts = [], []
    for taps, center, column in groups:
        starts.append((len(plan), center))
        for place, tap in enumerate(ordered(shifts_of(taps), center)):
            plan.append((tap, place == 0, column))

    def index(step):
        tap = 0
        for start, center in starts:
            tap = jnp.where(step >= start, start + center_first(step - start, center), tap)
        return (0, first_tap + tap, 0)

    return plan, index


def branch_convs(source, valid, weights, groups, columns, after):
    channels = source.shape[-1]
    pieces, _, width = weights.shape
    plan, index = tap_plan(groups, 0)
    result_shape = source.shape[:3] + (columns,)
    return call(
        functools.partial(branch_body, plan),
        [source, valid, weights],
        [whole(source), whole(valid), pl.BlockSpec((pieces, channels // pieces, width), index)],
        (len(plan),),
        [shaped(result_shape), shaped((2, columns))],
        [held(result_shape), held((2, columns))],
        after=after,
    )


def spatial_body(plan, first_ref, coef_ref, valid_ref, weight_ref, input_ref, result_ref, sums_ref):
    @pl.when(pl.program_id(0) == 0)
    def _():
        for row in range(first_ref.shape[0]):
            _, pre = unit_of(first_ref[row], coef_ref[...][:, None, :])
            input_ref[row] = (silu(pre) * valid_ref[row]).astype(BF16)

    branch_body(plan, input_ref, valid_ref, weight_ref, result_ref, sums_ref)


def spatial_conv(first, coef, valid, weights, taps, center, first_tap):
    channels = first.shape[-1]
    pieces, _, columns = weights.shape
    plan, index = tap_plan([(taps, center, 0)], first_tap)
    return call(
        functools.partial(spatial_body, plan),
        [first, coef, valid, weights],
        [
            whole(first),
            whole(coef),
            whole(valid),
            pl.BlockSpec((pieces, channels // pieces, columns), index),
        ],
        (len(plan),),
        [shaped(first.shape, BF16), shaped(first.shape), shaped((2, columns))],
        [held(first.shape), held(first.shape), held((2, columns))],
    )


def shifted_columns(tiles, row_taps, up_ref, padded_ref, width, first=None, last=None):
    tiles_i, tiles_j, pixels = tiles
    shift_i, columns = row_taps
    low_i, high_i = span(shift_i, tiles_i)
    line = tiles_j * pixels
    low, high = (low_i + shift_i) * line, (high_i + shift_i) * line

    def clear(start, stop, at):
        if stop > start:
            padded_ref[start:stop, at : at + width] = jnp.zeros((stop - start, width), BF16)

    for place, (shift_j, column) in enumerate(columns):
        at = place * width
        low_j, high_j = span(shift_j, tiles_j)
        begin, end = (low_j + shift_j) * pixels, (high_j + shift_j) * pixels
        for row in range(low_i, high_i):
            base = (row + shift_i) * line
            source = row * line + low_j * pixels
            clear(base, base + begin, at)
            padded_ref[base + begin : base + end, at : at + width] = up_ref[
                source : source + end - begin, column : column + width
            ]
            clear(base + end, base + line, at)
        if first is not None:
            clear(first, low, at)
            clear(high, last, at)
    return low, high


def back_step(tiles, row_taps, fresh, up_ref, weight_refs, padded_ref, weight_ref, total_ref):
    channels = total_ref.shape[1]
    width = weight_refs[0].shape[2]
    depth = len(row_taps[1]) * width
    low, high = shifted_columns(tiles, row_taps, up_ref, padded_ref, width)
    for place in range(len(row_taps[1])):
        weight_ref[:, place * width : (place + 1) * width] = weight_of(weight_refs[place])
    wide = min(512, channels)
    for start in range(0, channels, wide):
        product = lax.dot_general(
            padded_ref[low:high, :depth],
            weight_ref[start : start + wide, :depth],
            (((1,), (1,)), ((), ())),
            preferred_element_type=F32,
        )
        if fresh:
            total_ref[low:high, start : start + wide] = product
        else:
            total_ref[low:high, start : start + wide] += product


def row_plan(taps, columns):
    rows = []
    for tap, column in zip(taps, columns):
        if not rows or rows[-1][0] != tap[2]:
            rows.append((tap[2], []))
        rows[-1][1].append((tap[3], column))
    return rows


def row_weights(weights, channels, order, first_tap, side=0, sides=1):
    pieces, _, width = weights.shape
    rows = channels // pieces
    specs = []
    for column in range(3):

        def index(step, column=column):
            row = order[-1]
            for place, listed in enumerate(order[:-1]):
                row = jnp.where(step == place, listed, row)
            tap = first_tap + 3 * row + column
            return (0, tap * sides + side, 0) if pieces == 1 else (side, tap, 0)

        block = (1, rows // sides, width) if pieces == 1 else (pieces // sides, rows, width)
        specs.append(pl.BlockSpec(block, index))
    return specs


def grad_moments(grad, unit):
    return jnp.concatenate(
        [jnp.sum(grad, axis=0, keepdims=True), jnp.sum(grad * unit, axis=0, keepdims=True)]
    )


def feature_body(
    plan, tiles, up_ref, third_ref, source_ref, coef_ref, pooled_ref, valid_ref, *refs
):
    weight_refs = refs[:4]
    result_ref, sums_ref, padded_ref, weight_ref, total_ref = refs[4:]
    step_now = pl.program_id(0)
    for place, row_taps in enumerate(plan):

        @pl.when(step_now == place)
        def _(place=place, row_taps=row_taps):
            back_step(
                tiles, row_taps, place == 0, up_ref, weight_refs, padded_ref, weight_ref, total_ref
            )

    begun = len(plan)

    @pl.when(step_now >= begun)
    def _():
        height = third_ref.shape[0]
        row = pl.multiple_of((step_now - begun) * height, height)
        unit, pre = unit_of(third_ref[...], coef_ref[...])
        pre = pre + source_ref[...].astype(F32)
        grad = total_ref[pl.ds(row, height)] + pooled_ref[...]
        grad = grad * valid_ref[...] * silu_slope(pre)
        result_ref[...] = grad.astype(BF16)
        moments = grad_moments(grad, unit)

        @pl.when(step_now == begun)
        def _():
            sums_ref[...] = moments

        @pl.when(step_now > begun)
        def _():
            sums_ref[...] += moments


def feature_back(upstream, weights, plan, order, point, third, source, coef, pooled, valid, tiles, side, sides, after, passed):
    pixels, channels = third.shape
    part = channels // sides
    pieces, _, width = weights.shape
    rows = channels // pieces
    begun = len(plan)
    turns = tiles[0]
    height = pixels // turns

    def row_of(step):
        return jnp.clip(step - begun, 0, turns - 1)

    row_block = pl.BlockSpec((height, part), lambda step: (row_of(step), side))
    if pieces == 1:
        point_block = pl.BlockSpec((1, rows // sides, width), lambda step: (0, point * sides + side, 0))
    else:
        point_block = pl.BlockSpec((pieces // sides, rows, width), lambda step: (side, point, 0))
    return call(
        functools.partial(feature_body, plan, tiles),
        [upstream, third, source, coef, pooled, valid] + [weights] * 4,
        [
            whole(upstream),
            row_block,
            row_block,
            pl.BlockSpec((coef.shape[0], part), lambda step: (0, side)),
            pl.BlockSpec((1, part), lambda step: (0, side)),
            pl.BlockSpec((height, 1), lambda step: (row_of(step), 0)),
        ]
        + row_weights(weights, channels, order, 0, side, sides)
        + [point_block],
        (begun + turns,),
        [shaped((pixels, part), BF16), shaped((2, part))],
        [pl.BlockSpec((height, part), lambda step: (row_of(step), 0)), held((2, part))],
        [
            pltpu.VMEM((pixels, 4 * width), BF16),
            pltpu.VMEM((part, 4 * width), BF16),
            pltpu.VMEM((pixels, part), F32),
        ],
        after=after,
        passed=passed,
    )


def spatial_back_body(plan, tiles, up_ref, first_ref, coef_ref, valid_ref, *refs):
    weight_refs = refs[:3]
    result_ref, sums_ref, padded_ref, weight_ref = refs[3:]
    for place, row_taps in enumerate(plan):

        @pl.when(pl.program_id(0) == place)
        def _(place=place, row_taps=row_taps):
            back_step(
                tiles, row_taps, place == 0, up_ref, weight_refs, padded_ref, weight_ref, result_ref
            )

    @pl.when(pl.program_id(0) == len(plan) - 1)
    def _():
        total = jnp.zeros(sums_ref.shape, F32)
        height = result_ref.shape[0] // tiles[0]
        for row in range(tiles[0]):
            at = slice(row * height, (row + 1) * height)
            unit, pre = unit_of(first_ref[at], coef_ref[...])
            grad = result_ref[at] * valid_ref[at] * silu_slope(pre)
            result_ref[at] = grad
            total = total + grad_moments(grad, unit)
        sums_ref[...] = total


def spatial_back(upstream, first, coef, valid, weights, plan, order, tiles, first_tap, after, passed):
    pixels, channels = first.shape
    columns = weights.shape[2]
    return call(
        functools.partial(spatial_back_body, plan, tiles),
        [upstream, first, coef, valid] + [weights] * 3,
        [whole(upstream), whole(first), whole(coef), whole(valid)]
        + row_weights(weights, channels, order, first_tap),
        (len(plan),),
        [shaped(first.shape), shaped((2, channels))],
        [held(first.shape), held((2, channels))],
        [pltpu.VMEM((pixels, 3 * columns), BF16), pltpu.VMEM((channels, 3 * columns), BF16)],
        after=after,
        passed=passed,
    )


def weight_body(plan, tiles, extra, count, meta_ref, flipped_ref, up_ref, *refs):
    extra_ref = refs[0] if extra else None
    result_refs = refs[extra : extra + count]
    padded_ref, full_ref = refs[extra + count :]
    block_rows, width = result_refs[0].shape[1:]
    taps_held = padded_ref.shape[1] // width
    rows = block_rows // taps_held
    for place, row_taps in enumerate(plan):

        @pl.when(pl.program_id(0) == place)
        def _(row_taps=row_taps):
            taps = len(row_taps[1])
            low_i, high_i = span(row_taps[0], tiles[0])
            line = tiles[1] * tiles[2]
            first = (low_i + row_taps[0]) * line // 128 * 128
            last = -(-(high_i + row_taps[0]) * line // 128) * 128
            shifted_columns(tiles, row_taps, up_ref, padded_ref, width, first, last)
            for tap in range(taps):
                at = slice(tap * width, (tap + 1) * width)
                full_ref[:, at] = jnp.dot(
                    flipped_ref[:, first:last], padded_ref[first:last, at], preferred_element_type=F32
                ).astype(BF16)
                spread(meta_ref, full_ref, result_refs, tap * width, tap * rows, rows)

    if extra:

        @pl.when(pl.program_id(0) == len(plan) - 1)
        def _():
            core = meta_ref[0]
            taps = len(plan[-1][1])
            spare = (taps_held - taps - 1) * rows
            for owner in range(result_refs[0].shape[0]):
                slot = meta_ref[1 + owner]
                for ref, side in zip(result_refs, (core, 1 - core)):
                    start = pl.multiple_of((owner * 2 + side) * rows, rows)
                    ref[slot, taps * rows : (taps + 1) * rows] = extra_ref[pl.ds(start, rows)]
                    ref[slot, (taps + 1) * rows :] = jnp.zeros((spare, width), BF16)


def weight_grad(place, flipped, upstream, meta, plan, tiles, width, after=(), extra=None, passed=()):
    channels, padded = flipped.shape
    taps = max(len(row_taps[1]) for row_taps in plan)
    steps = len(plan)
    shapes = slotted(place, channels // place.size * taps * steps, width)
    blocks = [
        pl.BlockSpec((shape.shape[0], shape.shape[1] // steps, width), lambda step, _: (0, step, 0))
        for shape in shapes
    ]
    more = [] if extra is None else [extra]
    return call(
        functools.partial(weight_body, plan, tiles, len(more), len(shapes)),
        [flipped, upstream] + more,
        [whole(array) for array in [flipped, upstream] + more],
        (steps,),
        shapes,
        blocks,
        [pltpu.VMEM((padded, taps * width), BF16), pltpu.VMEM((channels, taps * width), BF16)],
        meta,
        after,
        passed,
    )


def tile_matrix(breadth):
    count = TILE * breadth
    matrix = np.zeros((count, count), np.float32)
    for row in range(TILE):
        for column in range(breadth):
            at = (column // TILE * TILE + row) * TILE + column % TILE
            matrix[at, row * breadth + column] = 1.0
    return matrix


def tile_body(matrix_ref, natural_ref, result_ref):
    result_ref[...] = jnp.dot(
        matrix_ref[...], natural_ref[...], preferred_element_type=F32
    ).astype(BF16)


def tile_rows(natural, matrix):
    rows = matrix.shape[0]
    return call(
        tile_body,
        [matrix, natural],
        [whole(matrix), rows_of(natural, rows)],
        (natural.shape[0] // rows,),
        [shaped(natural.shape, BF16)],
        [rows_of(natural, rows)],
    )[0]


def flip_body(source_ref, result_ref):
    pixels = source_ref.shape[0]
    result_ref[:, :pixels] = source_ref[...].T
    if result_ref.shape[1] > pixels:
        extra = result_ref.shape[1] - pixels
        result_ref[:, pixels:] = jnp.zeros((result_ref.shape[0], extra), BF16)


def flipped(values, after=()):
    pixels, channels = values.shape
    padded = pixels + -pixels % 128
    return call(
        flip_body,
        [values],
        [pl.BlockSpec((pixels, 128), lambda step: (0, step))],
        (channels // 128,),
        [shaped((channels, padded), BF16)],
        [pl.BlockSpec((128, padded), lambda step: (step, 0))],
        after=after,
    )[0]


def add_sums(sums_ref, sums):
    @pl.when(pl.program_id(0) == 0)
    def _():
        sums_ref[...] = sums

    @pl.when(pl.program_id(0) > 0)
    def _():
        sums_ref[...] += sums


def first_body(source_ref, valid_ref, weight_ref, result_ref, sums_ref):
    product = jnp.dot(source_ref[...], weight_of(weight_ref), preferred_element_type=F32)
    result_ref[...] = product
    add_sums(sums_ref, masked_sums(product, valid_ref[...]))


def fixed_block(weights, channels, at):
    pieces, _, columns = weights.shape
    return pl.BlockSpec((pieces, channels // pieces, columns), lambda step, *_: (0, at, 0))


def first_conv(source, valid, weights, turns, after):
    pixels, channels = source.shape
    rows = pixels // turns
    width = weights.shape[2]
    return call(
        first_body,
        [source, valid, weights],
        [rows_of(source, rows), rows_of(valid, rows), fixed_block(weights, channels, 0)],
        (turns,),
        [shaped((pixels, width)), shaped((2, width))],
        [pl.BlockSpec((rows, width), lambda step: (step, 0)), held((2, width))],
        after=after,
    )


def third_body(count, second_ref, coef_ref, valid_ref, *refs):
    weight_refs = refs[:count]
    middle_ref, result_ref, sums_ref = refs[count:]
    _, pre = unit_of(second_ref[...], coef_ref[...])
    middle = silu(pre).astype(BF16)
    middle_ref[...] = middle
    valid = valid_ref[...]
    sums = []
    for quarter, ref in enumerate(weight_refs):
        product = jnp.dot(middle, weight_of(ref), preferred_element_type=F32)
        width = product.shape[1]
        result_ref[:, quarter * width : (quarter + 1) * width] = product
        sums.append(masked_sums(product, valid))
    add_sums(sums_ref, jnp.concatenate(sums, axis=1))


def third_conv(second, coef, valid, weights, first, count, turns):
    pixels, narrow = second.shape
    height = pixels // turns
    channels = count * weights.shape[2]
    return call(
        functools.partial(third_body, count),
        [second, coef, valid] + [weights] * count,
        [rows_of(second, height), whole(coef), rows_of(valid, height)]
        + [fixed_block(weights, narrow, first + quarter) for quarter in range(count)],
        (turns,),
        [shaped((pixels, narrow), BF16), shaped((pixels, channels)), shaped((2, channels))],
        [
            pl.BlockSpec((height, narrow), lambda step: (step, 0)),
            pl.BlockSpec((height, channels), lambda step: (step, 0)),
            held((2, channels)),
        ],
    )


def output_body(third_ref, source_ref, coef_ref, valid_ref, result_ref, sums_ref):
    _, pre = unit_of(third_ref[...], coef_ref[...])
    values = (valid_ref[...] * silu(pre + source_ref[...].astype(F32))).astype(BF16)
    result_ref[...] = values
    add_sums(sums_ref, jnp.sum(values.astype(F32), axis=0, keepdims=True))


def block_output(third, source, coef, valid, turns):
    pixels, channels = third.shape
    rows = pixels // turns
    return call(
        output_body,
        [third, source, coef, valid],
        [rows_of(third, rows), rows_of(source, rows), whole(coef), rows_of(valid, rows)],
        (turns,),
        [shaped(third.shape, BF16), shaped((1, channels))],
        [rows_of(third, rows), held((1, channels))],
    )


def third_back_body(
    count, outs, meta_ref, low_ref, high_ref, third_ref, coef_ref, totals_ref, valid_ref, middle_ref, *refs
):
    weight_refs = refs[:count]
    result_ref = refs[count]
    slot_refs = refs[count + 1 : count + 1 + outs]
    grad_ref, total_ref = refs[count + 1 + outs :]
    step_now = pl.program_id(0)

    @pl.when(step_now == 0)
    def _():
        total_ref[...] = jnp.zeros_like(total_ref)

    part = low_ref.shape[1]
    coef, totals, valid = coef_ref[...], totals_ref[...], valid_ref[...]
    for start, part_ref in ((0, low_ref), (part, high_ref)):
        at = slice(start, start + part)
        unit = (third_ref[:, at] - coef[0:1, at]) * coef[1:2, at]
        centered = part_ref[...].astype(F32) - valid * (totals[0:1, at] + unit * totals[1:2, at])
        grad_ref[:, at] = (coef[2:3, at] * coef[1:2, at] * centered).astype(BF16)
    width = weight_refs[0].shape[2]
    result = None
    for quarter, ref in enumerate(weight_refs):
        grad = grad_ref[:, quarter * width : (quarter + 1) * width]
        product = lax.dot_general(
            grad, weight_of(ref), (((1,), (1,)), ((), ())), preferred_element_type=F32
        )
        result = product if result is None else result + product
    result_ref[...] = result
    total_ref[...] += lax.dot_general(
        middle_ref[...], grad_ref[...], (((0,), (0,)), ((), ())), preferred_element_type=F32
    )

    @pl.when(step_now == pl.num_programs(0) - 1)
    def _():
        rows = slot_refs[0].shape[1] // count
        for quarter in range(count):
            spread(meta_ref, total_ref, slot_refs, quarter * width, quarter * rows, rows)


def third_back(place, low, high, third, coef, totals, valid, middle, weights, meta, first, count, turns, after, passed):
    pixels, channels = third.shape
    narrow = middle.shape[1]
    height = pixels // turns
    shapes = slotted(place, narrow // place.size * count, weights.shape[2])
    return call(
        functools.partial(third_back_body, count, len(shapes)),
        [low, high, third, coef, totals, valid, middle] + [weights] * count,
        [
            rows_of(low, height),
            rows_of(high, height),
            rows_of(third, height),
            whole(coef),
            whole(totals),
            rows_of(valid, height),
            rows_of(middle, height),
        ]
        + [fixed_block(weights, narrow, first + quarter) for quarter in range(count)],
        (turns,),
        [shaped((pixels, narrow))] + shapes,
        [pl.BlockSpec((height, narrow), lambda step, _: (step, 0))] + [held(shape.shape) for shape in shapes],
        [pltpu.VMEM((height, channels), BF16), pltpu.VMEM((narrow, channels), F32)],
        meta,
        after,
        passed,
    )


def input_body(matrix_ref, low_ref, high_ref, grad_ref, weight_ref, result_ref):
    rows = matrix_ref.shape[0]
    part = low_ref.shape[1]
    matrix = matrix_ref[...]
    moved = []
    for start in range(0, result_ref.shape[0], rows):
        at = slice(start, start + rows)
        moved.append(jnp.dot(matrix, grad_ref[at], preferred_element_type=F32).astype(BF16))
        for column, part_ref in ((0, low_ref), (part, high_ref)):
            result_ref[at, column : column + part] = jnp.dot(
                matrix, part_ref[at], preferred_element_type=F32
            )
    result_ref[...] += lax.dot_general(
        jnp.concatenate(moved), weight_of(weight_ref), (((1,), (1,)), ((), ())), preferred_element_type=F32
    )


def input_back(matrix, low, high, grad, weights, turns, first, count, after, passed, into):
    pixels, part = low.shape
    rows = pixels // turns
    channels = 2 * part
    width = grad.shape[1]

    def block(columns):
        return pl.BlockSpec((rows, columns), lambda step: (first + step, 0))

    return call(
        input_body,
        [matrix, low, high, grad, weights],
        [whole(matrix), block(part), block(part), block(width), fixed_block(weights, channels, 0)],
        (count,),
        [shaped((pixels, channels))],
        [block(channels)],
        after=after,
        passed=passed,
        into=into,
        flops=10**10,
    )


def sigmoid(values):
    return 0.5 + 0.5 * jnp.tanh(0.5 * values)


def silu(values):
    return values * sigmoid(values)


def silu_slope(values):
    sigmoid_val = sigmoid(values)
    return sigmoid_val * (1.0 + values * (1.0 - sigmoid_val))


def sums(values, validity):
    weighted = values * validity
    return jnp.stack([jnp.sum(weighted, axis=0), jnp.sum(weighted * values, axis=0)])


def coefs(totals, counted, gain, shift):
    mean_value = totals[0] / counted
    scaling = lax.rsqrt(totals[1] / counted - mean_value * mean_value + EPSILON)
    return jnp.stack([mean_value, scaling, gain, shift])


def through_norm(grad_pre, unit, coef, counted, validity, totals):
    centered = grad_pre - validity * (totals[0] + unit * totals[1]) / counted
    return coef[2] * coef[1] * centered


def to_tiles(array):
    height, breadth = array.shape[:2]
    rest = array.shape[2:]
    cut = array.reshape((height // TILE, TILE, breadth // TILE, TILE) + rest)
    return jnp.swapaxes(cut, 1, 2).reshape((height * breadth,) + rest)


def per_device(
    features,
    reduce_weight,
    spatial_weight,
    expand_weight,
    bottle_gain,
    bottle_shift,
    point_weight,
    near_weight,
    middle_weight,
    far_weight,
    image_weight,
    project_weight,
    class_weight,
    pyramid_gain,
    pyramid_shift,
    head_gain,
    head_shift,
    crop_masks,
    crop_tasks,
    pixel_labels,
    task_norms,
):
    place = Place()
    size, core = place.size, place.core
    first_core = core == 0
    height, breadth, channels = features.shape[2:]
    pixels = height * breadth
    tiles = (height // TILE, breadth // TILE, TILE * TILE)
    narrow = reduce_weight.shape[1]
    branch = point_weight.shape[1]
    four_wide = 4 * branch
    rows = channels // size
    narrow_rows = narrow // size
    quarters = channels // narrow
    turns = 3
    meta = place.meta()
    matrix = tile_matrix(breadth)

    bottle_taps = tap_list(height, breadth, BOTTLE_RATE)
    near_taps = tap_list(height, breadth, NEAR_RATE)
    middle_taps = tap_list(height, breadth, MIDDLE_RATE)
    far_taps = tap_list(height, breadth, FAR_RATE)
    point_taps = [(1, 1, 0, 0)]

    def center_of(taps):
        return [tap[:2] for tap in taps].index((1, 1))

    def stacked(weight, taps):
        flat = weight.reshape((-1,) + weight.shape[2:])
        picked = [3 * tap[0] + tap[1] for tap in taps]
        if picked == list(range(picked[0], picked[-1] + 1)):
            flat = flat[picked[0] : picked[-1] + 1]
        else:
            flat = jnp.stack([flat[at] for at in picked])
        return flat.reshape(-1, flat.shape[2]), len(taps)

    mask = lax.dynamic_index_in_dim(crop_masks, core, 0, keepdims=False)[0]
    labels = lax.dynamic_index_in_dim(pixel_labels, core, 0, keepdims=False)[0]
    task = lax.dynamic_index_in_dim(crop_tasks, core, 0, keepdims=False)[0]
    validity = to_tiles(mask).astype(F32)[:, None]
    valid_tiles = validity.reshape(tiles + (1,))
    labels = to_tiles(labels)
    source = tile_rows(features.reshape(pixels, channels), jnp.array(matrix, BF16))
    source_flipped = flipped(source)

    wide_expand = expand_weight.reshape(-1, quarters, narrow)
    expand_parts = [(wide_expand[:, at], 1) for at in range(quarters)]
    bottle_all = place.gather([(reduce_weight, 1), stacked(spatial_weight, bottle_taps)] + expand_parts)
    spatial_at = channels // narrow
    expand_at = spatial_at + len(bottle_taps)
    pyramid_parts = [stacked(near_weight, near_taps), stacked(middle_weight, middle_taps)]
    pyramid_parts += [stacked(far_weight, far_taps), (point_weight, 1), (project_weight, 1)]
    pyramid_all = place.gather(pyramid_parts)
    middle_at = len(near_taps)
    far_at = middle_at + len(middle_taps)
    point_at = far_at + len(far_taps)
    project_at = (point_at + 1) * (channels // place.pieces)
    project_full = pyramid_all[:, project_at:].reshape(-1, branch)

    crop_valid_both = jnp.sum(crop_masks, axis=(1, 2, 3)).astype(F32)
    home_crop = (crop_tasks[:, 0] == 1).astype(F32)
    counts = jnp.concatenate(
        [
            crop_valid_both,
            jnp.sum(crop_valid_both * (1.0 - home_crop))[None],
            jnp.sum(crop_valid_both * home_crop)[None],
        ]
    )
    small = [bottle_gain, bottle_shift, pyramid_gain, pyramid_shift, head_gain, head_shift]
    small.append(class_weight.reshape(-1))
    small_widths = [part.shape[0] for part in small]
    small_own = jnp.concatenate(small).astype(F32)
    collected = place.everyone(jnp.concatenate([small_own, counts]))
    counts_all = jnp.sum(collected[:, small_own.size :], axis=0)
    small_all, start = [], 0
    for width in small_widths:
        small_all.append(collected[:, start : start + width].reshape(-1))
        start += width
    gain_bottle, shift_bottle, gain_pyramid, shift_pyramid, gain_head, shift_head = small_all[:6]
    class_full = small_all[6].reshape(size * class_weight.shape[0], -1).astype(BF16)
    counted = jnp.where(first_core, counts_all[0], counts_all[1])
    task_pixels = counts_all[2:4]
    crop_valid = jnp.where(first_core, crop_valid_both[0], crop_valid_both[1])

    first, first_sums = first_conv(source, validity, bottle_all, turns, [source_flipped])
    coef_one = coefs(place.total(first_sums), counted, gain_bottle[:narrow], shift_bottle[:narrow])
    first_tiles = first.reshape(tiles + (narrow,))
    conv_in, second, second_sums = spatial_conv(
        first_tiles, coef_one, valid_tiles, bottle_all, bottle_taps, center_of(bottle_taps), spatial_at
    )
    second = second.reshape(pixels, narrow)
    coef_two = coefs(
        place.total(second_sums), counted, gain_bottle[narrow : 2 * narrow], shift_bottle[narrow : 2 * narrow]
    )
    middle_act, third, third_sums = third_conv(
        second, coef_two, validity, bottle_all, expand_at, quarters, turns
    )
    coef_three = coefs(
        place.total(third_sums), counted, gain_bottle[2 * narrow :], shift_bottle[2 * narrow :]
    )
    block_out, pooled_sum = block_output(third, source, coef_three, validity, tiles[0])
    block_tiles = block_out.reshape(tiles + (channels,))

    pooled = (pooled_sum / crop_valid).astype(BF16)
    pooled_all = place.everyone(pooled[0])
    pooled_rows = lax.dynamic_slice_in_dim(pooled_all, place.index * rows, rows, axis=1)
    image_all = place.total(jnp.dot(pooled_rows, image_weight, preferred_element_type=F32))
    branches, branch_sums = branch_convs(
        block_tiles,
        valid_tiles,
        pyramid_all,
        [
            (near_taps, center_of(near_taps), branch),
            (middle_taps, center_of(middle_taps), 2 * branch),
            (far_taps, center_of(far_taps), 3 * branch),
            (point_taps, 0, 0),
        ],
        four_wide,
        [image_all],
    )
    branches = branches.reshape(pixels, four_wide)
    image_mean = jnp.sum(image_all, axis=0) / size
    image_scale = lax.rsqrt(
        jnp.sum(image_all * image_all, axis=0) / size - image_mean * image_mean + EPSILON
    )
    image_unit = (image_all - image_mean) * image_scale
    gain_image, shift_image = gain_pyramid[four_wide:], shift_pyramid[four_wide:]
    coef_image = jnp.stack([image_mean, image_scale, gain_image, shift_image])
    image_pre = gain_image * image_unit + shift_image
    image_act = silu(image_pre).astype(BF16)

    block_flipped = flipped(block_out, [branch_sums])
    conv_flipped = flipped(conv_in.reshape(pixels, narrow), [block_flipped])
    coef_branch = coefs(
        place.total(branch_sums), counted, gain_pyramid[:four_wide], shift_pyramid[:four_wide]
    )
    unit_branch, pre_branch = unit_of(branches, coef_branch)
    joined = silu(pre_branch).astype(BF16)

    own_act = lax.dynamic_slice_in_dim(image_act, place.index, 1, axis=0)
    crop_part = jnp.dot(own_act, project_full[four_wide:], preferred_element_type=F32)
    projected = jnp.dot(joined, project_full[:four_wide], preferred_element_type=F32) + crop_part
    coef_head = coefs(place.total(sums(projected, validity)), counted, gain_head, shift_head)
    unit_head, pre_head = unit_of(projected, coef_head)
    output_act = silu(pre_head).astype(BF16)
    logits = jnp.dot(output_act, class_full, preferred_element_type=F32)

    columns = jnp.arange(class_full.shape[1])
    allowed = (columns >= CITY_CLASSES) == (task == 1)
    masked = jnp.where(allowed, logits, FLOOR_LOGIT)
    raised = jnp.exp(masked - jnp.max(masked, axis=-1, keepdims=True))
    chances = raised / jnp.sum(raised, axis=-1, keepdims=True)
    target = jnp.where(task == 0, labels % CITY_CLASSES, CITY_CLASSES + labels % HOME_CLASSES)
    chosen = (columns == target[:, None]).astype(F32)
    inverse = 1.0 / task_norms.astype(F32)
    task_share = inverse / jnp.sum(inverse)
    crop_weight = jnp.where(
        task == 0, task_share[0] / task_pixels[0], task_share[1] / task_pixels[1]
    )
    logit_grad = (crop_weight * validity * (chances - chosen)).astype(BF16)
    class_grad = lax.dot_general(
        output_act, logit_grad, (((0,), (0,)), ((), ())), preferred_element_type=F32
    )

    output_grad = lax.dot_general(
        logit_grad, class_full, (((1,), (1,)), ((), ())), preferred_element_type=F32
    )
    grad_head = output_grad * silu_slope(pre_head)
    head_totals = place.total(grad_moments(grad_head, unit_head))
    proj_grad = through_norm(
        grad_head, unit_head, coef_head, counted, validity, head_totals
    ).astype(BF16)
    crop_grad = jnp.sum(proj_grad, axis=0, dtype=F32)
    joined_grad = lax.dot_general(
        proj_grad, project_full[:four_wide], (((1,), (1,)), ((), ())), preferred_element_type=F32
    )
    act_grad = jnp.dot(project_full[four_wide:].astype(F32), crop_grad, precision=HIGHEST)
    own_pre = lax.dynamic_slice_in_dim(image_pre, place.index, 1, axis=0)[0]
    image_pre_grad = act_grad * silu_slope(own_pre)
    grad_branch = joined_grad * silu_slope(pre_branch)
    branch_parts = place.everyone(
        jnp.concatenate([grad_moments(grad_branch, unit_branch).reshape(-1), image_pre_grad])
    )
    image_pre_all = branch_parts[:, 2 * four_wide :]
    branch_totals = jnp.sum(branch_parts[:, : 2 * four_wide], axis=0).reshape(2, four_wide)
    branch_grad = through_norm(
        grad_branch, unit_branch, coef_branch, counted, validity, branch_totals
    ).astype(BF16)
    image_totals = grad_moments(image_pre_all, image_unit)
    image_in_all = through_norm(
        image_pre_all, image_unit, coef_image, float(size), 1.0, image_totals
    )
    pooled_partial = lax.dot_general(
        image_in_all, image_weight.astype(F32), (((1,), (1,)), ((), ())), precision=HIGHEST
    )
    if place.direct:
        pooled_grad_all = lax.all_to_all(pooled_partial, "batch", 0, 0).reshape(1, channels)
    else:
        pooled_grad_all = lax.dynamic_slice_in_dim(
            lax.all_gather(pooled_partial, "batch", axis=1, tiled=True), place.index, 1, axis=0
        )
    image_partial = jnp.dot(pooled_rows.astype(F32).T, image_in_all, precision=HIGHEST)

    def columns_of(taps, block):
        return [block * branch] * len(taps)

    near_rows = row_plan(near_taps, columns_of(near_taps, 1))
    middle_rows = row_plan(middle_taps, columns_of(middle_taps, 2))
    far_row = row_plan(far_taps, columns_of(far_taps, 3))
    point_row = row_plan(point_taps, columns_of(point_taps, 0))
    project_grad = jnp.concatenate(
        [
            lax.dot_general(
                joined, proj_grad, (((0,), (0,)), ((), ())), preferred_element_type=F32
            ),
            own_act[0].astype(F32)[:, None] * crop_grad[None, :],
        ]
    )

    class_rows = class_grad.size // size // branch if place.direct else 0
    extra_rows = project_grad.shape[0] // size + class_rows

    def extra_halves():
        parts = [project_grad.reshape(size, 2, -1, branch), class_grad.reshape(size, 2, -1, branch)]
        spare = rows // 2 - extra_rows // 2
        parts.append(jnp.zeros((size, 2, spare, branch), F32))
        return jnp.concatenate(parts, axis=2).reshape(-1, branch).astype(BF16)

    def branch_weight_grad(plan, after, extra=None):
        return weight_grad(
            place, block_flipped, branch_grad, meta, plan, tiles, branch, after, extra
        )

    parts = 2 if place.direct else 1
    wide_grads = branch_weight_grad(
        middle_rows + far_row + point_row, [conv_flipped], extra_halves() if place.direct else None
    )
    wide_rows = [rows] * (len(middle_taps) + len(far_taps) + 1) + [extra_rows]
    if not place.direct:
        wide_grads = [jnp.concatenate([wide_grads[0], project_grad.astype(BF16)[None]], axis=1)]
        wide_rows = wide_rows[:-1] + [rows, rows] + wide_rows[-1:]
    wide_scatter = Scatter(place, wide_grads, wide_rows)
    near_grads = branch_weight_grad(near_rows, [wide_grads[0]])
    near_scatter = Scatter(place, near_grads, [rows] * len(near_taps))
    wide_scatter.first()

    pooled_grad = pooled_grad_all / crop_valid
    back_plan = [(far_row[0][0], far_row[0][1] + point_row[0][1])] + near_rows + middle_rows
    far_at = len(near_rows) + len(middle_rows)
    back_order = [far_at] + list(range(far_at))

    def half_back(side, after, scatters):
        low, moments, *passed = feature_back(
            branch_grad,
            pyramid_all,
            back_plan,
            back_order,
            3 * far_at + len(far_taps),
            third,
            source,
            coef_three,
            pooled_grad,
            validity,
            tiles,
            side,
            2,
            after,
            passing(scatters),
        )
        take_back(scatters, passed)
        return low, moments

    def sending(*scatters):
        return [array for scatter in scatters for array in scatter.sent]

    def passing(scatters):
        return [array for scatter in scatters for array in scatter.kept]

    def take_back(scatters, passed):
        for scatter in scatters:
            count = len(scatter.kept)
            scatter.kept, passed = passed[:count], passed[count:]

    low_grad, low_moments = half_back(0, [near_grads[0]] + sending(wide_scatter), [wide_scatter])
    high_grad, high_moments = half_back(1, [low_moments], [wide_scatter, near_scatter])
    wide_scatter.second()
    near_scatter.first()
    three_parts = place.total(low_moments, high_moments)
    three_totals = jnp.concatenate(three_parts, axis=1)

    middle_grad, *expand_grads = third_back(
        place,
        low_grad,
        high_grad,
        third,
        coef_three,
        three_totals / counted,
        validity,
        middle_act,
        bottle_all,
        meta,
        expand_at,
        quarters,
        turns,
        sending(near_scatter, wide_scatter),
        passing([near_scatter, wide_scatter]),
    )
    take_back([near_scatter, wide_scatter], expand_grads[parts:])
    expand_grads = expand_grads[:parts]
    wide_scatter.third()
    wide_scatter.launch()
    near_scatter.second()
    unit_two, pre_two = unit_of(second, coef_two)
    grad_two = middle_grad * silu_slope(pre_two)
    two_totals = place.total(grad_moments(grad_two, unit_two))
    second_grad = through_norm(
        grad_two, unit_two, coef_two, counted, validity, two_totals
    ).astype(BF16)
    spatial_rows = row_plan(bottle_taps, [0] * len(bottle_taps))
    spatial_grads = weight_grad(
        place,
        conv_flipped,
        second_grad,
        meta,
        spatial_rows,
        tiles,
        narrow,
        sending(wide_scatter, near_scatter),
        None,
        passing([wide_scatter, near_scatter]),
    )
    take_back([wide_scatter, near_scatter], spatial_grads[parts:])
    bottle_grads = [
        jnp.concatenate(pair, axis=1) for pair in zip(spatial_grads[:parts], expand_grads)
    ]
    bottle_rows = [narrow_rows] * (len(bottle_taps) + quarters)
    bottle_scatter = Scatter(place, bottle_grads, bottle_rows)
    near_scatter.third()
    grad_one, one_moments, *passed = spatial_back(
        second_grad,
        first,
        coef_one,
        validity,
        bottle_all,
        [spatial_rows[1], spatial_rows[0], spatial_rows[2]],
        [1, 0, 2],
        tiles,
        spatial_at,
        [spatial_grads[0]],
        passing([wide_scatter, near_scatter, bottle_scatter]) + near_scatter.sent,
    )
    held_back = len(passed) - len(near_scatter.sent)
    take_back([wide_scatter, near_scatter, bottle_scatter], passed[:held_back])
    near_scatter.sent = passed[held_back:]
    near_scatter.launch()
    if place.direct:
        one_moments = tied(one_moments, [bottle_scatter.arrived] + wide_scatter.arrived)
    bottle_scatter.first()
    one_totals = place.total(one_moments)
    unit_one, _ = unit_of(first, coef_one)
    first_grad = through_norm(
        grad_one, unit_one, coef_one, counted, validity, one_totals
    ).astype(BF16)
    reduce_grads = weight_grad(
        place,
        source_flipped,
        first_grad,
        meta,
        row_plan(point_taps, [0]),
        tiles,
        narrow,
        sending(bottle_scatter),
        None,
        passing([bottle_scatter, near_scatter]),
    )
    take_back([bottle_scatter, near_scatter], reduce_grads[parts:])
    reduce_scatter = Scatter(place, reduce_grads[:parts], [rows])
    bottle_scatter.second()

    def rows_back(first_turn, count, into, after, scatters):
        result, *passed = input_back(
            jnp.array(matrix.T, BF16),
            low_grad,
            high_grad,
            first_grad,
            bottle_all,
            turns,
            first_turn,
            count,
            after,
            passing(scatters),
            into,
        )
        take_back(scatters, passed)
        return result

    input_grad = rows_back(0, 2, None, sending(bottle_scatter), [bottle_scatter, reduce_scatter])
    reduce_scatter.first()
    bottle_scatter.third()
    bottle_scatter.launch()
    input_grad = rows_back(2, turns - 2, input_grad, sending(bottle_scatter, reduce_scatter), [bottle_scatter, reduce_scatter])
    reduce_scatter.second()
    reduce_scatter.third()
    reduce_scatter.launch()

    vectors = [one_totals, two_totals, three_totals, branch_totals, image_totals, head_totals]
    vectors += [image_partial]
    packed = jnp.concatenate([vector.reshape(-1) for vector in vectors])
    packed = packed + place.swap(packed)
    split, start = [], 0
    for vector in vectors:
        split.append(packed[start : start + vector.size].reshape(vector.shape))
        start += vector.size

    def own_part(vectors):
        vector = jnp.concatenate(vectors)
        length = vector.shape[0] // size
        return lax.dynamic_slice_in_dim(vector, place.index * length, length, axis=0)

    bottle_gain_grad = own_part([split[0][1], split[1][1], split[2][1]])
    bottle_shift_grad = own_part([split[0][0], split[1][0], split[2][0]])
    pyramid_gain_grad = own_part([split[3][1], split[4][1]])
    pyramid_shift_grad = own_part([split[3][0], split[4][0]])
    head_norm_grad = jnp.stack([own_part([split[5][1]]), own_part([split[5][0]])])
    image_out = split[6]

    def taps_out(full, taps, weight):
        full = full.reshape((len(taps),) + weight.shape[2:])
        if len(taps) == weight.shape[0] * weight.shape[1]:
            return full.reshape(weight.shape)
        result = jnp.zeros(weight.shape, F32)
        for at, tap in enumerate(taps):
            result = result.at[tap[0], tap[1]].set(full[at])
        return result

    for scatter in (near_scatter, wide_scatter, bottle_scatter, reduce_scatter):
        scatter.finish()
    near_count, middle_count, far_count = len(near_taps), len(middle_taps), len(far_taps)
    bottle_count = len(bottle_taps)
    expand_out = bottle_scatter.piece(bottle_count, quarters).reshape(quarters, narrow_rows, narrow)
    if place.direct:
        project_out, class_out = wide_scatter.extra([extra_rows - class_rows, class_rows])
    else:
        project_out = wide_scatter.piece(len(wide_rows) - 1, 1)
        class_out = own_part([lax.psum(class_grad, ("batch", "section"))])
    return (
        input_grad.reshape(features.shape),
        reduce_scatter.piece(0, 1),
        taps_out(bottle_scatter.piece(0, bottle_count), bottle_taps, spatial_weight),
        jnp.swapaxes(expand_out, 0, 1).reshape(expand_weight.shape),
        bottle_gain_grad,
        bottle_shift_grad,
        wide_scatter.piece(middle_count + far_count, 1),
        taps_out(near_scatter.piece(0, near_count), near_taps, near_weight),
        taps_out(wide_scatter.piece(0, middle_count), middle_taps, middle_weight),
        taps_out(wide_scatter.piece(middle_count, far_count), far_taps, far_weight),
        image_out,
        project_out,
        class_out.reshape(class_weight.shape),
        pyramid_gain_grad,
        pyramid_shift_grad,
        head_norm_grad,
    )


def solution(mesh):
    in_specs = (
        P("section", "batch", None, None, None),
        P("batch", None),
        P(None, None, "batch", None),
        P("batch", None),
        P("batch"),
        P("batch"),
        P("batch", None),
        P(None, None, "batch", None),
        P(None, None, "batch", None),
        P(None, None, "batch", None),
        P("batch", None),
        P("batch", None),
        P("batch", None),
        P("batch"),
        P("batch"),
        P("batch"),
        P("batch"),
        P(None, "batch", None, None),
        P(None, "batch"),
        P(None, "batch", None, None),
        P(),
    )
    out_specs = (
        P("section", "batch", None, None, None),
        P("batch", None),
        P(None, None, "batch", None),
        P("batch", None),
        P("batch"),
        P("batch"),
        P("batch", None),
        P(None, None, "batch", None),
        P(None, None, "batch", None),
        P(None, None, "batch", None),
        P("batch", None),
        P("batch", None),
        P("batch", None),
        P("batch"),
        P("batch"),
        P(None, "batch"),
    )
    return jax.shard_map(
        per_device, mesh=mesh, in_specs=in_specs, out_specs=out_specs, check_vma=False
    )
```

```python
import functools

import jax
import jax.numpy as jnp
import numpy as np
from jax import lax
from jax.experimental import pallas as pl
from jax.experimental.pallas import tpu as pltpu
from jax.sharding import PartitionSpec as P

CITY_CLASSES = 19
HOME_CLASSES = 13
BOTTLE_RATE = 4
NEAR_RATE = 12
MIDDLE_RATE = 24
FAR_RATE = 36
TILE = 4

EPSILON = 1e-05
FLOOR_LOGIT = -1e30
HIGHEST = lax.Precision.HIGHEST
F32 = jnp.float32
BF16 = jnp.bfloat16
SLOT_BITS = [0, 4, 2, 6, 1, 5, 3, 7, 8, 12, 9, 13, 10, 14, 11, 15]
VMEM_BYTES = 58 * 1024 * 1024


class Place:
    def __init__(self):
        self.size = lax.axis_size("batch")
        self.direct = self.size == len(SLOT_BITS)
        self.pieces = 2 * self.size if self.direct else 1
        self.core = lax.axis_index("section")
        self.index = lax.axis_index("batch")

    def meta(self):
        core = self.core[None].astype(jnp.int32)
        if not self.direct:
            return core
        table = [[SLOT_BITS.index(at ^ owner) for owner in range(self.size)] for at in range(self.size)]
        row = lax.dynamic_index_in_dim(jnp.array(table, jnp.int32), self.index, 0, keepdims=False)
        return jnp.concatenate([core, row])

    def flip(self, block, bits):
        return lax.ppermute(block, "batch", [(source, source ^ bits) for source in range(self.size)])

    def swap(self, block):
        return lax.ppermute(block, "section", [(0, 1), (1, 0)])

    def total(self, *arrays):
        if not self.direct:
            return lax.psum(arrays, "batch") if len(arrays) > 1 else lax.psum(arrays[0], "batch")
        summed = jnp.sum(self.everyone(jnp.concatenate([array.reshape(-1) for array in arrays])), axis=0)
        results, start = [], 0
        for array in arrays:
            results.append(summed[start : start + array.size].reshape(array.shape))
            start += array.size
        return results if len(arrays) > 1 else results[0]

    def everyone(self, vector):
        if not self.direct:
            return lax.all_gather(vector, "batch")
        sent = jnp.broadcast_to(vector, (self.size,) + vector.shape)
        return lax.all_to_all(sent, "batch", 0, 0)

    def gather(self, parts):
        blocks = []
        for part, count in parts:
            cut = part.reshape(count, -1, part.shape[1])
            if self.direct:
                half = cut.shape[1] // 2
                cut = lax.dynamic_slice_in_dim(cut, self.core * half, half, axis=1)
            else:
                cut = lax.all_gather(cut, "batch", axis=1, tiled=True)
            blocks.append(cut.reshape(-1, part.shape[1]))
        block = jnp.concatenate(blocks)
        if self.direct:
            return lax.all_gather(block, ("batch", "section"))
        return block[None]


class Scatter:
    def __init__(self, place, grads, rows):
        self.place, self.rows = place, rows
        self.kept, self.sent = [grads[0]], []
        self.arrived = place.swap(grads[1]) if place.direct else None

    def add(self, kept, arrived):
        return (kept.astype(F32) + arrived.astype(F32)).astype(BF16)

    def first(self):
        if not self.place.direct:
            return
        own, arrived = self.kept[0], self.arrived
        self.kept = []
        sent = []
        for start in (0, 8):
            self.kept.append(self.add(own[start : start + 4], arrived[start : start + 4]))
            sent.append(self.add(own[start + 4 : start + 8], arrived[start + 4 : start + 8]))
        self.sent = sent
        self.arrived = [self.place.flip(sent[0], 1), self.place.flip(sent[1], 2)]

    def second(self):
        if not self.place.direct:
            return
        kept, sent = [], []
        for held, came in zip(self.kept, self.arrived):
            kept.append(self.add(held[:2], came[:2]))
            sent.append(self.add(held[2:], came[2:]))
        self.kept, self.sent = kept, sent
        self.arrived = [self.place.flip(sent[0], 2), self.place.flip(sent[1], 1)]

    def third(self):
        if not self.place.direct:
            return
        near = self.kept[0].astype(F32) + self.arrived[0].astype(F32)
        away = self.kept[1].astype(F32) + self.arrived[1].astype(F32)
        self.kept = [near[0]]
        sent = [near[1].astype(BF16), away[0].astype(BF16), away[1].astype(BF16)]
        self.sent = sent

    def launch(self):
        if self.place.direct:
            self.arrived = [
                self.place.flip(piece, bits) for piece, bits in zip(self.sent, (4, 8, 12))
            ]

    def finish(self):
        if self.place.direct:
            parts = [piece.astype(F32) for piece in self.arrived]
            result = (self.kept[0] + parts[0]) + (parts[1] + parts[2])
            opposite = self.place.swap(result)
            first = self.place.core == 0
            self.result = [jnp.where(first, result, opposite), jnp.where(first, opposite, result)]
            return self
        pieces, start = [], 0
        for rows in self.rows:
            cut = self.kept[0][0, start : start + rows * self.place.size].astype(F32)
            cut = lax.psum_scatter(cut, "batch", scatter_dimension=0, tiled=True)
            pieces.append(lax.psum(cut, "section"))
            start += rows * self.place.size
        self.result = [jnp.concatenate(pieces)]
        return self

    def extra(self, sizes):
        start = sum(self.rows[:-1]) // 2
        found = []
        for rows in sizes:
            found.append(jnp.concatenate([part[start : start + rows // 2] for part in self.result]))
            start += rows // 2
        return found

    def piece(self, first, count):
        parts = len(self.result)
        start = sum(self.rows[:first]) // parts
        rows = self.rows[first] // parts
        cut = [part[start : start + count * rows].reshape(count, rows, -1) for part in self.result]
        return jnp.concatenate(cut, axis=1).reshape(count * rows * parts, -1)


def call(body, args, specs, grid, outs, out_specs, scratch=(), meta=None, after=(), passed=(), into=None, flops=1):
    used = len(args) + (meta is not None)
    passed = list(passed) if into is None else [into] + list(passed)
    waits = len(after) + len(passed)
    results = len(outs)
    filled = int(into is not None)
    kept = results - filled

    def inner(*refs):
        rest = refs[used + waits :]
        body(*refs[:used], *rest[:results], *rest[results + len(passed) - filled :])

    spec = pltpu.PrefetchScalarGridSpec(
        num_scalar_prefetch=int(meta is not None),
        grid=grid,
        in_specs=list(specs) + [pl.BlockSpec(memory_space=pl.ANY)] * waits,
        out_specs=list(out_specs) + [pl.BlockSpec(memory_space=pl.ANY)] * (len(passed) - filled),
        scratch_shapes=list(scratch),
    )
    arrays = ([] if meta is None else [meta]) + list(args) + list(after) + list(passed)
    first = len(arrays) - len(passed)
    return pl.pallas_call(
        inner,
        grid_spec=spec,
        out_shape=list(outs) + [shaped(array.shape, array.dtype) for array in passed[filled:]],
        input_output_aliases={first + at: kept + at for at in range(len(passed))},
        compiler_params=pltpu.CompilerParams(vmem_limit_bytes=VMEM_BYTES),
        cost_estimate=pl.CostEstimate(flops=flops, transcendentals=0, bytes_accessed=1),
    )(*arrays)


def copy_body(source_ref, result_ref):
    result_ref[...] = source_ref[...]


def tied(array, after):
    return call(
        copy_body, [array], [whole(array)], (1,), [shaped(array.shape)], [held(array.shape)], after=after
    )[0]


def whole(array):
    shape = array.shape
    return pl.BlockSpec(
        shape, lambda *_: (0,) * len(shape), pipeline_mode=pl.Buffered(buffer_count=1)
    )


def held(shape):
    return pl.BlockSpec(shape, lambda *_: (0,) * len(shape))


def rows_of(array, rows):
    return pl.BlockSpec((rows, array.shape[1]), lambda step, *_: (step, 0))


def shaped(shape, dtype=F32):
    return jax.ShapeDtypeStruct(tuple(shape), dtype)


def span(shift_by, length):
    return max(0, -shift_by), length - max(0, shift_by)


def tap_list(height, breadth, dilation):
    listed = []
    for row_tap in range(3):
        for col_tap in range(3):
            row_shift = (row_tap - 1) * dilation
            col_shift = (col_tap - 1) * dilation
            if abs(row_shift) < height and abs(col_shift) < breadth:
                listed.append((row_tap, col_tap, row_shift // TILE, col_shift // TILE))
    return listed


def weight_of(ref):
    return ref[...].reshape(-1, ref.shape[-1])


def spread(meta_ref, full_ref, result_refs, column=0, at=0, rows=None):
    width = result_refs[0].shape[2]
    rows = result_refs[0].shape[1] if rows is None else rows
    if len(result_refs) == 1:
        result_refs[0][0, at : at + rows] = full_ref[:, column : column + width].astype(BF16)
        return
    core = meta_ref[0]
    for owner in range(result_refs[0].shape[0]):
        for ref, side in zip(result_refs, (core, 1 - core)):
            start = pl.multiple_of(owner * 2 * rows + side * rows, rows)
            block = full_ref[pl.ds(start, rows), column : column + width]
            ref[meta_ref[1 + owner], at : at + rows] = block.astype(BF16)


def slotted(place, rows, width):
    if place.direct:
        return [shaped((place.size, rows // 2, width), BF16)] * 2
    return [shaped((1, rows * place.size, width), BF16)]


def center_first(step, center):
    return jnp.where(step == 0, center, jnp.where(step <= center, step - 1, step))


def ordered(taps, center):
    return [taps[center]] + [tap for place, tap in enumerate(taps) if place != center]


def shifts_of(taps):
    return [(tap[2], tap[3]) for tap in taps]


def area(tap, tiles):
    return (tiles[0] - abs(tap[0])) * (tiles[1] - abs(tap[1])) * tiles[2]


def repeat(count, body):
    lax.fori_loop(0, count, lambda turn, carry: (body(turn), carry)[1], 0)


def row_steps(count):
    return max(step for step in (1, 2, 3, 4) if count % step == 0)


FIELDS = 9


def tap_table(plan, tiles, places):
    table, classes = [], []
    for ((shift_i, shift_j), column), place in zip(plan, places):
        low_i, high_i = span(shift_i, tiles[0])
        low_j, high_j = span(shift_j, tiles[1])
        kind = (row_steps(high_i - low_i), high_j - low_j)
        if kind not in classes:
            classes.append(kind)
        table += [classes.index(kind), low_i, low_i + shift_i, (high_i - low_i) // kind[0]]
        table += [low_j, low_j + shift_j, column, place, 0]
    return np.array(table, np.int32), classes


def forward_taps(classes, table_ref, source_ref, weight_ref, result_ref):
    _, _, pixels, channels = source_ref.shape
    width = weight_ref.shape[2]
    at = pl.program_id(0) * FIELDS
    for kind, (rows, wide) in enumerate(classes):

        @pl.when(table_ref[at] == kind)
        def _(rows=rows, wide=wide):
            to_i, from_i, turns = table_ref[at + 1], table_ref[at + 2], table_ref[at + 3]
            to_j, from_j = table_ref[at + 4], table_ref[at + 5]
            column = pl.multiple_of(table_ref[at + 6], width)

            def body(turn):
                window = source_ref[pl.ds(from_i + turn * rows, rows), pl.ds(from_j, wide)]
                product = jnp.dot(
                    window.reshape(-1, channels), weight_of(weight_ref), preferred_element_type=F32
                )
                place = (
                    pl.ds(to_i + turn * rows, rows),
                    pl.ds(to_j, wide),
                    slice(None),
                    pl.ds(column, width),
                )
                result_ref[place] += product.reshape(rows, wide, pixels, width)

            repeat(turns, body)


def unit_of(values, coef):
    unit = (values - coef[0:1]) * coef[1:2]
    return unit, coef[2:3] * unit + coef[3:4]


def masked_sums(values, valid):
    weighted = values * valid
    return jnp.concatenate(
        [jnp.sum(weighted, axis=0, keepdims=True), jnp.sum(weighted * values, axis=0, keepdims=True)]
    )


def sum_rows(ref, valid_ref, sums_ref):
    sums_ref[...] = jnp.zeros_like(sums_ref)

    def body(row):
        values = ref[row].reshape(-1, ref.shape[-1])
        sums_ref[...] += masked_sums(values, valid_ref[row].reshape(-1, 1))

    repeat(ref.shape[0], body)


def branch_body(classes, table_ref, source_ref, valid_ref, weight_ref, result_ref, sums_ref):
    @pl.when(pl.program_id(0) == 0)
    def _():
        def clear(row):
            result_ref[row] = jnp.zeros(result_ref.shape[1:], F32)

        repeat(result_ref.shape[0], clear)

    forward_taps(classes, table_ref, source_ref, weight_ref, result_ref)

    @pl.when(pl.program_id(0) == pl.num_programs(0) - 1)
    def _():
        sum_rows(result_ref, valid_ref, sums_ref)


def placed_block(weights, channels):
    pieces, _, width = weights.shape
    return pl.BlockSpec(
        (pieces, channels // pieces, width), lambda step, table: (0, table[step * FIELDS + 7], 0)
    )


def branch_convs(source, valid, weights, groups, columns, after):
    channels = source.shape[-1]
    plan = [(shift, column) for taps, column in groups for shift in shifts_of(taps)]
    table, classes = tap_table(plan, source.shape, range(len(plan)))
    result_shape = source.shape[:3] + (columns,)
    return call(
        functools.partial(branch_body, classes),
        [source, valid, weights],
        [whole(source), whole(valid), placed_block(weights, channels)],
        (len(plan),),
        [shaped(result_shape), shaped((2, columns))],
        [held(result_shape), held((2, columns))],
        meta=jnp.array(table),
        after=after,
    )


def spatial_body(
    classes, table_ref, first_ref, coef_ref, valid_ref, weight_ref, input_ref, result_ref, sums_ref
):
    @pl.when(pl.program_id(0) == 0)
    def _():
        def body(row):
            _, pre = unit_of(first_ref[row], coef_ref[...][:, None, :])
            input_ref[row] = (silu(pre) * valid_ref[row]).astype(BF16)

        repeat(first_ref.shape[0], body)

    branch_body(classes, table_ref, input_ref, valid_ref, weight_ref, result_ref, sums_ref)


def spatial_conv(first, coef, valid, weights, taps, first_tap):
    channels = first.shape[-1]
    columns = weights.shape[2]
    plan = [(shift, 0) for shift in shifts_of(taps)]
    table, classes = tap_table(plan, first.shape, [first_tap + at for at in range(len(plan))])
    return call(
        functools.partial(spatial_body, classes),
        [first, coef, valid, weights],
        [whole(first), whole(coef), whole(valid), placed_block(weights, channels)],
        (len(plan),),
        [shaped(first.shape, BF16), shaped(first.shape), shaped((2, columns))],
        [held(first.shape), held(first.shape), held((2, columns))],
        meta=jnp.array(table),
    )


def shifted_columns(tiles, row_taps, up_ref, padded_ref, width, first=None, last=None):
    tiles_i, tiles_j, pixels = tiles
    shift_i, columns = row_taps
    low_i, high_i = span(shift_i, tiles_i)
    line = tiles_j * pixels
    low, high = (low_i + shift_i) * line, (high_i + shift_i) * line

    def clear(start, count, at):
        if count > 0:
            padded_ref[pl.ds(start, count), at : at + width] = jnp.zeros((count, width), BF16)

    def body(turn):
        base = pl.multiple_of((low_i + shift_i + turn) * line, pixels)
        source = pl.multiple_of((low_i + turn) * line, pixels)
        for place, (shift_j, column) in enumerate(columns):
            at = place * width
            low_j, high_j = span(shift_j, tiles_j)
            begin, end = (low_j + shift_j) * pixels, (high_j + shift_j) * pixels
            clear(base, begin, at)
            padded_ref[pl.ds(base + begin, end - begin), at : at + width] = up_ref[
                pl.ds(source + low_j * pixels, end - begin), column : column + width
            ]
            clear(base + end, line - end, at)

    repeat(high_i - low_i, body)
    if first is not None:
        for place in range(len(columns)):
            clear(first, low - first, place * width)
            clear(high, last - high, place * width)


def back_step(plan, tiles, up_ref, weight_refs, padded_ref, weight_ref, total_ref):
    channels = total_ref.shape[1]
    width = weight_refs[0].shape[2]
    line = tiles[1] * tiles[2]
    step_now = pl.program_id(0)
    kinds = {}
    for place, row_taps in enumerate(plan):
        low_i, high_i = span(row_taps[0], tiles[0])
        rows = row_steps(high_i - low_i)
        kind = (rows, len(row_taps[1]), place == 0)
        kinds.setdefault(kind, []).append((place, low_i + row_taps[0], (high_i - low_i) // rows))

        @pl.when(step_now == place)
        def _(row_taps=row_taps):
            shifted_columns(tiles, row_taps, up_ref, padded_ref, width)

    wide = min(512, channels)
    for (rows, taps, fresh), steps in kinds.items():
        depth = taps * width
        here = functools.reduce(jnp.logical_or, [step_now == place for place, _, _ in steps])
        first = functools.reduce(
            lambda value, step: jnp.where(step_now == step[0], step[1], value), steps, 0
        )
        turns = functools.reduce(
            lambda value, step: jnp.where(step_now == step[0], step[2], value), steps, 0
        )

        @pl.when(here)
        def _(rows=rows, taps=taps, fresh=fresh, depth=depth, first=first, turns=turns):
            for tap in range(taps):
                weight_ref[:, tap * width : (tap + 1) * width] = weight_of(weight_refs[tap])

            def body(turn):
                at = pl.ds(pl.multiple_of((first + turn * rows) * line, line), rows * line)
                for start in range(0, channels, wide):
                    product = lax.dot_general(
                        padded_ref[at, :depth],
                        weight_ref[start : start + wide, :depth],
                        (((1,), (1,)), ((), ())),
                        preferred_element_type=F32,
                    )
                    if fresh:
                        total_ref[at, start : start + wide] = product
                    else:
                        total_ref[at, start : start + wide] += product

            repeat(turns, body)


def row_plan(taps, columns):
    rows = []
    for tap, column in zip(taps, columns):
        if not rows or rows[-1][0] != tap[2]:
            rows.append((tap[2], []))
        rows[-1][1].append((tap[3], column))
    return rows


def row_weights(weights, channels, order, first_tap, side=0, sides=1):
    pieces, _, width = weights.shape
    rows = channels // pieces
    specs = []
    for column in range(3):

        def index(step, column=column):
            row = order[-1]
            for place, listed in enumerate(order[:-1]):
                row = jnp.where(step == place, listed, row)
            tap = first_tap + 3 * row + column
            return (0, tap * sides + side, 0) if pieces == 1 else (side, tap, 0)

        block = (1, rows // sides, width) if pieces == 1 else (pieces // sides, rows, width)
        specs.append(pl.BlockSpec(block, index))
    return specs


def grad_moments(grad, unit):
    return jnp.concatenate(
        [jnp.sum(grad, axis=0, keepdims=True), jnp.sum(grad * unit, axis=0, keepdims=True)]
    )


def feature_body(
    plan, tiles, up_ref, third_ref, source_ref, coef_ref, pooled_ref, valid_ref, *refs
):
    weight_refs = refs[:4]
    result_ref, sums_ref, padded_ref, weight_ref, total_ref = refs[4:]
    step_now = pl.program_id(0)
    back_step(plan, tiles, up_ref, weight_refs, padded_ref, weight_ref, total_ref)
    begun = len(plan)

    @pl.when(step_now >= begun)
    def _():
        height = third_ref.shape[0]
        row = pl.multiple_of((step_now - begun) * height, height)
        unit, pre = unit_of(third_ref[...], coef_ref[...])
        pre = pre + source_ref[...].astype(F32)
        grad = total_ref[pl.ds(row, height)] + pooled_ref[...]
        grad = grad * valid_ref[...] * silu_slope(pre)
        result_ref[...] = grad.astype(BF16)
        moments = grad_moments(grad, unit)

        @pl.when(step_now == begun)
        def _():
            sums_ref[...] = moments

        @pl.when(step_now > begun)
        def _():
            sums_ref[...] += moments


def feature_back(upstream, weights, plan, order, point, third, source, coef, pooled, valid, tiles, side, sides, after, passed):
    pixels, channels = third.shape
    part = channels // sides
    pieces, _, width = weights.shape
    rows = channels // pieces
    begun = len(plan)
    turns = tiles[0]
    height = pixels // turns

    def row_of(step):
        return jnp.clip(step - begun, 0, turns - 1)

    row_block = pl.BlockSpec((height, part), lambda step: (row_of(step), side))
    if pieces == 1:
        point_block = pl.BlockSpec((1, rows // sides, width), lambda step: (0, point * sides + side, 0))
    else:
        point_block = pl.BlockSpec((pieces // sides, rows, width), lambda step: (side, point, 0))
    return call(
        functools.partial(feature_body, plan, tiles),
        [upstream, third, source, coef, pooled, valid] + [weights] * 4,
        [
            whole(upstream),
            row_block,
            row_block,
            pl.BlockSpec((coef.shape[0], part), lambda step: (0, side)),
            pl.BlockSpec((1, part), lambda step: (0, side)),
            pl.BlockSpec((height, 1), lambda step: (row_of(step), 0)),
        ]
        + row_weights(weights, channels, order, 0, side, sides)
        + [point_block],
        (begun + turns,),
        [shaped((pixels, part), BF16), shaped((2, part))],
        [pl.BlockSpec((height, part), lambda step: (row_of(step), 0)), held((2, part))],
        [
            pltpu.VMEM((pixels, 4 * width), BF16),
            pltpu.VMEM((part, 4 * width), BF16),
            pltpu.VMEM((pixels, part), F32),
        ],
        after=after,
        passed=passed,
    )


def spatial_back_body(plan, tiles, up_ref, first_ref, coef_ref, valid_ref, *refs):
    weight_refs = refs[:3]
    result_ref, sums_ref, padded_ref, weight_ref = refs[3:]
    back_step(plan, tiles, up_ref, weight_refs, padded_ref, weight_ref, result_ref)

    @pl.when(pl.program_id(0) == len(plan) - 1)
    def _():
        height = result_ref.shape[0] // tiles[0]
        sums_ref[...] = jnp.zeros_like(sums_ref)

        def body(row):
            at = pl.ds(pl.multiple_of(row * height, height), height)
            unit, pre = unit_of(first_ref[at], coef_ref[...])
            grad = result_ref[at] * valid_ref[at] * silu_slope(pre)
            result_ref[at] = grad
            sums_ref[...] += grad_moments(grad, unit)

        repeat(tiles[0], body)


def spatial_back(upstream, first, coef, valid, weights, plan, order, tiles, first_tap, after, passed):
    pixels, channels = first.shape
    columns = weights.shape[2]
    return call(
        functools.partial(spatial_back_body, plan, tiles),
        [upstream, first, coef, valid] + [weights] * 3,
        [whole(upstream), whole(first), whole(coef), whole(valid)]
        + row_weights(weights, channels, order, first_tap),
        (len(plan),),
        [shaped(first.shape), shaped((2, channels))],
        [held(first.shape), held((2, channels))],
        [pltpu.VMEM((pixels, 3 * columns), BF16), pltpu.VMEM((channels, 3 * columns), BF16)],
        after=after,
        passed=passed,
    )


def weight_body(plan, tiles, extra, count, meta_ref, flipped_ref, up_ref, *refs):
    extra_ref = refs[0] if extra else None
    result_refs = refs[extra : extra + count]
    padded_ref, full_ref = refs[extra + count :]
    block_rows, width = result_refs[0].shape[1:]
    taps_held = padded_ref.shape[1] // width
    rows = block_rows // taps_held
    channels = flipped_ref.shape[0]
    chunk = min(512, channels)
    step_now = pl.program_id(0)
    line = tiles[1] * tiles[2]
    kinds = {}
    for place, row_taps in enumerate(plan):
        low_i, high_i = span(row_taps[0], tiles[0])
        low, high = (low_i + row_taps[0]) * line, (high_i + row_taps[0]) * line
        first, last = low // 128 * 128, -(-high // 128) * 128
        depth = max(
            -(-(high_k + shift_k) * line // 128) * 128 - (low_k + shift_k) * line // 128 * 128
            for shift_k in {row_taps[0], -row_taps[0]}
            for low_k, high_k in [span(shift_k, tiles[0])]
        )
        first = min(first, padded_ref.shape[0] - depth)
        last = first + depth
        kinds.setdefault(depth, []).append((place, first, len(row_taps[1])))

        @pl.when(step_now == place)
        def _(row_taps=row_taps, first=first, last=last):
            shifted_columns(tiles, row_taps, up_ref, padded_ref, width, first, last)

    for depth, steps in kinds.items():
        here = functools.reduce(jnp.logical_or, [step_now == place for place, _, _ in steps])
        first = functools.reduce(
            lambda value, step: jnp.where(step_now == step[0], step[1], value), steps, 0
        )
        taps = functools.reduce(
            lambda value, step: jnp.where(step_now == step[0], step[2], value), steps, 0
        )

        @pl.when(here)
        def _(depth=depth, first=first, taps=taps):
            span_at = pl.ds(pl.multiple_of(first, 128), depth)

            def body(turn):
                columns = pl.ds(pl.multiple_of(turn * width, width), width)

                def part(piece):
                    at = pl.ds(pl.multiple_of(piece * chunk, chunk), chunk)
                    full_ref[at, columns] = jnp.dot(
                        flipped_ref[at, span_at], padded_ref[span_at, columns], preferred_element_type=F32
                    ).astype(BF16)

                repeat(channels // chunk, part)

            repeat(taps, body)

    for tap in range(taps_held):
        spread(meta_ref, full_ref, result_refs, tap * width, tap * rows, rows)

    if extra:

        @pl.when(step_now == len(plan) - 1)
        def _():
            core = meta_ref[0]
            taps = len(plan[-1][1])
            spare = (taps_held - taps - 1) * rows
            for owner in range(result_refs[0].shape[0]):
                slot = meta_ref[1 + owner]
                for ref, side in zip(result_refs, (core, 1 - core)):
                    start = pl.multiple_of((owner * 2 + side) * rows, rows)
                    ref[slot, taps * rows : (taps + 1) * rows] = extra_ref[pl.ds(start, rows)]
                    ref[slot, (taps + 1) * rows :] = jnp.zeros((spare, width), BF16)


def weight_grad(place, flipped, upstream, meta, plan, tiles, width, after=(), extra=None, passed=()):
    channels, padded = flipped.shape
    taps = max(len(row_taps[1]) for row_taps in plan)
    steps = len(plan)
    shapes = slotted(place, channels // place.size * taps * steps, width)
    blocks = [
        pl.BlockSpec((shape.shape[0], shape.shape[1] // steps, width), lambda step, _: (0, step, 0))
        for shape in shapes
    ]
    more = [] if extra is None else [extra]
    return call(
        functools.partial(weight_body, plan, tiles, len(more), len(shapes)),
        [flipped, upstream] + more,
        [whole(array) for array in [flipped, upstream] + more],
        (steps,),
        shapes,
        blocks,
        [pltpu.VMEM((padded, taps * width), BF16), pltpu.VMEM((channels, taps * width), BF16)],
        meta,
        after,
        passed,
    )


def tile_matrix(breadth):
    count = TILE * breadth
    matrix = np.zeros((count, count), np.float32)
    for row in range(TILE):
        for column in range(breadth):
            at = (column // TILE * TILE + row) * TILE + column % TILE
            matrix[at, row * breadth + column] = 1.0
    return matrix


def tile_body(matrix_ref, natural_ref, result_ref):
    result_ref[...] = jnp.dot(
        matrix_ref[...], natural_ref[...], preferred_element_type=F32
    ).astype(BF16)


def tile_rows(natural, matrix):
    rows = matrix.shape[0]
    return call(
        tile_body,
        [matrix, natural],
        [whole(matrix), rows_of(natural, rows)],
        (natural.shape[0] // rows,),
        [shaped(natural.shape, BF16)],
        [rows_of(natural, rows)],
    )[0]


def flip_body(source_ref, result_ref):
    pixels = source_ref.shape[0]
    result_ref[:, :pixels] = source_ref[...].T
    if result_ref.shape[1] > pixels:
        extra = result_ref.shape[1] - pixels
        result_ref[:, pixels:] = jnp.zeros((result_ref.shape[0], extra), BF16)


def flipped(values, after=()):
    pixels, channels = values.shape
    padded = pixels + -pixels % 128
    return call(
        flip_body,
        [values],
        [pl.BlockSpec((pixels, 128), lambda step: (0, step))],
        (channels // 128,),
        [shaped((channels, padded), BF16)],
        [pl.BlockSpec((128, padded), lambda step: (step, 0))],
        after=after,
    )[0]


def add_sums(sums_ref, sums):
    @pl.when(pl.program_id(0) == 0)
    def _():
        sums_ref[...] = sums

    @pl.when(pl.program_id(0) > 0)
    def _():
        sums_ref[...] += sums


def first_body(source_ref, valid_ref, weight_ref, result_ref, sums_ref):
    product = jnp.dot(source_ref[...], weight_of(weight_ref), preferred_element_type=F32)
    result_ref[...] = product
    add_sums(sums_ref, masked_sums(product, valid_ref[...]))


def fixed_block(weights, channels, at):
    pieces, _, columns = weights.shape
    return pl.BlockSpec((pieces, channels // pieces, columns), lambda step, *_: (0, at, 0))


def first_conv(source, valid, weights, turns, after):
    pixels, channels = source.shape
    rows = pixels // turns
    width = weights.shape[2]
    return call(
        first_body,
        [source, valid, weights],
        [rows_of(source, rows), rows_of(valid, rows), fixed_block(weights, channels, 0)],
        (turns,),
        [shaped((pixels, width)), shaped((2, width))],
        [pl.BlockSpec((rows, width), lambda step: (step, 0)), held((2, width))],
        after=after,
    )


def third_body(count, second_ref, coef_ref, valid_ref, *refs):
    weight_refs = refs[:count]
    middle_ref, result_ref, sums_ref = refs[count:]
    _, pre = unit_of(second_ref[...], coef_ref[...])
    middle = silu(pre).astype(BF16)
    middle_ref[...] = middle
    valid = valid_ref[...]
    sums = []
    for quarter, ref in enumerate(weight_refs):
        product = jnp.dot(middle, weight_of(ref), preferred_element_type=F32)
        width = product.shape[1]
        result_ref[:, quarter * width : (quarter + 1) * width] = product
        sums.append(masked_sums(product, valid))
    add_sums(sums_ref, jnp.concatenate(sums, axis=1))


def third_conv(second, coef, valid, weights, first, count, turns):
    pixels, narrow = second.shape
    height = pixels // turns
    channels = count * weights.shape[2]
    return call(
        functools.partial(third_body, count),
        [second, coef, valid] + [weights] * count,
        [rows_of(second, height), whole(coef), rows_of(valid, height)]
        + [fixed_block(weights, narrow, first + quarter) for quarter in range(count)],
        (turns,),
        [shaped((pixels, narrow), BF16), shaped((pixels, channels)), shaped((2, channels))],
        [
            pl.BlockSpec((height, narrow), lambda step: (step, 0)),
            pl.BlockSpec((height, channels), lambda step: (step, 0)),
            held((2, channels)),
        ],
    )


def output_body(third_ref, source_ref, coef_ref, valid_ref, result_ref, sums_ref):
    _, pre = unit_of(third_ref[...], coef_ref[...])
    values = (valid_ref[...] * silu(pre + source_ref[...].astype(F32))).astype(BF16)
    result_ref[...] = values
    add_sums(sums_ref, jnp.sum(values.astype(F32), axis=0, keepdims=True))


def block_output(third, source, coef, valid, turns):
    pixels, channels = third.shape
    rows = pixels // turns
    return call(
        output_body,
        [third, source, coef, valid],
        [rows_of(third, rows), rows_of(source, rows), whole(coef), rows_of(valid, rows)],
        (turns,),
        [shaped(third.shape, BF16), shaped((1, channels))],
        [rows_of(third, rows), held((1, channels))],
    )


def third_back_body(
    count, outs, meta_ref, low_ref, high_ref, third_ref, coef_ref, totals_ref, valid_ref, middle_ref, *refs
):
    weight_refs = refs[:count]
    result_ref = refs[count]
    slot_refs = refs[count + 1 : count + 1 + outs]
    grad_ref, total_ref = refs[count + 1 + outs :]
    step_now = pl.program_id(0)

    @pl.when(step_now == 0)
    def _():
        total_ref[...] = jnp.zeros_like(total_ref)

    part = low_ref.shape[1]
    coef, totals, valid = coef_ref[...], totals_ref[...], valid_ref[...]
    for start, part_ref in ((0, low_ref), (part, high_ref)):
        at = slice(start, start + part)
        unit = (third_ref[:, at] - coef[0:1, at]) * coef[1:2, at]
        centered = part_ref[...].astype(F32) - valid * (totals[0:1, at] + unit * totals[1:2, at])
        grad_ref[:, at] = (coef[2:3, at] * coef[1:2, at] * centered).astype(BF16)
    width = weight_refs[0].shape[2]
    result = None
    for quarter, ref in enumerate(weight_refs):
        grad = grad_ref[:, quarter * width : (quarter + 1) * width]
        product = lax.dot_general(
            grad, weight_of(ref), (((1,), (1,)), ((), ())), preferred_element_type=F32
        )
        result = product if result is None else result + product
    result_ref[...] = result
    total_ref[...] += lax.dot_general(
        middle_ref[...], grad_ref[...], (((0,), (0,)), ((), ())), preferred_element_type=F32
    )

    @pl.when(step_now == pl.num_programs(0) - 1)
    def _():
        rows = slot_refs[0].shape[1] // count
        for quarter in range(count):
            spread(meta_ref, total_ref, slot_refs, quarter * width, quarter * rows, rows)


def third_back(place, low, high, third, coef, totals, valid, middle, weights, meta, first, count, turns, after, passed):
    pixels, channels = third.shape
    narrow = middle.shape[1]
    height = pixels // turns
    shapes = slotted(place, narrow // place.size * count, weights.shape[2])
    return call(
        functools.partial(third_back_body, count, len(shapes)),
        [low, high, third, coef, totals, valid, middle] + [weights] * count,
        [
            rows_of(low, height),
            rows_of(high, height),
            rows_of(third, height),
            whole(coef),
            whole(totals),
            rows_of(valid, height),
            rows_of(middle, height),
        ]
        + [fixed_block(weights, narrow, first + quarter) for quarter in range(count)],
        (turns,),
        [shaped((pixels, narrow))] + shapes,
        [pl.BlockSpec((height, narrow), lambda step, _: (step, 0))] + [held(shape.shape) for shape in shapes],
        [pltpu.VMEM((height, channels), BF16), pltpu.VMEM((narrow, channels), F32)],
        meta,
        after,
        passed,
    )


def input_body(matrix_ref, low_ref, high_ref, grad_ref, weight_ref, result_ref):
    rows = matrix_ref.shape[0]
    part = low_ref.shape[1]
    matrix = matrix_ref[...]
    moved = []
    for start in range(0, result_ref.shape[0], rows):
        at = slice(start, start + rows)
        moved.append(jnp.dot(matrix, grad_ref[at], preferred_element_type=F32).astype(BF16))
        for column, part_ref in ((0, low_ref), (part, high_ref)):
            result_ref[at, column : column + part] = jnp.dot(
                matrix, part_ref[at], preferred_element_type=F32
            )
    result_ref[...] += lax.dot_general(
        jnp.concatenate(moved), weight_of(weight_ref), (((1,), (1,)), ((), ())), preferred_element_type=F32
    )


def input_back(matrix, low, high, grad, weights, turns, first, count, after, passed, into):
    pixels, part = low.shape
    rows = pixels // turns
    channels = 2 * part
    width = grad.shape[1]

    def block(columns):
        return pl.BlockSpec((rows, columns), lambda step: (first + step, 0))

    return call(
        input_body,
        [matrix, low, high, grad, weights],
        [whole(matrix), block(part), block(part), block(width), fixed_block(weights, channels, 0)],
        (count,),
        [shaped((pixels, channels))],
        [block(channels)],
        after=after,
        passed=passed,
        into=into,
        flops=10**10,
    )


def sigmoid(values):
    return 0.5 + 0.5 * jnp.tanh(0.5 * values)


def silu(values):
    return values * sigmoid(values)


def silu_slope(values):
    sigmoid_val = sigmoid(values)
    return sigmoid_val * (1.0 + values * (1.0 - sigmoid_val))


def sums(values, validity):
    weighted = values * validity
    return jnp.stack([jnp.sum(weighted, axis=0), jnp.sum(weighted * values, axis=0)])


def coefs(totals, counted, gain, shift):
    mean_value = totals[0] / counted
    scaling = lax.rsqrt(totals[1] / counted - mean_value * mean_value + EPSILON)
    return jnp.stack([mean_value, scaling, gain, shift])


def through_norm(grad_pre, unit, coef, counted, validity, totals):
    centered = grad_pre - validity * (totals[0] + unit * totals[1]) / counted
    return coef[2] * coef[1] * centered


def to_tiles(array):
    height, breadth = array.shape[:2]
    rest = array.shape[2:]
    cut = array.reshape((height // TILE, TILE, breadth // TILE, TILE) + rest)
    return jnp.swapaxes(cut, 1, 2).reshape((height * breadth,) + rest)


def per_device(
    features,
    reduce_weight,
    spatial_weight,
    expand_weight,
    bottle_gain,
    bottle_shift,
    point_weight,
    near_weight,
    middle_weight,
    far_weight,
    image_weight,
    project_weight,
    class_weight,
    pyramid_gain,
    pyramid_shift,
    head_gain,
    head_shift,
    crop_masks,
    crop_tasks,
    pixel_labels,
    task_norms,
):
    place = Place()
    size, core = place.size, place.core
    first_core = core == 0
    height, breadth, channels = features.shape[2:]
    pixels = height * breadth
    tiles = (height // TILE, breadth // TILE, TILE * TILE)
    narrow = reduce_weight.shape[1]
    branch = point_weight.shape[1]
    four_wide = 4 * branch
    rows = channels // size
    narrow_rows = narrow // size
    quarters = channels // narrow
    turns = 3
    meta = place.meta()
    matrix = tile_matrix(breadth)

    bottle_taps = tap_list(height, breadth, BOTTLE_RATE)
    near_taps = tap_list(height, breadth, NEAR_RATE)
    middle_taps = tap_list(height, breadth, MIDDLE_RATE)
    far_taps = tap_list(height, breadth, FAR_RATE)
    point_taps = [(1, 1, 0, 0)]

    def center_of(taps):
        return [tap[:2] for tap in taps].index((1, 1))

    def stacked(weight, taps):
        flat = weight.reshape((-1,) + weight.shape[2:])
        picked = [3 * tap[0] + tap[1] for tap in taps]
        if picked == list(range(picked[0], picked[-1] + 1)):
            flat = flat[picked[0] : picked[-1] + 1]
        else:
            flat = jnp.stack([flat[at] for at in picked])
        return flat.reshape(-1, flat.shape[2]), len(taps)

    mask = lax.dynamic_index_in_dim(crop_masks, core, 0, keepdims=False)[0]
    labels = lax.dynamic_index_in_dim(pixel_labels, core, 0, keepdims=False)[0]
    task = lax.dynamic_index_in_dim(crop_tasks, core, 0, keepdims=False)[0]
    validity = to_tiles(mask).astype(F32)[:, None]
    valid_tiles = validity.reshape(tiles + (1,))
    labels = to_tiles(labels)
    source = tile_rows(features.reshape(pixels, channels), jnp.array(matrix, BF16))
    source_flipped = flipped(source)

    wide_expand = expand_weight.reshape(-1, quarters, narrow)
    expand_parts = [(wide_expand[:, at], 1) for at in range(quarters)]
    bottle_all = place.gather([(reduce_weight, 1), stacked(spatial_weight, bottle_taps)] + expand_parts)
    spatial_at = channels // narrow
    expand_at = spatial_at + len(bottle_taps)
    pyramid_parts = [stacked(near_weight, near_taps), stacked(middle_weight, middle_taps)]
    pyramid_parts += [stacked(far_weight, far_taps), (point_weight, 1), (project_weight, 1)]
    pyramid_all = place.gather(pyramid_parts)
    middle_at = len(near_taps)
    far_at = middle_at + len(middle_taps)
    point_at = far_at + len(far_taps)
    project_at = (point_at + 1) * (channels // place.pieces)
    project_full = pyramid_all[:, project_at:].reshape(-1, branch)

    crop_valid_both = jnp.sum(crop_masks, axis=(1, 2, 3)).astype(F32)
    home_crop = (crop_tasks[:, 0] == 1).astype(F32)
    counts = jnp.concatenate(
        [
            crop_valid_both,
            jnp.sum(crop_valid_both * (1.0 - home_crop))[None],
            jnp.sum(crop_valid_both * home_crop)[None],
        ]
    )
    small = [bottle_gain, bottle_shift, pyramid_gain, pyramid_shift, head_gain, head_shift]
    small.append(class_weight.reshape(-1))
    small_widths = [part.shape[0] for part in small]
    small_own = jnp.concatenate(small).astype(F32)
    collected = place.everyone(jnp.concatenate([small_own, counts]))
    counts_all = jnp.sum(collected[:, small_own.size :], axis=0)
    small_all, start = [], 0
    for width in small_widths:
        small_all.append(collected[:, start : start + width].reshape(-1))
        start += width
    gain_bottle, shift_bottle, gain_pyramid, shift_pyramid, gain_head, shift_head = small_all[:6]
    class_full = small_all[6].reshape(size * class_weight.shape[0], -1).astype(BF16)
    counted = jnp.where(first_core, counts_all[0], counts_all[1])
    task_pixels = counts_all[2:4]
    crop_valid = jnp.where(first_core, crop_valid_both[0], crop_valid_both[1])

    first, first_sums = first_conv(source, validity, bottle_all, turns, [source_flipped])
    coef_one = coefs(place.total(first_sums), counted, gain_bottle[:narrow], shift_bottle[:narrow])
    first_tiles = first.reshape(tiles + (narrow,))
    conv_in, second, second_sums = spatial_conv(
        first_tiles, coef_one, valid_tiles, bottle_all, bottle_taps, spatial_at
    )
    second = second.reshape(pixels, narrow)
    coef_two = coefs(
        place.total(second_sums), counted, gain_bottle[narrow : 2 * narrow], shift_bottle[narrow : 2 * narrow]
    )
    middle_act, third, third_sums = third_conv(
        second, coef_two, validity, bottle_all, expand_at, quarters, turns
    )
    coef_three = coefs(
        place.total(third_sums), counted, gain_bottle[2 * narrow :], shift_bottle[2 * narrow :]
    )
    block_out, pooled_sum = block_output(third, source, coef_three, validity, tiles[0])
    block_tiles = block_out.reshape(tiles + (channels,))

    pooled = (pooled_sum / crop_valid).astype(BF16)
    pooled_all = place.everyone(pooled[0])
    pooled_rows = lax.dynamic_slice_in_dim(pooled_all, place.index * rows, rows, axis=1)
    image_all = place.total(jnp.dot(pooled_rows, image_weight, preferred_element_type=F32))
    branches, branch_sums = branch_convs(
        block_tiles,
        valid_tiles,
        pyramid_all,
        [
            (near_taps, branch),
            (middle_taps, 2 * branch),
            (far_taps, 3 * branch),
            (point_taps, 0),
        ],
        four_wide,
        [image_all],
    )
    branches = branches.reshape(pixels, four_wide)
    image_mean = jnp.sum(image_all, axis=0) / size
    image_scale = lax.rsqrt(
        jnp.sum(image_all * image_all, axis=0) / size - image_mean * image_mean + EPSILON
    )
    image_unit = (image_all - image_mean) * image_scale
    gain_image, shift_image = gain_pyramid[four_wide:], shift_pyramid[four_wide:]
    coef_image = jnp.stack([image_mean, image_scale, gain_image, shift_image])
    image_pre = gain_image * image_unit + shift_image
    image_act = silu(image_pre).astype(BF16)

    block_flipped = flipped(block_out, [branch_sums])
    conv_flipped = flipped(conv_in.reshape(pixels, narrow), [block_flipped])
    coef_branch = coefs(
        place.total(branch_sums), counted, gain_pyramid[:four_wide], shift_pyramid[:four_wide]
    )
    unit_branch, pre_branch = unit_of(branches, coef_branch)
    joined = silu(pre_branch).astype(BF16)

    own_act = lax.dynamic_slice_in_dim(image_act, place.index, 1, axis=0)
    crop_part = jnp.dot(own_act, project_full[four_wide:], preferred_element_type=F32)
    projected = jnp.dot(joined, project_full[:four_wide], preferred_element_type=F32) + crop_part
    coef_head = coefs(place.total(sums(projected, validity)), counted, gain_head, shift_head)
    unit_head, pre_head = unit_of(projected, coef_head)
    output_act = silu(pre_head).astype(BF16)
    logits = jnp.dot(output_act, class_full, preferred_element_type=F32)

    columns = jnp.arange(class_full.shape[1])
    allowed = (columns >= CITY_CLASSES) == (task == 1)
    masked = jnp.where(allowed, logits, FLOOR_LOGIT)
    raised = jnp.exp(masked - jnp.max(masked, axis=-1, keepdims=True))
    chances = raised / jnp.sum(raised, axis=-1, keepdims=True)
    target = jnp.where(task == 0, labels % CITY_CLASSES, CITY_CLASSES + labels % HOME_CLASSES)
    chosen = (columns == target[:, None]).astype(F32)
    inverse = 1.0 / task_norms.astype(F32)
    task_share = inverse / jnp.sum(inverse)
    crop_weight = jnp.where(
        task == 0, task_share[0] / task_pixels[0], task_share[1] / task_pixels[1]
    )
    logit_grad = (crop_weight * validity * (chances - chosen)).astype(BF16)
    class_grad = lax.dot_general(
        output_act, logit_grad, (((0,), (0,)), ((), ())), preferred_element_type=F32
    )

    output_grad = lax.dot_general(
        logit_grad, class_full, (((1,), (1,)), ((), ())), preferred_element_type=F32
    )
    grad_head = output_grad * silu_slope(pre_head)
    head_totals = place.total(grad_moments(grad_head, unit_head))
    proj_grad = through_norm(
        grad_head, unit_head, coef_head, counted, validity, head_totals
    ).astype(BF16)
    crop_grad = jnp.sum(proj_grad, axis=0, dtype=F32)
    joined_grad = lax.dot_general(
        proj_grad, project_full[:four_wide], (((1,), (1,)), ((), ())), preferred_element_type=F32
    )
    act_grad = jnp.dot(project_full[four_wide:].astype(F32), crop_grad, precision=HIGHEST)
    own_pre = lax.dynamic_slice_in_dim(image_pre, place.index, 1, axis=0)[0]
    image_pre_grad = act_grad * silu_slope(own_pre)
    grad_branch = joined_grad * silu_slope(pre_branch)
    branch_parts = place.everyone(
        jnp.concatenate([grad_moments(grad_branch, unit_branch).reshape(-1), image_pre_grad])
    )
    image_pre_all = branch_parts[:, 2 * four_wide :]
    branch_totals = jnp.sum(branch_parts[:, : 2 * four_wide], axis=0).reshape(2, four_wide)
    branch_grad = through_norm(
        grad_branch, unit_branch, coef_branch, counted, validity, branch_totals
    ).astype(BF16)
    image_totals = grad_moments(image_pre_all, image_unit)
    image_in_all = through_norm(
        image_pre_all, image_unit, coef_image, float(size), 1.0, image_totals
    )
    pooled_partial = lax.dot_general(
        image_in_all, image_weight.astype(F32), (((1,), (1,)), ((), ())), precision=HIGHEST
    )
    if place.direct:
        pooled_grad_all = lax.all_to_all(pooled_partial, "batch", 0, 0).reshape(1, channels)
    else:
        pooled_grad_all = lax.dynamic_slice_in_dim(
            lax.all_gather(pooled_partial, "batch", axis=1, tiled=True), place.index, 1, axis=0
        )
    image_partial = jnp.dot(pooled_rows.astype(F32).T, image_in_all, precision=HIGHEST)

    def columns_of(taps, block):
        return [block * branch] * len(taps)

    near_rows = row_plan(near_taps, columns_of(near_taps, 1))
    middle_rows = row_plan(middle_taps, columns_of(middle_taps, 2))
    far_row = row_plan(far_taps, columns_of(far_taps, 3))
    point_row = row_plan(point_taps, columns_of(point_taps, 0))
    project_grad = jnp.concatenate(
        [
            lax.dot_general(
                joined, proj_grad, (((0,), (0,)), ((), ())), preferred_element_type=F32
            ),
            own_act[0].astype(F32)[:, None] * crop_grad[None, :],
        ]
    )

    class_rows = class_grad.size // size // branch if place.direct else 0
    extra_rows = project_grad.shape[0] // size + class_rows

    def extra_halves():
        parts = [project_grad.reshape(size, 2, -1, branch), class_grad.reshape(size, 2, -1, branch)]
        spare = rows // 2 - extra_rows // 2
        parts.append(jnp.zeros((size, 2, spare, branch), F32))
        return jnp.concatenate(parts, axis=2).reshape(-1, branch).astype(BF16)

    def branch_weight_grad(plan, after, extra=None):
        return weight_grad(
            place, block_flipped, branch_grad, meta, plan, tiles, branch, after, extra
        )

    parts = 2 if place.direct else 1
    wide_grads = branch_weight_grad(
        middle_rows + far_row + point_row, [conv_flipped], extra_halves() if place.direct else None
    )
    wide_rows = [rows] * (len(middle_taps) + len(far_taps) + 1) + [extra_rows]
    if not place.direct:
        wide_grads = [jnp.concatenate([wide_grads[0], project_grad.astype(BF16)[None]], axis=1)]
        wide_rows = wide_rows[:-1] + [rows, rows] + wide_rows[-1:]
    wide_scatter = Scatter(place, wide_grads, wide_rows)
    near_grads = branch_weight_grad(near_rows, [wide_grads[0]])
    near_scatter = Scatter(place, near_grads, [rows] * len(near_taps))
    wide_scatter.first()

    pooled_grad = pooled_grad_all / crop_valid
    back_plan = [(far_row[0][0], far_row[0][1] + point_row[0][1])] + near_rows + middle_rows
    far_at = len(near_rows) + len(middle_rows)
    back_order = [far_at] + list(range(far_at))

    def half_back(side, after, scatters):
        low, moments, *passed = feature_back(
            branch_grad,
            pyramid_all,
            back_plan,
            back_order,
            3 * far_at + len(far_taps),
            third,
            source,
            coef_three,
            pooled_grad,
            validity,
            tiles,
            side,
            2,
            after,
            passing(scatters),
        )
        take_back(scatters, passed)
        return low, moments

    def sending(*scatters):
        return [array for scatter in scatters for array in scatter.sent]

    def passing(scatters):
        return [array for scatter in scatters for array in scatter.kept]

    def take_back(scatters, passed):
        for scatter in scatters:
            count = len(scatter.kept)
            scatter.kept, passed = passed[:count], passed[count:]

    low_grad, low_moments = half_back(0, [near_grads[0]] + sending(wide_scatter), [wide_scatter])
    high_grad, high_moments = half_back(1, [low_moments], [wide_scatter, near_scatter])
    wide_scatter.second()
    near_scatter.first()
    three_parts = place.total(low_moments, high_moments)
    three_totals = jnp.concatenate(three_parts, axis=1)

    middle_grad, *expand_grads = third_back(
        place,
        low_grad,
        high_grad,
        third,
        coef_three,
        three_totals / counted,
        validity,
        middle_act,
        bottle_all,
        meta,
        expand_at,
        quarters,
        turns,
        sending(near_scatter, wide_scatter),
        passing([near_scatter, wide_scatter]),
    )
    take_back([near_scatter, wide_scatter], expand_grads[parts:])
    expand_grads = expand_grads[:parts]
    wide_scatter.third()
    wide_scatter.launch()
    near_scatter.second()
    unit_two, pre_two = unit_of(second, coef_two)
    grad_two = middle_grad * silu_slope(pre_two)
    two_totals = place.total(grad_moments(grad_two, unit_two))
    second_grad = through_norm(
        grad_two, unit_two, coef_two, counted, validity, two_totals
    ).astype(BF16)
    spatial_rows = row_plan(bottle_taps, [0] * len(bottle_taps))
    spatial_grads = weight_grad(
        place,
        conv_flipped,
        second_grad,
        meta,
        spatial_rows,
        tiles,
        narrow,
        sending(wide_scatter, near_scatter),
        None,
        passing([wide_scatter, near_scatter]),
    )
    take_back([wide_scatter, near_scatter], spatial_grads[parts:])
    bottle_grads = [
        jnp.concatenate(pair, axis=1) for pair in zip(spatial_grads[:parts], expand_grads)
    ]
    bottle_rows = [narrow_rows] * (len(bottle_taps) + quarters)
    bottle_scatter = Scatter(place, bottle_grads, bottle_rows)
    near_scatter.third()
    grad_one, one_moments, *passed = spatial_back(
        second_grad,
        first,
        coef_one,
        validity,
        bottle_all,
        [spatial_rows[1], spatial_rows[0], spatial_rows[2]],
        [1, 0, 2],
        tiles,
        spatial_at,
        [spatial_grads[0]],
        passing([wide_scatter, near_scatter, bottle_scatter]) + near_scatter.sent,
    )
    held_back = len(passed) - len(near_scatter.sent)
    take_back([wide_scatter, near_scatter, bottle_scatter], passed[:held_back])
    near_scatter.sent = passed[held_back:]
    near_scatter.launch()
    if place.direct:
        one_moments = tied(one_moments, [bottle_scatter.arrived] + wide_scatter.arrived)
    bottle_scatter.first()
    one_totals = place.total(one_moments)
    unit_one, _ = unit_of(first, coef_one)
    first_grad = through_norm(
        grad_one, unit_one, coef_one, counted, validity, one_totals
    ).astype(BF16)
    reduce_grads = weight_grad(
        place,
        source_flipped,
        first_grad,
        meta,
        row_plan(point_taps, [0]),
        tiles,
        narrow,
        sending(bottle_scatter),
        None,
        passing([bottle_scatter, near_scatter]),
    )
    take_back([bottle_scatter, near_scatter], reduce_grads[parts:])
    reduce_scatter = Scatter(place, reduce_grads[:parts], [rows])
    bottle_scatter.second()

    def rows_back(first_turn, count, into, after, scatters):
        result, *passed = input_back(
            jnp.array(matrix.T, BF16),
            low_grad,
            high_grad,
            first_grad,
            bottle_all,
            turns,
            first_turn,
            count,
            after,
            passing(scatters),
            into,
        )
        take_back(scatters, passed)
        return result

    input_grad = rows_back(0, 2, None, sending(bottle_scatter), [bottle_scatter, reduce_scatter])
    reduce_scatter.first()
    bottle_scatter.third()
    bottle_scatter.launch()
    input_grad = rows_back(2, turns - 2, input_grad, sending(bottle_scatter, reduce_scatter), [bottle_scatter, reduce_scatter])
    reduce_scatter.second()
    reduce_scatter.third()
    reduce_scatter.launch()

    vectors = [one_totals, two_totals, three_totals, branch_totals, image_totals, head_totals]
    vectors += [image_partial]
    packed = jnp.concatenate([vector.reshape(-1) for vector in vectors])
    packed = packed + place.swap(packed)
    split, start = [], 0
    for vector in vectors:
        split.append(packed[start : start + vector.size].reshape(vector.shape))
        start += vector.size

    def own_part(vectors):
        vector = jnp.concatenate(vectors)
        length = vector.shape[0] // size
        return lax.dynamic_slice_in_dim(vector, place.index * length, length, axis=0)

    bottle_gain_grad = own_part([split[0][1], split[1][1], split[2][1]])
    bottle_shift_grad = own_part([split[0][0], split[1][0], split[2][0]])
    pyramid_gain_grad = own_part([split[3][1], split[4][1]])
    pyramid_shift_grad = own_part([split[3][0], split[4][0]])
    head_norm_grad = jnp.stack([own_part([split[5][1]]), own_part([split[5][0]])])
    image_out = split[6]

    def taps_out(full, taps, weight):
        full = full.reshape((len(taps),) + weight.shape[2:])
        if len(taps) == weight.shape[0] * weight.shape[1]:
            return full.reshape(weight.shape)
        result = jnp.zeros(weight.shape, F32)
        for at, tap in enumerate(taps):
            result = result.at[tap[0], tap[1]].set(full[at])
        return result

    for scatter in (near_scatter, wide_scatter, bottle_scatter, reduce_scatter):
        scatter.finish()
    near_count, middle_count, far_count = len(near_taps), len(middle_taps), len(far_taps)
    bottle_count = len(bottle_taps)
    expand_out = bottle_scatter.piece(bottle_count, quarters).reshape(quarters, narrow_rows, narrow)
    if place.direct:
        project_out, class_out = wide_scatter.extra([extra_rows - class_rows, class_rows])
    else:
        project_out = wide_scatter.piece(len(wide_rows) - 1, 1)
        class_out = own_part([lax.psum(class_grad, ("batch", "section"))])
    return (
        input_grad.reshape(features.shape),
        reduce_scatter.piece(0, 1),
        taps_out(bottle_scatter.piece(0, bottle_count), bottle_taps, spatial_weight),
        jnp.swapaxes(expand_out, 0, 1).reshape(expand_weight.shape),
        bottle_gain_grad,
        bottle_shift_grad,
        wide_scatter.piece(middle_count + far_count, 1),
        taps_out(near_scatter.piece(0, near_count), near_taps, near_weight),
        taps_out(wide_scatter.piece(0, middle_count), middle_taps, middle_weight),
        taps_out(wide_scatter.piece(middle_count, far_count), far_taps, far_weight),
        image_out,
        project_out,
        class_out.reshape(class_weight.shape),
        pyramid_gain_grad,
        pyramid_shift_grad,
        head_norm_grad,
    )


def solution(mesh):
    in_specs = (
        P("section", "batch", None, None, None),
        P("batch", None),
        P(None, None, "batch", None),
        P("batch", None),
        P("batch"),
        P("batch"),
        P("batch", None),
        P(None, None, "batch", None),
        P(None, None, "batch", None),
        P(None, None, "batch", None),
        P("batch", None),
        P("batch", None),
        P("batch", None),
        P("batch"),
        P("batch"),
        P("batch"),
        P("batch"),
        P(None, "batch", None, None),
        P(None, "batch"),
        P(None, "batch", None, None),
        P(),
    )
    out_specs = (
        P("section", "batch", None, None, None),
        P("batch", None),
        P(None, None, "batch", None),
        P("batch", None),
        P("batch"),
        P("batch"),
        P("batch", None),
        P(None, None, "batch", None),
        P(None, None, "batch", None),
        P(None, None, "batch", None),
        P("batch", None),
        P("batch", None),
        P("batch", None),
        P("batch"),
        P("batch"),
        P(None, "batch"),
    )
    return jax.shard_map(
        per_device, mesh=mesh, in_specs=in_specs, out_specs=out_specs, check_vma=False
    )
```

```python
import functools

import jax
import jax.numpy as jnp
import numpy as np
from jax import lax
from jax.experimental import pallas as pl
from jax.experimental.pallas import tpu as pltpu
from jax.sharding import PartitionSpec as P

CITY_CLASSES = 19
HOME_CLASSES = 13
BOTTLE_RATE = 4
NEAR_RATE = 12
MIDDLE_RATE = 24
FAR_RATE = 36
TILE = 4

EPSILON = 1e-05
FLOOR_LOGIT = -1e30
HIGHEST = lax.Precision.HIGHEST
F32 = jnp.float32
BF16 = jnp.bfloat16
SLOT_BITS = [0, 4, 2, 6, 1, 5, 3, 7, 8, 12, 9, 13, 10, 14, 11, 15]
PLANE_BITS = [line ^ plane for plane in range(4) for line in (0, 4, 8, 12)]
VMEM_BYTES = 58 * 1024 * 1024


class Place:
    def __init__(self):
        self.size = lax.axis_size("batch")
        self.direct = self.size == len(SLOT_BITS)
        self.pieces = 2 * self.size if self.direct else 1
        self.core = lax.axis_index("section")
        self.index = lax.axis_index("batch")

    def meta(self, bits=SLOT_BITS):
        core = self.core[None].astype(jnp.int32)
        if not self.direct:
            return core
        table = [[bits.index(at ^ owner) for owner in range(self.size)] for at in range(self.size)]
        row = lax.dynamic_index_in_dim(jnp.array(table, jnp.int32), self.index, 0, keepdims=False)
        return jnp.concatenate([core, row])

    def flip(self, block, bits):
        return lax.ppermute(block, "batch", [(source, source ^ bits) for source in range(self.size)])

    def swap(self, block):
        return lax.ppermute(block, "section", [(0, 1), (1, 0)])

    def total(self, *arrays):
        if not self.direct:
            return lax.psum(arrays, "batch") if len(arrays) > 1 else lax.psum(arrays[0], "batch")
        summed = jnp.sum(self.everyone(jnp.concatenate([array.reshape(-1) for array in arrays])), axis=0)
        results, start = [], 0
        for array in arrays:
            results.append(summed[start : start + array.size].reshape(array.shape))
            start += array.size
        return results if len(arrays) > 1 else results[0]

    def everyone(self, vector):
        if not self.direct:
            return lax.all_gather(vector, "batch")
        sent = jnp.broadcast_to(vector, (self.size,) + vector.shape)
        return lax.all_to_all(sent, "batch", 0, 0)

    def along_line(self, part, count):
        cut = part.reshape(count, -1, part.shape[1])
        if not self.direct:
            return lax.all_gather(cut, "batch", axis=1, tiled=True).reshape(1, -1, part.shape[1])
        half = cut.shape[1] // 2
        block = lax.dynamic_slice_in_dim(cut, self.core * half, half, axis=1)
        block = block.reshape(-1, part.shape[1])
        return jnp.stack([block] + [self.flip(block, bits) for bits in (4, 8, 12)])

    def across_plane(self, line):
        if not self.direct:
            return line
        return jnp.concatenate([line] + [self.flip(line, bits) for bits in (1, 2, 3)])

    def gather(self, parts):
        blocks = []
        for part, count in parts:
            cut = part.reshape(count, -1, part.shape[1])
            if self.direct:
                half = cut.shape[1] // 2
                cut = lax.dynamic_slice_in_dim(cut, self.core * half, half, axis=1)
            else:
                cut = lax.all_gather(cut, "batch", axis=1, tiled=True)
            blocks.append(cut.reshape(-1, part.shape[1]))
        block = jnp.concatenate(blocks)
        if self.direct:
            return lax.all_gather(block, ("batch", "section"))
        return block[None]


class Scatter:
    def __init__(self, place, grads, rows):
        self.place, self.rows = place, rows
        self.kept, self.sent = [grads[0]], []
        self.arrived = place.swap(grads[1]) if place.direct else None

    def add(self, kept, arrived):
        return (kept.astype(F32) + arrived.astype(F32)).astype(BF16)

    def first(self):
        if not self.place.direct:
            return
        own, arrived = self.kept[0], self.arrived
        self.kept = []
        sent = []
        for start in (0, 8):
            self.kept.append(self.add(own[start : start + 4], arrived[start : start + 4]))
            sent.append(self.add(own[start + 4 : start + 8], arrived[start + 4 : start + 8]))
        self.sent = sent
        self.arrived = [self.place.flip(sent[0], 1), self.place.flip(sent[1], 2)]

    def second(self):
        if not self.place.direct:
            return
        kept, sent = [], []
        for held, came in zip(self.kept, self.arrived):
            kept.append(self.add(held[:2], came[:2]))
            sent.append(self.add(held[2:], came[2:]))
        self.kept, self.sent = kept, sent
        self.arrived = [self.place.flip(sent[0], 2), self.place.flip(sent[1], 1)]

    def third(self):
        if not self.place.direct:
            return
        near = self.kept[0].astype(F32) + self.arrived[0].astype(F32)
        away = self.kept[1].astype(F32) + self.arrived[1].astype(F32)
        self.kept = [near[0]]
        sent = [near[1].astype(BF16), away[0].astype(BF16), away[1].astype(BF16)]
        self.sent = sent

    def launch(self):
        if self.place.direct:
            self.arrived = [
                self.place.flip(piece, bits) for piece, bits in zip(self.sent, (4, 8, 12))
            ]

    def finish(self):
        if self.place.direct:
            parts = [piece.astype(F32) for piece in self.arrived]
            result = (self.kept[0] + parts[0]) + (parts[1] + parts[2])
            opposite = self.place.swap(result)
            first = self.place.core == 0
            self.result = [jnp.where(first, result, opposite), jnp.where(first, opposite, result)]
            return self
        pieces, start = [], 0
        for rows in self.rows:
            cut = self.kept[0][0, start : start + rows * self.place.size].astype(F32)
            cut = lax.psum_scatter(cut, "batch", scatter_dimension=0, tiled=True)
            pieces.append(lax.psum(cut, "section"))
            start += rows * self.place.size
        self.result = [jnp.concatenate(pieces)]
        return self

    def extra(self, sizes):
        start = sum(self.rows[:-1]) // 2
        found = []
        for rows in sizes:
            found.append(jnp.concatenate([part[start : start + rows // 2] for part in self.result]))
            start += rows // 2
        return found

    def piece(self, first, count):
        parts = len(self.result)
        start = sum(self.rows[:first]) // parts
        rows = self.rows[first] // parts
        cut = [part[start : start + count * rows].reshape(count, rows, -1) for part in self.result]
        return jnp.concatenate(cut, axis=1).reshape(count * rows * parts, -1)


def call(body, args, specs, grid, outs, out_specs, scratch=(), meta=None, after=(), passed=(), into=None, flops=1):
    used = len(args) + (meta is not None)
    passed = list(passed) if into is None else [into] + list(passed)
    waits = len(after) + len(passed)
    results = len(outs)
    filled = int(into is not None)
    kept = results - filled

    def inner(*refs):
        rest = refs[used + waits :]
        body(*refs[:used], *rest[:results], *rest[results + len(passed) - filled :])

    spec = pltpu.PrefetchScalarGridSpec(
        num_scalar_prefetch=int(meta is not None),
        grid=grid,
        in_specs=list(specs) + [pl.BlockSpec(memory_space=pl.ANY)] * waits,
        out_specs=list(out_specs) + [pl.BlockSpec(memory_space=pl.ANY)] * (len(passed) - filled),
        scratch_shapes=list(scratch),
    )
    arrays = ([] if meta is None else [meta]) + list(args) + list(after) + list(passed)
    first = len(arrays) - len(passed)
    return pl.pallas_call(
        inner,
        grid_spec=spec,
        out_shape=list(outs) + [shaped(array.shape, array.dtype) for array in passed[filled:]],
        input_output_aliases={first + at: kept + at for at in range(len(passed))},
        compiler_params=pltpu.CompilerParams(vmem_limit_bytes=VMEM_BYTES),
        cost_estimate=pl.CostEstimate(flops=flops, transcendentals=0, bytes_accessed=1),
    )(*arrays)


def copy_body(source_ref, result_ref):
    result_ref[...] = source_ref[...]


def tied(array, after):
    return call(
        copy_body, [array], [whole(array)], (1,), [shaped(array.shape)], [held(array.shape)], after=after
    )[0]


def whole(array):
    shape = array.shape
    return pl.BlockSpec(
        shape, lambda *_: (0,) * len(shape), pipeline_mode=pl.Buffered(buffer_count=1)
    )


def held(shape):
    return pl.BlockSpec(shape, lambda *_: (0,) * len(shape))


def rows_of(array, rows):
    return pl.BlockSpec((rows, array.shape[1]), lambda step, *_: (step, 0))


def shaped(shape, dtype=F32):
    return jax.ShapeDtypeStruct(tuple(shape), dtype)


def span(shift_by, length):
    return max(0, -shift_by), length - max(0, shift_by)


def tap_list(height, breadth, dilation):
    listed = []
    for row_tap in range(3):
        for col_tap in range(3):
            row_shift = (row_tap - 1) * dilation
            col_shift = (col_tap - 1) * dilation
            if abs(row_shift) < height and abs(col_shift) < breadth:
                listed.append((row_tap, col_tap, row_shift // TILE, col_shift // TILE))
    return listed


def weight_of(ref):
    return ref[...].reshape(-1, ref.shape[-1])


def spread(meta_ref, full_ref, result_refs, column=0, at=0, rows=None):
    width = result_refs[0].shape[2]
    rows = result_refs[0].shape[1] if rows is None else rows
    if len(result_refs) == 1:
        result_refs[0][0, at : at + rows] = full_ref[:, column : column + width].astype(BF16)
        return
    core = meta_ref[0]
    for owner in range(result_refs[0].shape[0]):
        for ref, side in zip(result_refs, (core, 1 - core)):
            start = pl.multiple_of(owner * 2 * rows + side * rows, rows)
            block = full_ref[pl.ds(start, rows), column : column + width]
            ref[meta_ref[1 + owner], at : at + rows] = block.astype(BF16)


def slotted(place, rows, width):
    if place.direct:
        return [shaped((place.size, rows // 2, width), BF16)] * 2
    return [shaped((1, rows * place.size, width), BF16)]


def center_first(step, center):
    return jnp.where(step == 0, center, jnp.where(step <= center, step - 1, step))


def ordered(taps, center):
    return [taps[center]] + [tap for place, tap in enumerate(taps) if place != center]


def shifts_of(taps):
    return [(tap[2], tap[3]) for tap in taps]


def area(tap, tiles):
    return (tiles[0] - abs(tap[0])) * (tiles[1] - abs(tap[1])) * tiles[2]


def forward_tap(tap, fresh, source_ref, weight, result_ref):
    tiles_i, tiles_j, pixels, channels = source_ref.shape
    columns = weight.shape[1]
    shift_i, shift_j = tap
    low_i, high_i = span(shift_i, tiles_i)
    low_j, high_j = span(shift_j, tiles_j)
    window = source_ref[
        low_i + shift_i : high_i + shift_i, low_j + shift_j : high_j + shift_j
    ].reshape(-1, channels)
    product = jnp.dot(window, weight, preferred_element_type=F32)
    product = product.reshape(high_i - low_i, high_j - low_j, pixels, columns)
    if fresh:
        result_ref[low_i:high_i, low_j:high_j] = product
    else:
        result_ref[low_i:high_i, low_j:high_j] += product


def unit_of(values, coef):
    unit = (values - coef[0:1]) * coef[1:2]
    return unit, coef[2:3] * unit + coef[3:4]


def masked_sums(values, valid):
    weighted = values * valid
    return jnp.concatenate(
        [jnp.sum(weighted, axis=0, keepdims=True), jnp.sum(weighted * values, axis=0, keepdims=True)]
    )


def sum_rows(ref, valid_ref, sums_ref):
    total = jnp.zeros(sums_ref.shape, F32)
    for row in range(ref.shape[0]):
        values = ref[row].reshape(-1, ref.shape[-1])
        total = total + masked_sums(values, valid_ref[row].reshape(-1, 1))
    sums_ref[...] = total


def branch_body(plan, table_ref, source_ref, valid_ref, *refs):
    count = 1 + max(group for _, _, _, group in plan)
    weight_refs, result_refs, sums_ref = refs[:count], refs[count:-1], refs[-1]
    for place, (tap, fresh, branch, group) in enumerate(plan):

        @pl.when(pl.program_id(0) == place)
        def _(tap=tap, fresh=fresh, branch=branch, group=group):
            forward_tap(tap, fresh, source_ref, weight_of(weight_refs[group]), result_refs[branch])

    @pl.when(pl.program_id(0) == len(plan) - 1)
    def _():
        width = result_refs[0].shape[-1]
        for branch, ref in enumerate(result_refs):
            sum_rows(ref, valid_ref, sums_ref.at[:, branch * width : (branch + 1) * width])


def branch_convs(source, valid, groups, branches, after):
    channels = source.shape[-1]
    width = groups[0].shape[2]
    plan, taps_at = [], [[] for _ in groups]
    for branch, (taps, center, group, first_tap) in enumerate(branches):
        order = ordered(list(enumerate(shifts_of(taps))), center)
        for place, (tap, shift) in enumerate(order):
            plan.append((shift, place == 0, branch, group))
            for at, listed in enumerate(taps_at):
                listed.append(first_tap + tap if at == group else None)
    table = []
    for listed in taps_at:
        known = next(tap for tap in listed if tap is not None)
        for tap in listed:
            known = known if tap is None else tap
            table.append(known)
    steps = len(plan)
    blocks = [
        pl.BlockSpec(
            (weights.shape[0], channels // weights.shape[0], width),
            lambda step, table, first=steps * at: (0, table[first + step], 0),
        )
        for at, weights in enumerate(groups)
    ]
    result_shape = source.shape[:3] + (width,)
    sums_shape = (2, width * len(branches))
    return call(
        functools.partial(branch_body, plan),
        [source, valid] + groups,
        [whole(source), whole(valid)] + blocks,
        (steps,),
        [shaped(result_shape)] * len(branches) + [shaped(sums_shape)],
        [held(result_shape)] * len(branches) + [held(sums_shape)],
        meta=jnp.array(np.array(table, np.int32)),
        after=after,
    )


def spatial_body(plan, first_ref, coef_ref, valid_ref, weight_ref, input_ref, result_ref, sums_ref):
    @pl.when(pl.program_id(0) == 0)
    def _():
        for row in range(first_ref.shape[0]):
            _, pre = unit_of(first_ref[row], coef_ref[...][:, None, :])
            input_ref[row] = (silu(pre) * valid_ref[row]).astype(BF16)

    for place, tap in enumerate(plan):

        @pl.when(pl.program_id(0) == place)
        def _(place=place, tap=tap):
            forward_tap(tap, place == 0, input_ref, weight_of(weight_ref), result_ref)

    @pl.when(pl.program_id(0) == len(plan) - 1)
    def _():
        sum_rows(result_ref, valid_ref, sums_ref)


def spatial_conv(first, coef, valid, weights, taps, center, first_tap):
    channels = first.shape[-1]
    pieces, _, columns = weights.shape
    plan = ordered(shifts_of(taps), center)
    return call(
        functools.partial(spatial_body, plan),
        [first, coef, valid, weights],
        [
            whole(first),
            whole(coef),
            whole(valid),
            pl.BlockSpec(
                (pieces, channels // pieces, columns),
                lambda step: (0, first_tap + center_first(step, center), 0),
            ),
        ],
        (len(plan),),
        [shaped(first.shape, BF16), shaped(first.shape), shaped((2, columns))],
        [held(first.shape), held(first.shape), held((2, columns))],
    )


def shifted_columns(tiles, row_taps, up_ref, padded_ref, width, first=None, last=None):
    tiles_i, tiles_j, pixels = tiles
    shift_i, columns = row_taps
    low_i, high_i = span(shift_i, tiles_i)
    line = tiles_j * pixels
    low, high = (low_i + shift_i) * line, (high_i + shift_i) * line

    def clear(start, stop, at):
        if stop > start:
            padded_ref[start:stop, at : at + width] = jnp.zeros((stop - start, width), BF16)

    for place, (shift_j, column) in enumerate(columns):
        at = place * width
        low_j, high_j = span(shift_j, tiles_j)
        begin, end = (low_j + shift_j) * pixels, (high_j + shift_j) * pixels
        for row in range(low_i, high_i):
            base = (row + shift_i) * line
            source = row * line + low_j * pixels
            clear(base, base + begin, at)
            padded_ref[base + begin : base + end, at : at + width] = up_ref[
                source : source + end - begin, column : column + width
            ]
            clear(base + end, base + line, at)
        if first is not None:
            clear(first, low, at)
            clear(high, last, at)
    return low, high


def back_step(tiles, row_taps, fresh, up_ref, weight_refs, padded_ref, weight_ref, total_ref):
    channels = total_ref.shape[1]
    width = weight_refs[0].shape[2]
    depth = len(row_taps[1]) * width
    low, high = shifted_columns(tiles, row_taps, up_ref, padded_ref, width)
    for place in range(len(row_taps[1])):
        weight_ref[:, place * width : (place + 1) * width] = weight_of(weight_refs[place])
    wide = min(512, channels)
    for start in range(0, channels, wide):
        product = lax.dot_general(
            padded_ref[low:high, :depth],
            weight_ref[start : start + wide, :depth],
            (((1,), (1,)), ((), ())),
            preferred_element_type=F32,
        )
        if fresh:
            total_ref[low:high, start : start + wide] = product
        else:
            total_ref[low:high, start : start + wide] += product


def row_plan(taps, columns):
    rows = []
    for tap, column in zip(taps, columns):
        if not rows or rows[-1][0] != tap[2]:
            rows.append((tap[2], []))
        rows[-1][1].append((tap[3], column))
    return rows


def row_weights(weights, channels, order, first_tap, side=0, sides=1):
    pieces, _, width = weights.shape
    rows = channels // pieces
    specs = []
    for column in range(3):

        def index(step, column=column):
            row = order[-1]
            for place, listed in enumerate(order[:-1]):
                row = jnp.where(step == place, listed, row)
            tap = first_tap + 3 * row + column
            return (0, tap * sides + side, 0) if pieces == 1 else (side, tap, 0)

        block = (1, rows // sides, width) if pieces == 1 else (pieces // sides, rows, width)
        specs.append(pl.BlockSpec(block, index))
    return specs


def grad_moments(grad, unit):
    return jnp.concatenate(
        [jnp.sum(grad, axis=0, keepdims=True), jnp.sum(grad * unit, axis=0, keepdims=True)]
    )


def feature_body(
    plan, groups, tiles, up_ref, third_ref, source_ref, coef_ref, pooled_ref, valid_ref, *refs
):
    result_ref, sums_ref, padded_ref, weight_ref, total_ref = refs[7:]
    step_now = pl.program_id(0)
    for place, row_taps in enumerate(plan):
        weight_refs = refs[3:6] if groups[place] else refs[0:3] + refs[6:7]

        @pl.when(step_now == place)
        def _(place=place, row_taps=row_taps, weight_refs=weight_refs):
            back_step(
                tiles, row_taps, place == 0, up_ref, weight_refs, padded_ref, weight_ref, total_ref
            )

    begun = len(plan)

    @pl.when(step_now >= begun)
    def _():
        height = third_ref.shape[0]
        row = pl.multiple_of((step_now - begun) * height, height)
        unit, pre = unit_of(third_ref[...], coef_ref[...])
        pre = pre + source_ref[...].astype(F32)
        grad = total_ref[pl.ds(row, height)] + pooled_ref[...]
        grad = grad * valid_ref[...] * silu_slope(pre)
        result_ref[...] = grad.astype(BF16)
        moments = grad_moments(grad, unit)

        @pl.when(step_now == begun)
        def _():
            sums_ref[...] = moments

        @pl.when(step_now > begun)
        def _():
            sums_ref[...] += moments


def feature_back(upstream, weights, plan, orders, point, third, source, coef, pooled, valid, tiles, side, sides, after, passed):
    pixels, channels = third.shape
    part = channels // sides
    pieces, _, width = weights[0].shape
    plan, groups = [row_taps for row_taps, _ in plan], [group for _, group in plan]
    rows = channels // pieces
    begun = len(plan)
    turns = tiles[0]
    height = pixels // turns

    def row_of(step):
        return jnp.clip(step - begun, 0, turns - 1)

    row_block = pl.BlockSpec((height, part), lambda step: (row_of(step), side))
    if pieces == 1:
        point_block = pl.BlockSpec((1, rows // sides, width), lambda step: (0, point * sides + side, 0))
    else:
        point_block = pl.BlockSpec((pieces // sides, rows, width), lambda step: (side, point, 0))
    return call(
        functools.partial(feature_body, plan, groups, tiles),
        [upstream, third, source, coef, pooled, valid] + [weights[0]] * 3 + [weights[1]] * 3 + [weights[0]],
        [
            whole(upstream),
            row_block,
            row_block,
            pl.BlockSpec((coef.shape[0], part), lambda step: (0, side)),
            pl.BlockSpec((1, part), lambda step: (0, side)),
            pl.BlockSpec((height, 1), lambda step: (row_of(step), 0)),
        ]
        + row_weights(weights[0], channels, orders[0], 0, side, sides)
        + row_weights(weights[1], channels, orders[1], 0, side, sides)
        + [point_block],
        (begun + turns,),
        [shaped((pixels, part), BF16), shaped((2, part))],
        [pl.BlockSpec((height, part), lambda step: (row_of(step), 0)), held((2, part))],
        [
            pltpu.VMEM((pixels, 4 * width), BF16),
            pltpu.VMEM((part, 4 * width), BF16),
            pltpu.VMEM((pixels, part), F32),
        ],
        after=after,
        passed=passed,
    )


def spatial_back_body(plan, tiles, up_ref, first_ref, coef_ref, valid_ref, *refs):
    weight_refs = refs[:3]
    result_ref, sums_ref, padded_ref, weight_ref = refs[3:]
    for place, row_taps in enumerate(plan):

        @pl.when(pl.program_id(0) == place)
        def _(place=place, row_taps=row_taps):
            back_step(
                tiles, row_taps, place == 0, up_ref, weight_refs, padded_ref, weight_ref, result_ref
            )

    @pl.when(pl.program_id(0) == len(plan) - 1)
    def _():
        total = jnp.zeros(sums_ref.shape, F32)
        height = result_ref.shape[0] // tiles[0]
        for row in range(tiles[0]):
            at = slice(row * height, (row + 1) * height)
            unit, pre = unit_of(first_ref[at], coef_ref[...])
            grad = result_ref[at] * valid_ref[at] * silu_slope(pre)
            result_ref[at] = grad
            total = total + grad_moments(grad, unit)
        sums_ref[...] = total


def spatial_back(upstream, first, coef, valid, weights, plan, order, tiles, first_tap, after, passed):
    pixels, channels = first.shape
    columns = weights.shape[2]
    return call(
        functools.partial(spatial_back_body, plan, tiles),
        [upstream, first, coef, valid] + [weights] * 3,
        [whole(upstream), whole(first), whole(coef), whole(valid)]
        + row_weights(weights, channels, order, first_tap),
        (len(plan),),
        [shaped(first.shape), shaped((2, channels))],
        [held(first.shape), held((2, channels))],
        [pltpu.VMEM((pixels, 3 * columns), BF16), pltpu.VMEM((channels, 3 * columns), BF16)],
        after=after,
        passed=passed,
    )


def weight_body(plan, tiles, extra, count, meta_ref, flipped_ref, up_ref, *refs):
    extra_ref = refs[0] if extra else None
    result_refs = refs[extra : extra + count]
    padded_ref, full_ref = refs[extra + count :]
    block_rows, width = result_refs[0].shape[1:]
    taps_held = padded_ref.shape[1] // width
    rows = block_rows // taps_held
    for place, row_taps in enumerate(plan):

        @pl.when(pl.program_id(0) == place)
        def _(row_taps=row_taps):
            taps = len(row_taps[1])
            low_i, high_i = span(row_taps[0], tiles[0])
            line = tiles[1] * tiles[2]
            first = (low_i + row_taps[0]) * line // 128 * 128
            last = -(-(high_i + row_taps[0]) * line // 128) * 128
            shifted_columns(tiles, row_taps, up_ref, padded_ref, width, first, last)
            for tap in range(taps):
                at = slice(tap * width, (tap + 1) * width)
                full_ref[:, at] = jnp.dot(
                    flipped_ref[:, first:last], padded_ref[first:last, at], preferred_element_type=F32
                ).astype(BF16)
                spread(meta_ref, full_ref, result_refs, tap * width, tap * rows, rows)

    if extra:

        @pl.when(pl.program_id(0) == len(plan) - 1)
        def _():
            core = meta_ref[0]
            taps = len(plan[-1][1])
            spare = (taps_held - taps - 1) * rows
            for owner in range(result_refs[0].shape[0]):
                slot = meta_ref[1 + owner]
                for ref, side in zip(result_refs, (core, 1 - core)):
                    start = pl.multiple_of((owner * 2 + side) * rows, rows)
                    ref[slot, taps * rows : (taps + 1) * rows] = extra_ref[pl.ds(start, rows)]
                    ref[slot, (taps + 1) * rows :] = jnp.zeros((spare, width), BF16)


def weight_grad(place, flipped, upstream, meta, plan, tiles, width, after=(), extra=None, passed=()):
    channels, padded = flipped.shape
    taps = max(len(row_taps[1]) for row_taps in plan)
    steps = len(plan)
    shapes = slotted(place, channels // place.size * taps * steps, width)
    blocks = [
        pl.BlockSpec((shape.shape[0], shape.shape[1] // steps, width), lambda step, _: (0, step, 0))
        for shape in shapes
    ]
    more = [] if extra is None else [extra]
    return call(
        functools.partial(weight_body, plan, tiles, len(more), len(shapes)),
        [flipped, upstream] + more,
        [whole(array) for array in [flipped, upstream] + more],
        (steps,),
        shapes,
        blocks,
        [pltpu.VMEM((padded, taps * width), BF16), pltpu.VMEM((channels, taps * width), BF16)],
        meta,
        after,
        passed,
    )


def tile_matrix(breadth):
    count = TILE * breadth
    matrix = np.zeros((count, count), np.float32)
    for row in range(TILE):
        for column in range(breadth):
            at = (column // TILE * TILE + row) * TILE + column % TILE
            matrix[at, row * breadth + column] = 1.0
    return matrix


def tile_body(matrix_ref, natural_ref, result_ref):
    result_ref[...] = jnp.dot(
        matrix_ref[...], natural_ref[...], preferred_element_type=F32
    ).astype(BF16)


def tile_rows(natural, matrix):
    rows = matrix.shape[0]
    return call(
        tile_body,
        [matrix, natural],
        [whole(matrix), rows_of(natural, rows)],
        (natural.shape[0] // rows,),
        [shaped(natural.shape, BF16)],
        [rows_of(natural, rows)],
    )[0]


def flip_body(source_ref, result_ref):
    pixels = source_ref.shape[0]
    result_ref[:, :pixels] = source_ref[...].T
    if result_ref.shape[1] > pixels:
        extra = result_ref.shape[1] - pixels
        result_ref[:, pixels:] = jnp.zeros((result_ref.shape[0], extra), BF16)


def flipped(values, after=()):
    pixels, channels = values.shape
    padded = pixels + -pixels % 128
    return call(
        flip_body,
        [values],
        [pl.BlockSpec((pixels, 128), lambda step: (0, step))],
        (channels // 128,),
        [shaped((channels, padded), BF16)],
        [pl.BlockSpec((128, padded), lambda step: (step, 0))],
        after=after,
    )[0]


def add_sums(sums_ref, sums):
    @pl.when(pl.program_id(0) == 0)
    def _():
        sums_ref[...] = sums

    @pl.when(pl.program_id(0) > 0)
    def _():
        sums_ref[...] += sums


def first_body(source_ref, valid_ref, weight_ref, result_ref, sums_ref):
    product = jnp.dot(source_ref[...], weight_of(weight_ref), preferred_element_type=F32)
    result_ref[...] = product
    add_sums(sums_ref, masked_sums(product, valid_ref[...]))


def fixed_block(weights, channels, at):
    pieces, _, columns = weights.shape
    return pl.BlockSpec((pieces, channels // pieces, columns), lambda step, *_: (0, at, 0))


def first_conv(source, valid, weights, turns, after):
    pixels, channels = source.shape
    rows = pixels // turns
    width = weights.shape[2]
    return call(
        first_body,
        [source, valid, weights],
        [rows_of(source, rows), rows_of(valid, rows), fixed_block(weights, channels, 0)],
        (turns,),
        [shaped((pixels, width)), shaped((2, width))],
        [pl.BlockSpec((rows, width), lambda step: (step, 0)), held((2, width))],
        after=after,
    )


def third_body(count, second_ref, coef_ref, valid_ref, *refs):
    weight_refs = refs[:count]
    middle_ref, result_ref, sums_ref = refs[count:]
    _, pre = unit_of(second_ref[...], coef_ref[...])
    middle = silu(pre).astype(BF16)
    middle_ref[...] = middle
    valid = valid_ref[...]
    sums = []
    for quarter, ref in enumerate(weight_refs):
        product = jnp.dot(middle, weight_of(ref), preferred_element_type=F32)
        width = product.shape[1]
        result_ref[:, quarter * width : (quarter + 1) * width] = product
        sums.append(masked_sums(product, valid))
    add_sums(sums_ref, jnp.concatenate(sums, axis=1))


def third_conv(second, coef, valid, weights, first, count, turns, passed):
    pixels, narrow = second.shape
    height = pixels // turns
    channels = count * weights.shape[2]
    return call(
        functools.partial(third_body, count),
        [second, coef, valid] + [weights] * count,
        [rows_of(second, height), whole(coef), rows_of(valid, height)]
        + [fixed_block(weights, narrow, first + quarter) for quarter in range(count)],
        (turns,),
        [shaped((pixels, narrow), BF16), shaped((pixels, channels)), shaped((2, channels))],
        [
            pl.BlockSpec((height, narrow), lambda step: (step, 0)),
            pl.BlockSpec((height, channels), lambda step: (step, 0)),
            held((2, channels)),
        ],
        passed=passed,
    )


def output_body(third_ref, source_ref, coef_ref, valid_ref, result_ref, sums_ref):
    _, pre = unit_of(third_ref[...], coef_ref[...])
    values = (valid_ref[...] * silu(pre + source_ref[...].astype(F32))).astype(BF16)
    result_ref[...] = values
    add_sums(sums_ref, jnp.sum(values.astype(F32), axis=0, keepdims=True))


def block_output(third, source, coef, valid, turns, passed):
    pixels, channels = third.shape
    rows = pixels // turns
    return call(
        output_body,
        [third, source, coef, valid],
        [rows_of(third, rows), rows_of(source, rows), whole(coef), rows_of(valid, rows)],
        (turns,),
        [shaped(third.shape, BF16), shaped((1, channels))],
        [rows_of(third, rows), held((1, channels))],
        passed=passed,
    )


def order_body(meta_ref, own_ref, other_ref, result_ref):
    side = pl.program_id(0) % 2

    @pl.when(side == meta_ref[0])
    def _():
        result_ref[...] = own_ref[...]

    @pl.when(side != meta_ref[0])
    def _():
        result_ref[...] = other_ref[...]


def in_order(own, other, meta):
    slots, rows, columns = own.shape
    block = pl.BlockSpec((1, rows, columns), lambda step, meta: (meta[1 + step // 2], 0, 0))
    return call(
        order_body,
        [own, other],
        [block, block],
        (2 * slots,),
        [shaped((2 * slots, rows, columns), BF16)],
        [pl.BlockSpec((1, rows, columns), lambda step, meta: (step, 0, 0))],
        meta=meta,
    )[0]


def third_back_body(
    count, outs, meta_ref, low_ref, high_ref, third_ref, coef_ref, totals_ref, valid_ref, middle_ref, *refs
):
    weight_refs = refs[:count]
    result_ref = refs[count]
    slot_refs = refs[count + 1 : count + 1 + outs]
    grad_ref, total_ref = refs[count + 1 + outs :]
    step_now = pl.program_id(0)

    @pl.when(step_now == 0)
    def _():
        total_ref[...] = jnp.zeros_like(total_ref)

    part = low_ref.shape[1]
    coef, totals, valid = coef_ref[...], totals_ref[...], valid_ref[...]
    for start, part_ref in ((0, low_ref), (part, high_ref)):
        at = slice(start, start + part)
        unit = (third_ref[:, at] - coef[0:1, at]) * coef[1:2, at]
        centered = part_ref[...].astype(F32) - valid * (totals[0:1, at] + unit * totals[1:2, at])
        grad_ref[:, at] = (coef[2:3, at] * coef[1:2, at] * centered).astype(BF16)
    width = weight_refs[0].shape[2]
    result = None
    for quarter, ref in enumerate(weight_refs):
        grad = grad_ref[:, quarter * width : (quarter + 1) * width]
        product = lax.dot_general(
            grad, weight_of(ref), (((1,), (1,)), ((), ())), preferred_element_type=F32
        )
        result = product if result is None else result + product
    result_ref[...] = result
    total_ref[...] += lax.dot_general(
        middle_ref[...], grad_ref[...], (((0,), (0,)), ((), ())), preferred_element_type=F32
    )

    @pl.when(step_now == pl.num_programs(0) - 1)
    def _():
        rows = slot_refs[0].shape[1] // count
        for quarter in range(count):
            spread(meta_ref, total_ref, slot_refs, quarter * width, quarter * rows, rows)


def third_back(place, low, high, third, coef, totals, valid, middle, weights, meta, first, count, turns, after, passed):
    pixels, channels = third.shape
    narrow = middle.shape[1]
    height = pixels // turns
    shapes = slotted(place, narrow // place.size * count, weights.shape[2])
    return call(
        functools.partial(third_back_body, count, len(shapes)),
        [low, high, third, coef, totals, valid, middle] + [weights] * count,
        [
            rows_of(low, height),
            rows_of(high, height),
            rows_of(third, height),
            whole(coef),
            whole(totals),
            rows_of(valid, height),
            rows_of(middle, height),
        ]
        + [fixed_block(weights, narrow, first + quarter) for quarter in range(count)],
        (turns,),
        [shaped((pixels, narrow))] + shapes,
        [pl.BlockSpec((height, narrow), lambda step, _: (step, 0))] + [held(shape.shape) for shape in shapes],
        [pltpu.VMEM((height, channels), BF16), pltpu.VMEM((narrow, channels), F32)],
        meta,
        after,
        passed,
    )


def input_body(matrix_ref, low_ref, high_ref, grad_ref, weight_ref, result_ref):
    rows = matrix_ref.shape[0]
    part = low_ref.shape[1]
    matrix = matrix_ref[...]
    moved = []
    for start in range(0, result_ref.shape[0], rows):
        at = slice(start, start + rows)
        moved.append(jnp.dot(matrix, grad_ref[at], preferred_element_type=F32).astype(BF16))
        for column, part_ref in ((0, low_ref), (part, high_ref)):
            result_ref[at, column : column + part] = jnp.dot(
                matrix, part_ref[at], preferred_element_type=F32
            )
    result_ref[...] += lax.dot_general(
        jnp.concatenate(moved), weight_of(weight_ref), (((1,), (1,)), ((), ())), preferred_element_type=F32
    )


def input_back(matrix, low, high, grad, weights, turns, first, count, after, passed, into):
    pixels, part = low.shape
    rows = pixels // turns
    channels = 2 * part
    width = grad.shape[1]

    def block(columns):
        return pl.BlockSpec((rows, columns), lambda step: (first + step, 0))

    return call(
        input_body,
        [matrix, low, high, grad, weights],
        [whole(matrix), block(part), block(part), block(width), fixed_block(weights, channels, 0)],
        (count,),
        [shaped((pixels, channels))],
        [block(channels)],
        after=after,
        passed=passed,
        into=into,
        flops=10**10,
    )


def sigmoid(values):
    return 0.5 + 0.5 * jnp.tanh(0.5 * values)


def silu(values):
    return values * sigmoid(values)


def silu_slope(values):
    sigmoid_val = sigmoid(values)
    return sigmoid_val * (1.0 + values * (1.0 - sigmoid_val))


def sums(values, validity):
    weighted = values * validity
    return jnp.stack([jnp.sum(weighted, axis=0), jnp.sum(weighted * values, axis=0)])


def coefs(totals, counted, gain, shift):
    mean_value = totals[0] / counted
    scaling = lax.rsqrt(totals[1] / counted - mean_value * mean_value + EPSILON)
    return jnp.stack([mean_value, scaling, gain, shift])


def through_norm(grad_pre, unit, coef, counted, validity, totals):
    centered = grad_pre - validity * (totals[0] + unit * totals[1]) / counted
    return coef[2] * coef[1] * centered


def to_tiles(array):
    height, breadth = array.shape[:2]
    rest = array.shape[2:]
    cut = array.reshape((height // TILE, TILE, breadth // TILE, TILE) + rest)
    return jnp.swapaxes(cut, 1, 2).reshape((height * breadth,) + rest)


def per_device(
    features,
    reduce_weight,
    spatial_weight,
    expand_weight,
    bottle_gain,
    bottle_shift,
    point_weight,
    near_weight,
    middle_weight,
    far_weight,
    image_weight,
    project_weight,
    class_weight,
    pyramid_gain,
    pyramid_shift,
    head_gain,
    head_shift,
    crop_masks,
    crop_tasks,
    pixel_labels,
    task_norms,
):
    place = Place()
    size, core = place.size, place.core
    first_core = core == 0
    height, breadth, channels = features.shape[2:]
    pixels = height * breadth
    tiles = (height // TILE, breadth // TILE, TILE * TILE)
    narrow = reduce_weight.shape[1]
    branch = point_weight.shape[1]
    four_wide = 4 * branch
    rows = channels // size
    narrow_rows = narrow // size
    quarters = channels // narrow
    turns = 3
    meta = place.meta()
    matrix = tile_matrix(breadth)

    bottle_taps = tap_list(height, breadth, BOTTLE_RATE)
    near_taps = tap_list(height, breadth, NEAR_RATE)
    middle_taps = tap_list(height, breadth, MIDDLE_RATE)
    far_taps = tap_list(height, breadth, FAR_RATE)
    point_taps = [(1, 1, 0, 0)]

    def center_of(taps):
        return [tap[:2] for tap in taps].index((1, 1))

    def stacked(weight, taps):
        flat = weight.reshape((-1,) + weight.shape[2:])
        picked = [3 * tap[0] + tap[1] for tap in taps]
        if picked == list(range(picked[0], picked[-1] + 1)):
            flat = flat[picked[0] : picked[-1] + 1]
        else:
            flat = jnp.stack([flat[at] for at in picked])
        return flat.reshape(-1, flat.shape[2]), len(taps)

    mask = lax.dynamic_index_in_dim(crop_masks, core, 0, keepdims=False)[0]
    labels = lax.dynamic_index_in_dim(pixel_labels, core, 0, keepdims=False)[0]
    task = lax.dynamic_index_in_dim(crop_tasks, core, 0, keepdims=False)[0]
    validity = to_tiles(mask).astype(F32)[:, None]
    valid_tiles = validity.reshape(tiles + (1,))
    labels = to_tiles(labels)
    source = tile_rows(features.reshape(pixels, channels), jnp.array(matrix, BF16))
    source_flipped = flipped(source)

    wide_expand = expand_weight.reshape(-1, quarters, narrow)
    expand_parts = [(wide_expand[:, at], 1) for at in range(quarters)]
    bottle_all = place.gather([(reduce_weight, 1), stacked(spatial_weight, bottle_taps)] + expand_parts)
    spatial_at = channels // narrow
    expand_at = spatial_at + len(bottle_taps)
    pyramid_parts = [stacked(near_weight, near_taps), stacked(far_weight, far_taps)]
    pyramid_parts += [(point_weight, 1), (image_weight, 1), (project_weight, 1)]
    pyramid_all = place.gather(pyramid_parts)
    far_at = len(near_taps)
    point_at = far_at + len(far_taps)
    piece_rows = channels // place.pieces
    image_full = pyramid_all[:, (point_at + 1) * piece_rows : (point_at + 2) * piece_rows]
    image_full = image_full.reshape(channels, branch)
    project_full = pyramid_all[:, (point_at + 2) * piece_rows :].reshape(-1, branch)
    middle_line = place.along_line(*stacked(middle_weight, middle_taps))

    crop_valid_both = jnp.sum(crop_masks, axis=(1, 2, 3)).astype(F32)
    home_crop = (crop_tasks[:, 0] == 1).astype(F32)
    counts = jnp.concatenate(
        [
            crop_valid_both,
            jnp.sum(crop_valid_both * (1.0 - home_crop))[None],
            jnp.sum(crop_valid_both * home_crop)[None],
        ]
    )
    small = [bottle_gain, bottle_shift, pyramid_gain, pyramid_shift, head_gain, head_shift]
    small.append(class_weight.reshape(-1))
    small_widths = [part.shape[0] for part in small]
    small_own = jnp.concatenate(small).astype(F32)
    collected = place.everyone(jnp.concatenate([small_own, counts]))
    counts_all = jnp.sum(collected[:, small_own.size :], axis=0)
    small_all, start = [], 0
    for width in small_widths:
        small_all.append(collected[:, start : start + width].reshape(-1))
        start += width
    gain_bottle, shift_bottle, gain_pyramid, shift_pyramid, gain_head, shift_head = small_all[:6]
    class_full = small_all[6].reshape(size * class_weight.shape[0], -1).astype(BF16)
    counted = jnp.where(first_core, counts_all[0], counts_all[1])
    task_pixels = counts_all[2:4]
    crop_valid = jnp.where(first_core, crop_valid_both[0], crop_valid_both[1])

    first, first_sums = first_conv(source, validity, bottle_all, turns, [source_flipped, middle_line])
    coef_one = coefs(place.total(first_sums), counted, gain_bottle[:narrow], shift_bottle[:narrow])
    first_tiles = first.reshape(tiles + (narrow,))
    conv_in, second, second_sums = spatial_conv(
        first_tiles, coef_one, valid_tiles, bottle_all, bottle_taps, center_of(bottle_taps), spatial_at
    )
    second = second.reshape(pixels, narrow)
    coef_two = coefs(
        place.total(second_sums), counted, gain_bottle[narrow : 2 * narrow], shift_bottle[narrow : 2 * narrow]
    )
    middle_plane = place.across_plane(middle_line)
    middle_act, third, third_sums, middle_line = third_conv(
        second, coef_two, validity, bottle_all, expand_at, quarters, turns, [middle_line]
    )
    if place.direct:
        middle_plane = jnp.concatenate([middle_line, middle_plane[middle_line.shape[0] :]])
    middle_other = place.swap(middle_plane)
    coef_three = coefs(
        place.total(third_sums), counted, gain_bottle[2 * narrow :], shift_bottle[2 * narrow :]
    )
    block_out, pooled_sum, middle_plane = block_output(
        third, source, coef_three, validity, tiles[0], [middle_plane]
    )
    middle_all = middle_plane
    if place.direct:
        middle_all = in_order(middle_plane, middle_other, place.meta(PLANE_BITS))
    block_tiles = block_out.reshape(tiles + (channels,))

    pooled = (pooled_sum / crop_valid).astype(BF16)
    pooled_all = place.everyone(pooled[0])
    pooled_rows = lax.dynamic_slice_in_dim(pooled_all, place.index * rows, rows, axis=1)
    image_all = jnp.dot(pooled_all, image_full, preferred_element_type=F32)
    *outs, branch_sums = branch_convs(
        block_tiles,
        valid_tiles,
        [pyramid_all, middle_all],
        [
            (point_taps, 0, 0, point_at),
            (near_taps, center_of(near_taps), 0, 0),
            (middle_taps, center_of(middle_taps), 1, 0),
            (far_taps, center_of(far_taps), 0, far_at),
        ],
        (),
    )
    branches = jnp.concatenate([part.reshape(pixels, branch) for part in outs], axis=1)
    image_mean = jnp.sum(image_all, axis=0) / size
    image_scale = lax.rsqrt(
        jnp.sum(image_all * image_all, axis=0) / size - image_mean * image_mean + EPSILON
    )
    image_unit = (image_all - image_mean) * image_scale
    gain_image, shift_image = gain_pyramid[four_wide:], shift_pyramid[four_wide:]
    coef_image = jnp.stack([image_mean, image_scale, gain_image, shift_image])
    image_pre = gain_image * image_unit + shift_image
    image_act = silu(image_pre).astype(BF16)

    block_flipped = flipped(block_out, [branch_sums])
    conv_flipped = flipped(conv_in.reshape(pixels, narrow), [block_flipped])
    coef_branch = coefs(
        place.total(branch_sums), counted, gain_pyramid[:four_wide], shift_pyramid[:four_wide]
    )
    unit_branch, pre_branch = unit_of(branches, coef_branch)
    joined = silu(pre_branch).astype(BF16)

    own_act = lax.dynamic_slice_in_dim(image_act, place.index, 1, axis=0)
    crop_part = jnp.dot(own_act, project_full[four_wide:], preferred_element_type=F32)
    projected = jnp.dot(joined, project_full[:four_wide], preferred_element_type=F32) + crop_part
    coef_head = coefs(place.total(sums(projected, validity)), counted, gain_head, shift_head)
    unit_head, pre_head = unit_of(projected, coef_head)
    output_act = silu(pre_head).astype(BF16)
    logits = jnp.dot(output_act, class_full, preferred_element_type=F32)

    columns = jnp.arange(class_full.shape[1])
    allowed = (columns >= CITY_CLASSES) == (task == 1)
    masked = jnp.where(allowed, logits, FLOOR_LOGIT)
    raised = jnp.exp(masked - jnp.max(masked, axis=-1, keepdims=True))
    chances = raised / jnp.sum(raised, axis=-1, keepdims=True)
    target = jnp.where(task == 0, labels % CITY_CLASSES, CITY_CLASSES + labels % HOME_CLASSES)
    chosen = (columns == target[:, None]).astype(F32)
    inverse = 1.0 / task_norms.astype(F32)
    task_share = inverse / jnp.sum(inverse)
    crop_weight = jnp.where(
        task == 0, task_share[0] / task_pixels[0], task_share[1] / task_pixels[1]
    )
    logit_grad = (crop_weight * validity * (chances - chosen)).astype(BF16)
    class_grad = lax.dot_general(
        output_act, logit_grad, (((0,), (0,)), ((), ())), preferred_element_type=F32
    )

    output_grad = lax.dot_general(
        logit_grad, class_full, (((1,), (1,)), ((), ())), preferred_element_type=F32
    )
    grad_head = output_grad * silu_slope(pre_head)
    head_totals = place.total(grad_moments(grad_head, unit_head))
    proj_grad = through_norm(
        grad_head, unit_head, coef_head, counted, validity, head_totals
    ).astype(BF16)
    crop_grad = jnp.sum(proj_grad, axis=0, dtype=F32)
    joined_grad = lax.dot_general(
        proj_grad, project_full[:four_wide], (((1,), (1,)), ((), ())), preferred_element_type=F32
    )
    act_grad = jnp.dot(project_full[four_wide:].astype(F32), crop_grad, precision=HIGHEST)
    own_pre = lax.dynamic_slice_in_dim(image_pre, place.index, 1, axis=0)[0]
    image_pre_grad = act_grad * silu_slope(own_pre)
    grad_branch = joined_grad * silu_slope(pre_branch)
    branch_parts = place.everyone(
        jnp.concatenate([grad_moments(grad_branch, unit_branch).reshape(-1), image_pre_grad])
    )
    image_pre_all = branch_parts[:, 2 * four_wide :]
    branch_totals = jnp.sum(branch_parts[:, : 2 * four_wide], axis=0).reshape(2, four_wide)
    branch_grad = through_norm(
        grad_branch, unit_branch, coef_branch, counted, validity, branch_totals
    ).astype(BF16)
    image_totals = grad_moments(image_pre_all, image_unit)
    image_in_all = through_norm(
        image_pre_all, image_unit, coef_image, float(size), 1.0, image_totals
    )
    pooled_grad_own = lax.dot_general(
        lax.dynamic_slice_in_dim(image_in_all, place.index, 1, axis=0),
        image_full.astype(F32),
        (((1,), (1,)), ((), ())),
        precision=HIGHEST,
    )
    image_partial = jnp.dot(pooled_rows.astype(F32).T, image_in_all, precision=HIGHEST)

    def columns_of(taps, block):
        return [block * branch] * len(taps)

    near_rows = row_plan(near_taps, columns_of(near_taps, 1))
    middle_rows = row_plan(middle_taps, columns_of(middle_taps, 2))
    far_row = row_plan(far_taps, columns_of(far_taps, 3))
    point_row = row_plan(point_taps, columns_of(point_taps, 0))
    project_grad = jnp.concatenate(
        [
            lax.dot_general(
                joined, proj_grad, (((0,), (0,)), ((), ())), preferred_element_type=F32
            ),
            own_act[0].astype(F32)[:, None] * crop_grad[None, :],
        ]
    )

    class_rows = class_grad.size // size // branch if place.direct else 0
    extra_rows = project_grad.shape[0] // size + class_rows

    def extra_halves():
        parts = [project_grad.reshape(size, 2, -1, branch), class_grad.reshape(size, 2, -1, branch)]
        spare = rows // 2 - extra_rows // 2
        parts.append(jnp.zeros((size, 2, spare, branch), F32))
        return jnp.concatenate(parts, axis=2).reshape(-1, branch).astype(BF16)

    def branch_weight_grad(plan, after, extra=None):
        return weight_grad(
            place, block_flipped, branch_grad, meta, plan, tiles, branch, after, extra
        )

    parts = 2 if place.direct else 1
    wide_grads = branch_weight_grad(
        middle_rows + far_row + point_row, [conv_flipped], extra_halves() if place.direct else None
    )
    wide_rows = [rows] * (len(middle_taps) + len(far_taps) + 1) + [extra_rows]
    if not place.direct:
        wide_grads = [jnp.concatenate([wide_grads[0], project_grad.astype(BF16)[None]], axis=1)]
        wide_rows = wide_rows[:-1] + [rows, rows] + wide_rows[-1:]
    wide_scatter = Scatter(place, wide_grads, wide_rows)
    near_grads = branch_weight_grad(near_rows, [wide_grads[0]])
    near_scatter = Scatter(place, near_grads, [rows] * len(near_taps))
    wide_scatter.first()

    pooled_grad = pooled_grad_own / crop_valid
    back_plan = [((far_row[0][0], far_row[0][1] + point_row[0][1]), 0)]
    back_plan += [(row_taps, 0) for row_taps in near_rows] + [(row_taps, 1) for row_taps in middle_rows]
    near_count, middle_count = len(near_rows), len(middle_rows)
    back_orders = [
        [near_count] + list(range(near_count)) + [near_count - 1] * middle_count,
        [0] * (1 + near_count) + list(range(middle_count)),
    ]

    def half_back(side, after, scatters):
        low, moments, *passed = feature_back(
            branch_grad,
            [pyramid_all, middle_all],
            back_plan,
            back_orders,
            point_at,
            third,
            source,
            coef_three,
            pooled_grad,
            validity,
            tiles,
            side,
            2,
            after,
            passing(scatters),
        )
        take_back(scatters, passed)
        return low, moments

    def sending(*scatters):
        return [array for scatter in scatters for array in scatter.sent]

    def passing(scatters):
        return [array for scatter in scatters for array in scatter.kept]

    def take_back(scatters, passed):
        for scatter in scatters:
            count = len(scatter.kept)
            scatter.kept, passed = passed[:count], passed[count:]

    low_grad, low_moments = half_back(0, [near_grads[0]] + sending(wide_scatter), [wide_scatter])
    high_grad, high_moments = half_back(1, [low_moments], [wide_scatter, near_scatter])
    wide_scatter.second()
    near_scatter.first()
    three_parts = place.total(low_moments, high_moments)
    three_totals = jnp.concatenate(three_parts, axis=1)

    middle_grad, *expand_grads = third_back(
        place,
        low_grad,
        high_grad,
        third,
        coef_three,
        three_totals / counted,
        validity,
        middle_act,
        bottle_all,
        meta,
        expand_at,
        quarters,
        turns,
        sending(near_scatter, wide_scatter),
        passing([near_scatter, wide_scatter]),
    )
    take_back([near_scatter, wide_scatter], expand_grads[parts:])
    expand_grads = expand_grads[:parts]
    wide_scatter.third()
    wide_scatter.launch()
    near_scatter.second()
    unit_two, pre_two = unit_of(second, coef_two)
    grad_two = middle_grad * silu_slope(pre_two)
    two_totals = place.total(grad_moments(grad_two, unit_two))
    second_grad = through_norm(
        grad_two, unit_two, coef_two, counted, validity, two_totals
    ).astype(BF16)
    spatial_rows = row_plan(bottle_taps, [0] * len(bottle_taps))
    spatial_grads = weight_grad(
        place,
        conv_flipped,
        second_grad,
        meta,
        spatial_rows,
        tiles,
        narrow,
        sending(wide_scatter, near_scatter),
        None,
        passing([wide_scatter, near_scatter]),
    )
    take_back([wide_scatter, near_scatter], spatial_grads[parts:])
    bottle_grads = [
        jnp.concatenate(pair, axis=1) for pair in zip(spatial_grads[:parts], expand_grads)
    ]
    bottle_rows = [narrow_rows] * (len(bottle_taps) + quarters)
    bottle_scatter = Scatter(place, bottle_grads, bottle_rows)
    near_scatter.third()
    grad_one, one_moments, *passed = spatial_back(
        second_grad,
        first,
        coef_one,
        validity,
        bottle_all,
        [spatial_rows[1], spatial_rows[0], spatial_rows[2]],
        [1, 0, 2],
        tiles,
        spatial_at,
        [spatial_grads[0]],
        passing([wide_scatter, near_scatter, bottle_scatter]) + near_scatter.sent,
    )
    held_back = len(passed) - len(near_scatter.sent)
    take_back([wide_scatter, near_scatter, bottle_scatter], passed[:held_back])
    near_scatter.sent = passed[held_back:]
    near_scatter.launch()
    if place.direct:
        one_moments = tied(one_moments, [bottle_scatter.arrived] + wide_scatter.arrived)
    bottle_scatter.first()
    one_totals = place.total(one_moments)
    unit_one, _ = unit_of(first, coef_one)
    first_grad = through_norm(
        grad_one, unit_one, coef_one, counted, validity, one_totals
    ).astype(BF16)
    reduce_grads = weight_grad(
        place,
        source_flipped,
        first_grad,
        meta,
        row_plan(point_taps, [0]),
        tiles,
        narrow,
        sending(bottle_scatter),
        None,
        passing([bottle_scatter, near_scatter]),
    )
    take_back([bottle_scatter, near_scatter], reduce_grads[parts:])
    reduce_scatter = Scatter(place, reduce_grads[:parts], [rows])
    bottle_scatter.second()

    def rows_back(first_turn, count, into, after, scatters):
        result, *passed = input_back(
            jnp.array(matrix.T, BF16),
            low_grad,
            high_grad,
            first_grad,
            bottle_all,
            turns,
            first_turn,
            count,
            after,
            passing(scatters),
            into,
        )
        take_back(scatters, passed)
        return result

    input_grad = rows_back(0, 2, None, sending(bottle_scatter), [bottle_scatter, reduce_scatter])
    reduce_scatter.first()
    bottle_scatter.third()
    bottle_scatter.launch()
    input_grad = rows_back(2, turns - 2, input_grad, sending(bottle_scatter, reduce_scatter), [bottle_scatter, reduce_scatter])
    reduce_scatter.second()
    reduce_scatter.third()
    reduce_scatter.launch()

    vectors = [one_totals, two_totals, three_totals, branch_totals, image_totals, head_totals]
    vectors += [image_partial]
    packed = jnp.concatenate([vector.reshape(-1) for vector in vectors])
    packed = packed + place.swap(packed)
    split, start = [], 0
    for vector in vectors:
        split.append(packed[start : start + vector.size].reshape(vector.shape))
        start += vector.size

    def own_part(vectors):
        vector = jnp.concatenate(vectors)
        length = vector.shape[0] // size
        return lax.dynamic_slice_in_dim(vector, place.index * length, length, axis=0)

    bottle_gain_grad = own_part([split[0][1], split[1][1], split[2][1]])
    bottle_shift_grad = own_part([split[0][0], split[1][0], split[2][0]])
    pyramid_gain_grad = own_part([split[3][1], split[4][1]])
    pyramid_shift_grad = own_part([split[3][0], split[4][0]])
    head_norm_grad = jnp.stack([own_part([split[5][1]]), own_part([split[5][0]])])
    image_out = split[6]

    def taps_out(full, taps, weight):
        full = full.reshape((len(taps),) + weight.shape[2:])
        if len(taps) == weight.shape[0] * weight.shape[1]:
            return full.reshape(weight.shape)
        result = jnp.zeros(weight.shape, F32)
        for at, tap in enumerate(taps):
            result = result.at[tap[0], tap[1]].set(full[at])
        return result

    for scatter in (near_scatter, wide_scatter, bottle_scatter, reduce_scatter):
        scatter.finish()
    near_count, middle_count, far_count = len(near_taps), len(middle_taps), len(far_taps)
    bottle_count = len(bottle_taps)
    expand_out = bottle_scatter.piece(bottle_count, quarters).reshape(quarters, narrow_rows, narrow)
    if place.direct:
        project_out, class_out = wide_scatter.extra([extra_rows - class_rows, class_rows])
    else:
        project_out = wide_scatter.piece(len(wide_rows) - 1, 1)
        class_out = own_part([lax.psum(class_grad, ("batch", "section"))])
    return (
        input_grad.reshape(features.shape),
        reduce_scatter.piece(0, 1),
        taps_out(bottle_scatter.piece(0, bottle_count), bottle_taps, spatial_weight),
        jnp.swapaxes(expand_out, 0, 1).reshape(expand_weight.shape),
        bottle_gain_grad,
        bottle_shift_grad,
        wide_scatter.piece(middle_count + far_count, 1),
        taps_out(near_scatter.piece(0, near_count), near_taps, near_weight),
        taps_out(wide_scatter.piece(0, middle_count), middle_taps, middle_weight),
        taps_out(wide_scatter.piece(middle_count, far_count), far_taps, far_weight),
        image_out,
        project_out,
        class_out.reshape(class_weight.shape),
        pyramid_gain_grad,
        pyramid_shift_grad,
        head_norm_grad,
    )


def solution(mesh):
    in_specs = (
        P("section", "batch", None, None, None),
        P("batch", None),
        P(None, None, "batch", None),
        P("batch", None),
        P("batch"),
        P("batch"),
        P("batch", None),
        P(None, None, "batch", None),
        P(None, None, "batch", None),
        P(None, None, "batch", None),
        P("batch", None),
        P("batch", None),
        P("batch", None),
        P("batch"),
        P("batch"),
        P("batch"),
        P("batch"),
        P(None, "batch", None, None),
        P(None, "batch"),
        P(None, "batch", None, None),
        P(),
    )
    out_specs = (
        P("section", "batch", None, None, None),
        P("batch", None),
        P(None, None, "batch", None),
        P("batch", None),
        P("batch"),
        P("batch"),
        P("batch", None),
        P(None, None, "batch", None),
        P(None, None, "batch", None),
        P(None, None, "batch", None),
        P("batch", None),
        P("batch", None),
        P("batch", None),
        P("batch"),
        P("batch"),
        P(None, "batch"),
    )
    return jax.shard_map(
        per_device, mesh=mesh, in_specs=in_specs, out_specs=out_specs, check_vma=False
    )
```

```python
import functools

import jax
import jax.numpy as jnp
import numpy as np
from jax import lax
from jax.experimental import pallas as pl
from jax.experimental.pallas import tpu as pltpu
from jax.sharding import PartitionSpec as P

CITY_CLASSES = 19
HOME_CLASSES = 13
BOTTLE_RATE = 4
NEAR_RATE = 12
MIDDLE_RATE = 24
FAR_RATE = 36
TILE = 4

EPSILON = 1e-05
FLOOR_LOGIT = -1e30
HIGHEST = lax.Precision.HIGHEST
F32 = jnp.float32
BF16 = jnp.bfloat16
SLOT_BITS = [0, 4, 2, 6, 1, 5, 3, 7, 8, 12, 9, 13, 10, 14, 11, 15]
VMEM_BYTES = 58 * 1024 * 1024


class Place:
    def __init__(self):
        self.size = lax.axis_size("batch")
        self.direct = self.size == len(SLOT_BITS)
        self.pieces = 2 * self.size if self.direct else 1
        self.core = lax.axis_index("section")
        self.index = lax.axis_index("batch")

    def meta(self):
        core = self.core[None].astype(jnp.int32)
        if not self.direct:
            return core
        table = [[SLOT_BITS.index(at ^ owner) for owner in range(self.size)] for at in range(self.size)]
        row = lax.dynamic_index_in_dim(jnp.array(table, jnp.int32), self.index, 0, keepdims=False)
        return jnp.concatenate([core, row])

    def flip(self, block, bits):
        return lax.ppermute(block, "batch", [(source, source ^ bits) for source in range(self.size)])

    def swap(self, block):
        return lax.ppermute(block, "section", [(0, 1), (1, 0)])

    def total(self, *arrays):
        if not self.direct:
            return lax.psum(arrays, "batch") if len(arrays) > 1 else lax.psum(arrays[0], "batch")
        summed = jnp.sum(self.everyone(jnp.concatenate([array.reshape(-1) for array in arrays])), axis=0)
        results, start = [], 0
        for array in arrays:
            results.append(summed[start : start + array.size].reshape(array.shape))
            start += array.size
        return results if len(arrays) > 1 else results[0]

    def everyone(self, vector):
        if not self.direct:
            return lax.all_gather(vector, "batch")
        sent = jnp.broadcast_to(vector, (self.size,) + vector.shape)
        return lax.all_to_all(sent, "batch", 0, 0)

    def gather(self, parts):
        blocks = []
        for part, count in parts:
            cut = part.reshape(count, -1, part.shape[1])
            if self.direct:
                half = cut.shape[1] // 2
                cut = lax.dynamic_slice_in_dim(cut, self.core * half, half, axis=1)
            else:
                cut = lax.all_gather(cut, "batch", axis=1, tiled=True)
            blocks.append(cut.reshape(-1, part.shape[1]))
        block = jnp.concatenate(blocks)
        if self.direct:
            return lax.all_gather(block, ("batch", "section"))
        return block[None]


class Scatter:
    def __init__(self, place, grads, rows):
        self.place, self.rows = place, rows
        self.kept, self.sent = [grads[0]], []
        self.paired = place.direct and len(grads) == 1
        self.settled = False
        self.arrived = place.swap(grads[1]) if len(grads) > 1 else None

    def add(self, kept, arrived):
        return (kept.astype(F32) + arrived.astype(F32)).astype(BF16)

    def first(self):
        if not self.place.direct:
            return
        own, arrived = self.kept[0], self.arrived
        if self.paired:
            self.kept = [own[:4], own[8:12]]
            self.sent = [own[4:8], own[12:]]
            self.arrived = [self.place.flip(self.sent[0], 1), self.place.flip(self.sent[1], 2)]
            return
        self.kept = []
        sent = []
        for start in (0, 8):
            self.kept.append(self.add(own[start : start + 4], arrived[start : start + 4]))
            sent.append(self.add(own[start + 4 : start + 8], arrived[start + 4 : start + 8]))
        self.sent = sent
        self.arrived = [self.place.flip(sent[0], 1), self.place.flip(sent[1], 2)]

    def second(self):
        if not self.place.direct:
            return
        kept, sent = [], []
        for held, came in zip(self.kept, self.arrived):
            kept.append(self.add(held[:2], came[:2]))
            sent.append(self.add(held[2:], came[2:]))
        self.kept, self.sent = kept, sent
        self.arrived = [self.place.flip(sent[0], 2), self.place.flip(sent[1], 1)]

    def third(self):
        if not self.place.direct:
            return
        near = self.kept[0].astype(F32) + self.arrived[0].astype(F32)
        away = self.kept[1].astype(F32) + self.arrived[1].astype(F32)
        self.kept = [near[0]]
        sent = [near[1].astype(BF16), away[0].astype(BF16), away[1].astype(BF16)]
        self.sent = sent

    def launch(self):
        if self.place.direct:
            self.arrived = [
                self.place.flip(piece, bits) for piece, bits in zip(self.sent, (4, 8, 12))
            ]

    def settle(self):
        if self.place.direct and not self.settled:
            parts = [piece.astype(F32) for piece in self.arrived]
            self.kept = [(self.kept[0] + parts[0]) + (parts[1] + parts[2])]
            self.settled = True

    def exchange(self):
        self.settle()
        if self.place.direct and len(self.kept) == 1:
            self.kept = [self.kept[0], self.place.swap(self.kept[0])]

    def finish(self):
        self.exchange()
        if self.place.direct:
            result, opposite = self.kept
            first = self.place.core == 0
            self.result = [jnp.where(first, result, opposite), jnp.where(first, opposite, result)]
            return self
        pieces, start = [], 0
        for rows in self.rows:
            cut = self.kept[0][0, start : start + rows * self.place.size].astype(F32)
            cut = lax.psum_scatter(cut, "batch", scatter_dimension=0, tiled=True)
            pieces.append(lax.psum(cut, "section"))
            start += rows * self.place.size
        self.result = [jnp.concatenate(pieces)]
        return self

    def extra(self, sizes):
        start = sum(self.rows[:-1]) // 2
        found = []
        for rows in sizes:
            found.append(jnp.concatenate([part[start : start + rows // 2] for part in self.result]))
            start += rows // 2
        return found

    def piece(self, first, count):
        parts = len(self.result)
        start = sum(self.rows[:first]) // parts
        rows = self.rows[first] // parts
        cut = [part[start : start + count * rows].reshape(count, rows, -1) for part in self.result]
        return jnp.concatenate(cut, axis=1).reshape(count * rows * parts, -1)


def call(body, args, specs, grid, outs, out_specs, scratch=(), meta=None, after=(), passed=(), into=None, flops=1):
    used = len(args) + (meta is not None)
    passed = list(passed) if into is None else [into] + list(passed)
    waits = len(after) + len(passed)
    results = len(outs)
    filled = int(into is not None)
    kept = results - filled

    def inner(*refs):
        rest = refs[used + waits :]
        body(*refs[:used], *rest[:results], *rest[results + len(passed) - filled :])

    spec = pltpu.PrefetchScalarGridSpec(
        num_scalar_prefetch=int(meta is not None),
        grid=grid,
        in_specs=list(specs) + [pl.BlockSpec(memory_space=pl.ANY)] * waits,
        out_specs=list(out_specs) + [pl.BlockSpec(memory_space=pl.ANY)] * (len(passed) - filled),
        scratch_shapes=list(scratch),
    )
    arrays = ([] if meta is None else [meta]) + list(args) + list(after) + list(passed)
    first = len(arrays) - len(passed)
    return pl.pallas_call(
        inner,
        grid_spec=spec,
        out_shape=list(outs) + [shaped(array.shape, array.dtype) for array in passed[filled:]],
        input_output_aliases={first + at: kept + at for at in range(len(passed))},
        compiler_params=pltpu.CompilerParams(vmem_limit_bytes=VMEM_BYTES),
        cost_estimate=pl.CostEstimate(flops=flops, transcendentals=0, bytes_accessed=1),
    )(*arrays)


def copy_body(source_ref, result_ref):
    result_ref[...] = source_ref[...]


def tied(array, after):
    return call(
        copy_body, [array], [whole(array)], (1,), [shaped(array.shape)], [held(array.shape)], after=after
    )[0]


def whole(array):
    shape = array.shape
    return pl.BlockSpec(
        shape, lambda *_: (0,) * len(shape), pipeline_mode=pl.Buffered(buffer_count=1)
    )


def held(shape):
    return pl.BlockSpec(shape, lambda *_: (0,) * len(shape))


def rows_of(array, rows):
    return pl.BlockSpec((rows, array.shape[1]), lambda step, *_: (step, 0))


def shaped(shape, dtype=F32):
    return jax.ShapeDtypeStruct(tuple(shape), dtype)


def span(shift_by, length):
    return max(0, -shift_by), length - max(0, shift_by)


def tap_list(height, breadth, dilation):
    listed = []
    for row_tap in range(3):
        for col_tap in range(3):
            row_shift = (row_tap - 1) * dilation
            col_shift = (col_tap - 1) * dilation
            if abs(row_shift) < height and abs(col_shift) < breadth:
                listed.append((row_tap, col_tap, row_shift // TILE, col_shift // TILE))
    return listed


def weight_of(ref):
    return ref[...].reshape(-1, ref.shape[-1])


def spread(meta_ref, full_ref, result_refs, column=0, at=0, rows=None):
    width = result_refs[0].shape[2]
    rows = result_refs[0].shape[1] if rows is None else rows
    if len(result_refs) == 1:
        result_refs[0][0, at : at + rows] = full_ref[:, column : column + width].astype(BF16)
        return
    core = meta_ref[0]
    for owner in range(result_refs[0].shape[0]):
        for ref, side in zip(result_refs, (core, 1 - core)):
            start = pl.multiple_of(owner * 2 * rows + side * rows, rows)
            block = full_ref[pl.ds(start, rows), column : column + width]
            ref[meta_ref[1 + owner], at : at + rows] = block.astype(BF16)


def slotted(place, rows, width):
    if place.direct:
        return [shaped((place.size, rows // 2, width), BF16)] * 2
    return [shaped((1, rows * place.size, width), BF16)]


def center_first(step, center):
    return jnp.where(step == 0, center, jnp.where(step <= center, step - 1, step))


def ordered(taps, center):
    return [taps[center]] + [tap for place, tap in enumerate(taps) if place != center]


def shifts_of(taps):
    return [(tap[2], tap[3]) for tap in taps]


def area(tap, tiles):
    return (tiles[0] - abs(tap[0])) * (tiles[1] - abs(tap[1])) * tiles[2]


def forward_tap(tap, fresh, source_ref, weight, result_ref):
    tiles_i, tiles_j, pixels, channels = source_ref.shape
    columns = weight.shape[1]
    shift_i, shift_j = tap
    low_i, high_i = span(shift_i, tiles_i)
    low_j, high_j = span(shift_j, tiles_j)
    window = source_ref[
        low_i + shift_i : high_i + shift_i, low_j + shift_j : high_j + shift_j
    ].reshape(-1, channels)
    product = jnp.dot(window, weight, preferred_element_type=F32)
    product = product.reshape(high_i - low_i, high_j - low_j, pixels, columns)
    if fresh:
        result_ref[low_i:high_i, low_j:high_j] = product
    else:
        result_ref[low_i:high_i, low_j:high_j] += product


def repeat(count, body):
    lax.fori_loop(0, count, lambda turn, carry: (body(turn), carry)[1], 0)


def row_steps(count):
    return max(step for step in (1, 2, 3, 4) if count % step == 0)


FIELDS = 9


def tap_table(plan, tiles, places):
    table, classes = [], []
    for ((shift_i, shift_j), column), place in zip(plan, places):
        low_i, high_i = span(shift_i, tiles[0])
        low_j, high_j = span(shift_j, tiles[1])
        kind = (row_steps(high_i - low_i), high_j - low_j)
        if kind not in classes:
            classes.append(kind)
        table += [classes.index(kind), low_i, low_i + shift_i, (high_i - low_i) // kind[0]]
        table += [low_j, low_j + shift_j, column, place, 0]
    return np.array(table, np.int32), classes


def forward_taps(classes, table_ref, source_ref, weight_ref, result_ref):
    _, _, pixels, channels = source_ref.shape
    width = weight_ref.shape[2]
    at = pl.program_id(0) * FIELDS
    for kind, (rows, wide) in enumerate(classes):

        @pl.when(table_ref[at] == kind)
        def _(rows=rows, wide=wide):
            to_i, from_i, turns = table_ref[at + 1], table_ref[at + 2], table_ref[at + 3]
            to_j, from_j = table_ref[at + 4], table_ref[at + 5]
            column = pl.multiple_of(table_ref[at + 6], width)

            def body(turn):
                window = source_ref[pl.ds(from_i + turn * rows, rows), pl.ds(from_j, wide)]
                product = jnp.dot(
                    window.reshape(-1, channels), weight_of(weight_ref), preferred_element_type=F32
                )
                place = (
                    pl.ds(to_i + turn * rows, rows),
                    pl.ds(to_j, wide),
                    slice(None),
                    pl.ds(column, width),
                )
                result_ref[place] += product.reshape(rows, wide, pixels, width)

            repeat(turns, body)


def unit_of(values, coef):
    unit = (values - coef[0:1]) * coef[1:2]
    return unit, coef[2:3] * unit + coef[3:4]


def masked_sums(values, valid):
    weighted = values * valid
    return jnp.concatenate(
        [jnp.sum(weighted, axis=0, keepdims=True), jnp.sum(weighted * values, axis=0, keepdims=True)]
    )


def sum_rows(ref, valid_ref, sums_ref):
    total = jnp.zeros(sums_ref.shape, F32)
    for row in range(ref.shape[0]):
        values = ref[row].reshape(-1, ref.shape[-1])
        total = total + masked_sums(values, valid_ref[row].reshape(-1, 1))
    sums_ref[...] = total


def branch_body(classes, table_ref, source_ref, valid_ref, weight_ref, result_ref, sums_ref):
    @pl.when(pl.program_id(0) == 0)
    def _():
        def clear(row):
            result_ref[row] = jnp.zeros(result_ref.shape[1:], F32)

        repeat(result_ref.shape[0], clear)

    forward_taps(classes, table_ref, source_ref, weight_ref, result_ref)

    @pl.when(pl.program_id(0) == pl.num_programs(0) - 1)
    def _():
        sum_rows(result_ref, valid_ref, sums_ref)


def placed_block(weights, channels):
    pieces, _, width = weights.shape
    return pl.BlockSpec(
        (pieces, channels // pieces, width), lambda step, table: (0, table[step * FIELDS + 7], 0)
    )


def branch_convs(source, valid, weights, groups, columns, after):
    channels = source.shape[-1]
    plan = [(shift, column) for taps, column in groups for shift in shifts_of(taps)]
    table, classes = tap_table(plan, source.shape, range(len(plan)))
    result_shape = source.shape[:3] + (columns,)
    return call(
        functools.partial(branch_body, classes),
        [source, valid, weights],
        [whole(source), whole(valid), placed_block(weights, channels)],
        (len(plan),),
        [shaped(result_shape), shaped((2, columns))],
        [held(result_shape), held((2, columns))],
        meta=jnp.array(table),
        after=after,
    )


def spatial_body(plan, first_ref, coef_ref, valid_ref, weight_ref, input_ref, result_ref, sums_ref):
    @pl.when(pl.program_id(0) == 0)
    def _():
        for row in range(first_ref.shape[0]):
            _, pre = unit_of(first_ref[row], coef_ref[...][:, None, :])
            input_ref[row] = (silu(pre) * valid_ref[row]).astype(BF16)

    for place, tap in enumerate(plan):

        @pl.when(pl.program_id(0) == place)
        def _(place=place, tap=tap):
            forward_tap(tap, place == 0, input_ref, weight_of(weight_ref), result_ref)

    @pl.when(pl.program_id(0) == len(plan) - 1)
    def _():
        sum_rows(result_ref, valid_ref, sums_ref)


def spatial_conv(first, coef, valid, weights, taps, center, first_tap):
    channels = first.shape[-1]
    pieces, _, columns = weights.shape
    plan = ordered(shifts_of(taps), center)
    return call(
        functools.partial(spatial_body, plan),
        [first, coef, valid, weights],
        [
            whole(first),
            whole(coef),
            whole(valid),
            pl.BlockSpec(
                (pieces, channels // pieces, columns),
                lambda step: (0, first_tap + center_first(step, center), 0),
            ),
        ],
        (len(plan),),
        [shaped(first.shape, BF16), shaped(first.shape), shaped((2, columns))],
        [held(first.shape), held(first.shape), held((2, columns))],
    )


def shifted_columns(tiles, row_taps, up_ref, padded_ref, width, first=None, last=None):
    tiles_i, tiles_j, pixels = tiles
    shift_i, columns = row_taps
    low_i, high_i = span(shift_i, tiles_i)
    line = tiles_j * pixels
    low, high = (low_i + shift_i) * line, (high_i + shift_i) * line

    def clear(start, stop, at):
        if stop > start:
            padded_ref[start:stop, at : at + width] = jnp.zeros((stop - start, width), BF16)

    for place, (shift_j, column) in enumerate(columns):
        at = place * width
        low_j, high_j = span(shift_j, tiles_j)
        begin, end = (low_j + shift_j) * pixels, (high_j + shift_j) * pixels
        for row in range(low_i, high_i):
            base = (row + shift_i) * line
            source = row * line + low_j * pixels
            clear(base, base + begin, at)
            padded_ref[base + begin : base + end, at : at + width] = up_ref[
                source : source + end - begin, column : column + width
            ]
            clear(base + end, base + line, at)
        if first is not None:
            clear(first, low, at)
            clear(high, last, at)
    return low, high


def back_step(tiles, row_taps, fresh, up_ref, weight_refs, padded_ref, weight_ref, total_ref):
    channels = total_ref.shape[1]
    width = weight_refs[0].shape[2]
    depth = len(row_taps[1]) * width
    low, high = shifted_columns(tiles, row_taps, up_ref, padded_ref, width)
    for place in range(len(row_taps[1])):
        weight_ref[:, place * width : (place + 1) * width] = weight_of(weight_refs[place])
    wide = min(512, channels)
    for start in range(0, channels, wide):
        product = lax.dot_general(
            padded_ref[low:high, :depth],
            weight_ref[start : start + wide, :depth],
            (((1,), (1,)), ((), ())),
            preferred_element_type=F32,
        )
        if fresh:
            total_ref[low:high, start : start + wide] = product
        else:
            total_ref[low:high, start : start + wide] += product


def row_plan(taps, columns):
    rows = []
    for tap, column in zip(taps, columns):
        if not rows or rows[-1][0] != tap[2]:
            rows.append((tap[2], []))
        rows[-1][1].append((tap[3], column))
    return rows


def row_weights(weights, channels, order, first_tap, side=0, sides=1):
    pieces, _, width = weights.shape
    rows = channels // pieces
    specs = []
    for column in range(3):

        def index(step, column=column):
            row = order[-1]
            for place, listed in enumerate(order[:-1]):
                row = jnp.where(step == place, listed, row)
            tap = first_tap + 3 * row + column
            return (0, tap * sides + side, 0) if pieces == 1 else (side, tap, 0)

        block = (1, rows // sides, width) if pieces == 1 else (pieces // sides, rows, width)
        specs.append(pl.BlockSpec(block, index))
    return specs


def grad_moments(grad, unit):
    return jnp.concatenate(
        [jnp.sum(grad, axis=0, keepdims=True), jnp.sum(grad * unit, axis=0, keepdims=True)]
    )


def feature_body(
    plan, tiles, up_ref, third_ref, source_ref, coef_ref, pooled_ref, valid_ref, *refs
):
    weight_refs = refs[:4]
    result_ref, sums_ref, padded_ref, weight_ref, total_ref = refs[4:]
    step_now = pl.program_id(0)
    for place, row_taps in enumerate(plan):

        @pl.when(step_now == place)
        def _(place=place, row_taps=row_taps):
            back_step(
                tiles, row_taps, place == 0, up_ref, weight_refs, padded_ref, weight_ref, total_ref
            )

    begun = len(plan)

    @pl.when(step_now >= begun)
    def _():
        height = third_ref.shape[0]
        row = pl.multiple_of((step_now - begun) * height, height)
        unit, pre = unit_of(third_ref[...], coef_ref[...])
        pre = pre + source_ref[...].astype(F32)
        grad = total_ref[pl.ds(row, height)] + pooled_ref[...]
        grad = grad * valid_ref[...] * silu_slope(pre)
        result_ref[...] = grad.astype(BF16)
        moments = grad_moments(grad, unit)

        @pl.when(step_now == begun)
        def _():
            sums_ref[...] = moments

        @pl.when(step_now > begun)
        def _():
            sums_ref[...] += moments


def feature_back(upstream, weights, plan, order, point, third, source, coef, pooled, valid, tiles, side, sides, after, passed):
    pixels, channels = third.shape
    part = channels // sides
    pieces, _, width = weights.shape
    rows = channels // pieces
    begun = len(plan)
    turns = tiles[0]
    height = pixels // turns

    def row_of(step):
        return jnp.clip(step - begun, 0, turns - 1)

    row_block = pl.BlockSpec((height, part), lambda step: (row_of(step), side))
    if pieces == 1:
        point_block = pl.BlockSpec((1, rows // sides, width), lambda step: (0, point * sides + side, 0))
    else:
        point_block = pl.BlockSpec((pieces // sides, rows, width), lambda step: (side, point, 0))
    return call(
        functools.partial(feature_body, plan, tiles),
        [upstream, third, source, coef, pooled, valid] + [weights] * 4,
        [
            whole(upstream),
            row_block,
            row_block,
            pl.BlockSpec((coef.shape[0], part), lambda step: (0, side)),
            pl.BlockSpec((1, part), lambda step: (0, side)),
            pl.BlockSpec((height, 1), lambda step: (row_of(step), 0)),
        ]
        + row_weights(weights, channels, order, 0, side, sides)
        + [point_block],
        (begun + turns,),
        [shaped((pixels, part), BF16), shaped((2, part))],
        [pl.BlockSpec((height, part), lambda step: (row_of(step), 0)), held((2, part))],
        [
            pltpu.VMEM((pixels, 4 * width), BF16),
            pltpu.VMEM((part, 4 * width), BF16),
            pltpu.VMEM((pixels, part), F32),
        ],
        after=after,
        passed=passed,
    )


def spatial_back_body(plan, tiles, up_ref, first_ref, coef_ref, valid_ref, *refs):
    weight_refs = refs[:3]
    result_ref, sums_ref, padded_ref, weight_ref = refs[3:]
    for place, row_taps in enumerate(plan):

        @pl.when(pl.program_id(0) == place)
        def _(place=place, row_taps=row_taps):
            back_step(
                tiles, row_taps, place == 0, up_ref, weight_refs, padded_ref, weight_ref, result_ref
            )

    @pl.when(pl.program_id(0) == len(plan) - 1)
    def _():
        total = jnp.zeros(sums_ref.shape, F32)
        height = result_ref.shape[0] // tiles[0]
        for row in range(tiles[0]):
            at = slice(row * height, (row + 1) * height)
            unit, pre = unit_of(first_ref[at], coef_ref[...])
            grad = result_ref[at] * valid_ref[at] * silu_slope(pre)
            result_ref[at] = grad
            total = total + grad_moments(grad, unit)
        sums_ref[...] = total


def spatial_back(upstream, first, coef, valid, weights, plan, order, tiles, first_tap, after, passed):
    pixels, channels = first.shape
    columns = weights.shape[2]
    return call(
        functools.partial(spatial_back_body, plan, tiles),
        [upstream, first, coef, valid] + [weights] * 3,
        [whole(upstream), whole(first), whole(coef), whole(valid)]
        + row_weights(weights, channels, order, first_tap),
        (len(plan),),
        [shaped(first.shape), shaped((2, channels))],
        [held(first.shape), held((2, channels))],
        [pltpu.VMEM((pixels, 3 * columns), BF16), pltpu.VMEM((channels, 3 * columns), BF16)],
        after=after,
        passed=passed,
    )


def weight_body(plan, tiles, extra, count, meta_ref, flipped_ref, up_ref, *refs):
    extra_ref = refs[0] if extra else None
    result_refs = refs[extra : extra + count]
    padded_ref, full_ref = refs[extra + count :]
    block_rows, width = result_refs[0].shape[1:]
    taps_held = padded_ref.shape[1] // width
    rows = block_rows // taps_held
    for place, row_taps in enumerate(plan):

        @pl.when(pl.program_id(0) == place)
        def _(row_taps=row_taps):
            taps = len(row_taps[1])
            low_i, high_i = span(row_taps[0], tiles[0])
            line = tiles[1] * tiles[2]
            first = (low_i + row_taps[0]) * line // 128 * 128
            last = -(-(high_i + row_taps[0]) * line // 128) * 128
            shifted_columns(tiles, row_taps, up_ref, padded_ref, width, first, last)
            for tap in range(taps):
                at = slice(tap * width, (tap + 1) * width)
                full_ref[:, at] = jnp.dot(
                    flipped_ref[:, first:last], padded_ref[first:last, at], preferred_element_type=F32
                ).astype(BF16)
                spread(meta_ref, full_ref, result_refs, tap * width, tap * rows, rows)

    if extra:

        @pl.when(pl.program_id(0) == len(plan) - 1)
        def _():
            core = meta_ref[0]
            taps = len(plan[-1][1])
            spare = (taps_held - taps - 1) * rows
            for owner in range(result_refs[0].shape[0]):
                slot = meta_ref[1 + owner]
                for ref, side in zip(result_refs, (core, 1 - core)):
                    start = pl.multiple_of((owner * 2 + side) * rows, rows)
                    ref[slot, taps * rows : (taps + 1) * rows] = extra_ref[pl.ds(start, rows)]
                    ref[slot, (taps + 1) * rows :] = jnp.zeros((spare, width), BF16)


def weight_grad(place, flipped, upstream, meta, plan, tiles, width, after=(), extra=None, passed=()):
    channels, padded = flipped.shape
    taps = max(len(row_taps[1]) for row_taps in plan)
    steps = len(plan)
    shapes = slotted(place, channels // place.size * taps * steps, width)
    blocks = [
        pl.BlockSpec((shape.shape[0], shape.shape[1] // steps, width), lambda step, _: (0, step, 0))
        for shape in shapes
    ]
    more = [] if extra is None else [extra]
    return call(
        functools.partial(weight_body, plan, tiles, len(more), len(shapes)),
        [flipped, upstream] + more,
        [whole(array) for array in [flipped, upstream] + more],
        (steps,),
        shapes,
        blocks,
        [pltpu.VMEM((padded, taps * width), BF16), pltpu.VMEM((channels, taps * width), BF16)],
        meta,
        after,
        passed,
    )


def paired_body(plan, tiles, extra, meta_ref, flipped_ref, mate_ref, up_ref, mate_up_ref, *refs):
    extra_ref = refs[0] if extra else None
    result_ref, padded_ref, mate_padded_ref, full_ref = refs[extra:]
    block_rows, width = result_ref.shape[1:]
    taps_held = padded_ref.shape[1] // width
    rows = block_rows // taps_held
    for place, row_taps in enumerate(plan):

        @pl.when(pl.program_id(0) == place)
        def _(row_taps=row_taps):
            low_i, high_i = span(row_taps[0], tiles[0])
            line = tiles[1] * tiles[2]
            first = (low_i + row_taps[0]) * line // 128 * 128
            last = -(-(high_i + row_taps[0]) * line // 128) * 128
            shifted_columns(tiles, row_taps, up_ref, padded_ref, width, first, last)
            shifted_columns(tiles, row_taps, mate_up_ref, mate_padded_ref, width, first, last)
            for tap in range(len(row_taps[1])):
                at = slice(tap * width, (tap + 1) * width)
                total = jnp.dot(
                    flipped_ref[:, first:last], padded_ref[first:last, at], preferred_element_type=F32
                ) + jnp.dot(
                    mate_ref[:, first:last], mate_padded_ref[first:last, at], preferred_element_type=F32
                )
                full_ref[:, at] = total.astype(BF16)
                for owner in range(result_ref.shape[0]):
                    result_ref[meta_ref[1 + owner], tap * rows : (tap + 1) * rows] = full_ref[
                        owner * rows : (owner + 1) * rows, at
                    ]

    if extra:

        @pl.when(pl.program_id(0) == len(plan) - 1)
        def _():
            taps = len(plan[-1][1])
            spare = (taps_held - taps - 1) * rows
            for owner in range(result_ref.shape[0]):
                slot = meta_ref[1 + owner]
                result_ref[slot, taps * rows : (taps + 1) * rows] = extra_ref[
                    owner * rows : (owner + 1) * rows
                ]
                result_ref[slot, (taps + 1) * rows :] = jnp.zeros((spare, width), BF16)


def paired_grad(place, flipped, mate, upstream, mate_upstream, meta, plan, tiles, width, after, extra, passed):
    channels, padded = flipped.shape
    taps = max(len(row_taps[1]) for row_taps in plan)
    rows = channels // place.size * taps
    more = [] if extra is None else [extra]
    args = [flipped, mate, upstream, mate_upstream] + more
    return call(
        functools.partial(paired_body, plan, tiles, len(more)),
        args,
        [whole(array) for array in args],
        (len(plan),),
        [shaped((place.size, rows * len(plan), width), BF16)],
        [pl.BlockSpec((place.size, rows, width), lambda step, _: (0, step, 0))],
        [
            pltpu.VMEM((padded, taps * width), BF16),
            pltpu.VMEM((padded, taps * width), BF16),
            pltpu.VMEM((channels, taps * width), BF16),
        ],
        meta,
        after,
        passed,
    )


def tile_matrix(breadth):
    count = TILE * breadth
    matrix = np.zeros((count, count), np.float32)
    for row in range(TILE):
        for column in range(breadth):
            at = (column // TILE * TILE + row) * TILE + column % TILE
            matrix[at, row * breadth + column] = 1.0
    return matrix


def tile_body(matrix_ref, natural_ref, result_ref):
    result_ref[...] = jnp.dot(
        matrix_ref[...], natural_ref[...], preferred_element_type=F32
    ).astype(BF16)


def tile_rows(natural, matrix):
    rows = matrix.shape[0]
    return call(
        tile_body,
        [matrix, natural],
        [whole(matrix), rows_of(natural, rows)],
        (natural.shape[0] // rows,),
        [shaped(natural.shape, BF16)],
        [rows_of(natural, rows)],
    )[0]


def flip_body(source_ref, result_ref):
    pixels = source_ref.shape[0]
    result_ref[:, :pixels] = source_ref[...].T
    if result_ref.shape[1] > pixels:
        extra = result_ref.shape[1] - pixels
        result_ref[:, pixels:] = jnp.zeros((result_ref.shape[0], extra), BF16)


def flipped(values, after=()):
    pixels, channels = values.shape
    padded = pixels + -pixels % 128
    return call(
        flip_body,
        [values],
        [pl.BlockSpec((pixels, 128), lambda step: (0, step))],
        (channels // 128,),
        [shaped((channels, padded), BF16)],
        [pl.BlockSpec((128, padded), lambda step: (step, 0))],
        after=after,
    )[0]


def flip_halves_body(meta_ref, source_ref, own_ref, other_ref, turned_ref):
    flip_body(source_ref, turned_ref)
    rows = own_ref.shape[0]
    core = meta_ref[0]
    own_ref[...] = turned_ref[pl.ds(pl.multiple_of(core * rows, rows), rows)]
    other_ref[...] = turned_ref[pl.ds(pl.multiple_of((1 - core) * rows, rows), rows)]


def flipped_halves(values, meta, after):
    pixels, channels = values.shape
    padded = pixels + -pixels % 128
    block = pl.BlockSpec((64, padded), lambda step, _: (step, 0))
    return call(
        flip_halves_body,
        [values],
        [pl.BlockSpec((pixels, 128), lambda step, _: (0, step))],
        (channels // 128,),
        [shaped((channels // 2, padded), BF16)] * 2,
        [block, block],
        [pltpu.VMEM((128, padded), BF16)],
        meta,
        after,
    )


def add_sums(sums_ref, sums):
    @pl.when(pl.program_id(0) == 0)
    def _():
        sums_ref[...] = sums

    @pl.when(pl.program_id(0) > 0)
    def _():
        sums_ref[...] += sums


def first_body(source_ref, valid_ref, weight_ref, result_ref, sums_ref):
    product = jnp.dot(source_ref[...], weight_of(weight_ref), preferred_element_type=F32)
    result_ref[...] = product
    add_sums(sums_ref, masked_sums(product, valid_ref[...]))


def fixed_block(weights, channels, at):
    pieces, _, columns = weights.shape
    return pl.BlockSpec((pieces, channels // pieces, columns), lambda step, *_: (0, at, 0))


def first_conv(source, valid, weights, turns, after):
    pixels, channels = source.shape
    rows = pixels // turns
    width = weights.shape[2]
    return call(
        first_body,
        [source, valid, weights],
        [rows_of(source, rows), rows_of(valid, rows), fixed_block(weights, channels, 0)],
        (turns,),
        [shaped((pixels, width)), shaped((2, width))],
        [pl.BlockSpec((rows, width), lambda step: (step, 0)), held((2, width))],
        after=after,
    )


def third_body(count, second_ref, coef_ref, valid_ref, *refs):
    weight_refs = refs[:count]
    middle_ref, result_ref, sums_ref = refs[count:]
    _, pre = unit_of(second_ref[...], coef_ref[...])
    middle = silu(pre).astype(BF16)
    middle_ref[...] = middle
    valid = valid_ref[...]
    sums = []
    for quarter, ref in enumerate(weight_refs):
        product = jnp.dot(middle, weight_of(ref), preferred_element_type=F32)
        width = product.shape[1]
        result_ref[:, quarter * width : (quarter + 1) * width] = product
        sums.append(masked_sums(product, valid))
    add_sums(sums_ref, jnp.concatenate(sums, axis=1))


def third_conv(second, coef, valid, weights, first, count, turns):
    pixels, narrow = second.shape
    height = pixels // turns
    channels = count * weights.shape[2]
    return call(
        functools.partial(third_body, count),
        [second, coef, valid] + [weights] * count,
        [rows_of(second, height), whole(coef), rows_of(valid, height)]
        + [fixed_block(weights, narrow, first + quarter) for quarter in range(count)],
        (turns,),
        [shaped((pixels, narrow), BF16), shaped((pixels, channels)), shaped((2, channels))],
        [
            pl.BlockSpec((height, narrow), lambda step: (step, 0)),
            pl.BlockSpec((height, channels), lambda step: (step, 0)),
            held((2, channels)),
        ],
    )


def output_body(third_ref, source_ref, coef_ref, valid_ref, result_ref, sums_ref):
    _, pre = unit_of(third_ref[...], coef_ref[...])
    values = (valid_ref[...] * silu(pre + source_ref[...].astype(F32))).astype(BF16)
    result_ref[...] = values
    add_sums(sums_ref, jnp.sum(values.astype(F32), axis=0, keepdims=True))


def block_output(third, source, coef, valid, turns):
    pixels, channels = third.shape
    rows = pixels // turns
    return call(
        output_body,
        [third, source, coef, valid],
        [rows_of(third, rows), rows_of(source, rows), whole(coef), rows_of(valid, rows)],
        (turns,),
        [shaped(third.shape, BF16), shaped((1, channels))],
        [rows_of(third, rows), held((1, channels))],
    )


def third_back_body(
    count, outs, meta_ref, low_ref, high_ref, third_ref, coef_ref, totals_ref, valid_ref, middle_ref, *refs
):
    weight_refs = refs[:count]
    result_ref = refs[count]
    slot_refs = refs[count + 1 : count + 1 + outs]
    grad_ref, total_ref = refs[count + 1 + outs :]
    step_now = pl.program_id(0)

    @pl.when(step_now == 0)
    def _():
        total_ref[...] = jnp.zeros_like(total_ref)

    part = low_ref.shape[1]
    coef, totals, valid = coef_ref[...], totals_ref[...], valid_ref[...]
    for start, part_ref in ((0, low_ref), (part, high_ref)):
        at = slice(start, start + part)
        unit = (third_ref[:, at] - coef[0:1, at]) * coef[1:2, at]
        centered = part_ref[...].astype(F32) - valid * (totals[0:1, at] + unit * totals[1:2, at])
        grad_ref[:, at] = (coef[2:3, at] * coef[1:2, at] * centered).astype(BF16)
    width = weight_refs[0].shape[2]
    result = None
    for quarter, ref in enumerate(weight_refs):
        grad = grad_ref[:, quarter * width : (quarter + 1) * width]
        product = lax.dot_general(
            grad, weight_of(ref), (((1,), (1,)), ((), ())), preferred_element_type=F32
        )
        result = product if result is None else result + product
    result_ref[...] = result
    total_ref[...] += lax.dot_general(
        middle_ref[...], grad_ref[...], (((0,), (0,)), ((), ())), preferred_element_type=F32
    )

    @pl.when(step_now == pl.num_programs(0) - 1)
    def _():
        rows = slot_refs[0].shape[1] // count
        for quarter in range(count):
            spread(meta_ref, total_ref, slot_refs, quarter * width, quarter * rows, rows)


def third_back(place, low, high, third, coef, totals, valid, middle, weights, meta, first, count, turns, after, passed):
    pixels, channels = third.shape
    narrow = middle.shape[1]
    height = pixels // turns
    shapes = slotted(place, narrow // place.size * count, weights.shape[2])
    return call(
        functools.partial(third_back_body, count, len(shapes)),
        [low, high, third, coef, totals, valid, middle] + [weights] * count,
        [
            rows_of(low, height),
            rows_of(high, height),
            rows_of(third, height),
            whole(coef),
            whole(totals),
            rows_of(valid, height),
            rows_of(middle, height),
        ]
        + [fixed_block(weights, narrow, first + quarter) for quarter in range(count)],
        (turns,),
        [shaped((pixels, narrow))] + shapes,
        [pl.BlockSpec((height, narrow), lambda step, _: (step, 0))] + [held(shape.shape) for shape in shapes],
        [pltpu.VMEM((height, channels), BF16), pltpu.VMEM((narrow, channels), F32)],
        meta,
        after,
        passed,
    )


def input_body(matrix_ref, low_ref, high_ref, grad_ref, weight_ref, result_ref):
    rows = matrix_ref.shape[0]
    part = low_ref.shape[1]
    matrix = matrix_ref[...]
    moved = []
    for start in range(0, result_ref.shape[0], rows):
        at = slice(start, start + rows)
        moved.append(jnp.dot(matrix, grad_ref[at], preferred_element_type=F32).astype(BF16))
        for column, part_ref in ((0, low_ref), (part, high_ref)):
            result_ref[at, column : column + part] = jnp.dot(
                matrix, part_ref[at], preferred_element_type=F32
            )
    result_ref[...] += lax.dot_general(
        jnp.concatenate(moved), weight_of(weight_ref), (((1,), (1,)), ((), ())), preferred_element_type=F32
    )


def input_back(matrix, low, high, grad, weights, turns, first, count, after, passed, into):
    pixels, part = low.shape
    rows = pixels // turns
    channels = 2 * part
    width = grad.shape[1]

    def block(columns):
        return pl.BlockSpec((rows, columns), lambda step: (first + step, 0))

    return call(
        input_body,
        [matrix, low, high, grad, weights],
        [whole(matrix), block(part), block(part), block(width), fixed_block(weights, channels, 0)],
        (count,),
        [shaped((pixels, channels))],
        [block(channels)],
        after=after,
        passed=passed,
        into=into,
        flops=10**10,
    )


def sigmoid(values):
    return 0.5 + 0.5 * jnp.tanh(0.5 * values)


def silu(values):
    return values * sigmoid(values)


def silu_slope(values):
    sigmoid_val = sigmoid(values)
    return sigmoid_val * (1.0 + values * (1.0 - sigmoid_val))


def sums(values, validity):
    weighted = values * validity
    return jnp.stack([jnp.sum(weighted, axis=0), jnp.sum(weighted * values, axis=0)])


def coefs(totals, counted, gain, shift):
    mean_value = totals[0] / counted
    scaling = lax.rsqrt(totals[1] / counted - mean_value * mean_value + EPSILON)
    return jnp.stack([mean_value, scaling, gain, shift])


def through_norm(grad_pre, unit, coef, counted, validity, totals):
    centered = grad_pre - validity * (totals[0] + unit * totals[1]) / counted
    return coef[2] * coef[1] * centered


def to_tiles(array):
    height, breadth = array.shape[:2]
    rest = array.shape[2:]
    cut = array.reshape((height // TILE, TILE, breadth // TILE, TILE) + rest)
    return jnp.swapaxes(cut, 1, 2).reshape((height * breadth,) + rest)


def per_device(
    features,
    reduce_weight,
    spatial_weight,
    expand_weight,
    bottle_gain,
    bottle_shift,
    point_weight,
    near_weight,
    middle_weight,
    far_weight,
    image_weight,
    project_weight,
    class_weight,
    pyramid_gain,
    pyramid_shift,
    head_gain,
    head_shift,
    crop_masks,
    crop_tasks,
    pixel_labels,
    task_norms,
):
    place = Place()
    size, core = place.size, place.core
    first_core = core == 0
    height, breadth, channels = features.shape[2:]
    pixels = height * breadth
    tiles = (height // TILE, breadth // TILE, TILE * TILE)
    narrow = reduce_weight.shape[1]
    branch = point_weight.shape[1]
    four_wide = 4 * branch
    rows = channels // size
    narrow_rows = narrow // size
    quarters = channels // narrow
    turns = 3
    meta = place.meta()
    matrix = tile_matrix(breadth)

    bottle_taps = tap_list(height, breadth, BOTTLE_RATE)
    near_taps = tap_list(height, breadth, NEAR_RATE)
    middle_taps = tap_list(height, breadth, MIDDLE_RATE)
    far_taps = tap_list(height, breadth, FAR_RATE)
    point_taps = [(1, 1, 0, 0)]

    def center_of(taps):
        return [tap[:2] for tap in taps].index((1, 1))

    def stacked(weight, taps):
        flat = weight.reshape((-1,) + weight.shape[2:])
        picked = [3 * tap[0] + tap[1] for tap in taps]
        if picked == list(range(picked[0], picked[-1] + 1)):
            flat = flat[picked[0] : picked[-1] + 1]
        else:
            flat = jnp.stack([flat[at] for at in picked])
        return flat.reshape(-1, flat.shape[2]), len(taps)

    mask = lax.dynamic_index_in_dim(crop_masks, core, 0, keepdims=False)[0]
    labels = lax.dynamic_index_in_dim(pixel_labels, core, 0, keepdims=False)[0]
    task = lax.dynamic_index_in_dim(crop_tasks, core, 0, keepdims=False)[0]
    validity = to_tiles(mask).astype(F32)[:, None]
    valid_tiles = validity.reshape(tiles + (1,))
    labels = to_tiles(labels)
    source = tile_rows(features.reshape(pixels, channels), jnp.array(matrix, BF16))
    source_flipped = flipped(source)

    wide_expand = expand_weight.reshape(-1, quarters, narrow)
    expand_parts = [(wide_expand[:, at], 1) for at in range(quarters)]
    bottle_all = place.gather([(reduce_weight, 1), stacked(spatial_weight, bottle_taps)] + expand_parts)
    spatial_at = channels // narrow
    expand_at = spatial_at + len(bottle_taps)
    pyramid_parts = [stacked(near_weight, near_taps), stacked(middle_weight, middle_taps)]
    pyramid_parts += [stacked(far_weight, far_taps), (point_weight, 1), (project_weight, 1)]
    pyramid_all = place.gather(pyramid_parts)
    middle_at = len(near_taps)
    far_at = middle_at + len(middle_taps)
    point_at = far_at + len(far_taps)
    project_at = (point_at + 1) * (channels // place.pieces)
    project_full = pyramid_all[:, project_at:].reshape(-1, branch)

    crop_valid_both = jnp.sum(crop_masks, axis=(1, 2, 3)).astype(F32)
    home_crop = (crop_tasks[:, 0] == 1).astype(F32)
    counts = jnp.concatenate(
        [
            crop_valid_both,
            jnp.sum(crop_valid_both * (1.0 - home_crop))[None],
            jnp.sum(crop_valid_both * home_crop)[None],
        ]
    )
    small = [bottle_gain, bottle_shift, pyramid_gain, pyramid_shift, head_gain, head_shift]
    small.append(class_weight.reshape(-1))
    small_widths = [part.shape[0] for part in small]
    small_own = jnp.concatenate(small).astype(F32)
    collected = place.everyone(jnp.concatenate([small_own, counts]))
    counts_all = jnp.sum(collected[:, small_own.size :], axis=0)
    small_all, start = [], 0
    for width in small_widths:
        small_all.append(collected[:, start : start + width].reshape(-1))
        start += width
    gain_bottle, shift_bottle, gain_pyramid, shift_pyramid, gain_head, shift_head = small_all[:6]
    class_full = small_all[6].reshape(size * class_weight.shape[0], -1).astype(BF16)
    counted = jnp.where(first_core, counts_all[0], counts_all[1])
    task_pixels = counts_all[2:4]
    crop_valid = jnp.where(first_core, crop_valid_both[0], crop_valid_both[1])

    first, first_sums = first_conv(source, validity, bottle_all, turns, [source_flipped])
    coef_one = coefs(place.total(first_sums), counted, gain_bottle[:narrow], shift_bottle[:narrow])
    first_tiles = first.reshape(tiles + (narrow,))
    conv_in, second, second_sums = spatial_conv(
        first_tiles, coef_one, valid_tiles, bottle_all, bottle_taps, center_of(bottle_taps), spatial_at
    )
    second = second.reshape(pixels, narrow)
    coef_two = coefs(
        place.total(second_sums), counted, gain_bottle[narrow : 2 * narrow], shift_bottle[narrow : 2 * narrow]
    )
    middle_act, third, third_sums = third_conv(
        second, coef_two, validity, bottle_all, expand_at, quarters, turns
    )
    coef_three = coefs(
        place.total(third_sums), counted, gain_bottle[2 * narrow :], shift_bottle[2 * narrow :]
    )
    block_out, pooled_sum = block_output(third, source, coef_three, validity, tiles[0])
    block_tiles = block_out.reshape(tiles + (channels,))

    pooled = (pooled_sum / crop_valid).astype(BF16)
    pooled_all = place.everyone(pooled[0])
    pooled_rows = lax.dynamic_slice_in_dim(pooled_all, place.index * rows, rows, axis=1)
    image_all = place.total(jnp.dot(pooled_rows, image_weight, preferred_element_type=F32))
    branches, branch_sums = branch_convs(
        block_tiles,
        valid_tiles,
        pyramid_all,
        [
            (near_taps, branch),
            (middle_taps, 2 * branch),
            (far_taps, 3 * branch),
            (point_taps, 0),
        ],
        four_wide,
        [image_all],
    )
    branches = branches.reshape(pixels, four_wide)
    image_mean = jnp.sum(image_all, axis=0) / size
    image_scale = lax.rsqrt(
        jnp.sum(image_all * image_all, axis=0) / size - image_mean * image_mean + EPSILON
    )
    image_unit = (image_all - image_mean) * image_scale
    gain_image, shift_image = gain_pyramid[four_wide:], shift_pyramid[four_wide:]
    coef_image = jnp.stack([image_mean, image_scale, gain_image, shift_image])
    image_pre = gain_image * image_unit + shift_image
    image_act = silu(image_pre).astype(BF16)

    if place.direct:
        block_flipped, mate_flipped = flipped_halves(block_out, meta, [branch_sums])
        mate_flipped = place.swap(mate_flipped)
    else:
        block_flipped = flipped(block_out, [branch_sums])
    conv_flipped = flipped(conv_in.reshape(pixels, narrow), [block_flipped])
    coef_branch = coefs(
        place.total(branch_sums), counted, gain_pyramid[:four_wide], shift_pyramid[:four_wide]
    )
    unit_branch, pre_branch = unit_of(branches, coef_branch)
    joined = silu(pre_branch).astype(BF16)

    own_act = lax.dynamic_slice_in_dim(image_act, place.index, 1, axis=0)
    crop_part = jnp.dot(own_act, project_full[four_wide:], preferred_element_type=F32)
    projected = jnp.dot(joined, project_full[:four_wide], preferred_element_type=F32) + crop_part
    coef_head = coefs(place.total(sums(projected, validity)), counted, gain_head, shift_head)
    unit_head, pre_head = unit_of(projected, coef_head)
    output_act = silu(pre_head).astype(BF16)
    logits = jnp.dot(output_act, class_full, preferred_element_type=F32)

    columns = jnp.arange(class_full.shape[1])
    allowed = (columns >= CITY_CLASSES) == (task == 1)
    masked = jnp.where(allowed, logits, FLOOR_LOGIT)
    raised = jnp.exp(masked - jnp.max(masked, axis=-1, keepdims=True))
    chances = raised / jnp.sum(raised, axis=-1, keepdims=True)
    target = jnp.where(task == 0, labels % CITY_CLASSES, CITY_CLASSES + labels % HOME_CLASSES)
    chosen = (columns == target[:, None]).astype(F32)
    inverse = 1.0 / task_norms.astype(F32)
    task_share = inverse / jnp.sum(inverse)
    crop_weight = jnp.where(
        task == 0, task_share[0] / task_pixels[0], task_share[1] / task_pixels[1]
    )
    logit_grad = (crop_weight * validity * (chances - chosen)).astype(BF16)
    class_grad = lax.dot_general(
        output_act, logit_grad, (((0,), (0,)), ((), ())), preferred_element_type=F32
    )

    output_grad = lax.dot_general(
        logit_grad, class_full, (((1,), (1,)), ((), ())), preferred_element_type=F32
    )
    grad_head = output_grad * silu_slope(pre_head)
    head_totals = place.total(grad_moments(grad_head, unit_head))
    proj_grad = through_norm(
        grad_head, unit_head, coef_head, counted, validity, head_totals
    ).astype(BF16)
    crop_grad = jnp.sum(proj_grad, axis=0, dtype=F32)
    joined_grad = lax.dot_general(
        proj_grad, project_full[:four_wide], (((1,), (1,)), ((), ())), preferred_element_type=F32
    )
    act_grad = jnp.dot(project_full[four_wide:].astype(F32), crop_grad, precision=HIGHEST)
    own_pre = lax.dynamic_slice_in_dim(image_pre, place.index, 1, axis=0)[0]
    image_pre_grad = act_grad * silu_slope(own_pre)
    grad_branch = joined_grad * silu_slope(pre_branch)
    branch_parts = place.everyone(
        jnp.concatenate([grad_moments(grad_branch, unit_branch).reshape(-1), image_pre_grad])
    )
    image_pre_all = branch_parts[:, 2 * four_wide :]
    branch_totals = jnp.sum(branch_parts[:, : 2 * four_wide], axis=0).reshape(2, four_wide)
    branch_grad = through_norm(
        grad_branch, unit_branch, coef_branch, counted, validity, branch_totals
    ).astype(BF16)
    image_totals = grad_moments(image_pre_all, image_unit)
    image_in_all = through_norm(
        image_pre_all, image_unit, coef_image, float(size), 1.0, image_totals
    )
    pooled_partial = lax.dot_general(
        image_in_all, image_weight.astype(F32), (((1,), (1,)), ((), ())), precision=HIGHEST
    )
    if place.direct:
        pooled_grad_all = lax.all_to_all(pooled_partial, "batch", 0, 0).reshape(1, channels)
    else:
        pooled_grad_all = lax.dynamic_slice_in_dim(
            lax.all_gather(pooled_partial, "batch", axis=1, tiled=True), place.index, 1, axis=0
        )
    image_partial = jnp.dot(pooled_rows.astype(F32).T, image_in_all, precision=HIGHEST)

    def columns_of(taps, block):
        return [block * branch] * len(taps)

    near_rows = row_plan(near_taps, columns_of(near_taps, 1))
    middle_rows = row_plan(middle_taps, columns_of(middle_taps, 2))
    far_row = row_plan(far_taps, columns_of(far_taps, 3))
    point_row = row_plan(point_taps, columns_of(point_taps, 0))
    project_grad = jnp.concatenate(
        [
            lax.dot_general(
                joined, proj_grad, (((0,), (0,)), ((), ())), preferred_element_type=F32
            ),
            own_act[0].astype(F32)[:, None] * crop_grad[None, :],
        ]
    )

    class_rows = class_grad.size // size // branch if place.direct else 0
    extra_rows = project_grad.shape[0] // size + class_rows

    def extra_halves():
        parts = [project_grad.reshape(size, 2, -1, branch), class_grad.reshape(size, 2, -1, branch)]
        spare = rows // 2 - extra_rows // 2
        parts.append(jnp.zeros((size, 2, spare, branch), F32))
        halves = jnp.concatenate(parts, axis=2).astype(BF16)
        own = lax.dynamic_index_in_dim(halves, core, 1, keepdims=False).astype(F32)
        other = lax.dynamic_index_in_dim(halves, 1 - core, 1, keepdims=False)
        return (own + place.swap(other).astype(F32)).astype(BF16).reshape(-1, branch)

    if place.direct:
        mate_grad = place.swap(branch_grad)

    def branch_weight_grad(plan, after, extra=None, passed=()):
        if place.direct:
            return paired_grad(
                place,
                block_flipped,
                mate_flipped,
                branch_grad,
                mate_grad,
                meta,
                plan,
                tiles,
                branch,
                after,
                extra,
                passed,
            )
        return weight_grad(place, block_flipped, branch_grad, meta, plan, tiles, branch, after)

    parts = 2 if place.direct else 1

    pooled_grad = pooled_grad_all / crop_valid
    back_plan = [(far_row[0][0], far_row[0][1] + point_row[0][1])] + near_rows + middle_rows
    far_at = len(near_rows) + len(middle_rows)
    back_order = [far_at] + list(range(far_at))

    def half_back(side, after, scatters):
        low, moments, *passed = feature_back(
            branch_grad,
            pyramid_all,
            back_plan,
            back_order,
            3 * far_at + len(far_taps),
            third,
            source,
            coef_three,
            pooled_grad,
            validity,
            tiles,
            side,
            2,
            after,
            passing(scatters),
        )
        take_back(scatters, passed)
        return low, moments

    def sending(*scatters):
        return [array for scatter in scatters for array in scatter.sent]

    def passing(scatters):
        return [array for scatter in scatters for array in scatter.kept]

    def take_back(scatters, passed):
        for scatter in scatters:
            count = len(scatter.kept)
            scatter.kept, passed = passed[:count], passed[count:]

    low_grad, low_moments = half_back(0, [conv_flipped], [])
    high_grad, high_moments = half_back(1, [low_moments], [])
    three_parts = place.total(low_moments, high_moments)
    three_totals = jnp.concatenate(three_parts, axis=1)

    near_grads = branch_weight_grad(near_rows, [high_moments])
    near_scatter = Scatter(place, near_grads, [rows] * len(near_taps))
    near_scatter.first()
    wide_grads = branch_weight_grad(
        middle_rows + far_row + point_row,
        [near_grads[0]] + sending(near_scatter),
        extra_halves() if place.direct else None,
        passing([near_scatter]) if place.direct else (),
    )
    if place.direct:
        take_back([near_scatter], wide_grads[1:])
        wide_grads = wide_grads[:1]
    wide_rows = [rows] * (len(middle_taps) + len(far_taps) + 1) + [extra_rows]
    if not place.direct:
        wide_grads = [jnp.concatenate([wide_grads[0], project_grad.astype(BF16)[None]], axis=1)]
        wide_rows = wide_rows[:-1] + [rows, rows] + wide_rows[-1:]
    wide_scatter = Scatter(place, wide_grads, wide_rows)
    wide_scatter.first()
    near_scatter.second()

    middle_grad, *expand_grads = third_back(
        place,
        low_grad,
        high_grad,
        third,
        coef_three,
        three_totals / counted,
        validity,
        middle_act,
        bottle_all,
        meta,
        expand_at,
        quarters,
        turns,
        sending(near_scatter, wide_scatter),
        passing([near_scatter]),
    )
    take_back([near_scatter], expand_grads[parts:])
    expand_grads = expand_grads[:parts]
    near_scatter.third()
    near_scatter.launch()
    unit_two, pre_two = unit_of(second, coef_two)
    grad_two = middle_grad * silu_slope(pre_two)
    two_totals = place.total(grad_moments(grad_two, unit_two))
    second_grad = through_norm(
        grad_two, unit_two, coef_two, counted, validity, two_totals
    ).astype(BF16)
    spatial_rows = row_plan(bottle_taps, [0] * len(bottle_taps))
    spatial_grads = weight_grad(
        place,
        conv_flipped,
        second_grad,
        meta,
        spatial_rows,
        tiles,
        narrow,
        sending(near_scatter),
        None,
        passing([wide_scatter, near_scatter]),
    )
    take_back([wide_scatter, near_scatter], spatial_grads[parts:])
    near_scatter.exchange()
    wide_scatter.second()
    bottle_grads = [
        jnp.concatenate(pair, axis=1) for pair in zip(spatial_grads[:parts], expand_grads)
    ]
    bottle_rows = [narrow_rows] * (len(bottle_taps) + quarters)
    bottle_scatter = Scatter(place, bottle_grads, bottle_rows)
    grad_one, one_moments, *passed = spatial_back(
        second_grad,
        first,
        coef_one,
        validity,
        bottle_all,
        [spatial_rows[1], spatial_rows[0], spatial_rows[2]],
        [1, 0, 2],
        tiles,
        spatial_at,
        [spatial_grads[0]] + sending(wide_scatter),
        passing([wide_scatter, bottle_scatter]),
    )
    take_back([wide_scatter, bottle_scatter], passed)
    wide_scatter.third()
    wide_scatter.launch()
    if place.direct:
        one_moments = tied(one_moments, [bottle_scatter.arrived])
    bottle_scatter.first()
    one_totals = place.total(one_moments)
    unit_one, _ = unit_of(first, coef_one)
    first_grad = through_norm(
        grad_one, unit_one, coef_one, counted, validity, one_totals
    ).astype(BF16)
    reduce_grads = weight_grad(
        place,
        source_flipped,
        first_grad,
        meta,
        row_plan(point_taps, [0]),
        tiles,
        narrow,
        sending(bottle_scatter),
        None,
        passing([bottle_scatter, wide_scatter, near_scatter]),
    )
    take_back([bottle_scatter, wide_scatter, near_scatter], reduce_grads[parts:])
    wide_scatter.exchange()
    reduce_scatter = Scatter(place, reduce_grads[:parts], [rows])
    bottle_scatter.second()

    def rows_back(first_turn, count, into, after, scatters):
        result, *passed = input_back(
            jnp.array(matrix.T, BF16),
            low_grad,
            high_grad,
            first_grad,
            bottle_all,
            turns,
            first_turn,
            count,
            after,
            passing(scatters),
            into,
        )
        take_back(scatters, passed)
        return result

    input_grad = rows_back(0, 2, None, sending(bottle_scatter), [bottle_scatter, reduce_scatter, wide_scatter])
    reduce_scatter.first()
    bottle_scatter.third()
    bottle_scatter.launch()
    input_grad = rows_back(2, turns - 2, input_grad, sending(bottle_scatter, reduce_scatter), [bottle_scatter, reduce_scatter, near_scatter, wide_scatter])
    reduce_scatter.second()
    reduce_scatter.third()
    reduce_scatter.launch()

    vectors = [one_totals, two_totals, three_totals, branch_totals, image_totals, head_totals]
    vectors += [image_partial]
    packed = jnp.concatenate([vector.reshape(-1) for vector in vectors])
    packed = packed + place.swap(packed)
    split, start = [], 0
    for vector in vectors:
        split.append(packed[start : start + vector.size].reshape(vector.shape))
        start += vector.size

    def own_part(vectors):
        vector = jnp.concatenate(vectors)
        length = vector.shape[0] // size
        return lax.dynamic_slice_in_dim(vector, place.index * length, length, axis=0)

    bottle_gain_grad = own_part([split[0][1], split[1][1], split[2][1]])
    bottle_shift_grad = own_part([split[0][0], split[1][0], split[2][0]])
    pyramid_gain_grad = own_part([split[3][1], split[4][1]])
    pyramid_shift_grad = own_part([split[3][0], split[4][0]])
    head_norm_grad = jnp.stack([own_part([split[5][1]]), own_part([split[5][0]])])
    image_out = split[6]

    def taps_out(full, taps, weight):
        full = full.reshape((len(taps),) + weight.shape[2:])
        if len(taps) == weight.shape[0] * weight.shape[1]:
            return full.reshape(weight.shape)
        result = jnp.zeros(weight.shape, F32)
        for at, tap in enumerate(taps):
            result = result.at[tap[0], tap[1]].set(full[at])
        return result

    for scatter in (near_scatter, wide_scatter, bottle_scatter, reduce_scatter):
        scatter.finish()
    near_count, middle_count, far_count = len(near_taps), len(middle_taps), len(far_taps)
    bottle_count = len(bottle_taps)
    expand_out = bottle_scatter.piece(bottle_count, quarters).reshape(quarters, narrow_rows, narrow)
    if place.direct:
        project_out, class_out = wide_scatter.extra([extra_rows - class_rows, class_rows])
    else:
        project_out = wide_scatter.piece(len(wide_rows) - 1, 1)
        class_out = own_part([lax.psum(class_grad, ("batch", "section"))])
    return (
        input_grad.reshape(features.shape),
        reduce_scatter.piece(0, 1),
        taps_out(bottle_scatter.piece(0, bottle_count), bottle_taps, spatial_weight),
        jnp.swapaxes(expand_out, 0, 1).reshape(expand_weight.shape),
        bottle_gain_grad,
        bottle_shift_grad,
        wide_scatter.piece(middle_count + far_count, 1),
        taps_out(near_scatter.piece(0, near_count), near_taps, near_weight),
        taps_out(wide_scatter.piece(0, middle_count), middle_taps, middle_weight),
        taps_out(wide_scatter.piece(middle_count, far_count), far_taps, far_weight),
        image_out,
        project_out,
        class_out.reshape(class_weight.shape),
        pyramid_gain_grad,
        pyramid_shift_grad,
        head_norm_grad,
    )


def solution(mesh):
    in_specs = (
        P("section", "batch", None, None, None),
        P("batch", None),
        P(None, None, "batch", None),
        P("batch", None),
        P("batch"),
        P("batch"),
        P("batch", None),
        P(None, None, "batch", None),
        P(None, None, "batch", None),
        P(None, None, "batch", None),
        P("batch", None),
        P("batch", None),
        P("batch", None),
        P("batch"),
        P("batch"),
        P("batch"),
        P("batch"),
        P(None, "batch", None, None),
        P(None, "batch"),
        P(None, "batch", None, None),
        P(),
    )
    out_specs = (
        P("section", "batch", None, None, None),
        P("batch", None),
        P(None, None, "batch", None),
        P("batch", None),
        P("batch"),
        P("batch"),
        P("batch", None),
        P(None, None, "batch", None),
        P(None, None, "batch", None),
        P(None, None, "batch", None),
        P("batch", None),
        P("batch", None),
        P("batch", None),
        P("batch"),
        P("batch"),
        P(None, "batch"),
    )
    return jax.shard_map(
        per_device, mesh=mesh, in_specs=in_specs, out_specs=out_specs, check_vma=False
    )
```

```python
import functools

import jax
import jax.numpy as jnp
import numpy as np
from jax import lax
from jax.experimental import pallas as pl
from jax.experimental.pallas import tpu as pltpu
from jax.sharding import PartitionSpec as P

CITY_CLASSES = 19
HOME_CLASSES = 13
BOTTLE_RATE = 4
NEAR_RATE = 12
MIDDLE_RATE = 24
FAR_RATE = 36
TILE = 4

EPSILON = 1e-05
FLOOR_LOGIT = -1e30
HIGHEST = lax.Precision.HIGHEST
F32 = jnp.float32
BF16 = jnp.bfloat16
SLOT_BITS = [0, 4, 2, 6, 1, 5, 3, 7, 8, 12, 9, 13, 10, 14, 11, 15]
VMEM_BYTES = 58 * 1024 * 1024


class Place:
    def __init__(self):
        self.size = lax.axis_size("batch")
        self.direct = self.size == len(SLOT_BITS)
        self.pieces = 2 * self.size if self.direct else 1
        self.core = lax.axis_index("section")
        self.index = lax.axis_index("batch")

    def meta(self):
        core = self.core[None].astype(jnp.int32)
        if not self.direct:
            return core
        table = [[SLOT_BITS.index(at ^ owner) for owner in range(self.size)] for at in range(self.size)]
        row = lax.dynamic_index_in_dim(jnp.array(table, jnp.int32), self.index, 0, keepdims=False)
        return jnp.concatenate([core, row])

    def flip(self, block, bits):
        return lax.ppermute(block, "batch", [(source, source ^ bits) for source in range(self.size)])

    def swap(self, block):
        return lax.ppermute(block, "section", [(0, 1), (1, 0)])

    def total(self, *arrays):
        if not self.direct:
            return lax.psum(arrays, "batch") if len(arrays) > 1 else lax.psum(arrays[0], "batch")
        summed = jnp.sum(self.everyone(jnp.concatenate([array.reshape(-1) for array in arrays])), axis=0)
        results, start = [], 0
        for array in arrays:
            results.append(summed[start : start + array.size].reshape(array.shape))
            start += array.size
        return results if len(arrays) > 1 else results[0]

    def everyone(self, vector):
        if not self.direct:
            return lax.all_gather(vector, "batch")
        sent = jnp.broadcast_to(vector, (self.size,) + vector.shape)
        return lax.all_to_all(sent, "batch", 0, 0)

    def gather(self, parts):
        blocks = []
        for part, count in parts:
            cut = part.reshape(count, -1, part.shape[1])
            if self.direct:
                half = cut.shape[1] // 2
                cut = lax.dynamic_slice_in_dim(cut, self.core * half, half, axis=1)
            else:
                cut = lax.all_gather(cut, "batch", axis=1, tiled=True)
            blocks.append(cut.reshape(-1, part.shape[1]))
        block = jnp.concatenate(blocks)
        if self.direct:
            return lax.all_gather(block, ("batch", "section"))
        return block[None]


class Scatter:
    def __init__(self, place, grads, rows):
        self.place, self.rows = place, rows
        self.kept, self.sent = [grads[0]], []
        self.arrived = place.swap(grads[1]) if place.direct else None

    def add(self, kept, arrived):
        return (kept.astype(F32) + arrived.astype(F32)).astype(BF16)

    def first(self):
        if not self.place.direct:
            return
        own, arrived = self.kept[0], self.arrived
        self.kept = []
        sent = []
        for start in (0, 8):
            self.kept.append(self.add(own[start : start + 4], arrived[start : start + 4]))
            sent.append(self.add(own[start + 4 : start + 8], arrived[start + 4 : start + 8]))
        self.sent = sent
        self.arrived = [self.place.flip(sent[0], 1), self.place.flip(sent[1], 2)]

    def second(self):
        if not self.place.direct:
            return
        kept, sent = [], []
        for held, came in zip(self.kept, self.arrived):
            kept.append(self.add(held[:2], came[:2]))
            sent.append(self.add(held[2:], came[2:]))
        self.kept, self.sent = kept, sent
        self.arrived = [self.place.flip(sent[0], 2), self.place.flip(sent[1], 1)]

    def third(self):
        if not self.place.direct:
            return
        near = self.kept[0].astype(F32) + self.arrived[0].astype(F32)
        away = self.kept[1].astype(F32) + self.arrived[1].astype(F32)
        self.kept = [near[0]]
        sent = [near[1].astype(BF16), away[0].astype(BF16), away[1].astype(BF16)]
        self.sent = sent

    def launch(self):
        if self.place.direct:
            self.arrived = [
                self.place.flip(piece, bits) for piece, bits in zip(self.sent, (4, 8, 12))
            ]

    def finish(self):
        if self.place.direct:
            parts = [piece.astype(F32) for piece in self.arrived]
            result = (self.kept[0] + parts[0]) + (parts[1] + parts[2])
            opposite = self.place.swap(result)
            first = self.place.core == 0
            self.result = [jnp.where(first, result, opposite), jnp.where(first, opposite, result)]
            return self
        pieces, start = [], 0
        for rows in self.rows:
            cut = self.kept[0][0, start : start + rows * self.place.size].astype(F32)
            cut = lax.psum_scatter(cut, "batch", scatter_dimension=0, tiled=True)
            pieces.append(lax.psum(cut, "section"))
            start += rows * self.place.size
        self.result = [jnp.concatenate(pieces)]
        return self

    def extra(self, sizes):
        start = sum(self.rows[:-1]) // 2
        found = []
        for rows in sizes:
            found.append(jnp.concatenate([part[start : start + rows // 2] for part in self.result]))
            start += rows // 2
        return found

    def piece(self, first, count):
        parts = len(self.result)
        start = sum(self.rows[:first]) // parts
        rows = self.rows[first] // parts
        cut = [part[start : start + count * rows].reshape(count, rows, -1) for part in self.result]
        return jnp.concatenate(cut, axis=1).reshape(count * rows * parts, -1)


def call(body, args, specs, grid, outs, out_specs, scratch=(), meta=None, after=(), passed=(), into=None, flops=1):
    used = len(args) + (meta is not None)
    passed = list(passed) if into is None else [into] + list(passed)
    waits = len(after) + len(passed)
    results = len(outs)
    filled = int(into is not None)
    kept = results - filled

    def inner(*refs):
        rest = refs[used + waits :]
        body(*refs[:used], *rest[:results], *rest[results + len(passed) - filled :])

    spec = pltpu.PrefetchScalarGridSpec(
        num_scalar_prefetch=int(meta is not None),
        grid=grid,
        in_specs=list(specs) + [pl.BlockSpec(memory_space=pl.ANY)] * waits,
        out_specs=list(out_specs) + [pl.BlockSpec(memory_space=pl.ANY)] * (len(passed) - filled),
        scratch_shapes=list(scratch),
    )
    arrays = ([] if meta is None else [meta]) + list(args) + list(after) + list(passed)
    first = len(arrays) - len(passed)
    return pl.pallas_call(
        inner,
        grid_spec=spec,
        out_shape=list(outs) + [shaped(array.shape, array.dtype) for array in passed[filled:]],
        input_output_aliases={first + at: kept + at for at in range(len(passed))},
        compiler_params=pltpu.CompilerParams(vmem_limit_bytes=VMEM_BYTES),
        cost_estimate=pl.CostEstimate(flops=flops, transcendentals=0, bytes_accessed=1),
    )(*arrays)


def copy_body(source_ref, result_ref):
    result_ref[...] = source_ref[...]


def tied(array, after):
    return call(
        copy_body, [array], [whole(array)], (1,), [shaped(array.shape)], [held(array.shape)], after=after
    )[0]


def whole(array):
    shape = array.shape
    return pl.BlockSpec(
        shape, lambda *_: (0,) * len(shape), pipeline_mode=pl.Buffered(buffer_count=1)
    )


def held(shape):
    return pl.BlockSpec(shape, lambda *_: (0,) * len(shape))


def rows_of(array, rows):
    return pl.BlockSpec((rows, array.shape[1]), lambda step, *_: (step, 0))


def shaped(shape, dtype=F32):
    return jax.ShapeDtypeStruct(tuple(shape), dtype)


def span(shift_by, length):
    return max(0, -shift_by), length - max(0, shift_by)


def tap_list(height, breadth, dilation):
    listed = []
    for row_tap in range(3):
        for col_tap in range(3):
            row_shift = (row_tap - 1) * dilation
            col_shift = (col_tap - 1) * dilation
            if abs(row_shift) < height and abs(col_shift) < breadth:
                listed.append((row_tap, col_tap, row_shift // TILE, col_shift // TILE))
    return listed


def weight_of(ref):
    return ref[...].reshape(-1, ref.shape[-1])


def spread(meta_ref, full_ref, result_refs, column=0, at=0, rows=None):
    width = result_refs[0].shape[2]
    rows = result_refs[0].shape[1] if rows is None else rows
    if len(result_refs) == 1:
        result_refs[0][0, at : at + rows] = full_ref[:, column : column + width].astype(BF16)
        return
    core = meta_ref[0]
    for owner in range(result_refs[0].shape[0]):
        for ref, side in zip(result_refs, (core, 1 - core)):
            start = pl.multiple_of(owner * 2 * rows + side * rows, rows)
            block = full_ref[pl.ds(start, rows), column : column + width]
            ref[meta_ref[1 + owner], at : at + rows] = block.astype(BF16)


def slotted(place, rows, width):
    if place.direct:
        return [shaped((place.size, rows // 2, width), BF16)] * 2
    return [shaped((1, rows * place.size, width), BF16)]


def center_first(step, center):
    return jnp.where(step == 0, center, jnp.where(step <= center, step - 1, step))


def ordered(taps, center):
    return [taps[center]] + [tap for place, tap in enumerate(taps) if place != center]


def shifts_of(taps):
    return [(tap[2], tap[3]) for tap in taps]


def area(tap, tiles):
    return (tiles[0] - abs(tap[0])) * (tiles[1] - abs(tap[1])) * tiles[2]


def forward_tap(tap, fresh, source_ref, weight, result_ref):
    tiles_i, tiles_j, pixels, channels = source_ref.shape
    columns = weight.shape[1]
    shift_i, shift_j = tap
    low_i, high_i = span(shift_i, tiles_i)
    low_j, high_j = span(shift_j, tiles_j)
    window = source_ref[
        low_i + shift_i : high_i + shift_i, low_j + shift_j : high_j + shift_j
    ].reshape(-1, channels)
    product = jnp.dot(window, weight, preferred_element_type=F32)
    product = product.reshape(high_i - low_i, high_j - low_j, pixels, columns)
    if fresh:
        result_ref[low_i:high_i, low_j:high_j] = product
    else:
        result_ref[low_i:high_i, low_j:high_j] += product


def repeat(count, body):
    lax.fori_loop(0, count, lambda turn, carry: (body(turn), carry)[1], 0)


def row_steps(count):
    return max(step for step in (1, 2, 3, 4) if count % step == 0)


FIELDS = 9


def tap_table(plan, tiles, places):
    table, classes = [], []
    for ((shift_i, shift_j), column), place in zip(plan, places):
        low_i, high_i = span(shift_i, tiles[0])
        low_j, high_j = span(shift_j, tiles[1])
        kind = (row_steps(high_i - low_i), high_j - low_j)
        if kind not in classes:
            classes.append(kind)
        table += [classes.index(kind), low_i, low_i + shift_i, (high_i - low_i) // kind[0]]
        table += [low_j, low_j + shift_j, column, place, 0]
    return np.array(table, np.int32), classes


def forward_taps(classes, table_ref, source_ref, weight_ref, result_ref):
    _, _, pixels, channels = source_ref.shape
    width = weight_ref.shape[2]
    at = pl.program_id(0) * FIELDS
    for kind, (rows, wide) in enumerate(classes):

        @pl.when(table_ref[at] == kind)
        def _(rows=rows, wide=wide):
            to_i, from_i, turns = table_ref[at + 1], table_ref[at + 2], table_ref[at + 3]
            to_j, from_j = table_ref[at + 4], table_ref[at + 5]
            column = pl.multiple_of(table_ref[at + 6], width)

            def body(turn):
                window = source_ref[pl.ds(from_i + turn * rows, rows), pl.ds(from_j, wide)]
                product = jnp.dot(
                    window.reshape(-1, channels), weight_of(weight_ref), preferred_element_type=F32
                )
                place = (
                    pl.ds(to_i + turn * rows, rows),
                    pl.ds(to_j, wide),
                    slice(None),
                    pl.ds(column, width),
                )
                result_ref[place] += product.reshape(rows, wide, pixels, width)

            repeat(turns, body)


def unit_of(values, coef):
    unit = (values - coef[0:1]) * coef[1:2]
    return unit, coef[2:3] * unit + coef[3:4]


def masked_sums(values, valid):
    weighted = values * valid
    return jnp.concatenate(
        [jnp.sum(weighted, axis=0, keepdims=True), jnp.sum(weighted * values, axis=0, keepdims=True)]
    )


def sum_rows(ref, valid_ref, sums_ref):
    total = jnp.zeros(sums_ref.shape, F32)
    for row in range(ref.shape[0]):
        values = ref[row].reshape(-1, ref.shape[-1])
        total = total + masked_sums(values, valid_ref[row].reshape(-1, 1))
    sums_ref[...] = total


def branch_body(classes, table_ref, source_ref, valid_ref, weight_ref, result_ref, sums_ref):
    @pl.when(pl.program_id(0) == 0)
    def _():
        def clear(row):
            result_ref[row] = jnp.zeros(result_ref.shape[1:], F32)

        repeat(result_ref.shape[0], clear)

    forward_taps(classes, table_ref, source_ref, weight_ref, result_ref)

    @pl.when(pl.program_id(0) == pl.num_programs(0) - 1)
    def _():
        sum_rows(result_ref, valid_ref, sums_ref)


def placed_block(weights, channels):
    pieces, _, width = weights.shape
    return pl.BlockSpec(
        (pieces, channels // pieces, width), lambda step, table: (0, table[step * FIELDS + 7], 0)
    )


def branch_convs(source, valid, weights, groups, columns, after):
    channels = source.shape[-1]
    plan = [(shift, column) for taps, column in groups for shift in shifts_of(taps)]
    table, classes = tap_table(plan, source.shape, range(len(plan)))
    result_shape = source.shape[:3] + (columns,)
    return call(
        functools.partial(branch_body, classes),
        [source, valid, weights],
        [whole(source), whole(valid), placed_block(weights, channels)],
        (len(plan),),
        [shaped(result_shape), shaped((2, columns))],
        [held(result_shape), held((2, columns))],
        meta=jnp.array(table),
        after=after,
    )


def spatial_body(plan, first_ref, coef_ref, valid_ref, weight_ref, input_ref, result_ref, sums_ref):
    @pl.when(pl.program_id(0) == 0)
    def _():
        for row in range(first_ref.shape[0]):
            _, pre = unit_of(first_ref[row], coef_ref[...][:, None, :])
            input_ref[row] = (silu(pre) * valid_ref[row]).astype(BF16)

    for place, tap in enumerate(plan):

        @pl.when(pl.program_id(0) == place)
        def _(place=place, tap=tap):
            forward_tap(tap, place == 0, input_ref, weight_of(weight_ref), result_ref)

    @pl.when(pl.program_id(0) == len(plan) - 1)
    def _():
        sum_rows(result_ref, valid_ref, sums_ref)


def spatial_conv(first, coef, valid, weights, taps, center, first_tap):
    channels = first.shape[-1]
    pieces, _, columns = weights.shape
    plan = ordered(shifts_of(taps), center)
    return call(
        functools.partial(spatial_body, plan),
        [first, coef, valid, weights],
        [
            whole(first),
            whole(coef),
            whole(valid),
            pl.BlockSpec(
                (pieces, channels // pieces, columns),
                lambda step: (0, first_tap + center_first(step, center), 0),
            ),
        ],
        (len(plan),),
        [shaped(first.shape, BF16), shaped(first.shape), shaped((2, columns))],
        [held(first.shape), held(first.shape), held((2, columns))],
    )


def shifted_columns(tiles, row_taps, up_ref, padded_ref, width, first=None, last=None):
    tiles_i, tiles_j, pixels = tiles
    shift_i, columns = row_taps
    low_i, high_i = span(shift_i, tiles_i)
    line = tiles_j * pixels
    low, high = (low_i + shift_i) * line, (high_i + shift_i) * line

    def clear(start, stop, at):
        if stop > start:
            padded_ref[start:stop, at : at + width] = jnp.zeros((stop - start, width), BF16)

    for place, (shift_j, column) in enumerate(columns):
        at = place * width
        low_j, high_j = span(shift_j, tiles_j)
        begin, end = (low_j + shift_j) * pixels, (high_j + shift_j) * pixels
        for row in range(low_i, high_i):
            base = (row + shift_i) * line
            source = row * line + low_j * pixels
            clear(base, base + begin, at)
            padded_ref[base + begin : base + end, at : at + width] = up_ref[
                source : source + end - begin, column : column + width
            ]
            clear(base + end, base + line, at)
        if first is not None:
            clear(first, low, at)
            clear(high, last, at)
    return low, high


def back_step(tiles, row_taps, fresh, up_ref, weight_refs, padded_ref, weight_ref, total_ref):
    channels = total_ref.shape[1]
    width = weight_refs[0].shape[2]
    depth = len(row_taps[1]) * width
    low, high = shifted_columns(tiles, row_taps, up_ref, padded_ref, width)
    for place in range(len(row_taps[1])):
        weight_ref[:, place * width : (place + 1) * width] = weight_of(weight_refs[place])
    wide = min(512, channels)
    for start in range(0, channels, wide):
        product = lax.dot_general(
            padded_ref[low:high, :depth],
            weight_ref[start : start + wide, :depth],
            (((1,), (1,)), ((), ())),
            preferred_element_type=F32,
        )
        if fresh:
            total_ref[low:high, start : start + wide] = product
        else:
            total_ref[low:high, start : start + wide] += product


def row_plan(taps, columns):
    rows = []
    for tap, column in zip(taps, columns):
        if not rows or rows[-1][0] != tap[2]:
            rows.append((tap[2], []))
        rows[-1][1].append((tap[3], column))
    return rows


def row_weights(weights, channels, order, first_tap, side=0, sides=1):
    pieces, _, width = weights.shape
    rows = channels // pieces
    specs = []
    for column in range(3):

        def index(step, column=column):
            row = order[-1]
            for place, listed in enumerate(order[:-1]):
                row = jnp.where(step == place, listed, row)
            tap = first_tap + 3 * row + column
            return (0, tap * sides + side, 0) if pieces == 1 else (side, tap, 0)

        block = (1, rows // sides, width) if pieces == 1 else (pieces // sides, rows, width)
        specs.append(pl.BlockSpec(block, index))
    return specs


def grad_moments(grad, unit):
    return jnp.concatenate(
        [jnp.sum(grad, axis=0, keepdims=True), jnp.sum(grad * unit, axis=0, keepdims=True)]
    )


def feature_body(
    plan, tiles, up_ref, third_ref, source_ref, coef_ref, pooled_ref, valid_ref, *refs
):
    weight_refs = refs[:4]
    result_ref, sums_ref, padded_ref, weight_ref, total_ref = refs[4:]
    step_now = pl.program_id(0)
    for place, row_taps in enumerate(plan):

        @pl.when(step_now == place)
        def _(place=place, row_taps=row_taps):
            back_step(
                tiles, row_taps, place == 0, up_ref, weight_refs, padded_ref, weight_ref, total_ref
            )

    begun = len(plan)

    @pl.when(step_now >= begun)
    def _():
        height = third_ref.shape[0]
        row = pl.multiple_of((step_now - begun) * height, height)
        unit, pre = unit_of(third_ref[...], coef_ref[...])
        pre = pre + source_ref[...].astype(F32)
        grad = total_ref[pl.ds(row, height)] + pooled_ref[...]
        grad = grad * valid_ref[...] * silu_slope(pre)
        result_ref[...] = grad.astype(BF16)
        moments = grad_moments(grad, unit)

        @pl.when(step_now == begun)
        def _():
            sums_ref[...] = moments

        @pl.when(step_now > begun)
        def _():
            sums_ref[...] += moments


def feature_back(upstream, weights, plan, order, point, third, source, coef, pooled, valid, tiles, side, sides, after, passed):
    pixels, channels = third.shape
    part = channels // sides
    pieces, _, width = weights.shape
    rows = channels // pieces
    begun = len(plan)
    turns = tiles[0]
    height = pixels // turns

    def row_of(step):
        return jnp.clip(step - begun, 0, turns - 1)

    row_block = pl.BlockSpec((height, part), lambda step: (row_of(step), side))
    if pieces == 1:
        point_block = pl.BlockSpec((1, rows // sides, width), lambda step: (0, point * sides + side, 0))
    else:
        point_block = pl.BlockSpec((pieces // sides, rows, width), lambda step: (side, point, 0))
    return call(
        functools.partial(feature_body, plan, tiles),
        [upstream, third, source, coef, pooled, valid] + [weights] * 4,
        [
            whole(upstream),
            row_block,
            row_block,
            pl.BlockSpec((coef.shape[0], part), lambda step: (0, side)),
            pl.BlockSpec((1, part), lambda step: (0, side)),
            pl.BlockSpec((height, 1), lambda step: (row_of(step), 0)),
        ]
        + row_weights(weights, channels, order, 0, side, sides)
        + [point_block],
        (begun + turns,),
        [shaped((pixels, part), BF16), shaped((2, part))],
        [pl.BlockSpec((height, part), lambda step: (row_of(step), 0)), held((2, part))],
        [
            pltpu.VMEM((pixels, 4 * width), BF16),
            pltpu.VMEM((part, 4 * width), BF16),
            pltpu.VMEM((pixels, part), F32),
        ],
        after=after,
        passed=passed,
    )


def spatial_back_body(plan, tiles, up_ref, first_ref, coef_ref, valid_ref, *refs):
    weight_refs = refs[:3]
    result_ref, sums_ref, padded_ref, weight_ref = refs[3:]
    for place, row_taps in enumerate(plan):

        @pl.when(pl.program_id(0) == place)
        def _(place=place, row_taps=row_taps):
            back_step(
                tiles, row_taps, place == 0, up_ref, weight_refs, padded_ref, weight_ref, result_ref
            )

    @pl.when(pl.program_id(0) == len(plan) - 1)
    def _():
        total = jnp.zeros(sums_ref.shape, F32)
        height = result_ref.shape[0] // tiles[0]
        for row in range(tiles[0]):
            at = slice(row * height, (row + 1) * height)
            unit, pre = unit_of(first_ref[at], coef_ref[...])
            grad = result_ref[at] * valid_ref[at] * silu_slope(pre)
            result_ref[at] = grad
            total = total + grad_moments(grad, unit)
        sums_ref[...] = total


def spatial_back(upstream, first, coef, valid, weights, plan, order, tiles, first_tap, after, passed):
    pixels, channels = first.shape
    columns = weights.shape[2]
    return call(
        functools.partial(spatial_back_body, plan, tiles),
        [upstream, first, coef, valid] + [weights] * 3,
        [whole(upstream), whole(first), whole(coef), whole(valid)]
        + row_weights(weights, channels, order, first_tap),
        (len(plan),),
        [shaped(first.shape), shaped((2, channels))],
        [held(first.shape), held((2, channels))],
        [pltpu.VMEM((pixels, 3 * columns), BF16), pltpu.VMEM((channels, 3 * columns), BF16)],
        after=after,
        passed=passed,
    )


def weight_body(plan, tiles, extra, count, meta_ref, flipped_ref, up_ref, *refs):
    extra_ref = refs[0] if extra else None
    result_refs = refs[extra : extra + count]
    padded_ref, full_ref = refs[extra + count :]
    block_rows, width = result_refs[0].shape[1:]
    taps_held = padded_ref.shape[1] // width
    rows = block_rows // taps_held
    for place, row_taps in enumerate(plan):

        @pl.when(pl.program_id(0) == place)
        def _(row_taps=row_taps):
            taps = len(row_taps[1])
            low_i, high_i = span(row_taps[0], tiles[0])
            line = tiles[1] * tiles[2]
            first = (low_i + row_taps[0]) * line // 128 * 128
            last = -(-(high_i + row_taps[0]) * line // 128) * 128
            shifted_columns(tiles, row_taps, up_ref, padded_ref, width, first, last)
            for tap in range(taps):
                at = slice(tap * width, (tap + 1) * width)
                full_ref[:, at] = jnp.dot(
                    flipped_ref[:, first:last], padded_ref[first:last, at], preferred_element_type=F32
                ).astype(BF16)
                spread(meta_ref, full_ref, result_refs, tap * width, tap * rows, rows)

    if extra:

        @pl.when(pl.program_id(0) == len(plan) - 1)
        def _():
            core = meta_ref[0]
            taps = len(plan[-1][1])
            spare = (taps_held - taps - 1) * rows
            for owner in range(result_refs[0].shape[0]):
                slot = meta_ref[1 + owner]
                for ref, side in zip(result_refs, (core, 1 - core)):
                    start = pl.multiple_of((owner * 2 + side) * rows, rows)
                    ref[slot, taps * rows : (taps + 1) * rows] = extra_ref[pl.ds(start, rows)]
                    ref[slot, (taps + 1) * rows :] = jnp.zeros((spare, width), BF16)


def weight_grad(place, flipped, upstream, meta, plan, tiles, width, after=(), extra=None, passed=()):
    channels, padded = flipped.shape
    taps = max(len(row_taps[1]) for row_taps in plan)
    steps = len(plan)
    shapes = slotted(place, channels // place.size * taps * steps, width)
    blocks = [
        pl.BlockSpec((shape.shape[0], shape.shape[1] // steps, width), lambda step, _: (0, step, 0))
        for shape in shapes
    ]
    more = [] if extra is None else [extra]
    return call(
        functools.partial(weight_body, plan, tiles, len(more), len(shapes)),
        [flipped, upstream] + more,
        [whole(array) for array in [flipped, upstream] + more],
        (steps,),
        shapes,
        blocks,
        [pltpu.VMEM((padded, taps * width), BF16), pltpu.VMEM((channels, taps * width), BF16)],
        meta,
        after,
        passed,
    )


def tile_matrix(breadth):
    count = TILE * breadth
    matrix = np.zeros((count, count), np.float32)
    for row in range(TILE):
        for column in range(breadth):
            at = (column // TILE * TILE + row) * TILE + column % TILE
            matrix[at, row * breadth + column] = 1.0
    return matrix


def tile_body(matrix_ref, natural_ref, result_ref):
    result_ref[...] = jnp.dot(
        matrix_ref[...], natural_ref[...], preferred_element_type=F32
    ).astype(BF16)


def tile_rows(natural, matrix):
    rows = matrix.shape[0]
    return call(
        tile_body,
        [matrix, natural],
        [whole(matrix), rows_of(natural, rows)],
        (natural.shape[0] // rows,),
        [shaped(natural.shape, BF16)],
        [rows_of(natural, rows)],
    )[0]


def flip_body(source_ref, result_ref):
    pixels = source_ref.shape[0]
    result_ref[:, :pixels] = source_ref[...].T
    if result_ref.shape[1] > pixels:
        extra = result_ref.shape[1] - pixels
        result_ref[:, pixels:] = jnp.zeros((result_ref.shape[0], extra), BF16)


def flipped(values, after=()):
    pixels, channels = values.shape
    padded = pixels + -pixels % 128
    return call(
        flip_body,
        [values],
        [pl.BlockSpec((pixels, 128), lambda step: (0, step))],
        (channels // 128,),
        [shaped((channels, padded), BF16)],
        [pl.BlockSpec((128, padded), lambda step: (step, 0))],
        after=after,
    )[0]


def add_sums(sums_ref, sums):
    @pl.when(pl.program_id(0) == 0)
    def _():
        sums_ref[...] = sums

    @pl.when(pl.program_id(0) > 0)
    def _():
        sums_ref[...] += sums


def first_body(source_ref, valid_ref, weight_ref, result_ref, sums_ref):
    product = jnp.dot(source_ref[...], weight_of(weight_ref), preferred_element_type=F32)
    result_ref[...] = product
    add_sums(sums_ref, masked_sums(product, valid_ref[...]))


def fixed_block(weights, channels, at):
    pieces, _, columns = weights.shape
    return pl.BlockSpec((pieces, channels // pieces, columns), lambda step, *_: (0, at, 0))


def first_conv(source, valid, weights, turns, after):
    pixels, channels = source.shape
    rows = pixels // turns
    width = weights.shape[2]
    return call(
        first_body,
        [source, valid, weights],
        [rows_of(source, rows), rows_of(valid, rows), fixed_block(weights, channels, 0)],
        (turns,),
        [shaped((pixels, width)), shaped((2, width))],
        [pl.BlockSpec((rows, width), lambda step: (step, 0)), held((2, width))],
        after=after,
    )


def third_body(count, second_ref, coef_ref, valid_ref, *refs):
    weight_refs = refs[:count]
    middle_ref, result_ref, sums_ref = refs[count:]
    _, pre = unit_of(second_ref[...], coef_ref[...])
    middle = silu(pre).astype(BF16)
    middle_ref[...] = middle
    valid = valid_ref[...]
    sums = []
    for quarter, ref in enumerate(weight_refs):
        product = jnp.dot(middle, weight_of(ref), preferred_element_type=F32)
        width = product.shape[1]
        result_ref[:, quarter * width : (quarter + 1) * width] = product
        sums.append(masked_sums(product, valid))
    add_sums(sums_ref, jnp.concatenate(sums, axis=1))


def third_conv(second, coef, valid, weights, first, count, turns):
    pixels, narrow = second.shape
    height = pixels // turns
    channels = count * weights.shape[2]
    return call(
        functools.partial(third_body, count),
        [second, coef, valid] + [weights] * count,
        [rows_of(second, height), whole(coef), rows_of(valid, height)]
        + [fixed_block(weights, narrow, first + quarter) for quarter in range(count)],
        (turns,),
        [shaped((pixels, narrow), BF16), shaped((pixels, channels)), shaped((2, channels))],
        [
            pl.BlockSpec((height, narrow), lambda step: (step, 0)),
            pl.BlockSpec((height, channels), lambda step: (step, 0)),
            held((2, channels)),
        ],
    )


def output_body(third_ref, source_ref, coef_ref, valid_ref, result_ref, sums_ref):
    _, pre = unit_of(third_ref[...], coef_ref[...])
    values = (valid_ref[...] * silu(pre + source_ref[...].astype(F32))).astype(BF16)
    result_ref[...] = values
    add_sums(sums_ref, jnp.sum(values.astype(F32), axis=0, keepdims=True))


def block_output(third, source, coef, valid, turns):
    pixels, channels = third.shape
    rows = pixels // turns
    return call(
        output_body,
        [third, source, coef, valid],
        [rows_of(third, rows), rows_of(source, rows), whole(coef), rows_of(valid, rows)],
        (turns,),
        [shaped(third.shape, BF16), shaped((1, channels))],
        [rows_of(third, rows), held((1, channels))],
    )


def third_back_body(
    count, outs, meta_ref, sum_ref, third_ref, coef_ref, totals_ref, valid_ref, middle_ref, *refs
):
    second_ref, second_coef_ref = refs[:2]
    refs = refs[2:]
    weight_refs = refs[:count]
    result_ref, sums_ref = refs[count : count + 2]
    slot_refs = refs[count + 2 : count + 2 + outs]
    grad_ref, total_ref = refs[count + 2 + outs :]
    step_now = pl.program_id(0)

    @pl.when(step_now == 0)
    def _():
        total_ref[...] = jnp.zeros_like(total_ref)

    part = 512
    coef, totals, valid = coef_ref[...], totals_ref[...], valid_ref[...]
    for start in range(0, sum_ref.shape[1], part):
        at = slice(start, start + part)
        unit = (third_ref[:, at] - coef[0:1, at]) * coef[1:2, at]
        centered = sum_ref[:, at].astype(F32) - valid * (totals[0:1, at] + unit * totals[1:2, at])
        grad_ref[:, at] = (coef[2:3, at] * coef[1:2, at] * centered).astype(BF16)
    width = weight_refs[0].shape[2]
    result = None
    for quarter, ref in enumerate(weight_refs):
        grad = grad_ref[:, quarter * width : (quarter + 1) * width]
        product = lax.dot_general(
            grad, weight_of(ref), (((1,), (1,)), ((), ())), preferred_element_type=F32
        )
        result = product if result is None else result + product
    unit, pre = unit_of(second_ref[...], second_coef_ref[...])
    result = result * silu_slope(pre)
    result_ref[...] = result
    add_sums(sums_ref, grad_moments(result, unit))
    total_ref[...] += lax.dot_general(
        middle_ref[...], grad_ref[...], (((0,), (0,)), ((), ())), preferred_element_type=F32
    )

    @pl.when(step_now == pl.num_programs(0) - 1)
    def _():
        rows = slot_refs[0].shape[1] // count
        for quarter in range(count):
            spread(meta_ref, total_ref, slot_refs, quarter * width, quarter * rows, rows)


def third_back(place, grad, third, coef, totals, valid, middle, second, second_coef, weights, meta, first, count, turns, after, passed):
    pixels, channels = third.shape
    narrow = middle.shape[1]
    height = pixels // turns
    shapes = slotted(place, narrow // place.size * count, weights.shape[2])
    return call(
        functools.partial(third_back_body, count, len(shapes)),
        [grad, third, coef, totals, valid, middle, second, second_coef] + [weights] * count,
        [
            rows_of(grad, height),
            rows_of(third, height),
            whole(coef),
            whole(totals),
            rows_of(valid, height),
            rows_of(middle, height),
            rows_of(second, height),
            whole(second_coef),
        ]
        + [fixed_block(weights, narrow, first + quarter) for quarter in range(count)],
        (turns,),
        [shaped((pixels, narrow)), shaped((2, narrow))] + shapes,
        [pl.BlockSpec((height, narrow), lambda step, _: (step, 0)), held((2, narrow))]
        + [held(shape.shape) for shape in shapes],
        [pltpu.VMEM((height, channels), BF16), pltpu.VMEM((narrow, channels), F32)],
        meta,
        after,
        passed,
    )


def input_body(matrix_ref, sum_ref, grad_ref, weight_ref, result_ref):
    rows = matrix_ref.shape[0]
    matrix = matrix_ref[...]
    moved = []
    for start in range(0, result_ref.shape[0], rows):
        at = slice(start, start + rows)
        moved.append(jnp.dot(matrix, grad_ref[at], preferred_element_type=F32).astype(BF16))
        result_ref[at] = jnp.dot(matrix, sum_ref[at], preferred_element_type=F32)
    result_ref[...] += lax.dot_general(
        jnp.concatenate(moved), weight_of(weight_ref), (((1,), (1,)), ((), ())), preferred_element_type=F32
    )


def input_back(matrix, sums, grad, weights, turns, first, count, after, passed, into):
    pixels, channels = sums.shape
    rows = pixels // turns
    width = grad.shape[1]

    def block(columns):
        return pl.BlockSpec((rows, columns), lambda step: (first + step, 0))

    return call(
        input_body,
        [matrix, sums, grad, weights],
        [whole(matrix), block(channels), block(width), fixed_block(weights, channels, 0)],
        (count,),
        [shaped((pixels, channels))],
        [block(channels)],
        after=after,
        passed=passed,
        into=into,
        flops=10**10,
    )


def sigmoid(values):
    return 0.5 + 0.5 * jnp.tanh(0.5 * values)


def silu(values):
    return values * sigmoid(values)


def silu_slope(values):
    sigmoid_val = sigmoid(values)
    return sigmoid_val * (1.0 + values * (1.0 - sigmoid_val))


def sums(values, validity):
    weighted = values * validity
    return jnp.stack([jnp.sum(weighted, axis=0), jnp.sum(weighted * values, axis=0)])


def coefs(totals, counted, gain, shift):
    mean_value = totals[0] / counted
    scaling = lax.rsqrt(totals[1] / counted - mean_value * mean_value + EPSILON)
    return jnp.stack([mean_value, scaling, gain, shift])


def through_norm(grad_pre, unit, coef, counted, validity, totals):
    centered = grad_pre - validity * (totals[0] + unit * totals[1]) / counted
    return coef[2] * coef[1] * centered


def to_tiles(array):
    height, breadth = array.shape[:2]
    rest = array.shape[2:]
    cut = array.reshape((height // TILE, TILE, breadth // TILE, TILE) + rest)
    return jnp.swapaxes(cut, 1, 2).reshape((height * breadth,) + rest)


def per_device(
    features,
    reduce_weight,
    spatial_weight,
    expand_weight,
    bottle_gain,
    bottle_shift,
    point_weight,
    near_weight,
    middle_weight,
    far_weight,
    image_weight,
    project_weight,
    class_weight,
    pyramid_gain,
    pyramid_shift,
    head_gain,
    head_shift,
    crop_masks,
    crop_tasks,
    pixel_labels,
    task_norms,
):
    place = Place()
    size, core = place.size, place.core
    first_core = core == 0
    height, breadth, channels = features.shape[2:]
    pixels = height * breadth
    tiles = (height // TILE, breadth // TILE, TILE * TILE)
    narrow = reduce_weight.shape[1]
    branch = point_weight.shape[1]
    four_wide = 4 * branch
    rows = channels // size
    narrow_rows = narrow // size
    quarters = channels // narrow
    turns = 3
    meta = place.meta()
    matrix = tile_matrix(breadth)

    bottle_taps = tap_list(height, breadth, BOTTLE_RATE)
    near_taps = tap_list(height, breadth, NEAR_RATE)
    middle_taps = tap_list(height, breadth, MIDDLE_RATE)
    far_taps = tap_list(height, breadth, FAR_RATE)
    point_taps = [(1, 1, 0, 0)]

    def center_of(taps):
        return [tap[:2] for tap in taps].index((1, 1))

    def stacked(weight, taps):
        flat = weight.reshape((-1,) + weight.shape[2:])
        picked = [3 * tap[0] + tap[1] for tap in taps]
        if picked == list(range(picked[0], picked[-1] + 1)):
            flat = flat[picked[0] : picked[-1] + 1]
        else:
            flat = jnp.stack([flat[at] for at in picked])
        return flat.reshape(-1, flat.shape[2]), len(taps)

    mask = lax.dynamic_index_in_dim(crop_masks, core, 0, keepdims=False)[0]
    labels = lax.dynamic_index_in_dim(pixel_labels, core, 0, keepdims=False)[0]
    task = lax.dynamic_index_in_dim(crop_tasks, core, 0, keepdims=False)[0]
    validity = to_tiles(mask).astype(F32)[:, None]
    valid_tiles = validity.reshape(tiles + (1,))
    labels = to_tiles(labels)
    source = tile_rows(features.reshape(pixels, channels), jnp.array(matrix, BF16))
    source_flipped = flipped(source)

    wide_expand = expand_weight.reshape(-1, quarters, narrow)
    expand_parts = [(wide_expand[:, at], 1) for at in range(quarters)]
    bottle_all = place.gather([(reduce_weight, 1), stacked(spatial_weight, bottle_taps)] + expand_parts)
    spatial_at = channels // narrow
    expand_at = spatial_at + len(bottle_taps)
    pyramid_parts = [stacked(near_weight, near_taps), stacked(middle_weight, middle_taps)]
    pyramid_parts += [stacked(far_weight, far_taps), (point_weight, 1), (project_weight, 1)]
    pyramid_all = place.gather(pyramid_parts)
    middle_at = len(near_taps)
    far_at = middle_at + len(middle_taps)
    point_at = far_at + len(far_taps)
    project_at = (point_at + 1) * (channels // place.pieces)
    project_full = pyramid_all[:, project_at:].reshape(-1, branch)

    crop_valid_both = jnp.sum(crop_masks, axis=(1, 2, 3)).astype(F32)
    home_crop = (crop_tasks[:, 0] == 1).astype(F32)
    counts = jnp.concatenate(
        [
            crop_valid_both,
            jnp.sum(crop_valid_both * (1.0 - home_crop))[None],
            jnp.sum(crop_valid_both * home_crop)[None],
        ]
    )
    small = [bottle_gain, bottle_shift, pyramid_gain, pyramid_shift, head_gain, head_shift]
    small.append(class_weight.reshape(-1))
    small_widths = [part.shape[0] for part in small]
    small_own = jnp.concatenate(small).astype(F32)
    collected = place.everyone(jnp.concatenate([small_own, counts]))
    counts_all = jnp.sum(collected[:, small_own.size :], axis=0)
    small_all, start = [], 0
    for width in small_widths:
        small_all.append(collected[:, start : start + width].reshape(-1))
        start += width
    gain_bottle, shift_bottle, gain_pyramid, shift_pyramid, gain_head, shift_head = small_all[:6]
    class_full = small_all[6].reshape(size * class_weight.shape[0], -1).astype(BF16)
    counted = jnp.where(first_core, counts_all[0], counts_all[1])
    task_pixels = counts_all[2:4]
    crop_valid = jnp.where(first_core, crop_valid_both[0], crop_valid_both[1])

    first, first_sums = first_conv(source, validity, bottle_all, turns, [source_flipped])
    coef_one = coefs(place.total(first_sums), counted, gain_bottle[:narrow], shift_bottle[:narrow])
    first_tiles = first.reshape(tiles + (narrow,))
    conv_in, second, second_sums = spatial_conv(
        first_tiles, coef_one, valid_tiles, bottle_all, bottle_taps, center_of(bottle_taps), spatial_at
    )
    second = second.reshape(pixels, narrow)
    coef_two = coefs(
        place.total(second_sums), counted, gain_bottle[narrow : 2 * narrow], shift_bottle[narrow : 2 * narrow]
    )
    middle_act, third, third_sums = third_conv(
        second, coef_two, validity, bottle_all, expand_at, quarters, turns
    )
    coef_three = coefs(
        place.total(third_sums), counted, gain_bottle[2 * narrow :], shift_bottle[2 * narrow :]
    )
    block_out, pooled_sum = block_output(third, source, coef_three, validity, tiles[0])
    block_tiles = block_out.reshape(tiles + (channels,))

    pooled = (pooled_sum / crop_valid).astype(BF16)
    pooled_all = place.everyone(pooled[0])
    pooled_rows = lax.dynamic_slice_in_dim(pooled_all, place.index * rows, rows, axis=1)
    image_all = place.total(jnp.dot(pooled_rows, image_weight, preferred_element_type=F32))
    branches, branch_sums = branch_convs(
        block_tiles,
        valid_tiles,
        pyramid_all,
        [
            (near_taps, branch),
            (middle_taps, 2 * branch),
            (far_taps, 3 * branch),
            (point_taps, 0),
        ],
        four_wide,
        [image_all],
    )
    branches = branches.reshape(pixels, four_wide)
    image_mean = jnp.sum(image_all, axis=0) / size
    image_scale = lax.rsqrt(
        jnp.sum(image_all * image_all, axis=0) / size - image_mean * image_mean + EPSILON
    )
    image_unit = (image_all - image_mean) * image_scale
    gain_image, shift_image = gain_pyramid[four_wide:], shift_pyramid[four_wide:]
    coef_image = jnp.stack([image_mean, image_scale, gain_image, shift_image])
    image_pre = gain_image * image_unit + shift_image
    image_act = silu(image_pre).astype(BF16)

    block_flipped = flipped(block_out, [branch_sums])
    conv_flipped = flipped(conv_in.reshape(pixels, narrow), [block_flipped])
    coef_branch = coefs(
        place.total(branch_sums), counted, gain_pyramid[:four_wide], shift_pyramid[:four_wide]
    )
    unit_branch, pre_branch = unit_of(branches, coef_branch)
    joined = silu(pre_branch).astype(BF16)

    own_act = lax.dynamic_slice_in_dim(image_act, place.index, 1, axis=0)
    crop_part = jnp.dot(own_act, project_full[four_wide:], preferred_element_type=F32)
    projected = jnp.dot(joined, project_full[:four_wide], preferred_element_type=F32) + crop_part
    coef_head = coefs(place.total(sums(projected, validity)), counted, gain_head, shift_head)
    unit_head, pre_head = unit_of(projected, coef_head)
    output_act = silu(pre_head).astype(BF16)
    logits = jnp.dot(output_act, class_full, preferred_element_type=F32)

    columns = jnp.arange(class_full.shape[1])
    allowed = (columns >= CITY_CLASSES) == (task == 1)
    masked = jnp.where(allowed, logits, FLOOR_LOGIT)
    raised = jnp.exp(masked - jnp.max(masked, axis=-1, keepdims=True))
    chances = raised / jnp.sum(raised, axis=-1, keepdims=True)
    target = jnp.where(task == 0, labels % CITY_CLASSES, CITY_CLASSES + labels % HOME_CLASSES)
    chosen = (columns == target[:, None]).astype(F32)
    inverse = 1.0 / task_norms.astype(F32)
    task_share = inverse / jnp.sum(inverse)
    crop_weight = jnp.where(
        task == 0, task_share[0] / task_pixels[0], task_share[1] / task_pixels[1]
    )
    logit_grad = (crop_weight * validity * (chances - chosen)).astype(BF16)
    class_grad = lax.dot_general(
        output_act, logit_grad, (((0,), (0,)), ((), ())), preferred_element_type=F32
    )

    output_grad = lax.dot_general(
        logit_grad, class_full, (((1,), (1,)), ((), ())), preferred_element_type=F32
    )
    grad_head = output_grad * silu_slope(pre_head)
    head_totals = place.total(grad_moments(grad_head, unit_head))
    proj_grad = through_norm(
        grad_head, unit_head, coef_head, counted, validity, head_totals
    ).astype(BF16)
    crop_grad = jnp.sum(proj_grad, axis=0, dtype=F32)
    joined_grad = lax.dot_general(
        proj_grad, project_full[:four_wide], (((1,), (1,)), ((), ())), preferred_element_type=F32
    )
    act_grad = jnp.dot(project_full[four_wide:].astype(F32), crop_grad, precision=HIGHEST)
    own_pre = lax.dynamic_slice_in_dim(image_pre, place.index, 1, axis=0)[0]
    image_pre_grad = act_grad * silu_slope(own_pre)
    grad_branch = joined_grad * silu_slope(pre_branch)
    branch_parts = place.everyone(
        jnp.concatenate([grad_moments(grad_branch, unit_branch).reshape(-1), image_pre_grad])
    )
    image_pre_all = branch_parts[:, 2 * four_wide :]
    branch_totals = jnp.sum(branch_parts[:, : 2 * four_wide], axis=0).reshape(2, four_wide)
    branch_grad = through_norm(
        grad_branch, unit_branch, coef_branch, counted, validity, branch_totals
    ).astype(BF16)
    image_totals = grad_moments(image_pre_all, image_unit)
    image_in_all = through_norm(
        image_pre_all, image_unit, coef_image, float(size), 1.0, image_totals
    )
    pooled_partial = lax.dot_general(
        image_in_all, image_weight.astype(F32), (((1,), (1,)), ((), ())), precision=HIGHEST
    )
    if place.direct:
        pooled_grad_all = lax.all_to_all(pooled_partial, "batch", 0, 0).reshape(1, channels)
    else:
        pooled_grad_all = lax.dynamic_slice_in_dim(
            lax.all_gather(pooled_partial, "batch", axis=1, tiled=True), place.index, 1, axis=0
        )
    image_partial = jnp.dot(pooled_rows.astype(F32).T, image_in_all, precision=HIGHEST)

    def columns_of(taps, block):
        return [block * branch] * len(taps)

    near_rows = row_plan(near_taps, columns_of(near_taps, 1))
    middle_rows = row_plan(middle_taps, columns_of(middle_taps, 2))
    far_row = row_plan(far_taps, columns_of(far_taps, 3))
    point_row = row_plan(point_taps, columns_of(point_taps, 0))
    project_grad = jnp.concatenate(
        [
            lax.dot_general(
                joined, proj_grad, (((0,), (0,)), ((), ())), preferred_element_type=F32
            ),
            own_act[0].astype(F32)[:, None] * crop_grad[None, :],
        ]
    )

    class_rows = class_grad.size // size // branch if place.direct else 0
    extra_rows = project_grad.shape[0] // size + class_rows

    def extra_halves():
        parts = [project_grad.reshape(size, 2, -1, branch), class_grad.reshape(size, 2, -1, branch)]
        spare = rows // 2 - extra_rows // 2
        parts.append(jnp.zeros((size, 2, spare, branch), F32))
        return jnp.concatenate(parts, axis=2).reshape(-1, branch).astype(BF16)

    def branch_weight_grad(plan, after, extra=None):
        return weight_grad(
            place, block_flipped, branch_grad, meta, plan, tiles, branch, after, extra
        )

    parts = 2 if place.direct else 1
    wide_grads = branch_weight_grad(
        middle_rows + far_row + point_row, [conv_flipped], extra_halves() if place.direct else None
    )
    wide_rows = [rows] * (len(middle_taps) + len(far_taps) + 1) + [extra_rows]
    if not place.direct:
        wide_grads = [jnp.concatenate([wide_grads[0], project_grad.astype(BF16)[None]], axis=1)]
        wide_rows = wide_rows[:-1] + [rows, rows] + wide_rows[-1:]
    wide_scatter = Scatter(place, wide_grads, wide_rows)
    near_grads = branch_weight_grad(near_rows, [wide_grads[0]])
    near_scatter = Scatter(place, near_grads, [rows] * len(near_taps))
    wide_scatter.first()

    pooled_grad = pooled_grad_all / crop_valid
    back_plan = [(far_row[0][0], far_row[0][1] + point_row[0][1])] + near_rows + middle_rows
    far_at = len(near_rows) + len(middle_rows)
    back_order = [far_at] + list(range(far_at))

    def bottle_back(after, scatters):
        grad, moments, *passed = feature_back(
            branch_grad,
            pyramid_all,
            back_plan,
            back_order,
            3 * far_at + len(far_taps),
            third,
            source,
            coef_three,
            pooled_grad,
            validity,
            tiles,
            0,
            1,
            after,
            passing(scatters),
        )
        take_back(scatters, passed)
        return grad, moments

    def sending(*scatters):
        return [array for scatter in scatters for array in scatter.sent]

    def passing(scatters):
        return [array for scatter in scatters for array in scatter.kept]

    def take_back(scatters, passed):
        for scatter in scatters:
            count = len(scatter.kept)
            scatter.kept, passed = passed[:count], passed[count:]

    sum_grad, three_moments = bottle_back(
        [near_grads[0]] + sending(wide_scatter), [wide_scatter, near_scatter]
    )
    wide_scatter.second()
    near_scatter.first()
    three_totals = place.total(three_moments)

    grad_two, two_moments, *expand_grads = third_back(
        place,
        sum_grad,
        third,
        coef_three,
        three_totals / counted,
        validity,
        middle_act,
        second,
        coef_two,
        bottle_all,
        meta,
        expand_at,
        quarters,
        turns,
        sending(near_scatter, wide_scatter),
        passing([near_scatter, wide_scatter]),
    )
    take_back([near_scatter, wide_scatter], expand_grads[parts:])
    expand_grads = expand_grads[:parts]
    wide_scatter.third()
    wide_scatter.launch()
    near_scatter.second()
    unit_two, _ = unit_of(second, coef_two)
    two_totals = place.total(two_moments)
    second_grad = through_norm(
        grad_two, unit_two, coef_two, counted, validity, two_totals
    ).astype(BF16)
    spatial_rows = row_plan(bottle_taps, [0] * len(bottle_taps))
    spatial_grads = weight_grad(
        place,
        conv_flipped,
        second_grad,
        meta,
        spatial_rows,
        tiles,
        narrow,
        sending(wide_scatter, near_scatter),
        None,
        passing([wide_scatter, near_scatter]),
    )
    take_back([wide_scatter, near_scatter], spatial_grads[parts:])
    bottle_grads = [
        jnp.concatenate(pair, axis=1) for pair in zip(spatial_grads[:parts], expand_grads)
    ]
    bottle_rows = [narrow_rows] * (len(bottle_taps) + quarters)
    bottle_scatter = Scatter(place, bottle_grads, bottle_rows)
    near_scatter.third()
    grad_one, one_moments, *passed = spatial_back(
        second_grad,
        first,
        coef_one,
        validity,
        bottle_all,
        [spatial_rows[1], spatial_rows[0], spatial_rows[2]],
        [1, 0, 2],
        tiles,
        spatial_at,
        [spatial_grads[0]],
        passing([wide_scatter, near_scatter, bottle_scatter]) + near_scatter.sent,
    )
    held_back = len(passed) - len(near_scatter.sent)
    take_back([wide_scatter, near_scatter, bottle_scatter], passed[:held_back])
    near_scatter.sent = passed[held_back:]
    near_scatter.launch()
    if place.direct:
        one_moments = tied(one_moments, [bottle_scatter.arrived] + wide_scatter.arrived)
    bottle_scatter.first()
    one_totals = place.total(one_moments)
    unit_one, _ = unit_of(first, coef_one)
    first_grad = through_norm(
        grad_one, unit_one, coef_one, counted, validity, one_totals
    ).astype(BF16)
    reduce_grads = weight_grad(
        place,
        source_flipped,
        first_grad,
        meta,
        row_plan(point_taps, [0]),
        tiles,
        narrow,
        sending(bottle_scatter),
        None,
        passing([bottle_scatter, near_scatter]),
    )
    take_back([bottle_scatter, near_scatter], reduce_grads[parts:])
    reduce_scatter = Scatter(place, reduce_grads[:parts], [rows])
    bottle_scatter.second()

    def rows_back(first_turn, count, into, after, scatters):
        result, *passed = input_back(
            jnp.array(matrix.T, BF16),
            sum_grad,
            first_grad,
            bottle_all,
            turns,
            first_turn,
            count,
            after,
            passing(scatters),
            into,
        )
        take_back(scatters, passed)
        return result

    input_grad = rows_back(0, 2, None, sending(bottle_scatter), [bottle_scatter, reduce_scatter])
    reduce_scatter.first()
    bottle_scatter.third()
    bottle_scatter.launch()
    input_grad = rows_back(2, turns - 2, input_grad, sending(bottle_scatter, reduce_scatter), [bottle_scatter, reduce_scatter])
    reduce_scatter.second()
    reduce_scatter.third()
    reduce_scatter.launch()

    vectors = [one_totals, two_totals, three_totals, branch_totals, image_totals, head_totals]
    vectors += [image_partial]
    packed = jnp.concatenate([vector.reshape(-1) for vector in vectors])
    packed = packed + place.swap(packed)
    split, start = [], 0
    for vector in vectors:
        split.append(packed[start : start + vector.size].reshape(vector.shape))
        start += vector.size

    def own_part(vectors):
        vector = jnp.concatenate(vectors)
        length = vector.shape[0] // size
        return lax.dynamic_slice_in_dim(vector, place.index * length, length, axis=0)

    bottle_gain_grad = own_part([split[0][1], split[1][1], split[2][1]])
    bottle_shift_grad = own_part([split[0][0], split[1][0], split[2][0]])
    pyramid_gain_grad = own_part([split[3][1], split[4][1]])
    pyramid_shift_grad = own_part([split[3][0], split[4][0]])
    head_norm_grad = jnp.stack([own_part([split[5][1]]), own_part([split[5][0]])])
    image_out = split[6]

    def taps_out(full, taps, weight):
        full = full.reshape((len(taps),) + weight.shape[2:])
        if len(taps) == weight.shape[0] * weight.shape[1]:
            return full.reshape(weight.shape)
        result = jnp.zeros(weight.shape, F32)
        for at, tap in enumerate(taps):
            result = result.at[tap[0], tap[1]].set(full[at])
        return result

    for scatter in (near_scatter, wide_scatter, bottle_scatter, reduce_scatter):
        scatter.finish()
    near_count, middle_count, far_count = len(near_taps), len(middle_taps), len(far_taps)
    bottle_count = len(bottle_taps)
    expand_out = bottle_scatter.piece(bottle_count, quarters).reshape(quarters, narrow_rows, narrow)
    if place.direct:
        project_out, class_out = wide_scatter.extra([extra_rows - class_rows, class_rows])
    else:
        project_out = wide_scatter.piece(len(wide_rows) - 1, 1)
        class_out = own_part([lax.psum(class_grad, ("batch", "section"))])
    return (
        input_grad.reshape(features.shape),
        reduce_scatter.piece(0, 1),
        taps_out(bottle_scatter.piece(0, bottle_count), bottle_taps, spatial_weight),
        jnp.swapaxes(expand_out, 0, 1).reshape(expand_weight.shape),
        bottle_gain_grad,
        bottle_shift_grad,
        wide_scatter.piece(middle_count + far_count, 1),
        taps_out(near_scatter.piece(0, near_count), near_taps, near_weight),
        taps_out(wide_scatter.piece(0, middle_count), middle_taps, middle_weight),
        taps_out(wide_scatter.piece(middle_count, far_count), far_taps, far_weight),
        image_out,
        project_out,
        class_out.reshape(class_weight.shape),
        pyramid_gain_grad,
        pyramid_shift_grad,
        head_norm_grad,
    )


def solution(mesh):
    in_specs = (
        P("section", "batch", None, None, None),
        P("batch", None),
        P(None, None, "batch", None),
        P("batch", None),
        P("batch"),
        P("batch"),
        P("batch", None),
        P(None, None, "batch", None),
        P(None, None, "batch", None),
        P(None, None, "batch", None),
        P("batch", None),
        P("batch", None),
        P("batch", None),
        P("batch"),
        P("batch"),
        P("batch"),
        P("batch"),
        P(None, "batch", None, None),
        P(None, "batch"),
        P(None, "batch", None, None),
        P(),
    )
    out_specs = (
        P("section", "batch", None, None, None),
        P("batch", None),
        P(None, None, "batch", None),
        P("batch", None),
        P("batch"),
        P("batch"),
        P("batch", None),
        P(None, None, "batch", None),
        P(None, None, "batch", None),
        P(None, None, "batch", None),
        P("batch", None),
        P("batch", None),
        P("batch", None),
        P("batch"),
        P("batch"),
        P(None, "batch"),
    )
    return jax.shard_map(
        per_device, mesh=mesh, in_specs=in_specs, out_specs=out_specs, check_vma=False
    )
```

```python
import functools

import jax
import jax.numpy as jnp
import numpy as np
from jax import lax
from jax.experimental import pallas as pl
from jax.experimental.pallas import tpu as pltpu
from jax.sharding import PartitionSpec as P

CITY_CLASSES = 19
HOME_CLASSES = 13
BOTTLE_RATE = 4
NEAR_RATE = 12
MIDDLE_RATE = 24
FAR_RATE = 36
TILE = 4

EPSILON = 1e-05
FLOOR_LOGIT = -1e30
HIGHEST = lax.Precision.HIGHEST
F32 = jnp.float32
BF16 = jnp.bfloat16
SLOT_BITS = [0, 4, 2, 6, 1, 5, 3, 7, 8, 12, 9, 13, 10, 14, 11, 15]
VMEM_BYTES = 58 * 1024 * 1024


class Place:
    def __init__(self):
        self.size = lax.axis_size("batch")
        self.direct = self.size == len(SLOT_BITS)
        self.pieces = 2 * self.size if self.direct else 1
        self.core = lax.axis_index("section")
        self.index = lax.axis_index("batch")

    def meta(self):
        core = self.core[None].astype(jnp.int32)
        if not self.direct:
            return core
        table = [[SLOT_BITS.index(at ^ owner) for owner in range(self.size)] for at in range(self.size)]
        row = lax.dynamic_index_in_dim(jnp.array(table, jnp.int32), self.index, 0, keepdims=False)
        return jnp.concatenate([core, row])

    def flip(self, block, bits):
        return lax.ppermute(block, "batch", [(source, source ^ bits) for source in range(self.size)])

    def swap(self, block):
        return lax.ppermute(block, "section", [(0, 1), (1, 0)])

    def total(self, *arrays):
        if not self.direct:
            return lax.psum(arrays, "batch") if len(arrays) > 1 else lax.psum(arrays[0], "batch")
        summed = jnp.sum(self.everyone(jnp.concatenate([array.reshape(-1) for array in arrays])), axis=0)
        results, start = [], 0
        for array in arrays:
            results.append(summed[start : start + array.size].reshape(array.shape))
            start += array.size
        return results if len(arrays) > 1 else results[0]

    def everyone(self, vector):
        if not self.direct:
            return lax.all_gather(vector, "batch")
        sent = jnp.broadcast_to(vector, (self.size,) + vector.shape)
        return lax.all_to_all(sent, "batch", 0, 0)

    def gather(self, parts):
        blocks = []
        for part, count in parts:
            cut = part.reshape(count, -1, part.shape[1])
            if self.direct:
                half = cut.shape[1] // 2
                cut = lax.dynamic_slice_in_dim(cut, self.core * half, half, axis=1)
            else:
                cut = lax.all_gather(cut, "batch", axis=1, tiled=True)
            blocks.append(cut.reshape(-1, part.shape[1]))
        block = jnp.concatenate(blocks)
        if self.direct:
            return lax.all_gather(block, ("batch", "section"))
        return block[None]


class Scatter:
    def __init__(self, place, grads, rows):
        self.place, self.rows = place, rows
        self.kept, self.sent = [grads[0]], []
        self.arrived = place.swap(grads[1]) if place.direct else None

    def add(self, kept, arrived):
        return (kept.astype(F32) + arrived.astype(F32)).astype(BF16)

    def first(self):
        if not self.place.direct:
            return
        own, arrived = self.kept[0], self.arrived
        self.kept = []
        sent = []
        for start in (0, 8):
            self.kept.append(self.add(own[start : start + 4], arrived[start : start + 4]))
            sent.append(self.add(own[start + 4 : start + 8], arrived[start + 4 : start + 8]))
        self.sent = sent
        self.arrived = [self.place.flip(sent[0], 1), self.place.flip(sent[1], 2)]

    def second(self):
        if not self.place.direct:
            return
        kept, sent = [], []
        for held, came in zip(self.kept, self.arrived):
            kept.append(self.add(held[:2], came[:2]))
            sent.append(self.add(held[2:], came[2:]))
        self.kept, self.sent = kept, sent
        self.arrived = [self.place.flip(sent[0], 2), self.place.flip(sent[1], 1)]

    def third(self):
        if not self.place.direct:
            return
        near = self.kept[0].astype(F32) + self.arrived[0].astype(F32)
        away = self.kept[1].astype(F32) + self.arrived[1].astype(F32)
        self.kept = [near[0]]
        sent = [near[1].astype(BF16), away[0].astype(BF16), away[1].astype(BF16)]
        self.sent = sent

    def launch(self):
        if self.place.direct:
            self.arrived = [
                self.place.flip(piece, bits) for piece, bits in zip(self.sent, (4, 8, 12))
            ]

    def finish(self):
        if self.place.direct:
            parts = [piece.astype(F32) for piece in self.arrived]
            result = (self.kept[0] + parts[0]) + (parts[1] + parts[2])
            opposite = self.place.swap(result)
            first = self.place.core == 0
            self.result = [jnp.where(first, result, opposite), jnp.where(first, opposite, result)]
            return self
        pieces, start = [], 0
        for rows in self.rows:
            cut = self.kept[0][0, start : start + rows * self.place.size].astype(F32)
            cut = lax.psum_scatter(cut, "batch", scatter_dimension=0, tiled=True)
            pieces.append(lax.psum(cut, "section"))
            start += rows * self.place.size
        self.result = [jnp.concatenate(pieces)]
        return self

    def extra(self, sizes):
        start = sum(self.rows[:-1]) // 2
        found = []
        for rows in sizes:
            found.append(jnp.concatenate([part[start : start + rows // 2] for part in self.result]))
            start += rows // 2
        return found

    def piece(self, first, count):
        parts = len(self.result)
        start = sum(self.rows[:first]) // parts
        rows = self.rows[first] // parts
        cut = [part[start : start + count * rows].reshape(count, rows, -1) for part in self.result]
        return jnp.concatenate(cut, axis=1).reshape(count * rows * parts, -1)


def call(body, args, specs, grid, outs, out_specs, scratch=(), meta=None, after=(), passed=(), into=None, flops=1):
    used = len(args) + (meta is not None)
    passed = list(passed) if into is None else [into] + list(passed)
    waits = len(after) + len(passed)
    results = len(outs)
    filled = int(into is not None)
    kept = results - filled

    def inner(*refs):
        rest = refs[used + waits :]
        body(*refs[:used], *rest[:results], *rest[results + len(passed) - filled :])

    spec = pltpu.PrefetchScalarGridSpec(
        num_scalar_prefetch=int(meta is not None),
        grid=grid,
        in_specs=list(specs) + [pl.BlockSpec(memory_space=pl.ANY)] * waits,
        out_specs=list(out_specs) + [pl.BlockSpec(memory_space=pl.ANY)] * (len(passed) - filled),
        scratch_shapes=list(scratch),
    )
    arrays = ([] if meta is None else [meta]) + list(args) + list(after) + list(passed)
    first = len(arrays) - len(passed)
    return pl.pallas_call(
        inner,
        grid_spec=spec,
        out_shape=list(outs) + [shaped(array.shape, array.dtype) for array in passed[filled:]],
        input_output_aliases={first + at: kept + at for at in range(len(passed))},
        compiler_params=pltpu.CompilerParams(vmem_limit_bytes=VMEM_BYTES),
        cost_estimate=pl.CostEstimate(flops=flops, transcendentals=0, bytes_accessed=1),
    )(*arrays)


def copy_body(source_ref, result_ref):
    result_ref[...] = source_ref[...]


def tied(array, after):
    return call(
        copy_body, [array], [whole(array)], (1,), [shaped(array.shape)], [held(array.shape)], after=after
    )[0]


def whole(array):
    shape = array.shape
    return pl.BlockSpec(
        shape, lambda *_: (0,) * len(shape), pipeline_mode=pl.Buffered(buffer_count=1)
    )


def held(shape):
    return pl.BlockSpec(shape, lambda *_: (0,) * len(shape))


def rows_of(array, rows):
    return pl.BlockSpec((rows, array.shape[1]), lambda step, *_: (step, 0))


def shaped(shape, dtype=F32):
    return jax.ShapeDtypeStruct(tuple(shape), dtype)


def span(shift_by, length):
    return max(0, -shift_by), length - max(0, shift_by)


def tap_list(height, breadth, dilation):
    listed = []
    for row_tap in range(3):
        for col_tap in range(3):
            row_shift = (row_tap - 1) * dilation
            col_shift = (col_tap - 1) * dilation
            if abs(row_shift) < height and abs(col_shift) < breadth:
                listed.append((row_tap, col_tap, row_shift // TILE, col_shift // TILE))
    return listed


def weight_of(ref):
    return ref[...].reshape(-1, ref.shape[-1])


def spread(meta_ref, full_ref, result_refs, column=0, at=0, rows=None):
    width = result_refs[0].shape[2]
    rows = result_refs[0].shape[1] if rows is None else rows
    if len(result_refs) == 1:
        result_refs[0][0, at : at + rows] = full_ref[:, column : column + width].astype(BF16)
        return
    core = meta_ref[0]
    for owner in range(result_refs[0].shape[0]):
        for ref, side in zip(result_refs, (core, 1 - core)):
            start = pl.multiple_of(owner * 2 * rows + side * rows, rows)
            block = full_ref[pl.ds(start, rows), column : column + width]
            ref[meta_ref[1 + owner], at : at + rows] = block.astype(BF16)


def slotted(place, rows, width):
    if place.direct:
        return [shaped((place.size, rows // 2, width), BF16)] * 2
    return [shaped((1, rows * place.size, width), BF16)]


def center_first(step, center):
    return jnp.where(step == 0, center, jnp.where(step <= center, step - 1, step))


def ordered(taps, center):
    return [taps[center]] + [tap for place, tap in enumerate(taps) if place != center]


def shifts_of(taps):
    return [(tap[2], tap[3]) for tap in taps]


def area(tap, tiles):
    return (tiles[0] - abs(tap[0])) * (tiles[1] - abs(tap[1])) * tiles[2]


def forward_tap(tap, fresh, source_ref, weight, result_ref):
    tiles_i, tiles_j, pixels, channels = source_ref.shape
    columns = weight.shape[1]
    shift_i, shift_j = tap
    low_i, high_i = span(shift_i, tiles_i)
    low_j, high_j = span(shift_j, tiles_j)
    window = source_ref[
        low_i + shift_i : high_i + shift_i, low_j + shift_j : high_j + shift_j
    ].reshape(-1, channels)
    product = jnp.dot(window, weight, preferred_element_type=F32)
    product = product.reshape(high_i - low_i, high_j - low_j, pixels, columns)
    if fresh:
        result_ref[low_i:high_i, low_j:high_j] = product
    else:
        result_ref[low_i:high_i, low_j:high_j] += product


def repeat(count, body):
    lax.fori_loop(0, count, lambda turn, carry: (body(turn), carry)[1], 0)


def row_steps(count):
    return max(step for step in (1, 2, 3, 4) if count % step == 0)


FIELDS = 9


def tap_table(plan, tiles, places):
    table, classes = [], []
    for ((shift_i, shift_j), column), place in zip(plan, places):
        low_i, high_i = span(shift_i, tiles[0])
        low_j, high_j = span(shift_j, tiles[1])
        kind = (row_steps(high_i - low_i), high_j - low_j)
        if kind not in classes:
            classes.append(kind)
        table += [classes.index(kind), low_i, low_i + shift_i, (high_i - low_i) // kind[0]]
        table += [low_j, low_j + shift_j, column, place, 0]
    return np.array(table, np.int32), classes


def forward_taps(classes, table_ref, source_ref, weight_ref, result_ref):
    _, _, pixels, channels = source_ref.shape
    width = weight_ref.shape[2]
    at = pl.program_id(0) * FIELDS
    for kind, (rows, wide) in enumerate(classes):

        @pl.when(table_ref[at] == kind)
        def _(rows=rows, wide=wide):
            to_i, from_i, turns = table_ref[at + 1], table_ref[at + 2], table_ref[at + 3]
            to_j, from_j = table_ref[at + 4], table_ref[at + 5]
            column = pl.multiple_of(table_ref[at + 6], width)

            def body(turn):
                window = source_ref[pl.ds(from_i + turn * rows, rows), pl.ds(from_j, wide)]
                product = jnp.dot(
                    window.reshape(-1, channels), weight_of(weight_ref), preferred_element_type=F32
                )
                place = (
                    pl.ds(to_i + turn * rows, rows),
                    pl.ds(to_j, wide),
                    slice(None),
                    pl.ds(column, width),
                )
                result_ref[place] += product.reshape(rows, wide, pixels, width)

            repeat(turns, body)


def unit_of(values, coef):
    unit = (values - coef[0:1]) * coef[1:2]
    return unit, coef[2:3] * unit + coef[3:4]


def masked_sums(values, valid):
    weighted = values * valid
    return jnp.concatenate(
        [jnp.sum(weighted, axis=0, keepdims=True), jnp.sum(weighted * values, axis=0, keepdims=True)]
    )


def sum_rows(ref, valid_ref, sums_ref):
    total = jnp.zeros(sums_ref.shape, F32)
    for row in range(ref.shape[0]):
        values = ref[row].reshape(-1, ref.shape[-1])
        total = total + masked_sums(values, valid_ref[row].reshape(-1, 1))
    sums_ref[...] = total


def branch_body(classes, table_ref, source_ref, valid_ref, weight_ref, result_ref, sums_ref):
    @pl.when(pl.program_id(0) == 0)
    def _():
        def clear(row):
            result_ref[row] = jnp.zeros(result_ref.shape[1:], F32)

        repeat(result_ref.shape[0], clear)

    forward_taps(classes, table_ref, source_ref, weight_ref, result_ref)

    @pl.when(pl.program_id(0) == pl.num_programs(0) - 1)
    def _():
        sum_rows(result_ref, valid_ref, sums_ref)


def placed_block(weights, channels):
    pieces, _, width = weights.shape
    return pl.BlockSpec(
        (pieces, channels // pieces, width), lambda step, table: (0, table[step * FIELDS + 7], 0)
    )


def branch_convs(source, valid, weights, groups, columns, after):
    channels = source.shape[-1]
    plan = [(shift, column) for taps, column in groups for shift in shifts_of(taps)]
    table, classes = tap_table(plan, source.shape, range(len(plan)))
    result_shape = source.shape[:3] + (columns,)
    return call(
        functools.partial(branch_body, classes),
        [source, valid, weights],
        [whole(source), whole(valid), placed_block(weights, channels)],
        (len(plan),),
        [shaped(result_shape), shaped((2, columns))],
        [held(result_shape), held((2, columns))],
        meta=jnp.array(table),
        after=after,
    )


def spatial_body(plan, first_ref, coef_ref, valid_ref, weight_ref, input_ref, result_ref, sums_ref):
    @pl.when(pl.program_id(0) == 0)
    def _():
        for row in range(first_ref.shape[0]):
            _, pre = unit_of(first_ref[row], coef_ref[...][:, None, :])
            input_ref[row] = (silu(pre) * valid_ref[row]).astype(BF16)

    for place, tap in enumerate(plan):

        @pl.when(pl.program_id(0) == place)
        def _(place=place, tap=tap):
            forward_tap(tap, place == 0, input_ref, weight_of(weight_ref), result_ref)

    @pl.when(pl.program_id(0) == len(plan) - 1)
    def _():
        sum_rows(result_ref, valid_ref, sums_ref)


def spatial_conv(first, coef, valid, weights, taps, center, first_tap):
    channels = first.shape[-1]
    pieces, _, columns = weights.shape
    plan = ordered(shifts_of(taps), center)
    return call(
        functools.partial(spatial_body, plan),
        [first, coef, valid, weights],
        [
            whole(first),
            whole(coef),
            whole(valid),
            pl.BlockSpec(
                (pieces, channels // pieces, columns),
                lambda step: (0, first_tap + center_first(step, center), 0),
            ),
        ],
        (len(plan),),
        [shaped(first.shape, BF16), shaped(first.shape), shaped((2, columns))],
        [held(first.shape), held(first.shape), held((2, columns))],
    )


def shifted_columns(tiles, row_taps, up_ref, padded_ref, width, first=None, last=None):
    tiles_i, tiles_j, pixels = tiles
    shift_i, columns = row_taps
    low_i, high_i = span(shift_i, tiles_i)
    line = tiles_j * pixels
    low, high = (low_i + shift_i) * line, (high_i + shift_i) * line

    def clear(start, stop, at):
        if stop > start:
            padded_ref[start:stop, at : at + width] = jnp.zeros((stop - start, width), BF16)

    for place, (shift_j, column) in enumerate(columns):
        at = place * width
        low_j, high_j = span(shift_j, tiles_j)
        begin, end = (low_j + shift_j) * pixels, (high_j + shift_j) * pixels
        for row in range(low_i, high_i):
            base = (row + shift_i) * line
            source = row * line + low_j * pixels
            clear(base, base + begin, at)
            padded_ref[base + begin : base + end, at : at + width] = up_ref[
                source : source + end - begin, column : column + width
            ]
            clear(base + end, base + line, at)
        if first is not None:
            clear(first, low, at)
            clear(high, last, at)
    return low, high


def back_step(tiles, row_taps, fresh, up_ref, weight_refs, padded_ref, weight_ref, total_ref):
    channels = total_ref.shape[1]
    width = weight_refs[0].shape[2]
    depth = len(row_taps[1]) * width
    low, high = shifted_columns(tiles, row_taps, up_ref, padded_ref, width)
    for place in range(len(row_taps[1])):
        weight_ref[:, place * width : (place + 1) * width] = weight_of(weight_refs[place])
    wide = min(512, channels)
    for start in range(0, channels, wide):
        product = lax.dot_general(
            padded_ref[low:high, :depth],
            weight_ref[start : start + wide, :depth],
            (((1,), (1,)), ((), ())),
            preferred_element_type=F32,
        )
        if fresh:
            total_ref[low:high, start : start + wide] = product
        else:
            total_ref[low:high, start : start + wide] += product


def row_plan(taps, columns):
    rows = []
    for tap, column in zip(taps, columns):
        if not rows or rows[-1][0] != tap[2]:
            rows.append((tap[2], []))
        rows[-1][1].append((tap[3], column))
    return rows


def row_weights(weights, channels, order, first_tap, side=0, sides=1):
    pieces, _, width = weights.shape
    rows = channels // pieces
    specs = []
    for column in range(3):

        def index(step, column=column):
            row = order[-1]
            for place, listed in enumerate(order[:-1]):
                row = jnp.where(step == place, listed, row)
            tap = first_tap + 3 * row + column
            return (0, tap * sides + side, 0) if pieces == 1 else (side, tap, 0)

        block = (1, rows // sides, width) if pieces == 1 else (pieces // sides, rows, width)
        specs.append(pl.BlockSpec(block, index))
    return specs


def grad_moments(grad, unit):
    return jnp.concatenate(
        [jnp.sum(grad, axis=0, keepdims=True), jnp.sum(grad * unit, axis=0, keepdims=True)]
    )


def feature_body(
    plan, tiles, up_ref, third_ref, source_ref, coef_ref, pooled_ref, valid_ref, *refs
):
    weight_refs = refs[:4]
    result_ref, sums_ref, padded_ref, weight_ref, total_ref = refs[4:]
    step_now = pl.program_id(0)
    for place, row_taps in enumerate(plan):

        @pl.when(step_now == place)
        def _(place=place, row_taps=row_taps):
            back_step(
                tiles, row_taps, place == 0, up_ref, weight_refs, padded_ref, weight_ref, total_ref
            )

    begun = len(plan)

    @pl.when(step_now >= begun)
    def _():
        height = third_ref.shape[0]
        row = pl.multiple_of((step_now - begun) * height, height)
        unit, pre = unit_of(third_ref[...], coef_ref[...])
        pre = pre + source_ref[...].astype(F32)
        grad = total_ref[pl.ds(row, height)] + pooled_ref[...]
        grad = grad * valid_ref[...] * silu_slope(pre)
        result_ref[...] = grad.astype(BF16)
        moments = grad_moments(grad, unit)

        @pl.when(step_now == begun)
        def _():
            sums_ref[...] = moments

        @pl.when(step_now > begun)
        def _():
            sums_ref[...] += moments


def feature_back(upstream, weights, plan, order, point, third, source, coef, pooled, valid, tiles, side, sides, after, passed):
    pixels, channels = third.shape
    part = channels // sides
    pieces, _, width = weights.shape
    rows = channels // pieces
    begun = len(plan)
    turns = tiles[0]
    height = pixels // turns

    def row_of(step):
        return jnp.clip(step - begun, 0, turns - 1)

    row_block = pl.BlockSpec((height, part), lambda step: (row_of(step), side))
    if pieces == 1:
        point_block = pl.BlockSpec((1, rows // sides, width), lambda step: (0, point * sides + side, 0))
    else:
        point_block = pl.BlockSpec((pieces // sides, rows, width), lambda step: (side, point, 0))
    return call(
        functools.partial(feature_body, plan, tiles),
        [upstream, third, source, coef, pooled, valid] + [weights] * 4,
        [
            whole(upstream),
            row_block,
            row_block,
            pl.BlockSpec((coef.shape[0], part), lambda step: (0, side)),
            pl.BlockSpec((1, part), lambda step: (0, side)),
            pl.BlockSpec((height, 1), lambda step: (row_of(step), 0)),
        ]
        + row_weights(weights, channels, order, 0, side, sides)
        + [point_block],
        (begun + turns,),
        [shaped((pixels, part), BF16), shaped((2, part))],
        [pl.BlockSpec((height, part), lambda step: (row_of(step), 0)), held((2, part))],
        [
            pltpu.VMEM((pixels, 4 * width), BF16),
            pltpu.VMEM((part, 4 * width), BF16),
            pltpu.VMEM((pixels, part), F32),
        ],
        after=after,
        passed=passed,
    )


def spatial_back_body(plan, tiles, up_ref, first_ref, coef_ref, valid_ref, *refs):
    weight_refs = refs[:3]
    result_ref, sums_ref, padded_ref, weight_ref = refs[3:]
    for place, row_taps in enumerate(plan):

        @pl.when(pl.program_id(0) == place)
        def _(place=place, row_taps=row_taps):
            back_step(
                tiles, row_taps, place == 0, up_ref, weight_refs, padded_ref, weight_ref, result_ref
            )

    @pl.when(pl.program_id(0) == len(plan) - 1)
    def _():
        total = jnp.zeros(sums_ref.shape, F32)
        height = result_ref.shape[0] // tiles[0]
        for row in range(tiles[0]):
            at = slice(row * height, (row + 1) * height)
            unit, pre = unit_of(first_ref[at], coef_ref[...])
            grad = result_ref[at] * valid_ref[at] * silu_slope(pre)
            result_ref[at] = grad
            total = total + grad_moments(grad, unit)
        sums_ref[...] = total


def spatial_back(upstream, first, coef, valid, weights, plan, order, tiles, first_tap, after, passed):
    pixels, channels = first.shape
    columns = weights.shape[2]
    return call(
        functools.partial(spatial_back_body, plan, tiles),
        [upstream, first, coef, valid] + [weights] * 3,
        [whole(upstream), whole(first), whole(coef), whole(valid)]
        + row_weights(weights, channels, order, first_tap),
        (len(plan),),
        [shaped(first.shape), shaped((2, channels))],
        [held(first.shape), held((2, channels))],
        [pltpu.VMEM((pixels, 3 * columns), BF16), pltpu.VMEM((channels, 3 * columns), BF16)],
        after=after,
        passed=passed,
    )


def weight_body(plan, tiles, extra, count, meta_ref, flipped_ref, up_ref, *refs):
    extra_ref = refs[0] if extra else None
    result_refs = refs[extra : extra + count]
    padded_ref, full_ref = refs[extra + count :]
    block_rows, width = result_refs[0].shape[1:]
    taps_held = padded_ref.shape[1] // width
    rows = block_rows // taps_held
    for place, row_taps in enumerate(plan):

        @pl.when(pl.program_id(0) == place)
        def _(row_taps=row_taps):
            taps = len(row_taps[1])
            low_i, high_i = span(row_taps[0], tiles[0])
            line = tiles[1] * tiles[2]
            first = (low_i + row_taps[0]) * line // 128 * 128
            last = -(-(high_i + row_taps[0]) * line // 128) * 128
            shifted_columns(tiles, row_taps, up_ref, padded_ref, width, first, last)
            for tap in range(taps):
                at = slice(tap * width, (tap + 1) * width)
                full_ref[:, at] = jnp.dot(
                    flipped_ref[:, first:last], padded_ref[first:last, at], preferred_element_type=F32
                ).astype(BF16)
                spread(meta_ref, full_ref, result_refs, tap * width, tap * rows, rows)

    if extra:

        @pl.when(pl.program_id(0) == len(plan) - 1)
        def _():
            core = meta_ref[0]
            taps = len(plan[-1][1])
            spare = (taps_held - taps - 1) * rows
            for owner in range(result_refs[0].shape[0]):
                slot = meta_ref[1 + owner]
                for ref, side in zip(result_refs, (core, 1 - core)):
                    start = pl.multiple_of((owner * 2 + side) * rows, rows)
                    ref[slot, taps * rows : (taps + 1) * rows] = extra_ref[pl.ds(start, rows)]
                    ref[slot, (taps + 1) * rows :] = jnp.zeros((spare, width), BF16)


def weight_grad(place, flipped, upstream, meta, plan, tiles, width, after=(), extra=None, passed=()):
    channels, padded = flipped.shape
    taps = max(len(row_taps[1]) for row_taps in plan)
    steps = len(plan)
    shapes = slotted(place, channels // place.size * taps * steps, width)
    blocks = [
        pl.BlockSpec((shape.shape[0], shape.shape[1] // steps, width), lambda step, _: (0, step, 0))
        for shape in shapes
    ]
    more = [] if extra is None else [extra]
    return call(
        functools.partial(weight_body, plan, tiles, len(more), len(shapes)),
        [flipped, upstream] + more,
        [whole(array) for array in [flipped, upstream] + more],
        (steps,),
        shapes,
        blocks,
        [pltpu.VMEM((padded, taps * width), BF16), pltpu.VMEM((channels, taps * width), BF16)],
        meta,
        after,
        passed,
    )


def tile_matrix(breadth):
    count = TILE * breadth
    matrix = np.zeros((count, count), np.float32)
    for row in range(TILE):
        for column in range(breadth):
            at = (column // TILE * TILE + row) * TILE + column % TILE
            matrix[at, row * breadth + column] = 1.0
    return matrix


def tile_body(matrix_ref, natural_ref, result_ref):
    result_ref[...] = jnp.dot(
        matrix_ref[...], natural_ref[...], preferred_element_type=F32
    ).astype(BF16)


def tile_rows(natural, matrix):
    rows = matrix.shape[0]
    return call(
        tile_body,
        [matrix, natural],
        [whole(matrix), rows_of(natural, rows)],
        (natural.shape[0] // rows,),
        [shaped(natural.shape, BF16)],
        [rows_of(natural, rows)],
    )[0]


def flip_body(source_ref, result_ref):
    pixels = source_ref.shape[0]
    result_ref[:, :pixels] = source_ref[...].T
    if result_ref.shape[1] > pixels:
        extra = result_ref.shape[1] - pixels
        result_ref[:, pixels:] = jnp.zeros((result_ref.shape[0], extra), BF16)


def flipped(values, after=()):
    pixels, channels = values.shape
    padded = pixels + -pixels % 128
    return call(
        flip_body,
        [values],
        [pl.BlockSpec((pixels, 128), lambda step: (0, step))],
        (channels // 128,),
        [shaped((channels, padded), BF16)],
        [pl.BlockSpec((128, padded), lambda step: (step, 0))],
        after=after,
    )[0]


def add_sums(sums_ref, sums):
    @pl.when(pl.program_id(0) == 0)
    def _():
        sums_ref[...] = sums

    @pl.when(pl.program_id(0) > 0)
    def _():
        sums_ref[...] += sums


def first_body(source_ref, valid_ref, weight_ref, result_ref, sums_ref):
    product = jnp.dot(source_ref[...], weight_of(weight_ref), preferred_element_type=F32)
    result_ref[...] = product
    add_sums(sums_ref, masked_sums(product, valid_ref[...]))


def fixed_block(weights, channels, at):
    pieces, _, columns = weights.shape
    return pl.BlockSpec((pieces, channels // pieces, columns), lambda step, *_: (0, at, 0))


def first_conv(source, valid, weights, turns, after):
    pixels, channels = source.shape
    rows = pixels // turns
    width = weights.shape[2]
    return call(
        first_body,
        [source, valid, weights],
        [rows_of(source, rows), rows_of(valid, rows), fixed_block(weights, channels, 0)],
        (turns,),
        [shaped((pixels, width)), shaped((2, width))],
        [pl.BlockSpec((rows, width), lambda step: (step, 0)), held((2, width))],
        after=after,
    )


def third_body(count, second_ref, coef_ref, valid_ref, *refs):
    weight_refs = refs[:count]
    middle_ref, result_ref, sums_ref = refs[count:]
    _, pre = unit_of(second_ref[...], coef_ref[...])
    middle = silu(pre).astype(BF16)
    middle_ref[...] = middle
    valid = valid_ref[...]
    sums = []
    for quarter, ref in enumerate(weight_refs):
        product = jnp.dot(middle, weight_of(ref), preferred_element_type=F32)
        width = product.shape[1]
        result_ref[:, quarter * width : (quarter + 1) * width] = product
        sums.append(masked_sums(product, valid))
    add_sums(sums_ref, jnp.concatenate(sums, axis=1))


def third_conv(second, coef, valid, weights, first, count, turns):
    pixels, narrow = second.shape
    height = pixels // turns
    channels = count * weights.shape[2]
    return call(
        functools.partial(third_body, count),
        [second, coef, valid] + [weights] * count,
        [rows_of(second, height), whole(coef), rows_of(valid, height)]
        + [fixed_block(weights, narrow, first + quarter) for quarter in range(count)],
        (turns,),
        [shaped((pixels, narrow), BF16), shaped((pixels, channels)), shaped((2, channels))],
        [
            pl.BlockSpec((height, narrow), lambda step: (step, 0)),
            pl.BlockSpec((height, channels), lambda step: (step, 0)),
            held((2, channels)),
        ],
    )


def output_body(third_ref, source_ref, coef_ref, valid_ref, result_ref, sums_ref):
    _, pre = unit_of(third_ref[...], coef_ref[...])
    values = (valid_ref[...] * silu(pre + source_ref[...].astype(F32))).astype(BF16)
    result_ref[...] = values
    add_sums(sums_ref, jnp.sum(values.astype(F32), axis=0, keepdims=True))


def block_output(third, source, coef, valid, turns):
    pixels, channels = third.shape
    rows = pixels // turns
    return call(
        output_body,
        [third, source, coef, valid],
        [rows_of(third, rows), rows_of(source, rows), whole(coef), rows_of(valid, rows)],
        (turns,),
        [shaped(third.shape, BF16), shaped((1, channels))],
        [rows_of(third, rows), held((1, channels))],
    )


def third_back_body(
    count, outs, meta_ref, low_ref, high_ref, third_ref, coef_ref, totals_ref, valid_ref, middle_ref, *refs
):
    second_ref, second_coef_ref = refs[:2]
    refs = refs[2:]
    weight_refs = refs[:count]
    result_ref, sums_ref = refs[count : count + 2]
    slot_refs = refs[count + 2 : count + 2 + outs]
    grad_ref, total_ref = refs[count + 2 + outs :]
    step_now = pl.program_id(0)

    @pl.when(step_now == 0)
    def _():
        total_ref[...] = jnp.zeros_like(total_ref)

    part = low_ref.shape[1]
    coef, totals, valid = coef_ref[...], totals_ref[...], valid_ref[...]
    for start, part_ref in ((0, low_ref), (part, high_ref)):
        at = slice(start, start + part)
        unit = (third_ref[:, at] - coef[0:1, at]) * coef[1:2, at]
        centered = part_ref[...].astype(F32) - valid * (totals[0:1, at] + unit * totals[1:2, at])
        grad_ref[:, at] = (coef[2:3, at] * coef[1:2, at] * centered).astype(BF16)
    width = weight_refs[0].shape[2]
    result = None
    for quarter, ref in enumerate(weight_refs):
        grad = grad_ref[:, quarter * width : (quarter + 1) * width]
        product = lax.dot_general(
            grad, weight_of(ref), (((1,), (1,)), ((), ())), preferred_element_type=F32
        )
        result = product if result is None else result + product
    unit, pre = unit_of(second_ref[...], second_coef_ref[...])
    result = result * silu_slope(pre)
    result_ref[...] = result
    add_sums(sums_ref, grad_moments(result, unit))
    total_ref[...] += lax.dot_general(
        middle_ref[...], grad_ref[...], (((0,), (0,)), ((), ())), preferred_element_type=F32
    )

    @pl.when(step_now == pl.num_programs(0) - 1)
    def _():
        rows = slot_refs[0].shape[1] // count
        for quarter in range(count):
            spread(meta_ref, total_ref, slot_refs, quarter * width, quarter * rows, rows)


def third_back(place, low, high, third, coef, totals, valid, middle, second, second_coef, weights, meta, first, count, turns, after, passed):
    pixels, channels = third.shape
    narrow = middle.shape[1]
    height = pixels // turns
    shapes = slotted(place, narrow // place.size * count, weights.shape[2])
    return call(
        functools.partial(third_back_body, count, len(shapes)),
        [low, high, third, coef, totals, valid, middle, second, second_coef] + [weights] * count,
        [
            rows_of(low, height),
            rows_of(high, height),
            rows_of(third, height),
            whole(coef),
            whole(totals),
            rows_of(valid, height),
            rows_of(middle, height),
            rows_of(second, height),
            whole(second_coef),
        ]
        + [fixed_block(weights, narrow, first + quarter) for quarter in range(count)],
        (turns,),
        [shaped((pixels, narrow)), shaped((2, narrow))] + shapes,
        [pl.BlockSpec((height, narrow), lambda step, _: (step, 0)), held((2, narrow))]
        + [held(shape.shape) for shape in shapes],
        [pltpu.VMEM((height, channels), BF16), pltpu.VMEM((narrow, channels), F32)],
        meta,
        after,
        passed,
    )


def input_body(matrix_ref, low_ref, high_ref, grad_ref, weight_ref, result_ref):
    rows = matrix_ref.shape[0]
    part = low_ref.shape[1]
    matrix = matrix_ref[...]
    moved = []
    for start in range(0, result_ref.shape[0], rows):
        at = slice(start, start + rows)
        moved.append(jnp.dot(matrix, grad_ref[at], preferred_element_type=F32).astype(BF16))
        for column, part_ref in ((0, low_ref), (part, high_ref)):
            result_ref[at, column : column + part] = jnp.dot(
                matrix, part_ref[at], preferred_element_type=F32
            )
    result_ref[...] += lax.dot_general(
        jnp.concatenate(moved), weight_of(weight_ref), (((1,), (1,)), ((), ())), preferred_element_type=F32
    )


def input_back(matrix, low, high, grad, weights, turns, first, count, after, passed, into):
    pixels, part = low.shape
    rows = pixels // turns
    channels = 2 * part
    width = grad.shape[1]

    def block(columns):
        return pl.BlockSpec((rows, columns), lambda step: (first + step, 0))

    return call(
        input_body,
        [matrix, low, high, grad, weights],
        [whole(matrix), block(part), block(part), block(width), fixed_block(weights, channels, 0)],
        (count,),
        [shaped((pixels, channels))],
        [block(channels)],
        after=after,
        passed=passed,
        into=into,
        flops=10**10,
    )


def sigmoid(values):
    return 0.5 + 0.5 * jnp.tanh(0.5 * values)


def silu(values):
    return values * sigmoid(values)


def silu_slope(values):
    sigmoid_val = sigmoid(values)
    return sigmoid_val * (1.0 + values * (1.0 - sigmoid_val))


def sums(values, validity):
    weighted = values * validity
    return jnp.stack([jnp.sum(weighted, axis=0), jnp.sum(weighted * values, axis=0)])


def coefs(totals, counted, gain, shift):
    mean_value = totals[0] / counted
    scaling = lax.rsqrt(totals[1] / counted - mean_value * mean_value + EPSILON)
    return jnp.stack([mean_value, scaling, gain, shift])


def through_norm(grad_pre, unit, coef, counted, validity, totals):
    centered = grad_pre - validity * (totals[0] + unit * totals[1]) / counted
    return coef[2] * coef[1] * centered


def to_tiles(array):
    height, breadth = array.shape[:2]
    rest = array.shape[2:]
    cut = array.reshape((height // TILE, TILE, breadth // TILE, TILE) + rest)
    return jnp.swapaxes(cut, 1, 2).reshape((height * breadth,) + rest)


def per_device(
    features,
    reduce_weight,
    spatial_weight,
    expand_weight,
    bottle_gain,
    bottle_shift,
    point_weight,
    near_weight,
    middle_weight,
    far_weight,
    image_weight,
    project_weight,
    class_weight,
    pyramid_gain,
    pyramid_shift,
    head_gain,
    head_shift,
    crop_masks,
    crop_tasks,
    pixel_labels,
    task_norms,
):
    place = Place()
    size, core = place.size, place.core
    first_core = core == 0
    height, breadth, channels = features.shape[2:]
    pixels = height * breadth
    tiles = (height // TILE, breadth // TILE, TILE * TILE)
    narrow = reduce_weight.shape[1]
    branch = point_weight.shape[1]
    four_wide = 4 * branch
    rows = channels // size
    narrow_rows = narrow // size
    quarters = channels // narrow
    turns = 3
    meta = place.meta()
    matrix = tile_matrix(breadth)

    bottle_taps = tap_list(height, breadth, BOTTLE_RATE)
    near_taps = tap_list(height, breadth, NEAR_RATE)
    middle_taps = tap_list(height, breadth, MIDDLE_RATE)
    far_taps = tap_list(height, breadth, FAR_RATE)
    point_taps = [(1, 1, 0, 0)]

    def center_of(taps):
        return [tap[:2] for tap in taps].index((1, 1))

    def stacked(weight, taps):
        flat = weight.reshape((-1,) + weight.shape[2:])
        picked = [3 * tap[0] + tap[1] for tap in taps]
        if picked == list(range(picked[0], picked[-1] + 1)):
            flat = flat[picked[0] : picked[-1] + 1]
        else:
            flat = jnp.stack([flat[at] for at in picked])
        return flat.reshape(-1, flat.shape[2]), len(taps)

    mask = lax.dynamic_index_in_dim(crop_masks, core, 0, keepdims=False)[0]
    labels = lax.dynamic_index_in_dim(pixel_labels, core, 0, keepdims=False)[0]
    task = lax.dynamic_index_in_dim(crop_tasks, core, 0, keepdims=False)[0]
    validity = to_tiles(mask).astype(F32)[:, None]
    valid_tiles = validity.reshape(tiles + (1,))
    labels = to_tiles(labels)
    source = tile_rows(features.reshape(pixels, channels), jnp.array(matrix, BF16))
    source_flipped = flipped(source)

    wide_expand = expand_weight.reshape(-1, quarters, narrow)
    expand_parts = [(wide_expand[:, at], 1) for at in range(quarters)]
    bottle_all = place.gather([(reduce_weight, 1), stacked(spatial_weight, bottle_taps)] + expand_parts)
    spatial_at = channels // narrow
    expand_at = spatial_at + len(bottle_taps)
    pyramid_parts = [stacked(near_weight, near_taps), stacked(middle_weight, middle_taps)]
    pyramid_parts += [stacked(far_weight, far_taps), (point_weight, 1), (project_weight, 1)]
    pyramid_all = place.gather(pyramid_parts)
    middle_at = len(near_taps)
    far_at = middle_at + len(middle_taps)
    point_at = far_at + len(far_taps)
    project_at = (point_at + 1) * (channels // place.pieces)
    project_full = pyramid_all[:, project_at:].reshape(-1, branch)

    crop_valid_both = jnp.sum(crop_masks, axis=(1, 2, 3)).astype(F32)
    home_crop = (crop_tasks[:, 0] == 1).astype(F32)
    counts = jnp.concatenate(
        [
            crop_valid_both,
            jnp.sum(crop_valid_both * (1.0 - home_crop))[None],
            jnp.sum(crop_valid_both * home_crop)[None],
        ]
    )
    small = [bottle_gain, bottle_shift, pyramid_gain, pyramid_shift, head_gain, head_shift]
    small.append(class_weight.reshape(-1))
    small_widths = [part.shape[0] for part in small]
    small_own = jnp.concatenate(small).astype(F32)
    collected = place.everyone(jnp.concatenate([small_own, counts]))
    counts_all = jnp.sum(collected[:, small_own.size :], axis=0)
    small_all, start = [], 0
    for width in small_widths:
        small_all.append(collected[:, start : start + width].reshape(-1))
        start += width
    gain_bottle, shift_bottle, gain_pyramid, shift_pyramid, gain_head, shift_head = small_all[:6]
    class_full = small_all[6].reshape(size * class_weight.shape[0], -1).astype(BF16)
    counted = jnp.where(first_core, counts_all[0], counts_all[1])
    task_pixels = counts_all[2:4]
    crop_valid = jnp.where(first_core, crop_valid_both[0], crop_valid_both[1])

    first, first_sums = first_conv(source, validity, bottle_all, turns, [source_flipped])
    coef_one = coefs(place.total(first_sums), counted, gain_bottle[:narrow], shift_bottle[:narrow])
    first_tiles = first.reshape(tiles + (narrow,))
    conv_in, second, second_sums = spatial_conv(
        first_tiles, coef_one, valid_tiles, bottle_all, bottle_taps, center_of(bottle_taps), spatial_at
    )
    second = second.reshape(pixels, narrow)
    coef_two = coefs(
        place.total(second_sums), counted, gain_bottle[narrow : 2 * narrow], shift_bottle[narrow : 2 * narrow]
    )
    middle_act, third, third_sums = third_conv(
        second, coef_two, validity, bottle_all, expand_at, quarters, turns
    )
    coef_three = coefs(
        place.total(third_sums), counted, gain_bottle[2 * narrow :], shift_bottle[2 * narrow :]
    )
    block_out, pooled_sum = block_output(third, source, coef_three, validity, tiles[0])
    block_tiles = block_out.reshape(tiles + (channels,))

    pooled = (pooled_sum / crop_valid).astype(BF16)
    pooled_all = place.everyone(pooled[0])
    pooled_rows = lax.dynamic_slice_in_dim(pooled_all, place.index * rows, rows, axis=1)
    image_all = place.total(jnp.dot(pooled_rows, image_weight, preferred_element_type=F32))
    branches, branch_sums = branch_convs(
        block_tiles,
        valid_tiles,
        pyramid_all,
        [
            (near_taps, branch),
            (middle_taps, 2 * branch),
            (far_taps, 3 * branch),
            (point_taps, 0),
        ],
        four_wide,
        [image_all],
    )
    branches = branches.reshape(pixels, four_wide)
    image_mean = jnp.sum(image_all, axis=0) / size
    image_scale = lax.rsqrt(
        jnp.sum(image_all * image_all, axis=0) / size - image_mean * image_mean + EPSILON
    )
    image_unit = (image_all - image_mean) * image_scale
    gain_image, shift_image = gain_pyramid[four_wide:], shift_pyramid[four_wide:]
    coef_image = jnp.stack([image_mean, image_scale, gain_image, shift_image])
    image_pre = gain_image * image_unit + shift_image
    image_act = silu(image_pre).astype(BF16)

    block_flipped = flipped(block_out, [branch_sums])
    conv_flipped = flipped(conv_in.reshape(pixels, narrow), [block_flipped])
    coef_branch = coefs(
        place.total(branch_sums), counted, gain_pyramid[:four_wide], shift_pyramid[:four_wide]
    )
    unit_branch, pre_branch = unit_of(branches, coef_branch)
    joined = silu(pre_branch).astype(BF16)

    own_act = lax.dynamic_slice_in_dim(image_act, place.index, 1, axis=0)
    crop_part = jnp.dot(own_act, project_full[four_wide:], preferred_element_type=F32)
    projected = jnp.dot(joined, project_full[:four_wide], preferred_element_type=F32) + crop_part
    coef_head = coefs(place.total(sums(projected, validity)), counted, gain_head, shift_head)
    unit_head, pre_head = unit_of(projected, coef_head)
    output_act = silu(pre_head).astype(BF16)
    logits = jnp.dot(output_act, class_full, preferred_element_type=F32)

    columns = jnp.arange(class_full.shape[1])
    allowed = (columns >= CITY_CLASSES) == (task == 1)
    masked = jnp.where(allowed, logits, FLOOR_LOGIT)
    raised = jnp.exp(masked - jnp.max(masked, axis=-1, keepdims=True))
    chances = raised / jnp.sum(raised, axis=-1, keepdims=True)
    target = jnp.where(task == 0, labels % CITY_CLASSES, CITY_CLASSES + labels % HOME_CLASSES)
    chosen = (columns == target[:, None]).astype(F32)
    inverse = 1.0 / task_norms.astype(F32)
    task_share = inverse / jnp.sum(inverse)
    crop_weight = jnp.where(
        task == 0, task_share[0] / task_pixels[0], task_share[1] / task_pixels[1]
    )
    logit_grad = (crop_weight * validity * (chances - chosen)).astype(BF16)
    class_grad = lax.dot_general(
        output_act, logit_grad, (((0,), (0,)), ((), ())), preferred_element_type=F32
    )

    output_grad = lax.dot_general(
        logit_grad, class_full, (((1,), (1,)), ((), ())), preferred_element_type=F32
    )
    grad_head = output_grad * silu_slope(pre_head)
    head_totals = place.total(grad_moments(grad_head, unit_head))
    proj_grad = through_norm(
        grad_head, unit_head, coef_head, counted, validity, head_totals
    ).astype(BF16)
    crop_grad = jnp.sum(proj_grad, axis=0, dtype=F32)
    joined_grad = lax.dot_general(
        proj_grad, project_full[:four_wide], (((1,), (1,)), ((), ())), preferred_element_type=F32
    )
    act_grad = jnp.dot(project_full[four_wide:].astype(F32), crop_grad, precision=HIGHEST)
    own_pre = lax.dynamic_slice_in_dim(image_pre, place.index, 1, axis=0)[0]
    image_pre_grad = act_grad * silu_slope(own_pre)
    grad_branch = joined_grad * silu_slope(pre_branch)
    branch_parts = place.everyone(
        jnp.concatenate([grad_moments(grad_branch, unit_branch).reshape(-1), image_pre_grad])
    )
    image_pre_all = branch_parts[:, 2 * four_wide :]
    branch_totals = jnp.sum(branch_parts[:, : 2 * four_wide], axis=0).reshape(2, four_wide)
    branch_grad = through_norm(
        grad_branch, unit_branch, coef_branch, counted, validity, branch_totals
    ).astype(BF16)
    image_totals = grad_moments(image_pre_all, image_unit)
    image_in_all = through_norm(
        image_pre_all, image_unit, coef_image, float(size), 1.0, image_totals
    )
    pooled_partial = lax.dot_general(
        image_in_all, image_weight.astype(F32), (((1,), (1,)), ((), ())), precision=HIGHEST
    )
    if place.direct:
        pooled_grad_all = lax.all_to_all(pooled_partial, "batch", 0, 0).reshape(1, channels)
    else:
        pooled_grad_all = lax.dynamic_slice_in_dim(
            lax.all_gather(pooled_partial, "batch", axis=1, tiled=True), place.index, 1, axis=0
        )
    image_partial = jnp.dot(pooled_rows.astype(F32).T, image_in_all, precision=HIGHEST)

    def columns_of(taps, block):
        return [block * branch] * len(taps)

    near_rows = row_plan(near_taps, columns_of(near_taps, 1))
    middle_rows = row_plan(middle_taps, columns_of(middle_taps, 2))
    far_row = row_plan(far_taps, columns_of(far_taps, 3))
    point_row = row_plan(point_taps, columns_of(point_taps, 0))
    project_grad = jnp.concatenate(
        [
            lax.dot_general(
                joined, proj_grad, (((0,), (0,)), ((), ())), preferred_element_type=F32
            ),
            own_act[0].astype(F32)[:, None] * crop_grad[None, :],
        ]
    )

    class_rows = class_grad.size // size // branch if place.direct else 0
    extra_rows = project_grad.shape[0] // size + class_rows

    def extra_halves():
        parts = [project_grad.reshape(size, 2, -1, branch), class_grad.reshape(size, 2, -1, branch)]
        spare = rows // 2 - extra_rows // 2
        parts.append(jnp.zeros((size, 2, spare, branch), F32))
        return jnp.concatenate(parts, axis=2).reshape(-1, branch).astype(BF16)

    def branch_weight_grad(plan, after, extra=None):
        return weight_grad(
            place, block_flipped, branch_grad, meta, plan, tiles, branch, after, extra
        )

    parts = 2 if place.direct else 1
    wide_grads = branch_weight_grad(
        middle_rows + far_row + point_row, [conv_flipped], extra_halves() if place.direct else None
    )
    wide_rows = [rows] * (len(middle_taps) + len(far_taps) + 1) + [extra_rows]
    if not place.direct:
        wide_grads = [jnp.concatenate([wide_grads[0], project_grad.astype(BF16)[None]], axis=1)]
        wide_rows = wide_rows[:-1] + [rows, rows] + wide_rows[-1:]
    wide_scatter = Scatter(place, wide_grads, wide_rows)
    near_grads = branch_weight_grad(near_rows, [wide_grads[0]])
    near_scatter = Scatter(place, near_grads, [rows] * len(near_taps))
    wide_scatter.first()

    pooled_grad = pooled_grad_all / crop_valid
    back_plan = [(far_row[0][0], far_row[0][1] + point_row[0][1])] + near_rows + middle_rows
    far_at = len(near_rows) + len(middle_rows)
    back_order = [far_at] + list(range(far_at))

    def half_back(side, after, scatters):
        low, moments, *passed = feature_back(
            branch_grad,
            pyramid_all,
            back_plan,
            back_order,
            3 * far_at + len(far_taps),
            third,
            source,
            coef_three,
            pooled_grad,
            validity,
            tiles,
            side,
            2,
            after,
            passing(scatters),
        )
        take_back(scatters, passed)
        return low, moments

    def sending(*scatters):
        return [array for scatter in scatters for array in scatter.sent]

    def passing(scatters):
        return [array for scatter in scatters for array in scatter.kept]

    def take_back(scatters, passed):
        for scatter in scatters:
            count = len(scatter.kept)
            scatter.kept, passed = passed[:count], passed[count:]

    low_grad, low_moments = half_back(0, [near_grads[0]] + sending(wide_scatter), [wide_scatter])
    high_grad, high_moments = half_back(1, [low_moments], [wide_scatter, near_scatter])
    wide_scatter.second()
    near_scatter.first()
    three_parts = place.total(low_moments, high_moments)
    three_totals = jnp.concatenate(three_parts, axis=1)

    grad_two, two_moments, *expand_grads = third_back(
        place,
        low_grad,
        high_grad,
        third,
        coef_three,
        three_totals / counted,
        validity,
        middle_act,
        second,
        coef_two,
        bottle_all,
        meta,
        expand_at,
        quarters,
        turns,
        sending(near_scatter, wide_scatter),
        passing([near_scatter, wide_scatter]),
    )
    take_back([near_scatter, wide_scatter], expand_grads[parts:])
    expand_grads = expand_grads[:parts]
    wide_scatter.third()
    wide_scatter.launch()
    near_scatter.second()
    unit_two, _ = unit_of(second, coef_two)
    two_totals = place.total(two_moments)
    second_grad = through_norm(
        grad_two, unit_two, coef_two, counted, validity, two_totals
    ).astype(BF16)
    spatial_rows = row_plan(bottle_taps, [0] * len(bottle_taps))
    spatial_grads = weight_grad(
        place,
        conv_flipped,
        second_grad,
        meta,
        spatial_rows,
        tiles,
        narrow,
        sending(wide_scatter, near_scatter),
        None,
        passing([wide_scatter, near_scatter]),
    )
    take_back([wide_scatter, near_scatter], spatial_grads[parts:])
    bottle_grads = [
        jnp.concatenate(pair, axis=1) for pair in zip(spatial_grads[:parts], expand_grads)
    ]
    bottle_rows = [narrow_rows] * (len(bottle_taps) + quarters)
    bottle_scatter = Scatter(place, bottle_grads, bottle_rows)
    near_scatter.third()
    grad_one, one_moments, *passed = spatial_back(
        second_grad,
        first,
        coef_one,
        validity,
        bottle_all,
        [spatial_rows[1], spatial_rows[0], spatial_rows[2]],
        [1, 0, 2],
        tiles,
        spatial_at,
        [spatial_grads[0]],
        passing([wide_scatter, near_scatter, bottle_scatter]) + near_scatter.sent,
    )
    held_back = len(passed) - len(near_scatter.sent)
    take_back([wide_scatter, near_scatter, bottle_scatter], passed[:held_back])
    near_scatter.sent = passed[held_back:]
    near_scatter.launch()
    if place.direct:
        one_moments = tied(one_moments, [bottle_scatter.arrived] + wide_scatter.arrived)
    bottle_scatter.first()
    one_totals = place.total(one_moments)
    unit_one, _ = unit_of(first, coef_one)
    first_grad = through_norm(
        grad_one, unit_one, coef_one, counted, validity, one_totals
    ).astype(BF16)
    reduce_grads = weight_grad(
        place,
        source_flipped,
        first_grad,
        meta,
        row_plan(point_taps, [0]),
        tiles,
        narrow,
        sending(bottle_scatter),
        None,
        passing([bottle_scatter, near_scatter]),
    )
    take_back([bottle_scatter, near_scatter], reduce_grads[parts:])
    reduce_scatter = Scatter(place, reduce_grads[:parts], [rows])
    bottle_scatter.second()

    def rows_back(first_turn, count, into, after, scatters):
        result, *passed = input_back(
            jnp.array(matrix.T, BF16),
            low_grad,
            high_grad,
            first_grad,
            bottle_all,
            turns,
            first_turn,
            count,
            after,
            passing(scatters),
            into,
        )
        take_back(scatters, passed)
        return result

    input_grad = rows_back(0, 2, None, sending(bottle_scatter), [bottle_scatter, reduce_scatter])
    reduce_scatter.first()
    bottle_scatter.third()
    bottle_scatter.launch()
    input_grad = rows_back(2, turns - 2, input_grad, sending(bottle_scatter, reduce_scatter), [bottle_scatter, reduce_scatter])
    reduce_scatter.second()
    reduce_scatter.third()
    reduce_scatter.launch()

    vectors = [one_totals, two_totals, three_totals, branch_totals, image_totals, head_totals]
    vectors += [image_partial]
    packed = jnp.concatenate([vector.reshape(-1) for vector in vectors])
    packed = packed + place.swap(packed)
    split, start = [], 0
    for vector in vectors:
        split.append(packed[start : start + vector.size].reshape(vector.shape))
        start += vector.size

    def own_part(vectors):
        vector = jnp.concatenate(vectors)
        length = vector.shape[0] // size
        return lax.dynamic_slice_in_dim(vector, place.index * length, length, axis=0)

    bottle_gain_grad = own_part([split[0][1], split[1][1], split[2][1]])
    bottle_shift_grad = own_part([split[0][0], split[1][0], split[2][0]])
    pyramid_gain_grad = own_part([split[3][1], split[4][1]])
    pyramid_shift_grad = own_part([split[3][0], split[4][0]])
    head_norm_grad = jnp.stack([own_part([split[5][1]]), own_part([split[5][0]])])
    image_out = split[6]

    def taps_out(full, taps, weight):
        full = full.reshape((len(taps),) + weight.shape[2:])
        if len(taps) == weight.shape[0] * weight.shape[1]:
            return full.reshape(weight.shape)
        result = jnp.zeros(weight.shape, F32)
        for at, tap in enumerate(taps):
            result = result.at[tap[0], tap[1]].set(full[at])
        return result

    for scatter in (near_scatter, wide_scatter, bottle_scatter, reduce_scatter):
        scatter.finish()
    near_count, middle_count, far_count = len(near_taps), len(middle_taps), len(far_taps)
    bottle_count = len(bottle_taps)
    expand_out = bottle_scatter.piece(bottle_count, quarters).reshape(quarters, narrow_rows, narrow)
    if place.direct:
        project_out, class_out = wide_scatter.extra([extra_rows - class_rows, class_rows])
    else:
        project_out = wide_scatter.piece(len(wide_rows) - 1, 1)
        class_out = own_part([lax.psum(class_grad, ("batch", "section"))])
    return (
        input_grad.reshape(features.shape),
        reduce_scatter.piece(0, 1),
        taps_out(bottle_scatter.piece(0, bottle_count), bottle_taps, spatial_weight),
        jnp.swapaxes(expand_out, 0, 1).reshape(expand_weight.shape),
        bottle_gain_grad,
        bottle_shift_grad,
        wide_scatter.piece(middle_count + far_count, 1),
        taps_out(near_scatter.piece(0, near_count), near_taps, near_weight),
        taps_out(wide_scatter.piece(0, middle_count), middle_taps, middle_weight),
        taps_out(wide_scatter.piece(middle_count, far_count), far_taps, far_weight),
        image_out,
        project_out,
        class_out.reshape(class_weight.shape),
        pyramid_gain_grad,
        pyramid_shift_grad,
        head_norm_grad,
    )


def solution(mesh):
    in_specs = (
        P("section", "batch", None, None, None),
        P("batch", None),
        P(None, None, "batch", None),
        P("batch", None),
        P("batch"),
        P("batch"),
        P("batch", None),
        P(None, None, "batch", None),
        P(None, None, "batch", None),
        P(None, None, "batch", None),
        P("batch", None),
        P("batch", None),
        P("batch", None),
        P("batch"),
        P("batch"),
        P("batch"),
        P("batch"),
        P(None, "batch", None, None),
        P(None, "batch"),
        P(None, "batch", None, None),
        P(),
    )
    out_specs = (
        P("section", "batch", None, None, None),
        P("batch", None),
        P(None, None, "batch", None),
        P("batch", None),
        P("batch"),
        P("batch"),
        P("batch", None),
        P(None, None, "batch", None),
        P(None, None, "batch", None),
        P(None, None, "batch", None),
        P("batch", None),
        P("batch", None),
        P("batch", None),
        P("batch"),
        P("batch"),
        P(None, "batch"),
    )
    return jax.shard_map(
        per_device, mesh=mesh, in_specs=in_specs, out_specs=out_specs, check_vma=False
    )
```
